32 devices in a mesh: grp: 4 (over z), wide: 8 (over y, x, core).
Axes of the slice: x: 2, y: 2, z: 4, core: 2. Of those that a mesh axis runs over, the one named last changes fastest.
Arguments:
- field: float32 [64, 8, 2048], P('wide', 'grp'), may hold values from -6 to 6
- conduct: float32 [64, 8, 2048], P('wide', 'grp'), may hold values from 0.05 to 0.5
- mode_index: int32 [8, 3], P('grp'), may hold values from 0 to 31
- mode_amp: float32 [8], P('grp'), may hold values from 0 to 0.0625
- mode_phase: float32 [8], P('grp'), may hold values from -3.140625 to 3.140625
- step_index: int32 [1], replicated, may hold values from 0 to 4095
Outputs:
- advanced: float32 [64, 8, 2048], P('wide', 'grp')
The draws below stay inside these ranges and needn't reach their ends.
All inputs are finite; a program needn't handle non-finite values.
Results may differ from the reference program's by a relative error of at most 0.0003.
Values sent between devices are 32-bit elements; how exact they have to be, the bound alone decides.
No kernel may reach another device: no remote copies, remote signals or barrier semaphores. Data moves between devices by JAX's collectives and lax.ppermute only.
A program may use at most 64 MiB of HBM per device.

```python
import math
import jax
import jax.numpy as jnp
from jax import lax

NX = 2048
NY = 64
NZ = 8
MODES = 8


def plant(array, own_key, low, largest):
    shape = array.shape
    place = [jax.random.randint(jax.random.fold_in(own_key, axis), (), 0, shape[axis]) for axis in range(len(shape))]
    array = array.at[tuple(place)].set(low)
    longest = shape.index(max(shape))
    place[longest] = (place[longest] + 1) % shape[longest]
    return array.at[tuple(place)].set(largest)


def block_scale(own_key, shape, pieces, smallest, largest):
    def one(axis_at, parts):
        draws = jax.random.uniform(jax.random.fold_in(jax.random.fold_in(own_key, 6), axis_at), (parts,), jnp.float32, smallest / len(pieces), largest / len(pieces))
        return jnp.repeat(jnp.exp(draws), shape[axis_at] // parts).reshape((-1,) + (1,) * (len(shape) - axis_at - 1))

    loudness = one(*pieces[0])
    for cut in pieces[1:]:
        loudness = loudness * one(*cut)
    return loudness


def gaussian(key, dims, width, limit, shards=(), held_as=jnp.bfloat16):
    entries = width * jax.random.normal(key, dims, jnp.float32)
    if shards:
        entries = entries * block_scale(key, dims, shards, -0.22, 0.18)
    return jnp.clip(entries, -limit, limit).astype(held_as)


def setup_inputs(seed: int = 0) -> dict:
    arg_keys = jax.random.split(jax.random.key(seed), 7)
    return {
        "field": gaussian(arg_keys[0], (NY, NZ, NX), 1.0, 6.0, ((0, 8), (1, 4)), jnp.float32),
        "conduct": jnp.clip(jnp.exp(math.log(0.5) - 2.3025851 * jax.random.uniform(arg_keys[1], (NY, NZ, NX), jnp.float32) ** block_scale(arg_keys[1], (NY, NZ, NX), ((0, 8), (1, 4)), -0.2, 0.2)), 0.05, 0.5),
        "mode_index": plant(jax.random.randint(arg_keys[2], (MODES, 3), 0, NY // 2), jax.random.fold_in(arg_keys[2], 1), 0, (NY // 2) - 1).astype(jnp.int32),
        "mode_amp": jnp.clip(0.0625 * jax.random.uniform(arg_keys[3], (MODES,), jnp.float32) ** block_scale(arg_keys[3], (MODES,), ((0, 4),), -0.2, 0.2), 0.0, 0.0625),
        "mode_phase": jnp.clip(jax.random.uniform(arg_keys[4], (MODES,), jnp.float32, -3.140625, 3.140625), -3.140625, 3.140625),
        "step_index": jax.random.randint(arg_keys[5], (1,), 0, 4096).astype(jnp.int32),
    }


time_step = 600.0
implicit_weight = 0.5
two_pi = 6.283185307179586


def boundary_height(mode_index, mode_amp, mode_phase, step_index, row_ids, col_ids, row_total, col_total):
    wave_x = mode_index[:, 0:1]
    wave_y = mode_index[:, 1:2]
    wave_time = mode_index[:, 2]
    moment = step_index[0]
    offset = mode_phase + (two_pi / 64.0) * ((wave_time * moment) % 64).astype(jnp.float32)
    angle_x = (two_pi / col_total) * ((wave_x * col_ids[None, :]) % col_total).astype(jnp.float32)
    angle_y = (two_pi / row_total) * ((wave_y * row_ids[None, :]) % row_total).astype(jnp.float32) + offset[:, None]
    left_cos = jnp.transpose(mode_amp[:, None] * jnp.cos(angle_y))
    left_sin = jnp.transpose(mode_amp[:, None] * jnp.sin(angle_y))
    part_cos = jnp.dot(left_cos, jnp.cos(angle_x), precision=lax.Precision.HIGHEST, preferred_element_type=jnp.float32)
    part_sin = jnp.dot(left_sin, jnp.sin(angle_x), precision=lax.Precision.HIGHEST, preferred_element_type=jnp.float32)
    return part_cos - part_sin


def face_values(coeff, axis):
    count = coeff.shape[axis]
    before = jnp.concatenate([lax.slice_in_dim(coeff, 0, 1, axis=axis), lax.slice_in_dim(coeff, 0, count - 1, axis=axis)], axis)
    after = jnp.concatenate([lax.slice_in_dim(coeff, 1, count, axis=axis), lax.slice_in_dim(coeff, count - 1, count, axis=axis)], axis)
    return 0.5 * (coeff + before), 0.5 * (coeff + after)


def spread(field, lower_face, upper_face, axis):
    count = field.shape[axis]
    zero_plane = jnp.zeros_like(lax.slice_in_dim(field, 0, 1, axis=axis))
    before = jnp.concatenate([zero_plane, lax.slice_in_dim(field, 0, count - 1, axis=axis)], axis)
    after = jnp.concatenate([lax.slice_in_dim(field, 1, count, axis=axis), zero_plane], axis)
    return upper_face * (after - field) - lower_face * (field - before)


def tridiagonal(lower_face, upper_face, axis):
    count = lower_face.shape[axis]
    weight = implicit_weight * time_step
    zero_plane = jnp.zeros_like(lax.slice_in_dim(lower_face, 0, 1, axis=axis))
    lower = jnp.concatenate([zero_plane, -weight * lax.slice_in_dim(lower_face, 1, count, axis=axis)], axis)
    upper = jnp.concatenate([-weight * lax.slice_in_dim(upper_face, 0, count - 1, axis=axis), zero_plane], axis)
    diagonal = 1.0 + weight * (lower_face + upper_face)
    return lower, diagonal, upper


def shift_forward(values, fill, axis):
    count = values.shape[axis]
    pad_plane = jnp.full_like(lax.slice_in_dim(values, 0, 1, axis=axis), fill)
    return jnp.concatenate([lax.slice_in_dim(values, 1, count, axis=axis), pad_plane], axis)


def shift_backward(values, axis):
    count = values.shape[axis]
    pad_plane = jnp.zeros_like(lax.slice_in_dim(values, 0, 1, axis=axis))
    return jnp.concatenate([pad_plane, lax.slice_in_dim(values, 0, count - 1, axis=axis)], axis)


def every_other(values, start, axis):
    return lax.slice_in_dim(values, start, values.shape[axis], 2, axis)


def cyclic_solve(lower, diagonal, upper, rhs, axis):
    count = rhs.shape[axis]
    if count == 1:
        return rhs / diagonal
    if count % 2 == 1:
        zero_plane = jnp.zeros_like(lax.slice_in_dim(rhs, 0, 1, axis=axis))
        padded = cyclic_solve(jnp.concatenate([lower, zero_plane], axis), jnp.concatenate([diagonal, zero_plane + 1.0], axis), jnp.concatenate([upper, zero_plane], axis), jnp.concatenate([rhs, zero_plane], axis), axis)
        return lax.slice_in_dim(padded, 0, count, axis=axis)
    low_even = every_other(lower, 0, axis)
    low_odd = every_other(lower, 1, axis)
    dia_even = every_other(diagonal, 0, axis)
    dia_odd = every_other(diagonal, 1, axis)
    up_even = every_other(upper, 0, axis)
    up_odd = every_other(upper, 1, axis)
    rhs_even = every_other(rhs, 0, axis)
    rhs_odd = every_other(rhs, 1, axis)
    low_next = shift_forward(low_even, 0.0, axis)
    dia_next = shift_forward(dia_even, 1.0, axis)
    up_next = shift_forward(up_even, 0.0, axis)
    rhs_next = shift_forward(rhs_even, 0.0, axis)
    alpha = -low_odd / dia_even
    gamma = -up_odd / dia_next
    reduced = cyclic_solve(alpha * low_even, dia_odd + alpha * up_even + gamma * low_next, gamma * up_next, rhs_odd + alpha * rhs_even + gamma * rhs_next, axis)
    before = shift_backward(reduced, axis)
    solved_even = (rhs_even - low_even * before - up_even * reduced) / dia_even
    joined = jnp.stack([solved_even, reduced], axis=axis + 1)
    return joined.reshape(rhs.shape)


def reference(field, conduct, mode_index, mode_amp, mode_phase, step_index):
    row_total, layer_total, col_total = field.shape
    height = boundary_height(mode_index, mode_amp, mode_phase, step_index, jnp.arange(row_total, dtype=jnp.int32), jnp.arange(col_total, dtype=jnp.int32), row_total, col_total)
    zeta = (jnp.arange(layer_total, dtype=jnp.int32).astype(jnp.float32) + 0.5) / layer_total
    jacobian = 1.0 + zeta[None, :, None] * height[:, None, :]
    across = conduct * jacobian
    x_lower, x_upper = face_values(across, 2)
    y_lower, y_upper = face_values(jacobian, 0)
    increment = time_step * (spread(field, x_lower, x_upper, 2) + spread(field, y_lower, y_upper, 0))
    lower, diagonal, upper = tridiagonal(x_lower, x_upper, 2)
    first = cyclic_solve(lower, diagonal, upper, increment, 2)
    lower, diagonal, upper = tridiagonal(y_lower, y_upper, 0)
    second = cyclic_solve(lower, diagonal, upper, first, 0)
    return field + second
```

```python
import functools
import math

import jax
import jax.numpy as jnp
from jax import lax
from jax.experimental import pallas as pl
from jax.experimental.pallas import tpu as pltpu
from jax.sharding import PartitionSpec as P

time_step = 600.0
implicit_weight = 0.5
weight = implicit_weight * time_step
LANES = 128
f32 = jnp.float32


def to_lines(block):
    rows, layers, columns = block.shape
    chunks = columns // LANES
    return (
        block.reshape(rows, layers, chunks, LANES)
        .transpose(0, 2, 1, 3)
        .reshape(rows * chunks * layers, LANES)
    )


def from_lines(lines, shape):
    rows, layers, columns = shape
    chunks = columns // LANES
    return (
        lines.reshape(rows, chunks, layers, LANES)
        .transpose(0, 2, 1, 3)
        .reshape(rows, layers, columns)
    )


def turns(wave, index, period):
    product = wave * index
    if period & (period - 1) == 0:
        product = product & (period - 1)
    else:
        product = lax.rem(product, jnp.int32(period))
    return product.astype(f32) * (1.0 / period)


def cos_sin(turn):
    part = turn - jnp.floor(turn + 0.5)
    square = part * part

    def series(first):
        terms = [
            (-1.0) ** n * math.pi ** (2 * n + first) / math.factorial(2 * n + first)
            for n in range(7)
        ]
        total = jnp.full_like(square, terms[-1])
        for term in terms[-2::-1]:
            total = total * square + term
        return total

    half_cos = series(0)
    half_sin = series(1) * part
    return 1.0 - 2.0 * half_sin * half_sin, 2.0 * half_sin * half_cos


def height_lines(modes, first_row, count, row_total, chunks, column_total):
    mode_count = modes.shape[0]
    wave_x = modes[:, 0:1].astype(jnp.int32)
    wave_y = modes[:, 1:2].astype(jnp.int32)
    offset = modes[:, 2:3]
    amp = modes[:, 3:4]
    spot = lax.broadcasted_iota(jnp.int32, (mode_count, count * chunks), 1)
    chunk = spot % chunks
    row = jnp.clip(first_row + spot // chunks, 0, row_total - 1)
    angle = (
        turns(wave_y, row, row_total) + turns(wave_x, chunk * LANES, column_total)
    ) + offset
    left_cos, left_sin = cos_sin(angle)
    lane = lax.broadcasted_iota(jnp.int32, (mode_count, LANES), 1)
    right_cos, right_sin = cos_sin(turns(wave_x, lane, column_total))
    left = jnp.concatenate([amp * left_cos, amp * left_sin], 0)
    right = jnp.concatenate([right_cos, -right_sin], 0)
    return lax.dot_general(
        left,
        right,
        (((0,), (0,)), ((), ())),
        precision=lax.Precision.HIGHEST,
        preferred_element_type=f32,
    )


def inverse(values):
    return pl.reciprocal(values, approx=False)


def from_left(values, stride, lane):
    moved = [pltpu.roll(v, stride, 1) for v in values]
    return [jnp.where(lane < stride, moved[c - 1], moved[c]) for c in range(len(values))]


def from_right(values, stride, lane):
    count = len(values)
    moved = [pltpu.roll(v, LANES - stride, 1) for v in values]
    return [
        jnp.where(lane >= LANES - stride, moved[(c + 1) % count], moved[c]) for c in range(count)
    ]


def solve_chunks(diagonal, link, rhs):
    count = len(rhs)
    if count == 1:
        return [rhs[0] * inverse(diagonal[0])]
    inv = {i: inverse(diagonal[i]) for i in range(0, count, 2)}
    scaled = {i: inv[i] * rhs[i] for i in inv}
    odd_diagonal, odd_link, odd_rhs = [], [], []
    for i in range(1, count, 2):
        d = diagonal[i] - link[i - 1] * (link[i - 1] * inv[i - 1])
        r = rhs[i] + link[i - 1] * scaled[i - 1]
        e = None
        if i + 1 < count:
            by = link[i] * inv[i + 1]
            d = d - link[i] * by
            r = r + link[i] * scaled[i + 1]
            e = by * link[i + 1] if i + 2 < count else None
        odd_diagonal.append(d)
        odd_rhs.append(r)
        odd_link.append(e)
    odd = solve_chunks(odd_diagonal, odd_link, odd_rhs)
    out = [None] * count
    out[1::2] = odd
    for i in range(0, count, 2):
        r = rhs[i]
        if i > 0:
            r = r + link[i - 1] * out[i - 1]
        if i + 1 < count:
            r = r + link[i] * out[i + 1]
        out[i] = r * inv[i]
    return out


def solve_x(diagonal, link, rhs, lane):
    stride = 1
    count = len(rhs)
    while stride < LANES:
        inv = [inverse(d) for d in diagonal]
        t = [q * r for q, r in zip(inv, rhs)]
        w = [q * e for q, e in zip(inv, link)]
        low_d = from_left([e * v for e, v in zip(link, w)], stride, lane)
        low_r = from_left([e * v for e, v in zip(link, t)], stride, lane)
        high_q = from_right(inv, stride, lane)
        high_t = from_right(t, stride, lane)
        high_w = from_right(w, stride, lane)
        diagonal = [
            diagonal[c] - low_d[c] - link[c] * (link[c] * high_q[c]) for c in range(count)
        ]
        rhs = [rhs[c] + low_r[c] + link[c] * high_t[c] for c in range(count)]
        link = [link[c] * high_w[c] for c in range(count)]
        stride *= 2
    return solve_chunks(diagonal, link, rhs)


def pack_kernel(index_ref, amp_ref, phase_ref, step_ref, out_ref):
    count = index_ref.shape[0]
    row = lax.broadcasted_iota(jnp.int32, out_ref.shape, 0)
    lane = lax.broadcasted_iota(jnp.int32, out_ref.shape, 1)
    total = jnp.zeros(out_ref.shape, f32)
    for m in range(count):
        moment = lax.rem(index_ref[m, 2] * step_ref[0], jnp.int32(64)).astype(f32)
        offset = phase_ref[m] * (0.5 / math.pi) + moment * (1.0 / 64.0)
        for place, value in enumerate(
            (index_ref[m, 0].astype(f32), index_ref[m, 1].astype(f32), offset, amp_ref[m])
        ):
            total = jnp.where((row == m) & (lane == place), value, total)
    out_ref[...] = total


def first_kernel(
    sizes, modes_ref, field_ref, low_ref, high_ref, conduct_ref,
    sent_ref, p_ref, u_ref, v_ref, framed, heights, solved,
):
    rows, layers, chunks, row_total, layer_total, column_total = sizes
    width = layers * chunks
    first_row = lax.axis_index("wide") * rows
    first_layer = lax.axis_index("grp") * layers
    zeta = [
        ((first_layer + k).astype(f32) + 0.5) * (1.0 / layer_total) for k in range(layers)
    ]
    framed[0:width] = low_ref[...]
    framed[width : (rows + 1) * width] = field_ref[...]
    framed[(rows + 1) * width : (rows + 2) * width] = high_ref[...]
    heights[...] = height_lines(
        modes_ref[...], first_row - 1, rows + 2, row_total, chunks, column_total
    )
    lane = lax.broadcasted_iota(jnp.int32, (rows, LANES), 1)
    at_start = lane == 0
    at_end = lane == LANES - 1
    half = 0.5 * weight

    for k in range(layers):
        g, f, along = [], [], []
        for c in range(chunks):
            jac_low, jac, jac_high = (
                1.0 + zeta[k] * heights[pl.ds(s * chunks + c, rows, stride=chunks), :]
                for s in range(3)
            )
            place = c * layers + k
            f_low, f_mid, f_high = (
                framed[pl.ds(s * width + place, rows, stride=width), :] for s in range(3)
            )
            g.append(conduct_ref[pl.ds(place, rows, stride=width), :] * jac)
            f.append(f_mid)
            along.append(
                half * (jac + jac_high) * (f_high - f_mid)
                - half * (jac + jac_low) * (f_mid - f_low)
            )
        g_next = from_right(g, 1, lane)
        f_next = from_right(f, 1, lane)
        g_next[-1] = jnp.where(at_end, g[-1], g_next[-1])
        f_next[-1] = jnp.where(at_end, 0.0, f_next[-1])
        face = [half * (a + b) for a, b in zip(g, g_next)]
        flux = [e * (b - a) for e, a, b in zip(face, f, f_next)]
        face_low = from_left(face, 1, lane)
        flux_low = from_left(flux, 1, lane)
        edge = weight * g[0]
        face_low[0] = jnp.where(at_start, edge, face_low[0])
        flux_low[0] = jnp.where(at_start, edge * f[0], flux_low[0])
        diagonal = [1.0 + (a + b) for a, b in zip(face, face_low)]
        rhs = [2.0 * (a - b + y) for a, b, y in zip(flux, flux_low, along)]
        link = face
        link[-1] = jnp.where(at_end, 0.0, link[-1])
        first = solve_x(diagonal, link, rhs, lane)
        for c in range(chunks):
            solved[pl.ds(k * chunks + c, rows, stride=width), :] = first[c]

    jac = [
        jnp.concatenate(
            [1.0 + zeta[k] * heights[j * chunks : (j + 1) * chunks] for k in range(layers)], 0
        )
        for j in range(rows + 2)
    ]
    face = [half * (jac[j] + jac[j + 1]) for j in range(rows + 1)]
    p, u, v = [], [], []
    for j in range(rows):
        r = solved[j * width : (j + 1) * width]
        d = 1.0 + (face[j] + face[j + 1])
        if j == 0:
            inv = inverse(d)
            p.append(r * inv)
            u.append(face[0] * inv)
        else:
            inv = inverse(d - face[j] * v[-1])
            scaled = face[j] * inv
            p.append(r * inv + scaled * p[-1])
            u.append(scaled * u[-1])
        v.append(face[j + 1] * inv)
    for j in range(rows - 2, -1, -1):
        p[j] = p[j] + v[j] * p[j + 1]
        u[j] = u[j] + v[j] * u[j + 1]
        v[j] = v[j] * v[j + 1]
    sent_ref[0:width] = p[0]
    sent_ref[width : 2 * width] = p[-1]
    for j in range(rows):
        p_ref[j * width : (j + 1) * width] = p[j]
        u_ref[j * width : (j + 1) * width] = u[j]
        v_ref[j * width : (j + 1) * width] = v[j]


def matrix_kernel(
    sizes, modes_ref, left_gain_ref, left_link_ref, right_gain_ref, right_link_ref, heights, ends
):
    rows, layers, chunks, row_total, layer_total, column_total = sizes
    width = layers * chunks
    blocks = row_total // rows
    first_layer = lax.axis_index("grp") * layers
    zeta = [
        ((first_layer + k).astype(f32) + 0.5) * (1.0 / layer_total) for k in range(layers)
    ]
    half = 0.5 * weight
    body = height_lines(modes_ref[...], 0, row_total, row_total, chunks, column_total)
    heights[chunks : (row_total + 1) * chunks] = body
    heights[0:chunks] = body[0:chunks]
    heights[(row_total + 1) * chunks : (row_total + 2) * chunks] = body[
        (row_total - 1) * chunks : row_total * chunks
    ]

    def condense(b):
        start = b * (rows * chunks)
        jac = []
        for j in range(rows + 2):
            h = heights[pl.ds(pl.multiple_of(start + j * chunks, 8), chunks), :]
            jac.append(jnp.concatenate([1.0 + z * h for z in zeta], 0))
        face = [half * (jac[j] + jac[j + 1]) for j in range(rows + 1)]
        u, v = [], []
        for j in range(rows):
            d = 1.0 + (face[j] + face[j + 1])
            if j == 0:
                inv = inverse(d)
                u.append(face[0] * inv)
            else:
                inv = inverse(d - face[j] * v[-1])
                u.append(face[j] * inv * u[-1])
            v.append(face[j + 1] * inv)
        u_last, v_last = u[-1], v[-1]
        u_first, v_first = u_last, v_last
        for j in range(rows - 2, -1, -1):
            u_first = u[j] + v[j] * u_first
            v_first = v[j] * v_first
        base = b * (4 * width)
        for n, value in enumerate((u_first, v_first, u_last, v_last)):
            ends[pl.ds(pl.multiple_of(base + n * width, 8), width), :] = value

    group = 4 if blocks % 4 == 0 else 1

    def several(step, carry):
        for n in range(group):
            condense(step * group + n)
        return carry

    lax.fori_loop(0, blocks // group, several, 0)

    def end(b, n):
        return ends[(4 * b + n) * width : (4 * b + n + 1) * width]

    left = jnp.zeros((width, LANES), f32)
    right = jnp.zeros((width, LANES), f32)
    for b in range(blocks):
        u_first, v_first, u_last, v_last = (end(b, n) for n in range(4))
        gain = u_last * inverse(1.0 - u_first * left)
        left_gain_ref[b * width : (b + 1) * width] = gain
        left_link_ref[b * width : (b + 1) * width] = left
        left = v_last + gain * left * v_first
        b = blocks - 1 - b
        u_first, v_first, u_last, v_last = (end(b, n) for n in range(4))
        gain = v_first * inverse(1.0 - v_last * right)
        right_gain_ref[b * width : (b + 1) * width] = gain
        right_link_ref[b * width : (b + 1) * width] = right
        right = u_first + gain * right * u_last


def last_kernel(
    sizes, all_ref, left_gain_ref, left_link_ref, right_gain_ref, right_link_ref,
    p_ref, u_ref, v_ref, field_ref, out_ref,
):
    rows, layers, chunks, row_total, layer_total, column_total = sizes
    width = layers * chunks
    blocks = row_total // rows
    me = lax.axis_index("wide")

    def part(ref, b):
        return ref[b * width : (b + 1) * width]

    left = jnp.zeros((width, LANES), f32)
    right = jnp.zeros((width, LANES), f32)
    for b in range(blocks - 1):
        first, last = part(all_ref, 2 * b), part(all_ref, 2 * b + 1)
        moved = last + part(left_gain_ref, b) * (left + part(left_link_ref, b) * first)
        left = jnp.where(b < me, moved, left)
        b = blocks - 1 - b
        first, last = part(all_ref, 2 * b), part(all_ref, 2 * b + 1)
        moved = first + part(right_gain_ref, b) * (right + part(right_link_ref, b) * last)
        right = jnp.where(b > me, moved, right)

    own = pl.ds(pl.multiple_of(me * width, 8), width)
    left_link, right_link = left_link_ref[own, :], right_link_ref[own, :]
    p_first, u_first, v_first = (part(ref, 0) for ref in (p_ref, u_ref, v_ref))
    p_last, u_last, v_last = (part(ref, rows - 1) for ref in (p_ref, u_ref, v_ref))
    a = 1.0 - left_link * u_first
    b = left_link * v_first
    c = right_link * u_last
    d = 1.0 - right_link * v_last
    y = left + left_link * p_first
    z = right + right_link * p_last
    inv = inverse(a * d - b * c)
    before = (d * y + b * z) * inv
    after = (c * y + a * z) * inv
    for j in range(rows):
        x = part(p_ref, j) + part(u_ref, j) * before + part(v_ref, j) * after
        for k in range(layers):
            spot = pl.ds(j * width + k, chunks, stride=layers)
            out_ref[spot, :] = field_ref[spot, :] + x[k * chunks : (k + 1) * chunks]


def on_device(field, conduct, mode_index, mode_amp, mode_phase, step_index):
    rows, layers, columns = field.shape
    wide_count = lax.axis_size("wide")
    row_total = rows * wide_count
    layer_total = layers * lax.axis_size("grp")
    chunks = columns // LANES
    width = layers * chunks
    sizes = (rows, layers, chunks, row_total, layer_total, columns)
    smem = pl.BlockSpec(memory_space=pltpu.SMEM)

    field_lines = to_lines(field)
    conduct_lines = to_lines(conduct)
    forward = [(i, i + 1) for i in range(wide_count - 1)]
    backward = [(target, source) for source, target in forward]
    low = lax.ppermute(field_lines[(rows - 1) * width :], "wide", forward)
    high = lax.ppermute(field_lines[:width], "wide", backward)

    packed = pl.pallas_call(
        pack_kernel,
        out_shape=jax.ShapeDtypeStruct((mode_index.shape[0], 8), f32),
        in_specs=[smem] * 4,
    )(mode_index, mode_amp, mode_phase, step_index)
    modes = lax.all_gather(packed, "grp", axis=0, tiled=True)

    def lines(count):
        return jax.ShapeDtypeStruct((count * width, LANES), f32)

    sent, p, u, v = pl.pallas_call(
        functools.partial(first_kernel, sizes),
        out_shape=(lines(2), lines(rows), lines(rows), lines(rows)),
        scratch_shapes=[
            pltpu.VMEM(((rows + 2) * width, LANES), f32),
            pltpu.VMEM(((rows + 2) * chunks, LANES), f32),
            pltpu.VMEM((rows * width, LANES), f32),
        ],
        compiler_params=pltpu.CompilerParams(vmem_limit_bytes=16 * 1024 * 1024),
    )(modes, field_lines, low, high, conduct_lines)

    gathered = lax.all_gather(sent, "wide", axis=0, tiled=True)

    scans = pl.pallas_call(
        functools.partial(matrix_kernel, sizes),
        out_shape=(lines(wide_count),) * 4,
        scratch_shapes=[
            pltpu.VMEM(((row_total + 2) * chunks, LANES), f32),
            pltpu.VMEM((4 * wide_count * width, LANES), f32),
        ],
        compiler_params=pltpu.CompilerParams(vmem_limit_bytes=16 * 1024 * 1024),
    )(modes)

    advanced = pl.pallas_call(
        functools.partial(last_kernel, sizes),
        out_shape=lines(rows),
        compiler_params=pltpu.CompilerParams(vmem_limit_bytes=16 * 1024 * 1024),
    )(gathered, *scans, p, u, v, field_lines)
    return from_lines(advanced, field.shape)


def solution(mesh):
    return jax.shard_map(
        on_device,
        mesh=mesh,
        in_specs=(
            P("wide", "grp", None),
            P("wide", "grp", None),
            P("grp", None),
            P("grp"),
            P("grp"),
            P(),
        ),
        out_specs=P("wide", "grp", None),
        check_vma=False,
    )
```

```python
import functools
import math

import jax
import jax.numpy as jnp
from jax import lax
from jax.experimental import pallas as pl
from jax.experimental.pallas import tpu as pltpu
from jax.sharding import PartitionSpec as P

time_step = 600.0
implicit_weight = 0.5
weight = implicit_weight * time_step
LANES = 128
f32 = jnp.float32


def to_lines(block):
    rows, layers, columns = block.shape
    chunks = columns // LANES
    return (
        block.reshape(rows, layers, chunks, LANES)
        .transpose(0, 2, 1, 3)
        .reshape(rows * chunks * layers, LANES)
    )


def from_lines(lines, shape):
    rows, layers, columns = shape
    chunks = columns // LANES
    return (
        lines.reshape(rows, chunks, layers, LANES)
        .transpose(0, 2, 1, 3)
        .reshape(rows, layers, columns)
    )


def turns(wave, index, period):
    product = wave * index
    if period & (period - 1) == 0:
        product = product & (period - 1)
    else:
        product = lax.rem(product, jnp.int32(period))
    return product.astype(f32) * (1.0 / period)


def cos_sin(turn):
    part = turn - jnp.floor(turn + 0.5)
    square = part * part

    def series(first):
        terms = [
            (-1.0) ** n * math.pi ** (2 * n + first) / math.factorial(2 * n + first)
            for n in range(7)
        ]
        total = jnp.full_like(square, terms[-1])
        for term in terms[-2::-1]:
            total = total * square + term
        return total

    half_cos = series(0)
    half_sin = series(1) * part
    return 1.0 - 2.0 * half_sin * half_sin, 2.0 * half_sin * half_cos


def height_lines(modes, first_row, count, row_total, chunks, column_total):
    mode_count = modes.shape[0]
    wave_x = modes[:, 0:1].astype(jnp.int32)
    wave_y = modes[:, 1:2].astype(jnp.int32)
    offset = modes[:, 2:3]
    amp = modes[:, 3:4]
    spot = lax.broadcasted_iota(jnp.int32, (mode_count, count * chunks), 1)
    chunk = spot % chunks
    row = jnp.clip(first_row + spot // chunks, 0, row_total - 1)
    angle = (
        turns(wave_y, row, row_total) + turns(wave_x, chunk * LANES, column_total)
    ) + offset
    left_cos, left_sin = cos_sin(angle)
    lane = lax.broadcasted_iota(jnp.int32, (mode_count, LANES), 1)
    right_cos, right_sin = cos_sin(turns(wave_x, lane, column_total))
    left = jnp.concatenate([amp * left_cos, amp * left_sin], 0)
    right = jnp.concatenate([right_cos, -right_sin], 0)
    return lax.dot_general(
        left,
        right,
        (((0,), (0,)), ((), ())),
        precision=lax.Precision.HIGHEST,
        preferred_element_type=f32,
    )


def inverse(values):
    return pl.reciprocal(values, approx=False)


def from_left(values, stride, lane):
    moved = [pltpu.roll(v, stride, 1) for v in values]
    return [jnp.where(lane < stride, moved[c - 1], moved[c]) for c in range(len(values))]


def from_right(values, stride, lane):
    count = len(values)
    moved = [pltpu.roll(v, LANES - stride, 1) for v in values]
    return [
        jnp.where(lane >= LANES - stride, moved[(c + 1) % count], moved[c]) for c in range(count)
    ]


def solve_chunks(diagonal, link, rhs):
    count = len(rhs)
    if count == 1:
        return [rhs[0] * inverse(diagonal[0])]
    inv = {i: inverse(diagonal[i]) for i in range(0, count, 2)}
    scaled = {i: inv[i] * rhs[i] for i in inv}
    odd_diagonal, odd_link, odd_rhs = [], [], []
    for i in range(1, count, 2):
        d = diagonal[i] - link[i - 1] * (link[i - 1] * inv[i - 1])
        r = rhs[i] + link[i - 1] * scaled[i - 1]
        e = None
        if i + 1 < count:
            by = link[i] * inv[i + 1]
            d = d - link[i] * by
            r = r + link[i] * scaled[i + 1]
            e = by * link[i + 1] if i + 2 < count else None
        odd_diagonal.append(d)
        odd_rhs.append(r)
        odd_link.append(e)
    odd = solve_chunks(odd_diagonal, odd_link, odd_rhs)
    out = [None] * count
    out[1::2] = odd
    for i in range(0, count, 2):
        r = rhs[i]
        if i > 0:
            r = r + link[i - 1] * out[i - 1]
        if i + 1 < count:
            r = r + link[i] * out[i + 1]
        out[i] = r * inv[i]
    return out


def solve_x(diagonal, link, rhs, lane):
    stride = 1
    count = len(rhs)
    while stride < LANES:
        inv = [inverse(d) for d in diagonal]
        t = [q * r for q, r in zip(inv, rhs)]
        w = [q * e for q, e in zip(inv, link)]
        low_d = from_left([e * v for e, v in zip(link, w)], stride, lane)
        low_r = from_left([e * v for e, v in zip(link, t)], stride, lane)
        high_q = from_right(inv, stride, lane)
        high_t = from_right(t, stride, lane)
        high_w = from_right(w, stride, lane)
        diagonal = [
            diagonal[c] - low_d[c] - link[c] * (link[c] * high_q[c]) for c in range(count)
        ]
        rhs = [rhs[c] + low_r[c] + link[c] * high_t[c] for c in range(count)]
        link = [link[c] * high_w[c] for c in range(count)]
        stride *= 2
    return solve_chunks(diagonal, link, rhs)


def load_kernel(
    index_ref, amp_ref, phase_ref, step_ref, field_ref, conduct_ref,
    packed_ref, field_out, conduct_out, top_ref, bottom_ref,
    index_in, amp_in, phase_in, step_in, sems,
):
    width = top_ref.shape[0]
    size = field_ref.shape[0]
    pairs = (
        (index_ref, index_in),
        (amp_ref, amp_in),
        (phase_ref, phase_in),
        (step_ref, step_in),
        (field_ref.at[pl.ds(0, width)], top_ref),
        (field_ref.at[pl.ds(size - width, width)], bottom_ref),
        (field_ref, field_out),
        (conduct_ref, conduct_out),
    )
    copies = [pltpu.make_async_copy(a, b, sems.at[n]) for n, (a, b) in enumerate(pairs)]
    for copy in copies:
        copy.start()
    for copy in copies[:4]:
        copy.wait()
    count = index_in.shape[0]
    row = lax.broadcasted_iota(jnp.int32, packed_ref.shape, 0)
    lane = lax.broadcasted_iota(jnp.int32, packed_ref.shape, 1)
    total = jnp.zeros(packed_ref.shape, f32)
    for m in range(count):
        moment = lax.rem(index_in[m, 2] * step_in[0], jnp.int32(64)).astype(f32)
        offset = phase_in[m] * (0.5 / math.pi) + moment * (1.0 / 64.0)
        for place, value in enumerate(
            (index_in[m, 0].astype(f32), index_in[m, 1].astype(f32), offset, amp_in[m])
        ):
            total = jnp.where((row == m) & (lane == place), value, total)
    packed_ref[...] = total
    for copy in copies[4:]:
        copy.wait()


def condense(face):
    u, v = [], []
    rows = len(face) - 1
    for j in range(rows):
        d = 1.0 + (face[j] + face[j + 1])
        if j == 0:
            inv = inverse(d)
            u.append(face[0] * inv)
        else:
            inv = inverse(d - face[j] * v[-1])
            u.append(face[j] * inv * u[-1])
        v.append(face[j + 1] * inv)
    u_first, v_first = u[-1], v[-1]
    for j in range(rows - 2, -1, -1):
        u_first = u[j] + v[j] * u_first
        v_first = v[j] * v_first
    return u_first, v_first, u[-1], v[-1]


def main_kernel(
    sizes, modes_ref, field_ref, low_ref, high_ref, conduct_ref,
    sent_ref, p_ref, u_ref, v_ref, left_gain_ref, left_link_ref, right_gain_ref, right_link_ref,
    framed, heights, solved, ends,
):
    rows, layers, chunks, row_total, layer_total, column_total = sizes
    width = layers * chunks
    blocks = row_total // rows
    me = lax.axis_index("wide")
    first_layer = lax.axis_index("grp") * layers
    zeta = [
        ((first_layer + k).astype(f32) + 0.5) * (1.0 / layer_total) for k in range(layers)
    ]
    half = 0.5 * weight
    framed[0:width] = low_ref[...]
    framed[width : (rows + 1) * width] = field_ref[...]
    framed[(rows + 1) * width : (rows + 2) * width] = high_ref[...]
    body = height_lines(modes_ref[...], 0, row_total, row_total, chunks, column_total)
    heights[chunks : (row_total + 1) * chunks] = body
    heights[0:chunks] = body[0:chunks]
    heights[(row_total + 1) * chunks : (row_total + 2) * chunks] = body[
        (row_total - 1) * chunks : row_total * chunks
    ]
    lane = lax.broadcasted_iota(jnp.int32, (rows, LANES), 1)
    at_start = lane == 0
    at_end = lane == LANES - 1

    def faces(start):
        jac = []
        for j in range(rows + 2):
            h = heights[pl.ds(start + j * chunks, chunks), :]
            jac.append(jnp.concatenate([1.0 + z * h for z in zeta], 0))
        return [half * (jac[j] + jac[j + 1]) for j in range(rows + 1)]

    def block_ends(b):
        start, base = b * (rows * chunks), b * (4 * width)
        if not isinstance(b, int):
            start, base = pl.multiple_of(start, 8), pl.multiple_of(base, 8)
        for n, value in enumerate(condense(faces(start))):
            ends[pl.ds(base + n * width, width), :] = value

    if blocks <= 8:
        for b in range(blocks):
            block_ends(b)
    else:
        lax.fori_loop(0, blocks, lambda b, carry: (block_ends(b), carry)[1], 0)

    def end(b, n):
        return ends[(4 * b + n) * width : (4 * b + n + 1) * width]

    left = jnp.zeros((width, LANES), f32)
    right = jnp.zeros((width, LANES), f32)
    for b in range(blocks):
        u_first, v_first, u_last, v_last = (end(b, n) for n in range(4))
        gain = u_last * inverse(1.0 - u_first * left)
        left_gain_ref[b * width : (b + 1) * width] = gain
        left_link_ref[b * width : (b + 1) * width] = left
        left = v_last + gain * left * v_first
        b = blocks - 1 - b
        u_first, v_first, u_last, v_last = (end(b, n) for n in range(4))
        gain = v_first * inverse(1.0 - v_last * right)
        right_gain_ref[b * width : (b + 1) * width] = gain
        right_link_ref[b * width : (b + 1) * width] = right
        right = u_first + gain * right * u_last

    own_heights = pl.multiple_of(me * (rows * chunks), 8)
    for k in range(layers):
        g, f, along = [], [], []
        for c in range(chunks):
            jac_low, jac, jac_high = (
                1.0 + zeta[k] * heights[pl.ds(own_heights + s * chunks + c, rows, stride=chunks), :]
                for s in range(3)
            )
            place = c * layers + k
            f_low, f_mid, f_high = (
                framed[pl.ds(s * width + place, rows, stride=width), :] for s in range(3)
            )
            g.append(conduct_ref[pl.ds(place, rows, stride=width), :] * jac)
            f.append(f_mid)
            along.append(
                half * (jac + jac_high) * (f_high - f_mid)
                - half * (jac + jac_low) * (f_mid - f_low)
            )
        g_next = from_right(g, 1, lane)
        f_next = from_right(f, 1, lane)
        g_next[-1] = jnp.where(at_end, g[-1], g_next[-1])
        f_next[-1] = jnp.where(at_end, 0.0, f_next[-1])
        face = [half * (a + b) for a, b in zip(g, g_next)]
        flux = [e * (b - a) for e, a, b in zip(face, f, f_next)]
        face_low = from_left(face, 1, lane)
        flux_low = from_left(flux, 1, lane)
        edge = weight * g[0]
        face_low[0] = jnp.where(at_start, edge, face_low[0])
        flux_low[0] = jnp.where(at_start, edge * f[0], flux_low[0])
        diagonal = [1.0 + (a + b) for a, b in zip(face, face_low)]
        rhs = [2.0 * (a - b + y) for a, b, y in zip(flux, flux_low, along)]
        link = face
        link[-1] = jnp.where(at_end, 0.0, link[-1])
        first = solve_x(diagonal, link, rhs, lane)
        for c in range(chunks):
            solved[pl.ds(k * chunks + c, rows, stride=width), :] = first[c]

    face = faces(own_heights)
    p, u, v = [], [], []
    for j in range(rows):
        r = solved[j * width : (j + 1) * width]
        d = 1.0 + (face[j] + face[j + 1])
        if j == 0:
            inv = inverse(d)
            p.append(r * inv)
            u.append(face[0] * inv)
        else:
            inv = inverse(d - face[j] * v[-1])
            scaled = face[j] * inv
            p.append(r * inv + scaled * p[-1])
            u.append(scaled * u[-1])
        v.append(face[j + 1] * inv)
    for j in range(rows - 2, -1, -1):
        p[j] = p[j] + v[j] * p[j + 1]
        u[j] = u[j] + v[j] * u[j + 1]
        v[j] = v[j] * v[j + 1]
    for j in range(rows):
        p_ref[j * width : (j + 1) * width] = p[j]
        u_ref[j * width : (j + 1) * width] = u[j]
        v_ref[j * width : (j + 1) * width] = v[j]

    own = pl.ds(pl.multiple_of(me * width, 8), width)
    upward = p[-1] + left_gain_ref[own, :] * (left_link_ref[own, :] * p[0])
    downward = p[0] + right_gain_ref[own, :] * (right_link_ref[own, :] * p[-1])
    for b in range(blocks):
        sent_ref[b * width : (b + 1) * width] = jnp.where(b > me, upward, downward)


def last_kernel(
    sizes, came_ref, left_gain_ref, left_link_ref, right_gain_ref, right_link_ref,
    p_ref, u_ref, v_ref, field_ref, out_ref,
):
    rows, layers, chunks, row_total, layer_total, column_total = sizes
    width = layers * chunks
    blocks = row_total // rows
    me = lax.axis_index("wide")

    def part(ref, b):
        return ref[b * width : (b + 1) * width]

    left = jnp.zeros((width, LANES), f32)
    right = jnp.zeros((width, LANES), f32)
    for b in range(blocks - 1):
        left = jnp.where(b < me, part(came_ref, b) + part(left_gain_ref, b) * left, left)
        b = blocks - 1 - b
        right = jnp.where(b > me, part(came_ref, b) + part(right_gain_ref, b) * right, right)

    own = pl.ds(pl.multiple_of(me * width, 8), width)
    left_link, right_link = left_link_ref[own, :], right_link_ref[own, :]
    p_first, u_first, v_first = (part(ref, 0) for ref in (p_ref, u_ref, v_ref))
    p_last, u_last, v_last = (part(ref, rows - 1) for ref in (p_ref, u_ref, v_ref))
    a = 1.0 - left_link * u_first
    b = left_link * v_first
    c = right_link * u_last
    d = 1.0 - right_link * v_last
    y = left + left_link * p_first
    z = right + right_link * p_last
    inv = inverse(a * d - b * c)
    before = (d * y + b * z) * inv
    after = (c * y + a * z) * inv
    for j in range(rows):
        x = part(p_ref, j) + part(u_ref, j) * before + part(v_ref, j) * after
        for k in range(layers):
            spot = pl.ds(j * width + k, chunks, stride=layers)
            out_ref[spot, :] = field_ref[spot, :] + x[k * chunks : (k + 1) * chunks]


def on_device(field, conduct, mode_index, mode_amp, mode_phase, step_index):
    rows, layers, columns = field.shape
    wide_count = lax.axis_size("wide")
    row_total = rows * wide_count
    layer_total = layers * lax.axis_size("grp")
    chunks = columns // LANES
    width = layers * chunks
    sizes = (rows, layers, chunks, row_total, layer_total, columns)
    limit = pltpu.CompilerParams(vmem_limit_bytes=16 * 1024 * 1024)
    anywhere = pl.BlockSpec(memory_space=pl.ANY)

    def lines(count):
        return jax.ShapeDtypeStruct((count * width, LANES), f32)

    packed, field_lines, conduct_lines, top, bottom = pl.pallas_call(
        load_kernel,
        out_shape=(
            jax.ShapeDtypeStruct((mode_index.shape[0], 8), f32),
            lines(rows),
            lines(rows),
            lines(1),
            lines(1),
        ),
        in_specs=[anywhere] * 6,
        scratch_shapes=[
            pltpu.SMEM(mode_index.shape, jnp.int32),
            pltpu.SMEM(mode_amp.shape, f32),
            pltpu.SMEM(mode_phase.shape, f32),
            pltpu.SMEM(step_index.shape, jnp.int32),
            pltpu.SemaphoreType.DMA((8,)),
        ],
        compiler_params=limit,
    )(mode_index, mode_amp, mode_phase, step_index, to_lines(field), to_lines(conduct))

    forward = [(i, i + 1) for i in range(wide_count - 1)]
    backward = [(target, source) for source, target in forward]
    low = lax.ppermute(bottom, "wide", forward)
    high = lax.ppermute(top, "wide", backward)
    modes = lax.all_gather(packed, "grp", axis=0, tiled=True)

    sent, p, u, v, *scans = pl.pallas_call(
        functools.partial(main_kernel, sizes),
        out_shape=(lines(wide_count),) + (lines(rows),) * 3 + (lines(wide_count),) * 4,
        scratch_shapes=[
            pltpu.VMEM(((rows + 2) * width, LANES), f32),
            pltpu.VMEM(((row_total + 2) * chunks, LANES), f32),
            pltpu.VMEM((rows * width, LANES), f32),
            pltpu.VMEM((4 * wide_count * width, LANES), f32),
        ],
        compiler_params=limit,
    )(modes, field_lines, low, high, conduct_lines)

    came = lax.all_to_all(
        sent.reshape(wide_count, width, LANES), "wide", split_axis=0, concat_axis=0
    ).reshape(wide_count * width, LANES)

    advanced = pl.pallas_call(
        functools.partial(last_kernel, sizes),
        out_shape=lines(rows),
        compiler_params=limit,
    )(came, *scans, p, u, v, field_lines)
    return from_lines(advanced, field.shape)


def solution(mesh):
    return jax.shard_map(
        on_device,
        mesh=mesh,
        in_specs=(
            P("wide", "grp", None),
            P("wide", "grp", None),
            P("grp", None),
            P("grp"),
            P("grp"),
            P(),
        ),
        out_specs=P("wide", "grp", None),
        check_vma=False,
    )
```

```python
import functools
import math

import jax
import jax.numpy as jnp
from jax import lax
from jax.experimental import pallas as pl
from jax.experimental.pallas import tpu as pltpu
from jax.sharding import PartitionSpec as P

time_step = 600.0
implicit_weight = 0.5
weight = implicit_weight * time_step
LANES = 128
f32 = jnp.float32


def to_lines(block):
    rows, layers, columns = block.shape
    chunks = columns // LANES
    return (
        block.reshape(rows, layers, chunks, LANES)
        .transpose(0, 2, 1, 3)
        .reshape(rows * chunks * layers, LANES)
    )


def from_lines(lines, shape):
    rows, layers, columns = shape
    chunks = columns // LANES
    return (
        lines.reshape(rows, chunks, layers, LANES)
        .transpose(0, 2, 1, 3)
        .reshape(rows, layers, columns)
    )


def turns(wave, index, period):
    product = wave * index
    if period & (period - 1) == 0:
        product = product & (period - 1)
    else:
        product = lax.rem(product, jnp.int32(period))
    return product.astype(f32) * (1.0 / period)


def cos_sin(turn):
    part = turn - jnp.floor(turn + 0.5)
    square = part * part

    def series(first):
        terms = [
            (-1.0) ** n * math.pi ** (2 * n + first) / math.factorial(2 * n + first)
            for n in range(7)
        ]
        total = jnp.full_like(square, terms[-1])
        for term in terms[-2::-1]:
            total = total * square + term
        return total

    half_cos = series(0)
    half_sin = series(1) * part
    return 1.0 - 2.0 * half_sin * half_sin, 2.0 * half_sin * half_cos


def height_lines(modes, first_row, count, row_total, chunks, column_total):
    mode_count = modes.shape[0]
    wave_x = modes[:, 0:1].astype(jnp.int32)
    wave_y = modes[:, 1:2].astype(jnp.int32)
    offset = modes[:, 2:3]
    amp = modes[:, 3:4]
    spot = lax.broadcasted_iota(jnp.int32, (mode_count, count * chunks), 1)
    chunk = spot % chunks
    row = jnp.clip(first_row + spot // chunks, 0, row_total - 1)
    angle = (
        turns(wave_y, row, row_total) + turns(wave_x, chunk * LANES, column_total)
    ) + offset
    left_cos, left_sin = cos_sin(angle)
    lane = lax.broadcasted_iota(jnp.int32, (mode_count, LANES), 1)
    right_cos, right_sin = cos_sin(turns(wave_x, lane, column_total))
    left = jnp.concatenate([amp * left_cos, amp * left_sin], 0)
    right = jnp.concatenate([right_cos, -right_sin], 0)
    return lax.dot_general(
        left,
        right,
        (((0,), (0,)), ((), ())),
        precision=lax.Precision.HIGHEST,
        preferred_element_type=f32,
    )


def inverse(values):
    return pl.reciprocal(values, approx=False)


def from_left(values, stride, lane):
    moved = [pltpu.roll(v, stride, 1) for v in values]
    return [jnp.where(lane < stride, moved[c - 1], moved[c]) for c in range(len(values))]


def from_right(values, stride, lane):
    count = len(values)
    moved = [pltpu.roll(v, LANES - stride, 1) for v in values]
    return [
        jnp.where(lane >= LANES - stride, moved[(c + 1) % count], moved[c]) for c in range(count)
    ]


def solve_chunks(diagonal, link, rhs):
    count = len(rhs)
    if count == 1:
        return [rhs[0] * inverse(diagonal[0])]
    inv = {i: inverse(diagonal[i]) for i in range(0, count, 2)}
    scaled = {i: inv[i] * rhs[i] for i in inv}
    odd_diagonal, odd_link, odd_rhs = [], [], []
    for i in range(1, count, 2):
        d = diagonal[i] - link[i - 1] * (link[i - 1] * inv[i - 1])
        r = rhs[i] + link[i - 1] * scaled[i - 1]
        e = None
        if i + 1 < count:
            by = link[i] * inv[i + 1]
            d = d - link[i] * by
            r = r + link[i] * scaled[i + 1]
            e = by * link[i + 1] if i + 2 < count else None
        odd_diagonal.append(d)
        odd_rhs.append(r)
        odd_link.append(e)
    odd = solve_chunks(odd_diagonal, odd_link, odd_rhs)
    out = [None] * count
    out[1::2] = odd
    for i in range(0, count, 2):
        r = rhs[i]
        if i > 0:
            r = r + link[i - 1] * out[i - 1]
        if i + 1 < count:
            r = r + link[i] * out[i + 1]
        out[i] = r * inv[i]
    return out


def solve_x(diagonal, link, rhs, lane):
    stride = 1
    count = len(rhs)
    while stride < LANES:
        inv = [inverse(d) for d in diagonal]
        t = [q * r for q, r in zip(inv, rhs)]
        w = [q * e for q, e in zip(inv, link)]
        low_d = from_left([e * v for e, v in zip(link, w)], stride, lane)
        low_r = from_left([e * v for e, v in zip(link, t)], stride, lane)
        high_q = from_right(inv, stride, lane)
        high_t = from_right(t, stride, lane)
        high_w = from_right(w, stride, lane)
        diagonal = [
            diagonal[c] - low_d[c] - link[c] * (link[c] * high_q[c]) for c in range(count)
        ]
        rhs = [rhs[c] + low_r[c] + link[c] * high_t[c] for c in range(count)]
        link = [link[c] * high_w[c] for c in range(count)]
        stride *= 2
    return solve_chunks(diagonal, link, rhs)


def load_kernel(
    step_ref, index_ref, amp_ref, phase_ref, field_ref, conduct_ref,
    packed_ref, field_out, conduct_out, top_ref, bottom_ref,
    index_in, amp_in, phase_in, sems,
):
    width = top_ref.shape[0]
    size = field_ref.shape[0]
    pairs = (
        (index_ref, index_in),
        (amp_ref, amp_in),
        (phase_ref, phase_in),
        (field_ref.at[pl.ds(0, width)], top_ref),
        (field_ref.at[pl.ds(size - width, width)], bottom_ref),
        (field_ref, field_out),
        (conduct_ref, conduct_out),
    )
    copies = [pltpu.make_async_copy(a, b, sems.at[n]) for n, (a, b) in enumerate(pairs)]
    for copy in copies:
        copy.start()
    for copy in copies[:3]:
        copy.wait()
    count = index_in.shape[0]
    row = lax.broadcasted_iota(jnp.int32, packed_ref.shape[1:], 0)
    lane = lax.broadcasted_iota(jnp.int32, packed_ref.shape[1:], 1)
    total = jnp.zeros(packed_ref.shape[1:], f32)
    for m in range(count):
        moment = lax.rem(index_in[m, 2] * step_ref[0], jnp.int32(64)).astype(f32)
        offset = phase_in[m] * (0.5 / math.pi) + moment * (1.0 / 64.0)
        for place, value in enumerate(
            (index_in[m, 0].astype(f32), index_in[m, 1].astype(f32), offset, amp_in[m])
        ):
            total = jnp.where((row == m) & (lane == place), value, total)
    for n in range(packed_ref.shape[0]):
        packed_ref[n] = total
    for copy in copies[3:]:
        copy.wait()


def condense(face):
    u, v = [], []
    rows = len(face) - 1
    for j in range(rows):
        d = 1.0 + (face[j] + face[j + 1])
        if j == 0:
            inv = inverse(d)
            u.append(face[0] * inv)
        else:
            inv = inverse(d - face[j] * v[-1])
            u.append(face[j] * inv * u[-1])
        v.append(face[j + 1] * inv)
    u_first, v_first = u[-1], v[-1]
    for j in range(rows - 2, -1, -1):
        u_first = u[j] + v[j] * u_first
        v_first = v[j] * v_first
    return u_first, v_first, u[-1], v[-1]


def main_kernel(
    sizes, modes_ref, field_ref, low_ref, high_ref, late_low_ref, late_high_ref, conduct_ref,
    sent_ref, p_ref, u_ref, v_ref, left_gain_ref, left_link_ref, right_gain_ref, right_link_ref,
    framed, heights, solved, ends,
):
    rows, layers, chunks, row_total, layer_total, column_total = sizes
    width = layers * chunks
    blocks = row_total // rows
    me = lax.axis_index("wide")
    first_layer = lax.axis_index("grp") * layers
    zeta = [
        ((first_layer + k).astype(f32) + 0.5) * (1.0 / layer_total) for k in range(layers)
    ]
    half = 0.5 * weight
    framed[0:width] = low_ref[...] + late_low_ref[...]
    framed[width : (rows + 1) * width] = field_ref[...]
    framed[(rows + 1) * width : (rows + 2) * width] = high_ref[...] + late_high_ref[...]
    body = height_lines(modes_ref[...], 0, row_total, row_total, chunks, column_total)
    heights[chunks : (row_total + 1) * chunks] = body
    heights[0:chunks] = body[0:chunks]
    heights[(row_total + 1) * chunks : (row_total + 2) * chunks] = body[
        (row_total - 1) * chunks : row_total * chunks
    ]
    lane = lax.broadcasted_iota(jnp.int32, (rows, LANES), 1)
    at_start = lane == 0
    at_end = lane == LANES - 1

    def faces(start):
        jac = []
        for j in range(rows + 2):
            h = heights[pl.ds(start + j * chunks, chunks), :]
            jac.append(jnp.concatenate([1.0 + z * h for z in zeta], 0))
        return [half * (jac[j] + jac[j + 1]) for j in range(rows + 1)]

    def block_ends(b):
        start, base = b * (rows * chunks), b * (4 * width)
        if not isinstance(b, int):
            start, base = pl.multiple_of(start, 8), pl.multiple_of(base, 8)
        for n, value in enumerate(condense(faces(start))):
            ends[pl.ds(base + n * width, width), :] = value

    if blocks <= 8:
        for b in range(blocks):
            block_ends(b)
    else:
        lax.fori_loop(0, blocks, lambda b, carry: (block_ends(b), carry)[1], 0)

    def end(b, n):
        return ends[(4 * b + n) * width : (4 * b + n + 1) * width]

    left = jnp.zeros((width, LANES), f32)
    right = jnp.zeros((width, LANES), f32)
    for b in range(blocks):
        u_first, v_first, u_last, v_last = (end(b, n) for n in range(4))
        gain = u_last * inverse(1.0 - u_first * left)
        left_gain_ref[b * width : (b + 1) * width] = gain
        left_link_ref[b * width : (b + 1) * width] = left
        left = v_last + gain * left * v_first
        b = blocks - 1 - b
        u_first, v_first, u_last, v_last = (end(b, n) for n in range(4))
        gain = v_first * inverse(1.0 - v_last * right)
        right_gain_ref[b * width : (b + 1) * width] = gain
        right_link_ref[b * width : (b + 1) * width] = right
        right = u_first + gain * right * u_last

    own_heights = pl.multiple_of(me * (rows * chunks), 8)
    for k in range(layers):
        g, f, along = [], [], []
        for c in range(chunks):
            jac_low, jac, jac_high = (
                1.0 + zeta[k] * heights[pl.ds(own_heights + s * chunks + c, rows, stride=chunks), :]
                for s in range(3)
            )
            place = c * layers + k
            f_low, f_mid, f_high = (
                framed[pl.ds(s * width + place, rows, stride=width), :] for s in range(3)
            )
            g.append(conduct_ref[pl.ds(place, rows, stride=width), :] * jac)
            f.append(f_mid)
            along.append(
                half * (jac + jac_high) * (f_high - f_mid)
                - half * (jac + jac_low) * (f_mid - f_low)
            )
        g_next = from_right(g, 1, lane)
        g_next[-1] = jnp.where(at_end, g[-1], g_next[-1])
        face = [half * (a + b) for a, b in zip(g, g_next)]
        face_low = from_left(face, 1, lane)
        face_low[0] = jnp.where(at_start, weight * g[0], face_low[0])
        diagonal = [1.0 + (a + b) for a, b in zip(face, face_low)]
        rhs = [2.0 * (a + b) for a, b in zip(f, along)]
        link = face
        link[-1] = jnp.where(at_end, 0.0, link[-1])
        both = solve_x(diagonal, link, rhs, lane)
        for c in range(chunks):
            solved[pl.ds(k * chunks + c, rows, stride=width), :] = both[c] - 2.0 * f[c]

    face = faces(own_heights)
    p, u, v = [], [], []
    for j in range(rows):
        r = solved[j * width : (j + 1) * width]
        d = 1.0 + (face[j] + face[j + 1])
        if j == 0:
            inv = inverse(d)
            p.append(r * inv)
            u.append(face[0] * inv)
        else:
            inv = inverse(d - face[j] * v[-1])
            scaled = face[j] * inv
            p.append(r * inv + scaled * p[-1])
            u.append(scaled * u[-1])
        v.append(face[j + 1] * inv)
    for j in range(rows - 2, -1, -1):
        p[j] = p[j] + v[j] * p[j + 1]
        u[j] = u[j] + v[j] * u[j + 1]
        v[j] = v[j] * v[j + 1]
    for j in range(rows):
        p_ref[j * width : (j + 1) * width] = p[j]
        u_ref[j * width : (j + 1) * width] = u[j]
        v_ref[j * width : (j + 1) * width] = v[j]

    own = pl.ds(pl.multiple_of(me * width, 8), width)
    upward = p[-1] + left_gain_ref[own, :] * (left_link_ref[own, :] * p[0])
    downward = p[0] + right_gain_ref[own, :] * (right_link_ref[own, :] * p[-1])
    for b in range(blocks):
        sent_ref[b * width : (b + 1) * width] = jnp.where(b > me, upward, downward)


def last_kernel(
    sizes, came_ref, left_gain_ref, left_link_ref, right_gain_ref, right_link_ref,
    p_ref, u_ref, v_ref, field_ref, out_ref,
):
    rows, layers, chunks, row_total, layer_total, column_total = sizes
    width = layers * chunks
    blocks = row_total // rows
    me = lax.axis_index("wide")

    def part(ref, b):
        return ref[b * width : (b + 1) * width]

    left = jnp.zeros((width, LANES), f32)
    right = jnp.zeros((width, LANES), f32)
    for b in range(blocks - 1):
        left = jnp.where(b < me, part(came_ref, b) + part(left_gain_ref, b) * left, left)
        b = blocks - 1 - b
        right = jnp.where(b > me, part(came_ref, b) + part(right_gain_ref, b) * right, right)

    own = pl.ds(pl.multiple_of(me * width, 8), width)
    left_link, right_link = left_link_ref[own, :], right_link_ref[own, :]
    p_first, u_first, v_first = (part(ref, 0) for ref in (p_ref, u_ref, v_ref))
    p_last, u_last, v_last = (part(ref, rows - 1) for ref in (p_ref, u_ref, v_ref))
    a = 1.0 - left_link * u_first
    b = left_link * v_first
    c = right_link * u_last
    d = 1.0 - right_link * v_last
    y = left + left_link * p_first
    z = right + right_link * p_last
    inv = inverse(a * d - b * c)
    before = (d * y + b * z) * inv
    after = (c * y + a * z) * inv
    for j in range(rows):
        x = part(p_ref, j) + part(u_ref, j) * before + part(v_ref, j) * after
        for k in range(layers):
            spot = pl.ds(j * width + k, chunks, stride=layers)
            out_ref[spot, :] = field_ref[spot, :] + x[k * chunks : (k + 1) * chunks]


def on_device(field, conduct, mode_index, mode_amp, mode_phase, step_index):
    rows, layers, columns = field.shape
    wide_count = lax.axis_size("wide")
    row_total = rows * wide_count
    grp_count = lax.axis_size("grp")
    layer_total = layers * grp_count
    chunks = columns // LANES
    width = layers * chunks
    sizes = (rows, layers, chunks, row_total, layer_total, columns)
    limit = pltpu.CompilerParams(vmem_limit_bytes=16 * 1024 * 1024)
    hbm = pl.BlockSpec(memory_space=pltpu.HBM)

    def lines(count):
        return jax.ShapeDtypeStruct((count * width, LANES), f32)

    packed, field_lines, conduct_lines, top, bottom = pl.pallas_call(
        load_kernel,
        out_shape=(
            jax.ShapeDtypeStruct((grp_count, mode_index.shape[0], 8), f32),
            lines(rows),
            lines(rows),
            lines(1),
            lines(1),
        ),
        in_specs=[pl.BlockSpec(memory_space=pltpu.SMEM)] + [hbm] * 5,
        scratch_shapes=[
            pltpu.SMEM(mode_index.shape, jnp.int32),
            pltpu.SMEM(mode_amp.shape, f32),
            pltpu.SMEM(mode_phase.shape, f32),
            pltpu.SemaphoreType.DMA((7,)),
        ],
        compiler_params=limit,
    )(
        step_index,
        *(
            pltpu.with_memory_space_constraint(a, pltpu.HBM)
            for a in (mode_index, mode_amp, mode_phase, to_lines(field), to_lines(conduct))
        ),
    )

    def neighbour_rows(top, bottom, groups):
        pairs = [
            (g * wide_count + i, g * wide_count + i + 1)
            for g in groups
            for i in range(wide_count - 1)
        ]
        low = lax.ppermute(bottom, ("grp", "wide"), pairs)
        high = lax.ppermute(top, ("grp", "wide"), [(b, a) for a, b in pairs])
        return low, high

    early = neighbour_rows(top, bottom, [0])
    packed, *early = lax.optimization_barrier((packed, *early))
    modes = lax.all_to_all(packed, "grp", split_axis=0, concat_axis=0)
    modes, top, bottom = lax.optimization_barrier((modes, top, bottom))
    late = neighbour_rows(top, bottom, range(1, grp_count))
    modes = modes.reshape(-1, modes.shape[-1])

    sent, p, u, v, *scans = pl.pallas_call(
        functools.partial(main_kernel, sizes),
        out_shape=(lines(wide_count),) + (lines(rows),) * 3 + (lines(wide_count),) * 4,
        scratch_shapes=[
            pltpu.VMEM(((rows + 2) * width, LANES), f32),
            pltpu.VMEM(((row_total + 2) * chunks, LANES), f32),
            pltpu.VMEM((rows * width, LANES), f32),
            pltpu.VMEM((4 * wide_count * width, LANES), f32),
        ],
        compiler_params=limit,
    )(modes, field_lines, *early, *late, conduct_lines)

    came = lax.all_to_all(
        sent.reshape(wide_count, width, LANES), "wide", split_axis=0, concat_axis=0
    ).reshape(wide_count * width, LANES)

    advanced = pl.pallas_call(
        functools.partial(last_kernel, sizes),
        out_shape=lines(rows),
        compiler_params=limit,
    )(came, *scans, p, u, v, field_lines)
    return from_lines(advanced, field.shape)


def solution(mesh):
    return jax.shard_map(
        on_device,
        mesh=mesh,
        in_specs=(
            P("wide", "grp", None),
            P("wide", "grp", None),
            P("grp", None),
            P("grp"),
            P("grp"),
            P(),
        ),
        out_specs=P("wide", "grp", None),
        check_vma=False,
    )
```

```python
import functools
import math

import jax
import jax.numpy as jnp
from jax import lax
from jax.experimental import pallas as pl
from jax.experimental.pallas import tpu as pltpu
from jax.sharding import PartitionSpec as P

time_step = 600.0
implicit_weight = 0.5
weight = implicit_weight * time_step
LANES = 128
f32 = jnp.float32


def to_lines(block):
    rows, layers, columns = block.shape
    chunks = columns // LANES
    return (
        block.reshape(rows, layers, chunks, LANES)
        .transpose(0, 2, 1, 3)
        .reshape(rows * chunks * layers, LANES)
    )


def from_lines(lines, shape):
    rows, layers, columns = shape
    chunks = columns // LANES
    return (
        lines.reshape(rows, chunks, layers, LANES)
        .transpose(0, 2, 1, 3)
        .reshape(rows, layers, columns)
    )


def turns(wave, index, period):
    product = wave * index
    if period & (period - 1) == 0:
        product = product & (period - 1)
    else:
        product = lax.rem(product, jnp.int32(period))
    return product.astype(f32) * (1.0 / period)


def cos_sin(turn):
    part = turn - jnp.floor(turn + 0.5)
    square = part * part

    def series(first):
        terms = [
            (-1.0) ** n * math.pi ** (2 * n + first) / math.factorial(2 * n + first)
            for n in range(7)
        ]
        total = jnp.full_like(square, terms[-1])
        for term in terms[-2::-1]:
            total = total * square + term
        return total

    half_cos = series(0)
    half_sin = series(1) * part
    return 1.0 - 2.0 * half_sin * half_sin, 2.0 * half_sin * half_cos


def height_lines(modes, first_row, count, row_total, chunks, column_total):
    mode_count = modes.shape[0]
    wave_x = modes[:, 0:1].astype(jnp.int32)
    wave_y = modes[:, 1:2].astype(jnp.int32)
    offset = modes[:, 2:3]
    amp = modes[:, 3:4]
    spot = lax.broadcasted_iota(jnp.int32, (mode_count, count * chunks), 1)
    chunk = spot % chunks
    row = jnp.clip(first_row + spot // chunks, 0, row_total - 1)
    angle = (
        turns(wave_y, row, row_total) + turns(wave_x, chunk * LANES, column_total)
    ) + offset
    left_cos, left_sin = cos_sin(angle)
    lane = lax.broadcasted_iota(jnp.int32, (mode_count, LANES), 1)
    right_cos, right_sin = cos_sin(turns(wave_x, lane, column_total))
    left = jnp.concatenate([amp * left_cos, amp * left_sin], 0)
    right = jnp.concatenate([right_cos, -right_sin], 0)
    return lax.dot_general(
        left,
        right,
        (((0,), (0,)), ((), ())),
        precision=lax.Precision.HIGHEST,
        preferred_element_type=f32,
    )


def inverse(values):
    return pl.reciprocal(values, approx=False)


def from_left(values, stride, lane):
    moved = [pltpu.roll(v, stride, 1) for v in values]
    return [jnp.where(lane < stride, moved[c - 1], moved[c]) for c in range(len(values))]


def from_right(values, stride, lane):
    count = len(values)
    moved = [pltpu.roll(v, LANES - stride, 1) for v in values]
    return [
        jnp.where(lane >= LANES - stride, moved[(c + 1) % count], moved[c]) for c in range(count)
    ]


def solve_chunks(diagonal, link, rhs):
    count = len(rhs)
    if count == 1:
        return [rhs[0] * inverse(diagonal[0])]
    inv = {i: inverse(diagonal[i]) for i in range(0, count, 2)}
    scaled = {i: inv[i] * rhs[i] for i in inv}
    odd_diagonal, odd_link, odd_rhs = [], [], []
    for i in range(1, count, 2):
        d = diagonal[i] - link[i - 1] * (link[i - 1] * inv[i - 1])
        r = rhs[i] + link[i - 1] * scaled[i - 1]
        e = None
        if i + 1 < count:
            by = link[i] * inv[i + 1]
            d = d - link[i] * by
            r = r + link[i] * scaled[i + 1]
            e = by * link[i + 1] if i + 2 < count else None
        odd_diagonal.append(d)
        odd_rhs.append(r)
        odd_link.append(e)
    odd = solve_chunks(odd_diagonal, odd_link, odd_rhs)
    out = [None] * count
    out[1::2] = odd
    for i in range(0, count, 2):
        r = rhs[i]
        if i > 0:
            r = r + link[i - 1] * out[i - 1]
        if i + 1 < count:
            r = r + link[i] * out[i + 1]
        out[i] = r * inv[i]
    return out


def solve_x(diagonal, link, rhs, lane):
    stride = 1
    count = len(rhs)
    while stride < LANES:
        inv = [inverse(d) for d in diagonal]
        t = [q * r for q, r in zip(inv, rhs)]
        w = [q * e for q, e in zip(inv, link)]
        low_d = from_left([e * v for e, v in zip(link, w)], stride, lane)
        low_r = from_left([e * v for e, v in zip(link, t)], stride, lane)
        high_q = from_right(inv, stride, lane)
        high_t = from_right(t, stride, lane)
        high_w = from_right(w, stride, lane)
        diagonal = [
            diagonal[c] - low_d[c] - link[c] * (link[c] * high_q[c]) for c in range(count)
        ]
        rhs = [rhs[c] + low_r[c] + link[c] * high_t[c] for c in range(count)]
        link = [link[c] * high_w[c] for c in range(count)]
        stride *= 2
    return solve_chunks(diagonal, link, rhs)


def load_kernel(
    step_ref, index_ref, amp_ref, phase_ref, field_ref, conduct_ref,
    packed_ref, field_out, conduct_out, inner_ref, outer_ref,
    index_in, amp_in, phase_in, sems,
):
    width = inner_ref.shape[0]
    last = field_ref.shape[0] - width
    odd = lax.rem(lax.axis_index("wide"), 2)
    inner_rows = pl.ds(pl.multiple_of((1 - odd) * last, 8), width)
    outer_rows = pl.ds(pl.multiple_of(odd * last, 8), width)
    pairs = (
        (index_ref, index_in),
        (amp_ref, amp_in),
        (phase_ref, phase_in),
        (field_ref.at[inner_rows], inner_ref),
        (field_ref.at[outer_rows], outer_ref),
        (field_ref, field_out),
        (conduct_ref, conduct_out),
    )
    copies = [pltpu.make_async_copy(a, b, sems.at[n]) for n, (a, b) in enumerate(pairs)]
    for copy in copies:
        copy.start()
    for copy in copies[:3]:
        copy.wait()
    count = index_in.shape[0]
    row = lax.broadcasted_iota(jnp.int32, packed_ref.shape, 0)
    lane = lax.broadcasted_iota(jnp.int32, packed_ref.shape, 1)
    total = jnp.zeros(packed_ref.shape, f32)
    for m in range(count):
        moment = lax.rem(index_in[m, 2] * step_ref[0], jnp.int32(64)).astype(f32)
        offset = phase_in[m] * (0.5 / math.pi) + moment * (1.0 / 64.0)
        for place, value in enumerate(
            (index_in[m, 0].astype(f32), index_in[m, 1].astype(f32), offset, amp_in[m])
        ):
            total = jnp.where((row == m) & (lane == place), value, total)
    packed_ref[...] = total
    for copy in copies[3:]:
        copy.wait()


def condense(face):
    inv, scaled, u, v = [], [], [], []
    rows = len(face) - 1
    for j in range(rows):
        d = 1.0 + (face[j] + face[j + 1])
        if j == 0:
            inv.append(inverse(d))
            scaled.append(face[0] * inv[0])
            u.append(scaled[0])
        else:
            inv.append(inverse(d - face[j] * v[-1]))
            scaled.append(face[j] * inv[-1])
            u.append(scaled[-1] * u[-1])
        v.append(face[j + 1] * inv[-1])
    u_all, v_all = list(u), list(v)
    for j in range(rows - 2, -1, -1):
        u_all[j] = u[j] + v[j] * u_all[j + 1]
        v_all[j] = v[j] * v_all[j + 1]
    return inv, scaled, v, u_all, v_all


def matrix_kernel(
    sizes, modes_ref,
    own_heights_ref, inv_ref, scaled_ref, chain_ref, u_ref, v_ref, left_gain_ref, right_gain_ref,
    joint_ref, heights, ends, links,
):
    rows, layers, chunks, row_total, layer_total, column_total = sizes
    width = layers * chunks
    blocks = row_total // rows
    me = lax.axis_index("wide")
    first_layer = lax.axis_index("grp") * layers
    zeta = [
        ((first_layer + k).astype(f32) + 0.5) * (1.0 / layer_total) for k in range(layers)
    ]
    half = 0.5 * weight
    body = height_lines(modes_ref[...], 0, row_total, row_total, chunks, column_total)
    heights[chunks : (row_total + 1) * chunks] = body
    heights[0:chunks] = body[0:chunks]
    heights[(row_total + 1) * chunks : (row_total + 2) * chunks] = body[
        (row_total - 1) * chunks : row_total * chunks
    ]
    own_start = pl.multiple_of(me * (rows * chunks), 8)
    own_heights_ref[...] = heights[pl.ds(own_start, (rows + 2) * chunks), :]

    def faces(start):
        jac = []
        for j in range(rows + 2):
            h = heights[pl.ds(start + j * chunks, chunks), :]
            jac.append(jnp.concatenate([1.0 + z * h for z in zeta], 0))
        return [half * (jac[j] + jac[j + 1]) for j in range(rows + 1)]

    def keep_ends(b, u, v):
        base = pl.multiple_of(b * (4 * width), 8)
        for n, value in enumerate((u[0], v[0], u[-1], v[-1])):
            ends[pl.ds(base + n * width, width), :] = value

    inv, scaled, chain, u, v = condense(faces(own_start))
    for ref, values in (
        (inv_ref, inv), (scaled_ref, scaled), (chain_ref, chain), (u_ref, u), (v_ref, v)
    ):
        for j in range(rows):
            ref[j * width : (j + 1) * width] = values[j]
    keep_ends(me, u, v)

    def other_block(n):
        b = lax.rem(me + 1 + n, blocks)
        _, _, _, u, v = condense(faces(pl.multiple_of(b * (rows * chunks), 8)))
        keep_ends(b, u, v)

    if blocks <= 8:
        for n in range(blocks - 1):
            other_block(n)
    else:
        lax.fori_loop(0, blocks - 1, lambda n, carry: (other_block(n), carry)[1], 0)

    def end(b, n):
        return ends[(4 * b + n) * width : (4 * b + n + 1) * width]

    left = jnp.zeros((width, LANES), f32)
    right = jnp.zeros((width, LANES), f32)
    for b in range(blocks):
        u_first, v_first, u_last, v_last = (end(b, n) for n in range(4))
        gain = u_last * inverse(1.0 - u_first * left)
        left_gain_ref[b * width : (b + 1) * width] = gain
        links[b * width : (b + 1) * width] = left
        left = v_last + gain * left * v_first
        b = blocks - 1 - b
        u_first, v_first, u_last, v_last = (end(b, n) for n in range(4))
        gain = v_first * inverse(1.0 - v_last * right)
        right_gain_ref[b * width : (b + 1) * width] = gain
        links[(blocks + b) * width : (blocks + b + 1) * width] = right
        right = u_first + gain * right * u_last

    own = pl.ds(pl.multiple_of(me * width, 8), width)
    left_link = links[own, :]
    right_link = links[pl.ds(pl.multiple_of((blocks + me) * width, 8), width), :]
    a = 1.0 - left_link * u[0]
    b = left_link * v[0]
    c = right_link * u[-1]
    d = 1.0 - right_link * v[-1]
    inv = inverse(a * d - b * c)
    joint = (
        left_gain_ref[own, :] * left_link, right_gain_ref[own, :] * right_link,
        left_link, right_link, d * inv, b * inv, c * inv, a * inv,
    )
    for n, value in enumerate(joint):
        joint_ref[n * width : (n + 1) * width] = value


def first_kernel(
    sizes, field_ref, inner_ref, outer_ref, late_outer_ref, conduct_ref,
    heights, inv_ref, scaled_ref, chain_ref, joint_ref,
    sent_ref, p_ref, framed, solved,
):
    rows, layers, chunks, row_total, layer_total, column_total = sizes
    width = layers * chunks
    blocks = row_total // rows
    me = lax.axis_index("wide")
    odd = lax.rem(me, 2)
    first_layer = lax.axis_index("grp") * layers
    zeta = [
        ((first_layer + k).astype(f32) + 0.5) * (1.0 / layer_total) for k in range(layers)
    ]
    half = 0.5 * weight
    beyond = (rows + 1) * width
    framed[width:beyond] = field_ref[...]
    framed[pl.ds(pl.multiple_of((1 - odd) * beyond, 8), width), :] = inner_ref[...]
    framed[pl.ds(pl.multiple_of(odd * beyond, 8), width), :] = (
        outer_ref[...] + late_outer_ref[...]
    )
    lane = lax.broadcasted_iota(jnp.int32, (rows, LANES), 1)
    at_start = lane == 0
    at_end = lane == LANES - 1

    for k in range(layers):
        g, f, along = [], [], []
        for c in range(chunks):
            jac_low, jac, jac_high = (
                1.0 + zeta[k] * heights[pl.ds(s * chunks + c, rows, stride=chunks), :]
                for s in range(3)
            )
            place = c * layers + k
            f_low, f_mid, f_high = (
                framed[pl.ds(s * width + place, rows, stride=width), :] for s in range(3)
            )
            g.append(conduct_ref[pl.ds(place, rows, stride=width), :] * jac)
            f.append(f_mid)
            along.append(
                half * (jac + jac_high) * (f_high - f_mid)
                - half * (jac + jac_low) * (f_mid - f_low)
            )
        g_next = from_right(g, 1, lane)
        g_next[-1] = jnp.where(at_end, g[-1], g_next[-1])
        face = [half * (a + b) for a, b in zip(g, g_next)]
        face_low = from_left(face, 1, lane)
        face_low[0] = jnp.where(at_start, weight * g[0], face_low[0])
        diagonal = [1.0 + (a + b) for a, b in zip(face, face_low)]
        rhs = [2.0 * (a + b) for a, b in zip(f, along)]
        link = face
        link[-1] = jnp.where(at_end, 0.0, link[-1])
        both = solve_x(diagonal, link, rhs, lane)
        for c in range(chunks):
            solved[pl.ds(k * chunks + c, rows, stride=width), :] = both[c] - 2.0 * f[c]

    def part(ref, j):
        return ref[j * width : (j + 1) * width]

    p = [part(solved, 0) * part(inv_ref, 0)]
    for j in range(1, rows):
        p.append(part(solved, j) * part(inv_ref, j) + part(scaled_ref, j) * p[-1])
    for j in range(rows - 2, -1, -1):
        p[j] = p[j] + part(chain_ref, j) * p[j + 1]
    for j in range(rows):
        p_ref[j * width : (j + 1) * width] = p[j]

    upward = p[-1] + part(joint_ref, 0) * p[0]
    downward = p[0] + part(joint_ref, 1) * p[-1]
    for b in range(blocks):
        sent_ref[b * width : (b + 1) * width] = jnp.where(b > me, upward, downward)


def last_kernel(
    sizes, came_ref, left_gain_ref, right_gain_ref, joint_ref, p_ref, u_ref, v_ref, field_ref,
    out_ref,
):
    rows, layers, chunks, row_total, layer_total, column_total = sizes
    width = layers * chunks
    blocks = row_total // rows
    me = lax.axis_index("wide")

    def part(ref, b):
        return ref[b * width : (b + 1) * width]

    left = jnp.zeros((width, LANES), f32)
    right = jnp.zeros((width, LANES), f32)
    for b in range(blocks - 1):
        left = jnp.where(b < me, part(came_ref, b) + part(left_gain_ref, b) * left, left)
        b = blocks - 1 - b
        right = jnp.where(b > me, part(came_ref, b) + part(right_gain_ref, b) * right, right)

    y = left + part(joint_ref, 2) * part(p_ref, 0)
    z = right + part(joint_ref, 3) * part(p_ref, rows - 1)
    before = part(joint_ref, 4) * y + part(joint_ref, 5) * z
    after = part(joint_ref, 6) * y + part(joint_ref, 7) * z
    for j in range(rows):
        x = part(p_ref, j) + part(u_ref, j) * before + part(v_ref, j) * after
        for k in range(layers):
            spot = pl.ds(j * width + k, chunks, stride=layers)
            out_ref[spot, :] = field_ref[spot, :] + x[k * chunks : (k + 1) * chunks]


def on_device(field, conduct, mode_index, mode_amp, mode_phase, step_index):
    rows, layers, columns = field.shape
    wide_count = lax.axis_size("wide")
    row_total = rows * wide_count
    grp_count = lax.axis_size("grp")
    layer_total = layers * grp_count
    chunks = columns // LANES
    width = layers * chunks
    sizes = (rows, layers, chunks, row_total, layer_total, columns)
    limit = pltpu.CompilerParams(vmem_limit_bytes=16 * 1024 * 1024)
    hbm = pl.BlockSpec(memory_space=pltpu.HBM)

    def lines(count):
        return jax.ShapeDtypeStruct((count * width, LANES), f32)

    packed, field_lines, conduct_lines, inner, outer = pl.pallas_call(
        load_kernel,
        out_shape=(
            jax.ShapeDtypeStruct((mode_index.shape[0], 8), f32),
            lines(rows),
            lines(rows),
            lines(1),
            lines(1),
        ),
        in_specs=[pl.BlockSpec(memory_space=pltpu.SMEM)] + [hbm] * 5,
        scratch_shapes=[
            pltpu.SMEM(mode_index.shape, jnp.int32),
            pltpu.SMEM(mode_amp.shape, f32),
            pltpu.SMEM(mode_phase.shape, f32),
            pltpu.SemaphoreType.DMA((7,)),
        ],
        compiler_params=limit,
    )(
        step_index,
        *(
            pltpu.with_memory_space_constraint(a, pltpu.HBM)
            for a in (mode_index, mode_amp, mode_phase, to_lines(field), to_lines(conduct))
        ),
    )

    def swap(rows_sent, first, groups):
        pairs = []
        for g in groups:
            for i in range(g * wide_count + first, (g + 1) * wide_count - 1, 2):
                pairs += [(i, i + 1), (i + 1, i)]
        return lax.ppermute(rows_sent, ("grp", "wide"), pairs)

    inner_came = swap(inner, 0, range(grp_count))
    outer_came = swap(outer, 1, [0])
    modes = lax.all_gather(packed, "grp", axis=0, tiled=True)
    modes, outer = lax.optimization_barrier((modes, outer))
    late_outer_came = swap(outer, 1, range(1, grp_count))

    own_heights, inv, scaled, chain, u, v, left_gain, right_gain, joint = pl.pallas_call(
        functools.partial(matrix_kernel, sizes),
        out_shape=(jax.ShapeDtypeStruct(((rows + 2) * chunks, LANES), f32),)
        + (lines(rows),) * 5
        + (lines(wide_count),) * 2
        + (lines(8),),
        scratch_shapes=[
            pltpu.VMEM(((row_total + 2) * chunks, LANES), f32),
            pltpu.VMEM((4 * wide_count * width, LANES), f32),
            pltpu.VMEM((2 * wide_count * width, LANES), f32),
        ],
        compiler_params=limit,
    )(modes)

    sent, p = pl.pallas_call(
        functools.partial(first_kernel, sizes),
        out_shape=(lines(wide_count), lines(rows)),
        scratch_shapes=[
            pltpu.VMEM(((rows + 2) * width, LANES), f32),
            pltpu.VMEM((rows * width, LANES), f32),
        ],
        compiler_params=limit,
    )(
        field_lines, inner_came, outer_came, late_outer_came, conduct_lines,
        own_heights, inv, scaled, chain, joint,
    )

    came = lax.all_to_all(
        sent.reshape(wide_count, width, LANES), "wide", split_axis=0, concat_axis=0
    ).reshape(wide_count * width, LANES)

    advanced = pl.pallas_call(
        functools.partial(last_kernel, sizes),
        out_shape=lines(rows),
        compiler_params=limit,
    )(came, left_gain, right_gain, joint, p, u, v, field_lines)
    return from_lines(advanced, field.shape)


def solution(mesh):
    return jax.shard_map(
        on_device,
        mesh=mesh,
        in_specs=(
            P("wide", "grp", None),
            P("wide", "grp", None),
            P("grp", None),
            P("grp"),
            P("grp"),
            P(),
        ),
        out_specs=P("wide", "grp", None),
        check_vma=False,
    )
```

```python
import functools
import math

import jax
import jax.numpy as jnp
from jax import lax
from jax.experimental import pallas as pl
from jax.experimental.pallas import tpu as pltpu
from jax.sharding import PartitionSpec as P

time_step = 600.0
implicit_weight = 0.5
weight = implicit_weight * time_step
LANES = 128
f32 = jnp.float32


def to_lines(block):
    rows, layers, columns = block.shape
    chunks = columns // LANES
    return (
        block.reshape(rows, layers, chunks, LANES)
        .transpose(0, 2, 1, 3)
        .reshape(rows * chunks * layers, LANES)
    )


def from_lines(lines, shape):
    rows, layers, columns = shape
    chunks = columns // LANES
    return (
        lines.reshape(rows, chunks, layers, LANES)
        .transpose(0, 2, 1, 3)
        .reshape(rows, layers, columns)
    )


def turns(wave, index, period):
    product = wave * index
    if period & (period - 1) == 0:
        product = product & (period - 1)
    else:
        product = lax.rem(product, jnp.int32(period))
    return product.astype(f32) * (1.0 / period)


def cos_sin(turn):
    part = turn - jnp.floor(turn + 0.5)
    square = part * part

    def series(first):
        terms = [
            (-1.0) ** n * math.pi ** (2 * n + first) / math.factorial(2 * n + first)
            for n in range(7)
        ]
        total = jnp.full_like(square, terms[-1])
        for term in terms[-2::-1]:
            total = total * square + term
        return total

    half_cos = series(0)
    half_sin = series(1) * part
    return 1.0 - 2.0 * half_sin * half_sin, 2.0 * half_sin * half_cos


def height_lines(modes, first_row, count, row_total, chunks, column_total):
    mode_count = modes.shape[0]
    wave_x = modes[:, 0:1].astype(jnp.int32)
    wave_y = modes[:, 1:2].astype(jnp.int32)
    offset = modes[:, 2:3]
    amp = modes[:, 3:4]
    spot = lax.broadcasted_iota(jnp.int32, (mode_count, count * chunks), 1)
    chunk = spot % chunks
    row = jnp.clip(first_row + spot // chunks, 0, row_total - 1)
    angle = (
        turns(wave_y, row, row_total) + turns(wave_x, chunk * LANES, column_total)
    ) + offset
    left_cos, left_sin = cos_sin(angle)
    lane = lax.broadcasted_iota(jnp.int32, (mode_count, LANES), 1)
    right_cos, right_sin = cos_sin(turns(wave_x, lane, column_total))
    left = jnp.concatenate([amp * left_cos, amp * left_sin], 0)
    right = jnp.concatenate([right_cos, -right_sin], 0)
    return lax.dot_general(
        left,
        right,
        (((0,), (0,)), ((), ())),
        precision=lax.Precision.HIGHEST,
        preferred_element_type=f32,
    )


def inverse(values):
    return pl.reciprocal(values, approx=False)


def from_left(values, stride, lane):
    moved = [pltpu.roll(v, stride, 1) for v in values]
    return [jnp.where(lane < stride, moved[c - 1], moved[c]) for c in range(len(values))]


def from_right(values, stride, lane):
    count = len(values)
    moved = [pltpu.roll(v, LANES - stride, 1) for v in values]
    return [
        jnp.where(lane >= LANES - stride, moved[(c + 1) % count], moved[c]) for c in range(count)
    ]


def solve_chunks(diagonal, link, rhs):
    count = len(rhs)
    if count == 1:
        return [rhs[0] * inverse(diagonal[0])]
    inv = {i: inverse(diagonal[i]) for i in range(0, count, 2)}
    scaled = {i: inv[i] * rhs[i] for i in inv}
    odd_diagonal, odd_link, odd_rhs = [], [], []
    for i in range(1, count, 2):
        d = diagonal[i] - link[i - 1] * (link[i - 1] * inv[i - 1])
        r = rhs[i] + link[i - 1] * scaled[i - 1]
        e = None
        if i + 1 < count:
            by = link[i] * inv[i + 1]
            d = d - link[i] * by
            r = r + link[i] * scaled[i + 1]
            e = by * link[i + 1] if i + 2 < count else None
        odd_diagonal.append(d)
        odd_rhs.append(r)
        odd_link.append(e)
    odd = solve_chunks(odd_diagonal, odd_link, odd_rhs)
    out = [None] * count
    out[1::2] = odd
    for i in range(0, count, 2):
        r = rhs[i]
        if i > 0:
            r = r + link[i - 1] * out[i - 1]
        if i + 1 < count:
            r = r + link[i] * out[i + 1]
        out[i] = r * inv[i]
    return out


def solve_x(diagonal, link, rhs, lane):
    stride = 1
    count = len(rhs)
    while stride < LANES:
        inv = [inverse(d) for d in diagonal]
        t = [q * r for q, r in zip(inv, rhs)]
        w = [q * e for q, e in zip(inv, link)]
        low_d = from_left([e * v for e, v in zip(link, w)], stride, lane)
        low_r = from_left([e * v for e, v in zip(link, t)], stride, lane)
        high_q = from_right(inv, stride, lane)
        high_t = from_right(t, stride, lane)
        high_w = from_right(w, stride, lane)
        diagonal = [
            diagonal[c] - low_d[c] - link[c] * (link[c] * high_q[c]) for c in range(count)
        ]
        rhs = [rhs[c] + low_r[c] + link[c] * high_t[c] for c in range(count)]
        link = [link[c] * high_w[c] for c in range(count)]
        stride *= 2
    return solve_chunks(diagonal, link, rhs)


def load_kernel(
    step_ref, index_ref, amp_ref, phase_ref, field_ref, conduct_ref,
    packed_ref, field_out, conduct_out, inner_ref, outer_ref,
    index_in, amp_in, phase_in, sems,
):
    width = inner_ref.shape[0]
    last = field_ref.shape[0] - width
    odd = lax.rem(lax.axis_index("wide"), 2)
    inner_rows = pl.ds(pl.multiple_of((1 - odd) * last, 8), width)
    outer_rows = pl.ds(pl.multiple_of(odd * last, 8), width)
    pairs = (
        (index_ref, index_in),
        (amp_ref, amp_in),
        (phase_ref, phase_in),
        (field_ref.at[inner_rows], inner_ref),
        (field_ref.at[outer_rows], outer_ref),
        (field_ref, field_out),
        (conduct_ref, conduct_out),
    )
    copies = [pltpu.make_async_copy(a, b, sems.at[n]) for n, (a, b) in enumerate(pairs)]
    for copy in copies:
        copy.start()
    for copy in copies[:3]:
        copy.wait()
    count = index_in.shape[0]
    row = lax.broadcasted_iota(jnp.int32, packed_ref.shape, 0)
    lane = lax.broadcasted_iota(jnp.int32, packed_ref.shape, 1)
    total = jnp.zeros(packed_ref.shape, f32)
    for m in range(count):
        moment = lax.rem(index_in[m, 2] * step_ref[0], jnp.int32(64)).astype(f32)
        offset = phase_in[m] * (0.5 / math.pi) + moment * (1.0 / 64.0)
        for place, value in enumerate(
            (index_in[m, 0].astype(f32), index_in[m, 1].astype(f32), offset, amp_in[m])
        ):
            total = jnp.where((row == m) & (lane == place), value, total)
    packed_ref[...] = total
    for copy in copies[3:]:
        copy.wait()


def condense(face):
    inv, scaled, u, v = [], [], [], []
    rows = len(face) - 1
    for j in range(rows):
        d = 1.0 + (face[j] + face[j + 1])
        if j == 0:
            inv.append(inverse(d))
            scaled.append(face[0] * inv[0])
            u.append(scaled[0])
        else:
            inv.append(inverse(d - face[j] * v[-1]))
            scaled.append(face[j] * inv[-1])
            u.append(scaled[-1] * u[-1])
        v.append(face[j + 1] * inv[-1])
    u_all, v_all = list(u), list(v)
    for j in range(rows - 2, -1, -1):
        u_all[j] = u[j] + v[j] * u_all[j + 1]
        v_all[j] = v[j] * v_all[j + 1]
    return inv, scaled, v, u_all, v_all


def main_kernel(
    sizes, modes_ref, field_ref, inner_ref, outer_ref, late_outer_ref, conduct_ref,
    sent_ref, p_ref, u_ref, v_ref, left_gain_ref, right_gain_ref, joint_ref,
    heights, ends, links, framed, solved,
):
    rows, layers, chunks, row_total, layer_total, column_total = sizes
    width = layers * chunks
    blocks = row_total // rows
    me = lax.axis_index("wide")
    first_layer = lax.axis_index("grp") * layers
    zeta = [
        ((first_layer + k).astype(f32) + 0.5) * (1.0 / layer_total) for k in range(layers)
    ]
    half = 0.5 * weight
    body = height_lines(modes_ref[...], 0, row_total, row_total, chunks, column_total)
    heights[chunks : (row_total + 1) * chunks] = body
    heights[0:chunks] = body[0:chunks]
    heights[(row_total + 1) * chunks : (row_total + 2) * chunks] = body[
        (row_total - 1) * chunks : row_total * chunks
    ]
    own_start = pl.multiple_of(me * (rows * chunks), 8)

    def faces(start):
        jac = []
        for j in range(rows + 2):
            h = heights[pl.ds(start + j * chunks, chunks), :]
            jac.append(jnp.concatenate([1.0 + z * h for z in zeta], 0))
        return [half * (jac[j] + jac[j + 1]) for j in range(rows + 1)]

    def keep_ends(b, u, v):
        base = pl.multiple_of(b * (4 * width), 8)
        for n, value in enumerate((u[0], v[0], u[-1], v[-1])):
            ends[pl.ds(base + n * width, width), :] = value

    inv, scaled, chain, u, v = condense(faces(own_start))
    for j in range(rows):
        u_ref[j * width : (j + 1) * width] = u[j]
        v_ref[j * width : (j + 1) * width] = v[j]
    keep_ends(me, u, v)

    def other_block(n):
        b = lax.rem(me + 1 + n, blocks)
        _, _, _, u, v = condense(faces(pl.multiple_of(b * (rows * chunks), 8)))
        keep_ends(b, u, v)

    if blocks <= 8:
        for n in range(blocks - 1):
            other_block(n)
    else:
        lax.fori_loop(0, blocks - 1, lambda n, carry: (other_block(n), carry)[1], 0)

    def end(b, n):
        return ends[(4 * b + n) * width : (4 * b + n + 1) * width]

    left = jnp.zeros((width, LANES), f32)
    right = jnp.zeros((width, LANES), f32)
    for b in range(blocks):
        u_first, v_first, u_last, v_last = (end(b, n) for n in range(4))
        gain = u_last * inverse(1.0 - u_first * left)
        left_gain_ref[b * width : (b + 1) * width] = gain
        links[b * width : (b + 1) * width] = left
        left = v_last + gain * left * v_first
        b = blocks - 1 - b
        u_first, v_first, u_last, v_last = (end(b, n) for n in range(4))
        gain = v_first * inverse(1.0 - v_last * right)
        right_gain_ref[b * width : (b + 1) * width] = gain
        links[(blocks + b) * width : (blocks + b + 1) * width] = right
        right = u_first + gain * right * u_last

    own = pl.ds(pl.multiple_of(me * width, 8), width)
    left_link = links[own, :]
    right_link = links[pl.ds(pl.multiple_of((blocks + me) * width, 8), width), :]
    a = 1.0 - left_link * u[0]
    b = left_link * v[0]
    c = right_link * u[-1]
    d = 1.0 - right_link * v[-1]
    by = inverse(a * d - b * c)
    joint = (
        left_gain_ref[own, :] * left_link, right_gain_ref[own, :] * right_link,
        left_link, right_link, d * by, b * by, c * by, a * by,
    )
    for n, value in enumerate(joint):
        joint_ref[n * width : (n + 1) * width] = value

    odd = lax.rem(me, 2)
    beyond = (rows + 1) * width
    framed[width:beyond] = field_ref[...]
    framed[pl.ds(pl.multiple_of((1 - odd) * beyond, 8), width), :] = inner_ref[...]
    framed[pl.ds(pl.multiple_of(odd * beyond, 8), width), :] = (
        outer_ref[...] + late_outer_ref[...]
    )
    lane = lax.broadcasted_iota(jnp.int32, (rows, LANES), 1)
    at_start = lane == 0
    at_end = lane == LANES - 1

    for k in range(layers):
        g, f, along = [], [], []
        for c in range(chunks):
            jac_low, jac, jac_high = (
                1.0 + zeta[k] * heights[pl.ds(own_start + s * chunks + c, rows, stride=chunks), :]
                for s in range(3)
            )
            place = c * layers + k
            f_low, f_mid, f_high = (
                framed[pl.ds(s * width + place, rows, stride=width), :] for s in range(3)
            )
            g.append(conduct_ref[pl.ds(place, rows, stride=width), :] * jac)
            f.append(f_mid)
            along.append(
                half * (jac + jac_high) * (f_high - f_mid)
                - half * (jac + jac_low) * (f_mid - f_low)
            )
        g_next = from_right(g, 1, lane)
        g_next[-1] = jnp.where(at_end, g[-1], g_next[-1])
        face = [half * (a + b) for a, b in zip(g, g_next)]
        face_low = from_left(face, 1, lane)
        face_low[0] = jnp.where(at_start, weight * g[0], face_low[0])
        diagonal = [1.0 + (a + b) for a, b in zip(face, face_low)]
        rhs = [2.0 * (a + b) for a, b in zip(f, along)]
        link = face
        link[-1] = jnp.where(at_end, 0.0, link[-1])
        both = solve_x(diagonal, link, rhs, lane)
        for c in range(chunks):
            solved[pl.ds(k * chunks + c, rows, stride=width), :] = both[c] - 2.0 * f[c]

    def part(ref, j):
        return ref[j * width : (j + 1) * width]

    p = [part(solved, 0) * inv[0]]
    for j in range(1, rows):
        p.append(part(solved, j) * inv[j] + scaled[j] * p[-1])
    for j in range(rows - 2, -1, -1):
        p[j] = p[j] + chain[j] * p[j + 1]
    for j in range(rows):
        p_ref[j * width : (j + 1) * width] = p[j]

    upward = p[-1] + part(joint_ref, 0) * p[0]
    downward = p[0] + part(joint_ref, 1) * p[-1]
    for b in range(blocks):
        sent_ref[b * width : (b + 1) * width] = jnp.where(b > me, upward, downward)


def last_kernel(
    sizes, came_ref, left_gain_ref, right_gain_ref, joint_ref, p_ref, u_ref, v_ref, field_ref,
    out_ref,
):
    rows, layers, chunks, row_total, layer_total, column_total = sizes
    width = layers * chunks
    blocks = row_total // rows
    me = lax.axis_index("wide")

    def part(ref, b):
        return ref[b * width : (b + 1) * width]

    left = jnp.zeros((width, LANES), f32)
    right = jnp.zeros((width, LANES), f32)
    for b in range(blocks - 1):
        left = jnp.where(b < me, part(came_ref, b) + part(left_gain_ref, b) * left, left)
        b = blocks - 1 - b
        right = jnp.where(b > me, part(came_ref, b) + part(right_gain_ref, b) * right, right)

    y = left + part(joint_ref, 2) * part(p_ref, 0)
    z = right + part(joint_ref, 3) * part(p_ref, rows - 1)
    before = part(joint_ref, 4) * y + part(joint_ref, 5) * z
    after = part(joint_ref, 6) * y + part(joint_ref, 7) * z
    for j in range(rows):
        x = part(p_ref, j) + part(u_ref, j) * before + part(v_ref, j) * after
        for k in range(layers):
            spot = pl.ds(j * width + k, chunks, stride=layers)
            out_ref[spot, :] = field_ref[spot, :] + x[k * chunks : (k + 1) * chunks]


def on_device(field, conduct, mode_index, mode_amp, mode_phase, step_index):
    rows, layers, columns = field.shape
    wide_count = lax.axis_size("wide")
    row_total = rows * wide_count
    grp_count = lax.axis_size("grp")
    layer_total = layers * grp_count
    chunks = columns // LANES
    width = layers * chunks
    sizes = (rows, layers, chunks, row_total, layer_total, columns)
    limit = pltpu.CompilerParams(vmem_limit_bytes=16 * 1024 * 1024)
    hbm = pl.BlockSpec(memory_space=pltpu.HBM)

    def lines(count):
        return jax.ShapeDtypeStruct((count * width, LANES), f32)

    packed, field_lines, conduct_lines, inner, outer = pl.pallas_call(
        load_kernel,
        out_shape=(
            jax.ShapeDtypeStruct((mode_index.shape[0], 8), f32),
            lines(rows),
            lines(rows),
            lines(1),
            lines(1),
        ),
        in_specs=[pl.BlockSpec(memory_space=pltpu.SMEM)] + [hbm] * 5,
        scratch_shapes=[
            pltpu.SMEM(mode_index.shape, jnp.int32),
            pltpu.SMEM(mode_amp.shape, f32),
            pltpu.SMEM(mode_phase.shape, f32),
            pltpu.SemaphoreType.DMA((7,)),
        ],
        compiler_params=limit,
    )(
        step_index,
        *(
            pltpu.with_memory_space_constraint(a, pltpu.HBM)
            for a in (mode_index, mode_amp, mode_phase, to_lines(field), to_lines(conduct))
        ),
    )

    def swap(rows_sent, first, groups):
        pairs = []
        for g in groups:
            for i in range(g * wide_count + first, (g + 1) * wide_count - 1, 2):
                pairs += [(i, i + 1), (i + 1, i)]
        return lax.ppermute(rows_sent, ("grp", "wide"), pairs)

    inner_came = swap(inner, 0, range(grp_count))
    outer_came = swap(outer, 1, [0])
    modes = lax.all_gather(packed, "grp", axis=0, tiled=True)
    modes, outer = lax.optimization_barrier((modes, outer))
    late_outer_came = swap(outer, 1, range(1, grp_count))

    sent, p, u, v, left_gain, right_gain, joint = pl.pallas_call(
        functools.partial(main_kernel, sizes),
        out_shape=(lines(wide_count),)
        + (lines(rows),) * 3
        + (lines(wide_count),) * 2
        + (lines(8),),
        scratch_shapes=[
            pltpu.VMEM(((row_total + 2) * chunks, LANES), f32),
            pltpu.VMEM((4 * wide_count * width, LANES), f32),
            pltpu.VMEM((2 * wide_count * width, LANES), f32),
            pltpu.VMEM(((rows + 2) * width, LANES), f32),
            pltpu.VMEM((rows * width, LANES), f32),
        ],
        compiler_params=limit,
    )(modes, field_lines, inner_came, outer_came, late_outer_came, conduct_lines)

    came = lax.all_to_all(
        sent.reshape(wide_count, width, LANES), "wide", split_axis=0, concat_axis=0
    ).reshape(wide_count * width, LANES)

    advanced = pl.pallas_call(
        functools.partial(last_kernel, sizes),
        out_shape=lines(rows),
        compiler_params=limit,
    )(came, left_gain, right_gain, joint, p, u, v, field_lines)
    return from_lines(advanced, field.shape)


def solution(mesh):
    return jax.shard_map(
        on_device,
        mesh=mesh,
        in_specs=(
            P("wide", "grp", None),
            P("wide", "grp", None),
            P("grp", None),
            P("grp"),
            P("grp"),
            P(),
        ),
        out_specs=P("wide", "grp", None),
        check_vma=False,
    )
```

```python
import functools
import math

import jax
import jax.numpy as jnp
from jax import lax
from jax.experimental import pallas as pl
from jax.experimental.pallas import tpu as pltpu
from jax.sharding import PartitionSpec as P

time_step = 600.0
implicit_weight = 0.5
weight = implicit_weight * time_step
LANES = 128
f32 = jnp.float32


def to_lines(block):
    rows, layers, columns = block.shape
    chunks = columns // LANES
    return (
        block.reshape(rows, layers, chunks, LANES)
        .transpose(0, 2, 1, 3)
        .reshape(rows * chunks * layers, LANES)
    )


def from_lines(lines, shape):
    rows, layers, columns = shape
    chunks = columns // LANES
    return (
        lines.reshape(rows, chunks, layers, LANES)
        .transpose(0, 2, 1, 3)
        .reshape(rows, layers, columns)
    )


def turns(wave, index, period):
    product = wave * index
    if period & (period - 1) == 0:
        product = product & (period - 1)
    else:
        product = lax.rem(product, jnp.int32(period))
    return product.astype(f32) * (1.0 / period)


def cos_sin(turn):
    part = turn - jnp.floor(turn + 0.5)
    square = part * part

    def series(first):
        terms = [
            (-1.0) ** n * math.pi ** (2 * n + first) / math.factorial(2 * n + first)
            for n in range(7)
        ]
        total = jnp.full_like(square, terms[-1])
        for term in terms[-2::-1]:
            total = total * square + term
        return total

    half_cos = series(0)
    half_sin = series(1) * part
    return 1.0 - 2.0 * half_sin * half_sin, 2.0 * half_sin * half_cos


def height_lines(modes, first_row, count, row_total, chunks, column_total):
    mode_count = modes.shape[0]
    wave_x = modes[:, 0:1].astype(jnp.int32)
    wave_y = modes[:, 1:2].astype(jnp.int32)
    offset = modes[:, 2:3]
    amp = modes[:, 3:4]
    spot = lax.broadcasted_iota(jnp.int32, (mode_count, count * chunks), 1)
    chunk = spot % chunks
    row = jnp.clip(first_row + spot // chunks, 0, row_total - 1)
    angle = (
        turns(wave_y, row, row_total) + turns(wave_x, chunk * LANES, column_total)
    ) + offset
    left_cos, left_sin = cos_sin(angle)
    lane = lax.broadcasted_iota(jnp.int32, (mode_count, LANES), 1)
    right_cos, right_sin = cos_sin(turns(wave_x, lane, column_total))
    left = jnp.concatenate([amp * left_cos, amp * left_sin], 0)
    right = jnp.concatenate([right_cos, -right_sin], 0)
    return lax.dot_general(
        left,
        right,
        (((0,), (0,)), ((), ())),
        precision=lax.Precision.HIGHEST,
        preferred_element_type=f32,
    )


def inverse(values):
    return pl.reciprocal(values, approx=False)


def from_left(values, stride, lane):
    moved = [pltpu.roll(v, stride, 1) for v in values]
    return [jnp.where(lane < stride, moved[c - 1], moved[c]) for c in range(len(values))]


def from_right(values, stride, lane):
    count = len(values)
    moved = [pltpu.roll(v, LANES - stride, 1) for v in values]
    return [
        jnp.where(lane >= LANES - stride, moved[(c + 1) % count], moved[c]) for c in range(count)
    ]


def solve_chunks(diagonal, link, rhs):
    count = len(rhs)
    if count == 1:
        return [rhs[0] * inverse(diagonal[0])]
    inv = {i: inverse(diagonal[i]) for i in range(0, count, 2)}
    scaled = {i: inv[i] * rhs[i] for i in inv}
    odd_diagonal, odd_link, odd_rhs = [], [], []
    for i in range(1, count, 2):
        d = diagonal[i] - link[i - 1] * (link[i - 1] * inv[i - 1])
        r = rhs[i] + link[i - 1] * scaled[i - 1]
        e = None
        if i + 1 < count:
            by = link[i] * inv[i + 1]
            d = d - link[i] * by
            r = r + link[i] * scaled[i + 1]
            e = by * link[i + 1] if i + 2 < count else None
        odd_diagonal.append(d)
        odd_rhs.append(r)
        odd_link.append(e)
    odd = solve_chunks(odd_diagonal, odd_link, odd_rhs)
    out = [None] * count
    out[1::2] = odd
    for i in range(0, count, 2):
        r = rhs[i]
        if i > 0:
            r = r + link[i - 1] * out[i - 1]
        if i + 1 < count:
            r = r + link[i] * out[i + 1]
        out[i] = r * inv[i]
    return out


def solve_x(diagonal, link, rhs, lane):
    stride = 1
    count = len(rhs)
    while stride < LANES:
        inv = [inverse(d) for d in diagonal]
        t = [q * r for q, r in zip(inv, rhs)]
        w = [q * e for q, e in zip(inv, link)]
        low_d = from_left([e * v for e, v in zip(link, w)], stride, lane)
        low_r = from_left([e * v for e, v in zip(link, t)], stride, lane)
        high_q = from_right(inv, stride, lane)
        high_t = from_right(t, stride, lane)
        high_w = from_right(w, stride, lane)
        diagonal = [
            diagonal[c] - low_d[c] - link[c] * (link[c] * high_q[c]) for c in range(count)
        ]
        rhs = [rhs[c] + low_r[c] + link[c] * high_t[c] for c in range(count)]
        link = [link[c] * high_w[c] for c in range(count)]
        stride *= 2
    return solve_chunks(diagonal, link, rhs)


def load_kernel(
    step_ref, index_ref, amp_ref, phase_ref, field_ref, conduct_ref,
    packed_ref, field_out, conduct_out, inner_ref, outer_ref,
    index_in, amp_in, phase_in, sems,
):
    width = inner_ref.shape[0]
    last = field_ref.shape[0] - width
    odd = lax.rem(lax.axis_index("wide"), 2)
    inner_rows = pl.ds(pl.multiple_of((1 - odd) * last, 8), width)
    outer_rows = pl.ds(pl.multiple_of(odd * last, 8), width)
    pairs = (
        (index_ref, index_in),
        (amp_ref, amp_in),
        (phase_ref, phase_in),
        (field_ref.at[inner_rows], inner_ref),
        (field_ref.at[outer_rows], outer_ref),
        (field_ref, field_out),
        (conduct_ref, conduct_out),
    )
    copies = [pltpu.make_async_copy(a, b, sems.at[n]) for n, (a, b) in enumerate(pairs)]
    for copy in copies:
        copy.start()
    for copy in copies[:3]:
        copy.wait()
    count = index_in.shape[0]
    row = lax.broadcasted_iota(jnp.int32, packed_ref.shape, 0)
    lane = lax.broadcasted_iota(jnp.int32, packed_ref.shape, 1)
    total = jnp.zeros(packed_ref.shape, f32)
    for m in range(count):
        moment = lax.rem(index_in[m, 2] * step_ref[0], jnp.int32(64)).astype(f32)
        offset = phase_in[m] * (0.5 / math.pi) + moment * (1.0 / 64.0)
        for place, value in enumerate(
            (index_in[m, 0].astype(f32), index_in[m, 1].astype(f32), offset, amp_in[m])
        ):
            total = jnp.where((row == m) & (lane == place), value, total)
    packed_ref[...] = total
    for copy in copies[3:]:
        copy.wait()


def block_factors(face):
    inv, scaled, chain, u = [], [], [], []
    rows = len(face) - 1
    rest = 1.0 + face[0]
    for j in range(rows):
        inv.append(inverse(rest + face[j + 1]))
        scaled.append(face[j] * inv[j])
        chain.append(face[j + 1] * inv[j])
        u.append(scaled[j] * u[-1] if j else scaled[j])
        rest = 1.0 + rest * chain[j]
    v = list(chain)
    for j in range(rows - 2, -1, -1):
        u[j] = u[j] + chain[j] * u[j + 1]
        v[j] = chain[j] * v[j + 1]
    return inv, scaled, chain, u, v


def block_ends(face):
    rows = len(face) - 1
    down = 1.0 + face[0]
    up = 1.0 + face[rows]
    v_first = None
    for j in range(rows):
        v_last = face[j + 1] * inverse(down + face[j + 1])
        v_first = v_last if v_first is None else v_first * v_last
        u_first = face[rows - 1 - j] * inverse(up + face[rows - 1 - j])
        if j < rows - 1:
            down = 1.0 + down * v_last
            up = 1.0 + up * u_first
    u_last = v_first * (face[0] * inverse(face[rows]))
    return u_first, v_first, u_last, v_last


def main_kernel(
    sizes, modes_ref, field_ref, inner_ref, outer_ref, late_outer_ref, conduct_ref,
    sent_ref, p_ref, u_ref, v_ref, left_gain_ref, right_gain_ref, joint_ref,
    heights, ends, links, framed, solved,
):
    rows, layers, chunks, row_total, layer_total, column_total = sizes
    width = layers * chunks
    blocks = row_total // rows
    me = lax.axis_index("wide")
    first_layer = lax.axis_index("grp") * layers
    zeta = [
        ((first_layer + k).astype(f32) + 0.5) * (1.0 / layer_total) for k in range(layers)
    ]
    half = 0.5 * weight
    body = height_lines(modes_ref[...], 0, row_total, row_total, chunks, column_total)
    heights[chunks : (row_total + 1) * chunks] = body
    heights[0:chunks] = body[0:chunks]
    heights[(row_total + 1) * chunks : (row_total + 2) * chunks] = body[
        (row_total - 1) * chunks : row_total * chunks
    ]
    own_start = pl.multiple_of(me * (rows * chunks), 8)

    def faces(start):
        h = [heights[pl.ds(start + j * chunks, chunks), :] for j in range(rows + 2)]
        out = []
        for j in range(rows + 1):
            both = h[j] + h[j + 1]
            out.append(jnp.concatenate([weight + (half * z) * both for z in zeta], 0))
        return out

    def keep_ends(b, values):
        base = pl.multiple_of(b * (4 * width), 8)
        for n, value in enumerate(values):
            ends[pl.ds(base + n * width, width), :] = value

    inv, scaled, chain, u, v = block_factors(faces(own_start))
    for j in range(rows):
        u_ref[j * width : (j + 1) * width] = u[j]
        v_ref[j * width : (j + 1) * width] = v[j]
    keep_ends(me, (u[0], v[0], u[-1], v[-1]))

    def other_block(n):
        b = lax.rem(me + 1 + n, blocks)
        keep_ends(b, block_ends(faces(pl.multiple_of(b * (rows * chunks), 8))))

    if blocks <= 8:
        for n in range(blocks - 1):
            other_block(n)
    else:
        lax.fori_loop(0, blocks - 1, lambda n, carry: (other_block(n), carry)[1], 0)

    def end(b, n):
        return ends[(4 * b + n) * width : (4 * b + n + 1) * width]

    left = jnp.zeros((width, LANES), f32)
    right = jnp.zeros((width, LANES), f32)
    for b in range(blocks):
        u_first, v_first, u_last, v_last = (end(b, n) for n in range(4))
        gain = u_last * inverse(1.0 - u_first * left)
        left_gain_ref[b * width : (b + 1) * width] = gain
        links[b * width : (b + 1) * width] = left
        left = v_last + gain * left * v_first
        b = blocks - 1 - b
        u_first, v_first, u_last, v_last = (end(b, n) for n in range(4))
        gain = v_first * inverse(1.0 - v_last * right)
        right_gain_ref[b * width : (b + 1) * width] = gain
        links[(blocks + b) * width : (blocks + b + 1) * width] = right
        right = u_first + gain * right * u_last

    own = pl.ds(pl.multiple_of(me * width, 8), width)
    left_link = links[own, :]
    right_link = links[pl.ds(pl.multiple_of((blocks + me) * width, 8), width), :]
    a = 1.0 - left_link * u[0]
    b = left_link * v[0]
    c = right_link * u[-1]
    d = 1.0 - right_link * v[-1]
    by = inverse(a * d - b * c)
    joint = (
        left_gain_ref[own, :] * left_link, right_gain_ref[own, :] * right_link,
        left_link, right_link, d * by, b * by, c * by, a * by,
    )
    for n, value in enumerate(joint):
        joint_ref[n * width : (n + 1) * width] = value

    odd = lax.rem(me, 2)
    beyond = (rows + 1) * width
    framed[width:beyond] = field_ref[...]
    framed[pl.ds(pl.multiple_of((1 - odd) * beyond, 8), width), :] = inner_ref[...]
    outer_rows = jnp.where(first_layer == 0, outer_ref[...], late_outer_ref[...])
    at_edge = (me == 0) | (me == blocks - 1)
    framed[pl.ds(pl.multiple_of(odd * beyond, 8), width), :] = jnp.where(at_edge, 0.0, outer_rows)
    lane = lax.broadcasted_iota(jnp.int32, (rows, LANES), 1)
    at_start = lane == 0
    at_end = lane == LANES - 1

    for k in range(layers):
        g, f, along = [], [], []
        for c in range(chunks):
            jac_low, jac, jac_high = (
                1.0 + zeta[k] * heights[pl.ds(own_start + s * chunks + c, rows, stride=chunks), :]
                for s in range(3)
            )
            place = c * layers + k
            f_low, f_mid, f_high = (
                framed[pl.ds(s * width + place, rows, stride=width), :] for s in range(3)
            )
            g.append(conduct_ref[pl.ds(place, rows, stride=width), :] * jac)
            f.append(f_mid)
            along.append(
                half * (jac + jac_high) * (f_high - f_mid)
                - half * (jac + jac_low) * (f_mid - f_low)
            )
        g_next = from_right(g, 1, lane)
        g_next[-1] = jnp.where(at_end, g[-1], g_next[-1])
        face = [half * (a + b) for a, b in zip(g, g_next)]
        face_low = from_left(face, 1, lane)
        face_low[0] = jnp.where(at_start, weight * g[0], face_low[0])
        diagonal = [1.0 + (a + b) for a, b in zip(face, face_low)]
        rhs = [2.0 * (a + b) for a, b in zip(f, along)]
        link = face
        link[-1] = jnp.where(at_end, 0.0, link[-1])
        both = solve_x(diagonal, link, rhs, lane)
        for c in range(chunks):
            solved[pl.ds(k * chunks + c, rows, stride=width), :] = both[c] - 2.0 * f[c]

    def part(ref, j):
        return ref[j * width : (j + 1) * width]

    p = [part(solved, 0) * inv[0]]
    for j in range(1, rows):
        p.append(part(solved, j) * inv[j] + scaled[j] * p[-1])
    for j in range(rows - 2, -1, -1):
        p[j] = p[j] + chain[j] * p[j + 1]
    for j in range(rows):
        p_ref[j * width : (j + 1) * width] = p[j]

    upward = p[-1] + part(joint_ref, 0) * p[0]
    downward = p[0] + part(joint_ref, 1) * p[-1]
    for b in range(blocks):
        sent_ref[b * width : (b + 1) * width] = jnp.where(b > me, upward, downward)


def last_kernel(
    sizes, came_ref, left_gain_ref, right_gain_ref, joint_ref, p_ref, u_ref, v_ref, field_ref,
    out_ref,
):
    rows, layers, chunks, row_total, layer_total, column_total = sizes
    width = layers * chunks
    blocks = row_total // rows
    me = lax.axis_index("wide")

    def part(ref, b):
        return ref[b * width : (b + 1) * width]

    left = jnp.zeros((width, LANES), f32)
    right = jnp.zeros((width, LANES), f32)
    for b in range(blocks - 1):
        left = jnp.where(b < me, part(came_ref, b) + part(left_gain_ref, b) * left, left)
        b = blocks - 1 - b
        right = jnp.where(b > me, part(came_ref, b) + part(right_gain_ref, b) * right, right)

    y = left + part(joint_ref, 2) * part(p_ref, 0)
    z = right + part(joint_ref, 3) * part(p_ref, rows - 1)
    before = part(joint_ref, 4) * y + part(joint_ref, 5) * z
    after = part(joint_ref, 6) * y + part(joint_ref, 7) * z
    for j in range(rows):
        x = part(p_ref, j) + part(u_ref, j) * before + part(v_ref, j) * after
        for k in range(layers):
            spot = pl.ds(j * width + k, chunks, stride=layers)
            out_ref[spot, :] = field_ref[spot, :] + x[k * chunks : (k + 1) * chunks]


def on_device(field, conduct, mode_index, mode_amp, mode_phase, step_index):
    rows, layers, columns = field.shape
    wide_count = lax.axis_size("wide")
    row_total = rows * wide_count
    grp_count = lax.axis_size("grp")
    layer_total = layers * grp_count
    chunks = columns // LANES
    width = layers * chunks
    sizes = (rows, layers, chunks, row_total, layer_total, columns)
    limit = pltpu.CompilerParams(vmem_limit_bytes=16 * 1024 * 1024)
    hbm = pl.BlockSpec(memory_space=pltpu.HBM)

    def lines(count):
        return jax.ShapeDtypeStruct((count * width, LANES), f32)

    packed, field_lines, conduct_lines, inner, outer = pl.pallas_call(
        load_kernel,
        out_shape=(
            jax.ShapeDtypeStruct((mode_index.shape[0], 8), f32),
            lines(rows),
            lines(rows),
            lines(1),
            lines(1),
        ),
        in_specs=[pl.BlockSpec(memory_space=pltpu.SMEM)] + [hbm] * 5,
        scratch_shapes=[
            pltpu.SMEM(mode_index.shape, jnp.int32),
            pltpu.SMEM(mode_amp.shape, f32),
            pltpu.SMEM(mode_phase.shape, f32),
            pltpu.SemaphoreType.DMA((7,)),
        ],
        compiler_params=limit,
    )(
        step_index,
        *(
            pltpu.with_memory_space_constraint(a, pltpu.HBM)
            for a in (mode_index, mode_amp, mode_phase, to_lines(field), to_lines(conduct))
        ),
    )

    def swap(rows_sent, first, groups):
        pairs = []
        for g in range(grp_count):
            for i in range(wide_count):
                partner = i + 1 if (i - first) % 2 == 0 else i - 1
                if g not in groups or not 0 <= partner < wide_count:
                    partner = i
                pairs.append((g * wide_count + i, g * wide_count + partner))
        return lax.ppermute(rows_sent, ("grp", "wide"), pairs)

    inner_came = swap(inner, 0, range(grp_count))
    outer_came = swap(outer, 1, [0])
    packed, inner_came, outer_came = lax.optimization_barrier((packed, inner_came, outer_came))
    modes = lax.all_gather(packed, "grp", axis=0, tiled=True)
    modes, outer = lax.optimization_barrier((modes, outer))
    late_outer_came = swap(outer, 1, range(1, grp_count))

    sent, p, u, v, left_gain, right_gain, joint = pl.pallas_call(
        functools.partial(main_kernel, sizes),
        out_shape=(lines(wide_count),)
        + (lines(rows),) * 3
        + (lines(wide_count),) * 2
        + (lines(8),),
        scratch_shapes=[
            pltpu.VMEM(((row_total + 2) * chunks, LANES), f32),
            pltpu.VMEM((4 * wide_count * width, LANES), f32),
            pltpu.VMEM((2 * wide_count * width, LANES), f32),
            pltpu.VMEM(((rows + 2) * width, LANES), f32),
            pltpu.VMEM((rows * width, LANES), f32),
        ],
        compiler_params=limit,
    )(modes, field_lines, inner_came, outer_came, late_outer_came, conduct_lines)

    came = lax.all_to_all(
        sent.reshape(wide_count, width, LANES), "wide", split_axis=0, concat_axis=0
    ).reshape(wide_count * width, LANES)

    advanced = pl.pallas_call(
        functools.partial(last_kernel, sizes),
        out_shape=lines(rows),
        compiler_params=limit,
    )(came, left_gain, right_gain, joint, p, u, v, field_lines)
    return from_lines(advanced, field.shape)


def solution(mesh):
    return jax.shard_map(
        on_device,
        mesh=mesh,
        in_specs=(
            P("wide", "grp", None),
            P("wide", "grp", None),
            P("grp", None),
            P("grp"),
            P("grp"),
            P(),
        ),
        out_specs=P("wide", "grp", None),
        check_vma=False,
    )
```

```python
import functools
import math

import jax
import jax.numpy as jnp
from jax import lax
from jax.experimental import pallas as pl
from jax.experimental.pallas import tpu as pltpu
from jax.sharding import PartitionSpec as P

time_step = 600.0
implicit_weight = 0.5
weight = implicit_weight * time_step
LANES = 128
f32 = jnp.float32


def to_lines(block):
    rows, layers, columns = block.shape
    chunks = columns // LANES
    return (
        block.reshape(rows, layers, chunks, LANES)
        .transpose(0, 2, 1, 3)
        .reshape(rows * chunks * layers, LANES)
    )


def from_lines(lines, shape):
    rows, layers, columns = shape
    chunks = columns // LANES
    return (
        lines.reshape(rows, chunks, layers, LANES)
        .transpose(0, 2, 1, 3)
        .reshape(rows, layers, columns)
    )


def turns(wave, index, period):
    product = wave * index
    if period & (period - 1) == 0:
        product = product & (period - 1)
    else:
        product = lax.rem(product, jnp.int32(period))
    return product.astype(f32) * (1.0 / period)


def cos_sin(turn):
    part = turn - jnp.floor(turn + 0.5)
    square = part * part

    def series(first):
        terms = [
            (-1.0) ** n * math.pi ** (2 * n + first) / math.factorial(2 * n + first)
            for n in range(7)
        ]
        total = jnp.full_like(square, terms[-1])
        for term in terms[-2::-1]:
            total = total * square + term
        return total

    half_cos = series(0)
    half_sin = series(1) * part
    return 1.0 - 2.0 * half_sin * half_sin, 2.0 * half_sin * half_cos


def height_lines(modes, first_row, count, row_total, chunks, column_total):
    mode_count = modes.shape[0]
    wave_x = modes[:, 0:1].astype(jnp.int32)
    wave_y = modes[:, 1:2].astype(jnp.int32)
    offset = modes[:, 2:3]
    amp = modes[:, 3:4]
    spot = lax.broadcasted_iota(jnp.int32, (mode_count, count * chunks), 1)
    chunk = spot % chunks
    row = jnp.clip(first_row + spot // chunks, 0, row_total - 1)
    angle = (
        turns(wave_y, row, row_total) + turns(wave_x, chunk * LANES, column_total)
    ) + offset
    left_cos, left_sin = cos_sin(angle)
    lane = lax.broadcasted_iota(jnp.int32, (mode_count, LANES), 1)
    right_cos, right_sin = cos_sin(turns(wave_x, lane, column_total))
    left = jnp.concatenate([amp * left_cos, amp * left_sin], 0)
    right = jnp.concatenate([right_cos, -right_sin], 0)
    return lax.dot_general(
        left,
        right,
        (((0,), (0,)), ((), ())),
        precision=lax.Precision.HIGHEST,
        preferred_element_type=f32,
    )


def inverse(values):
    return pl.reciprocal(values, approx=False)


def from_left(values, stride, lane):
    moved = [pltpu.roll(v, stride, 1) for v in values]
    return [jnp.where(lane < stride, moved[c - 1], moved[c]) for c in range(len(values))]


def from_right(values, stride, lane):
    count = len(values)
    moved = [pltpu.roll(v, LANES - stride, 1) for v in values]
    return [
        jnp.where(lane >= LANES - stride, moved[(c + 1) % count], moved[c]) for c in range(count)
    ]


def solve_chunks(diagonal, link, rhs):
    count = len(rhs)
    if count == 1:
        return [rhs[0] * inverse(diagonal[0])]
    inv = {i: inverse(diagonal[i]) for i in range(0, count, 2)}
    scaled = {i: inv[i] * rhs[i] for i in inv}
    odd_diagonal, odd_link, odd_rhs = [], [], []
    for i in range(1, count, 2):
        d = diagonal[i] - link[i - 1] * (link[i - 1] * inv[i - 1])
        r = rhs[i] + link[i - 1] * scaled[i - 1]
        e = None
        if i + 1 < count:
            by = link[i] * inv[i + 1]
            d = d - link[i] * by
            r = r + link[i] * scaled[i + 1]
            e = by * link[i + 1] if i + 2 < count else None
        odd_diagonal.append(d)
        odd_rhs.append(r)
        odd_link.append(e)
    odd = solve_chunks(odd_diagonal, odd_link, odd_rhs)
    out = [None] * count
    out[1::2] = odd
    for i in range(0, count, 2):
        r = rhs[i]
        if i > 0:
            r = r + link[i - 1] * out[i - 1]
        if i + 1 < count:
            r = r + link[i] * out[i + 1]
        out[i] = r * inv[i]
    return out


def solve_x(diagonal, link, rhs, lane):
    stride = 1
    count = len(rhs)
    while stride < LANES:
        inv = [inverse(d) for d in diagonal]
        t = [q * r for q, r in zip(inv, rhs)]
        w = [q * e for q, e in zip(inv, link)]
        low_d = from_left([e * v for e, v in zip(link, w)], stride, lane)
        low_r = from_left([e * v for e, v in zip(link, t)], stride, lane)
        high_q = from_right(inv, stride, lane)
        high_t = from_right(t, stride, lane)
        high_w = from_right(w, stride, lane)
        diagonal = [
            diagonal[c] - low_d[c] - link[c] * (link[c] * high_q[c]) for c in range(count)
        ]
        rhs = [rhs[c] + low_r[c] + link[c] * high_t[c] for c in range(count)]
        link = [link[c] * high_w[c] for c in range(count)]
        stride *= 2
    return solve_chunks(diagonal, link, rhs)


def load_kernel(
    step_ref, index_ref, amp_ref, phase_ref, field_ref, conduct_ref,
    packed_ref, field_out, conduct_out, inner_ref, outer_ref,
    index_in, amp_in, phase_in, sems,
):
    width = inner_ref.shape[0]
    last = field_ref.shape[0] - width
    odd = lax.rem(lax.axis_index("wide"), 2)
    inner_rows = pl.ds(pl.multiple_of((1 - odd) * last, 8), width)
    outer_rows = pl.ds(pl.multiple_of(odd * last, 8), width)
    pairs = (
        (index_ref, index_in),
        (amp_ref, amp_in),
        (phase_ref, phase_in),
        (field_ref.at[inner_rows], inner_ref),
        (field_ref.at[outer_rows], outer_ref),
        (field_ref, field_out),
        (conduct_ref, conduct_out),
    )
    copies = [pltpu.make_async_copy(a, b, sems.at[n]) for n, (a, b) in enumerate(pairs)]
    for copy in copies:
        copy.start()
    for copy in copies[:3]:
        copy.wait()
    count = index_in.shape[0]
    row = lax.broadcasted_iota(jnp.int32, packed_ref.shape, 0)
    lane = lax.broadcasted_iota(jnp.int32, packed_ref.shape, 1)
    total = jnp.zeros(packed_ref.shape, f32)
    for m in range(count):
        moment = lax.rem(index_in[m, 2] * step_ref[0], jnp.int32(64)).astype(f32)
        offset = phase_in[m] * (0.5 / math.pi) + moment * (1.0 / 64.0)
        for place, value in enumerate(
            (index_in[m, 0].astype(f32), index_in[m, 1].astype(f32), offset, amp_in[m])
        ):
            total = jnp.where((row == m) & (lane == place), value, total)
    packed_ref[...] = total
    for copy in copies[3:]:
        copy.wait()


def block_factors(face):
    inv, scaled, chain, u = [], [], [], []
    rows = len(face) - 1
    rest = 1.0 + face[0]
    for j in range(rows):
        inv.append(inverse(rest + face[j + 1]))
        scaled.append(face[j] * inv[j])
        chain.append(face[j + 1] * inv[j])
        u.append(scaled[j] * u[-1] if j else scaled[j])
        rest = 1.0 + rest * chain[j]
    v = list(chain)
    for j in range(rows - 2, -1, -1):
        u[j] = u[j] + chain[j] * u[j + 1]
        v[j] = chain[j] * v[j + 1]
    return inv, scaled, chain, u, v


def block_ends(face):
    rows = len(face) - 1
    down = 1.0 + face[0]
    up = 1.0 + face[rows]
    v_first = None
    for j in range(rows):
        v_last = face[j + 1] * inverse(down + face[j + 1])
        v_first = v_last if v_first is None else v_first * v_last
        u_first = face[rows - 1 - j] * inverse(up + face[rows - 1 - j])
        if j < rows - 1:
            down = 1.0 + down * v_last
            up = 1.0 + up * u_first
    u_last = v_first * (face[0] * inverse(face[rows]))
    return u_first, v_first, u_last, v_last


def height_kernel(sizes, modes_ref, inner_ref, outer_ref, heights_ref, halo_ref):
    rows, layers, chunks, row_total, layer_total, column_total = sizes
    width = layers * chunks
    body = height_lines(modes_ref[...], 0, row_total, row_total, chunks, column_total)
    heights_ref[chunks : (row_total + 1) * chunks] = body
    heights_ref[0:chunks] = body[0:chunks]
    heights_ref[(row_total + 1) * chunks : (row_total + 2) * chunks] = body[
        (row_total - 1) * chunks : row_total * chunks
    ]
    halo_ref[0:width] = inner_ref[...]
    halo_ref[width : 2 * width] = outer_ref[...]


def main_kernel(
    sizes, heights, halo_ref, field_ref, late_outer_ref, conduct_ref,
    sent_ref, p_ref, u_ref, v_ref, left_gain_ref, right_gain_ref, joint_ref,
    ends, links, framed, solved,
):
    rows, layers, chunks, row_total, layer_total, column_total = sizes
    width = layers * chunks
    blocks = row_total // rows
    me = lax.axis_index("wide")
    first_layer = lax.axis_index("grp") * layers
    zeta = [
        ((first_layer + k).astype(f32) + 0.5) * (1.0 / layer_total) for k in range(layers)
    ]
    half = 0.5 * weight
    own_start = pl.multiple_of(me * (rows * chunks), 8)

    def faces(start):
        h = [heights[pl.ds(start + j * chunks, chunks), :] for j in range(rows + 2)]
        out = []
        for j in range(rows + 1):
            both = h[j] + h[j + 1]
            out.append(jnp.concatenate([weight + (half * z) * both for z in zeta], 0))
        return out

    def keep_ends(b, values):
        base = pl.multiple_of(b * (4 * width), 8)
        for n, value in enumerate(values):
            ends[pl.ds(base + n * width, width), :] = value

    inv, scaled, chain, u, v = block_factors(faces(own_start))
    for j in range(rows):
        u_ref[j * width : (j + 1) * width] = u[j]
        v_ref[j * width : (j + 1) * width] = v[j]
    keep_ends(me, (u[0], v[0], u[-1], v[-1]))

    def other_block(n):
        b = lax.rem(me + 1 + n, blocks)
        keep_ends(b, block_ends(faces(pl.multiple_of(b * (rows * chunks), 8))))

    if blocks <= 8:
        for n in range(blocks - 1):
            other_block(n)
    else:
        lax.fori_loop(0, blocks - 1, lambda n, carry: (other_block(n), carry)[1], 0)

    def end(b, n):
        return ends[(4 * b + n) * width : (4 * b + n + 1) * width]

    left = jnp.zeros((width, LANES), f32)
    right = jnp.zeros((width, LANES), f32)
    for b in range(blocks):
        u_first, v_first, u_last, v_last = (end(b, n) for n in range(4))
        gain = u_last * inverse(1.0 - u_first * left)
        left_gain_ref[b * width : (b + 1) * width] = gain
        links[b * width : (b + 1) * width] = left
        left = v_last + gain * left * v_first
        b = blocks - 1 - b
        u_first, v_first, u_last, v_last = (end(b, n) for n in range(4))
        gain = v_first * inverse(1.0 - v_last * right)
        right_gain_ref[b * width : (b + 1) * width] = gain
        links[(blocks + b) * width : (blocks + b + 1) * width] = right
        right = u_first + gain * right * u_last

    own = pl.ds(pl.multiple_of(me * width, 8), width)
    left_link = links[own, :]
    right_link = links[pl.ds(pl.multiple_of((blocks + me) * width, 8), width), :]
    a = 1.0 - left_link * u[0]
    b = left_link * v[0]
    c = right_link * u[-1]
    d = 1.0 - right_link * v[-1]
    by = inverse(a * d - b * c)
    joint = (
        left_gain_ref[own, :] * left_link, right_gain_ref[own, :] * right_link,
        left_link, right_link, d * by, b * by, c * by, a * by,
    )
    for n, value in enumerate(joint):
        joint_ref[n * width : (n + 1) * width] = value

    odd = lax.rem(me, 2)
    beyond = (rows + 1) * width
    framed[width:beyond] = field_ref[...]
    framed[pl.ds(pl.multiple_of((1 - odd) * beyond, 8), width), :] = halo_ref[0:width]
    outer_rows = jnp.where(first_layer == 0, halo_ref[width : 2 * width], late_outer_ref[...])
    at_edge = (me == 0) | (me == blocks - 1)
    framed[pl.ds(pl.multiple_of(odd * beyond, 8), width), :] = jnp.where(at_edge, 0.0, outer_rows)
    lane = lax.broadcasted_iota(jnp.int32, (rows, LANES), 1)
    at_start = lane == 0
    at_end = lane == LANES - 1

    for k in range(layers):
        g, f, along = [], [], []
        for c in range(chunks):
            jac_low, jac, jac_high = (
                1.0 + zeta[k] * heights[pl.ds(own_start + s * chunks + c, rows, stride=chunks), :]
                for s in range(3)
            )
            place = c * layers + k
            f_low, f_mid, f_high = (
                framed[pl.ds(s * width + place, rows, stride=width), :] for s in range(3)
            )
            g.append(conduct_ref[pl.ds(place, rows, stride=width), :] * jac)
            f.append(f_mid)
            along.append(
                half * (jac + jac_high) * (f_high - f_mid)
                - half * (jac + jac_low) * (f_mid - f_low)
            )
        g_next = from_right(g, 1, lane)
        g_next[-1] = jnp.where(at_end, g[-1], g_next[-1])
        face = [half * (a + b) for a, b in zip(g, g_next)]
        face_low = from_left(face, 1, lane)
        face_low[0] = jnp.where(at_start, weight * g[0], face_low[0])
        diagonal = [1.0 + (a + b) for a, b in zip(face, face_low)]
        rhs = [2.0 * (a + b) for a, b in zip(f, along)]
        link = face
        link[-1] = jnp.where(at_end, 0.0, link[-1])
        both = solve_x(diagonal, link, rhs, lane)
        for c in range(chunks):
            solved[pl.ds(k * chunks + c, rows, stride=width), :] = both[c] - 2.0 * f[c]

    def part(ref, j):
        return ref[j * width : (j + 1) * width]

    p = [part(solved, 0) * inv[0]]
    for j in range(1, rows):
        p.append(part(solved, j) * inv[j] + scaled[j] * p[-1])
    for j in range(rows - 2, -1, -1):
        p[j] = p[j] + chain[j] * p[j + 1]
    for j in range(rows):
        p_ref[j * width : (j + 1) * width] = p[j]

    upward = p[-1] + part(joint_ref, 0) * p[0]
    downward = p[0] + part(joint_ref, 1) * p[-1]
    for b in range(blocks):
        sent_ref[b * width : (b + 1) * width] = jnp.where(b > me, upward, downward)


def last_kernel(
    sizes, came_ref, left_gain_ref, right_gain_ref, joint_ref, p_ref, u_ref, v_ref, field_ref,
    out_ref,
):
    rows, layers, chunks, row_total, layer_total, column_total = sizes
    width = layers * chunks
    blocks = row_total // rows
    me = lax.axis_index("wide")

    def part(ref, b):
        return ref[b * width : (b + 1) * width]

    left = jnp.zeros((width, LANES), f32)
    right = jnp.zeros((width, LANES), f32)
    for b in range(blocks - 1):
        left = jnp.where(b < me, part(came_ref, b) + part(left_gain_ref, b) * left, left)
        b = blocks - 1 - b
        right = jnp.where(b > me, part(came_ref, b) + part(right_gain_ref, b) * right, right)

    y = left + part(joint_ref, 2) * part(p_ref, 0)
    z = right + part(joint_ref, 3) * part(p_ref, rows - 1)
    before = part(joint_ref, 4) * y + part(joint_ref, 5) * z
    after = part(joint_ref, 6) * y + part(joint_ref, 7) * z
    for j in range(rows):
        x = part(p_ref, j) + part(u_ref, j) * before + part(v_ref, j) * after
        for k in range(layers):
            spot = pl.ds(j * width + k, chunks, stride=layers)
            out_ref[spot, :] = field_ref[spot, :] + x[k * chunks : (k + 1) * chunks]


def on_device(field, conduct, mode_index, mode_amp, mode_phase, step_index):
    rows, layers, columns = field.shape
    wide_count = lax.axis_size("wide")
    row_total = rows * wide_count
    grp_count = lax.axis_size("grp")
    layer_total = layers * grp_count
    chunks = columns // LANES
    width = layers * chunks
    sizes = (rows, layers, chunks, row_total, layer_total, columns)
    limit = pltpu.CompilerParams(vmem_limit_bytes=16 * 1024 * 1024)
    hbm = pl.BlockSpec(memory_space=pltpu.HBM)

    def lines(count):
        return jax.ShapeDtypeStruct((count * width, LANES), f32)

    packed, field_lines, conduct_lines, inner, outer = pl.pallas_call(
        load_kernel,
        out_shape=(
            jax.ShapeDtypeStruct((mode_index.shape[0], 8), f32),
            lines(rows),
            lines(rows),
            lines(1),
            lines(1),
        ),
        in_specs=[pl.BlockSpec(memory_space=pltpu.SMEM)] + [hbm] * 5,
        scratch_shapes=[
            pltpu.SMEM(mode_index.shape, jnp.int32),
            pltpu.SMEM(mode_amp.shape, f32),
            pltpu.SMEM(mode_phase.shape, f32),
            pltpu.SemaphoreType.DMA((7,)),
        ],
        compiler_params=limit,
    )(
        step_index,
        *(
            pltpu.with_memory_space_constraint(a, pltpu.HBM)
            for a in (mode_index, mode_amp, mode_phase, to_lines(field), to_lines(conduct))
        ),
    )

    def swap(rows_sent, first, groups):
        pairs = []
        for g in range(grp_count):
            for i in range(wide_count):
                partner = i + 1 if (i - first) % 2 == 0 else i - 1
                if g not in groups or not 0 <= partner < wide_count:
                    partner = i
                pairs.append((g * wide_count + i, g * wide_count + partner))
        return lax.ppermute(rows_sent, ("grp", "wide"), pairs)

    inner_came = swap(inner, 0, range(grp_count))
    outer_came = swap(outer, 1, [0])
    modes = lax.all_gather(packed, "grp", axis=0, tiled=True)
    modes, outer = lax.optimization_barrier((modes, outer))
    late_outer_came = swap(outer, 1, range(1, grp_count))

    heights, halo = pl.pallas_call(
        functools.partial(height_kernel, sizes),
        out_shape=(jax.ShapeDtypeStruct(((row_total + 2) * chunks, LANES), f32), lines(2)),
        compiler_params=limit,
    )(modes, inner_came, outer_came)

    sent, p, u, v, left_gain, right_gain, joint = pl.pallas_call(
        functools.partial(main_kernel, sizes),
        out_shape=(lines(wide_count),)
        + (lines(rows),) * 3
        + (lines(wide_count),) * 2
        + (lines(8),),
        scratch_shapes=[
            pltpu.VMEM((4 * wide_count * width, LANES), f32),
            pltpu.VMEM((2 * wide_count * width, LANES), f32),
            pltpu.VMEM(((rows + 2) * width, LANES), f32),
            pltpu.VMEM((rows * width, LANES), f32),
        ],
        compiler_params=limit,
    )(heights, halo, field_lines, late_outer_came, conduct_lines)

    came = lax.all_to_all(
        sent.reshape(wide_count, width, LANES), "wide", split_axis=0, concat_axis=0
    ).reshape(wide_count * width, LANES)

    advanced = pl.pallas_call(
        functools.partial(last_kernel, sizes),
        out_shape=lines(rows),
        compiler_params=limit,
    )(came, left_gain, right_gain, joint, p, u, v, field_lines)
    return from_lines(advanced, field.shape)


def solution(mesh):
    return jax.shard_map(
        on_device,
        mesh=mesh,
        in_specs=(
            P("wide", "grp", None),
            P("wide", "grp", None),
            P("grp", None),
            P("grp"),
            P("grp"),
            P(),
        ),
        out_specs=P("wide", "grp", None),
        check_vma=False,
    )
```

```python
import functools
import math

import jax
import jax.numpy as jnp
from jax import lax
from jax.experimental import pallas as pl
from jax.experimental.pallas import tpu as pltpu
from jax.sharding import PartitionSpec as P

time_step = 600.0
implicit_weight = 0.5
weight = implicit_weight * time_step
LANES = 128
f32 = jnp.float32


def to_lines(block):
    rows, layers, columns = block.shape
    chunks = columns // LANES
    return (
        block.reshape(rows, layers, chunks, LANES)
        .transpose(0, 2, 1, 3)
        .reshape(rows * chunks * layers, LANES)
    )


def from_lines(lines, shape):
    rows, layers, columns = shape
    chunks = columns // LANES
    return (
        lines.reshape(rows, chunks, layers, LANES)
        .transpose(0, 2, 1, 3)
        .reshape(rows, layers, columns)
    )


def turns(wave, index, period):
    product = wave * index
    if period & (period - 1) == 0:
        product = product & (period - 1)
    else:
        product = lax.rem(product, jnp.int32(period))
    return product.astype(f32) * (1.0 / period)


def cos_sin(turn):
    part = turn - jnp.floor(turn + 0.5)
    square = part * part

    def series(first):
        terms = [
            (-1.0) ** n * math.pi ** (2 * n + first) / math.factorial(2 * n + first)
            for n in range(7)
        ]
        total = jnp.full_like(square, terms[-1])
        for term in terms[-2::-1]:
            total = total * square + term
        return total

    half_cos = series(0)
    half_sin = series(1) * part
    return 1.0 - 2.0 * half_sin * half_sin, 2.0 * half_sin * half_cos


def halves(values):
    high = values.astype(jnp.bfloat16)
    return high, (values - high.astype(f32)).astype(jnp.bfloat16)


def height_lines(modes, first_row, count, row_total, chunks, column_total):
    mode_count = modes.shape[0]
    wave_x = modes[:, 0:1].astype(jnp.int32)
    wave_y = modes[:, 1:2].astype(jnp.int32)
    offset = modes[:, 2:3]
    amp = modes[:, 3:4]
    spot = lax.broadcasted_iota(jnp.int32, (mode_count, count * chunks), 1)
    chunk = spot % chunks
    row = jnp.clip(first_row + spot // chunks, 0, row_total - 1)
    angle = (
        turns(wave_y, row, row_total) + turns(wave_x, chunk * LANES, column_total)
    ) + offset
    left_cos, left_sin = cos_sin(angle)
    lane = lax.broadcasted_iota(jnp.int32, (mode_count, LANES), 1)
    right_cos, right_sin = cos_sin(turns(wave_x, lane, column_total))
    left = jnp.concatenate([amp * left_cos, amp * left_sin], 0)
    right = jnp.concatenate([right_cos, -right_sin], 0)
    left_high, left_low = halves(left)
    right_high, right_low = halves(right)
    return lax.dot_general(
        jnp.concatenate([left_high, left_high, left_low], 0),
        jnp.concatenate([right_high, right_low, right_high], 0),
        (((0,), (0,)), ((), ())),
        preferred_element_type=f32,
    )


def inverse(values):
    return pl.reciprocal(values, approx=False)


def from_left(values, stride, lane):
    moved = [pltpu.roll(v, stride, 1) for v in values]
    return [jnp.where(lane < stride, moved[c - 1], moved[c]) for c in range(len(values))]


def from_right(values, stride, lane):
    count = len(values)
    moved = [pltpu.roll(v, LANES - stride, 1) for v in values]
    return [
        jnp.where(lane >= LANES - stride, moved[(c + 1) % count], moved[c]) for c in range(count)
    ]


def solve_chunks(diagonal, link, rhs):
    count = len(rhs)
    if count == 1:
        return [rhs[0] * inverse(diagonal[0])]
    inv = {i: inverse(diagonal[i]) for i in range(0, count, 2)}
    scaled = {i: inv[i] * rhs[i] for i in inv}
    odd_diagonal, odd_link, odd_rhs = [], [], []
    for i in range(1, count, 2):
        d = diagonal[i] - link[i - 1] * (link[i - 1] * inv[i - 1])
        r = rhs[i] + link[i - 1] * scaled[i - 1]
        e = None
        if i + 1 < count:
            by = link[i] * inv[i + 1]
            d = d - link[i] * by
            r = r + link[i] * scaled[i + 1]
            e = by * link[i + 1] if i + 2 < count else None
        odd_diagonal.append(d)
        odd_rhs.append(r)
        odd_link.append(e)
    odd = solve_chunks(odd_diagonal, odd_link, odd_rhs)
    out = [None] * count
    out[1::2] = odd
    for i in range(0, count, 2):
        r = rhs[i]
        if i > 0:
            r = r + link[i - 1] * out[i - 1]
        if i + 1 < count:
            r = r + link[i] * out[i + 1]
        out[i] = r * inv[i]
    return out


def reduce_lanes(diagonal, link, rhs, lane, stride):
    count = len(rhs)
    while stride < LANES:
        inv = [inverse(d) for d in diagonal]
        t = [q * r for q, r in zip(inv, rhs)]
        w = [q * e for q, e in zip(inv, link)]
        low_d = from_left([e * v for e, v in zip(link, w)], stride, lane)
        low_r = from_left([e * v for e, v in zip(link, t)], stride, lane)
        high_q = from_right(inv, stride, lane)
        high_t = from_right(t, stride, lane)
        high_w = from_right(w, stride, lane)
        diagonal = [
            diagonal[c] - low_d[c] - link[c] * (link[c] * high_q[c]) for c in range(count)
        ]
        rhs = [rhs[c] + low_r[c] + link[c] * high_t[c] for c in range(count)]
        link = [link[c] * high_w[c] for c in range(count)]
        stride *= 2
    return solve_chunks(diagonal, link, rhs)


def pack_pair(a, b, odd_lane):
    even = [jnp.where(odd_lane, pltpu.roll(x, 1, 1), y) for x, y in zip(a, b)]
    odd = [jnp.where(odd_lane, x, pltpu.roll(y, LANES - 1, 1)) for x, y in zip(a, b)]
    return even, odd


def unpack_pair(even, odd, odd_lane):
    a = [jnp.where(odd_lane, y, pltpu.roll(x, LANES - 1, 1)) for x, y in zip(even, odd)]
    b = [jnp.where(odd_lane, pltpu.roll(y, 1, 1), x) for x, y in zip(even, odd)]
    return a, b


def solve_x_pair(g_pair, rhs_pair, lane):
    odd_lane = (lane & 1) == 1
    first_cell = lane < 2
    last_cell = lane >= LANES - 2
    half = 0.5 * weight
    g_even, g_odd = pack_pair(*g_pair, odd_lane)
    r_even, r_odd = pack_pair(*rhs_pair, odd_lane)
    face = [half * (a + b) for a, b in zip(g_even, g_odd)]
    after = from_right(g_even, 2, lane)
    after[-1] = jnp.where(last_cell, g_odd[-1], after[-1])
    face_after = [half * (a + b) for a, b in zip(g_odd, after)]
    face_before = from_left(face_after, 2, lane)
    face_before[0] = jnp.where(first_cell, weight * g_even[0], face_before[0])
    inv = [inverse(1.0 + (a + b)) for a, b in zip(face_before, face)]
    d_odd = [1.0 + (a + b) for a, b in zip(face, face_after)]
    link = list(face_after)
    link[-1] = jnp.where(last_cell, 0.0, link[-1])
    link_before = list(face_before)
    link_before[0] = jnp.where(first_cell, 0.0, link_before[0])
    t = [q * r for q, r in zip(inv, r_even)]
    w = [q * e for q, e in zip(inv, face)]
    next_q = from_right(inv, 2, lane)
    next_t = from_right(t, 2, lane)
    next_w = from_right(w, 2, lane)
    diagonal = [
        d - e * v - l * (l * q) for d, e, v, l, q in zip(d_odd, face, w, link, next_q)
    ]
    rhs = [r + e * v + l * n for r, e, v, l, n in zip(r_odd, face, t, link, next_t)]
    x_odd = reduce_lanes(diagonal, [l * n for l, n in zip(link, next_w)], rhs, lane, 2)
    x_before = from_left(x_odd, 2, lane)
    x_even = [
        v + q * (l * b) + u * x for v, q, l, b, u, x in zip(t, inv, link_before, x_before, w, x_odd)
    ]
    return unpack_pair(x_even, x_odd, odd_lane)


def load_kernel(
    step_ref, index_ref, amp_ref, phase_ref, field_ref, conduct_ref,
    packed_ref, field_out, conduct_out, inner_ref, outer_ref,
    index_in, amp_in, phase_in, sems,
):
    width = inner_ref.shape[0]
    last = field_ref.shape[0] - width
    odd = lax.rem(lax.axis_index("wide"), 2)
    inner_rows = pl.ds(pl.multiple_of((1 - odd) * last, 8), width)
    outer_rows = pl.ds(pl.multiple_of(odd * last, 8), width)
    pairs = (
        (index_ref, index_in),
        (amp_ref, amp_in),
        (phase_ref, phase_in),
        (field_ref.at[inner_rows], inner_ref),
        (field_ref.at[outer_rows], outer_ref),
        (field_ref, field_out),
        (conduct_ref, conduct_out),
    )
    copies = [pltpu.make_async_copy(a, b, sems.at[n]) for n, (a, b) in enumerate(pairs)]
    for copy in copies:
        copy.start()
    for copy in copies[:3]:
        copy.wait()
    count = index_in.shape[0]
    row = lax.broadcasted_iota(jnp.int32, packed_ref.shape, 0)
    lane = lax.broadcasted_iota(jnp.int32, packed_ref.shape, 1)
    total = jnp.zeros(packed_ref.shape, f32)
    for m in range(count):
        moment = lax.rem(index_in[m, 2] * step_ref[0], jnp.int32(64)).astype(f32)
        offset = phase_in[m] * (0.5 / math.pi) + moment * (1.0 / 64.0)
        for place, value in enumerate(
            (index_in[m, 0].astype(f32), index_in[m, 1].astype(f32), offset, amp_in[m])
        ):
            total = jnp.where((row == m) & (lane == place), value, total)
    packed_ref[...] = total
    for copy in copies[3:]:
        copy.wait()


def block_factors(face):
    inv, scaled, chain, u = [], [], [], []
    rows = len(face) - 1
    rest = 1.0 + face[0]
    for j in range(rows):
        inv.append(inverse(rest + face[j + 1]))
        scaled.append(face[j] * inv[j])
        chain.append(face[j + 1] * inv[j])
        u.append(scaled[j] * u[-1] if j else scaled[j])
        rest = 1.0 + rest * chain[j]
    v = list(chain)
    for j in range(rows - 2, -1, -1):
        u[j] = u[j] + chain[j] * u[j + 1]
        v[j] = chain[j] * v[j + 1]
    return inv, scaled, chain, u, v


def block_ends(face):
    rows = len(face) - 1
    down = 1.0 + face[0]
    up = 1.0 + face[rows]
    v_first = None
    for j in range(rows):
        v_last = face[j + 1] * inverse(down + face[j + 1])
        v_first = v_last if v_first is None else v_first * v_last
        u_first = face[rows - 1 - j] * inverse(up + face[rows - 1 - j])
        if j < rows - 1:
            down = 1.0 + down * v_last
            up = 1.0 + up * u_first
    u_last = v_first * (face[0] * inverse(face[rows]))
    return u_first, v_first, u_last, v_last


def height_kernel(sizes, modes_ref, inner_ref, outer_ref, heights_ref, halo_ref):
    rows, layers, chunks, row_total, layer_total, column_total = sizes
    width = layers * chunks
    body = height_lines(modes_ref[...], 0, row_total, row_total, chunks, column_total)
    heights_ref[chunks : (row_total + 1) * chunks] = body
    heights_ref[0:chunks] = body[0:chunks]
    heights_ref[(row_total + 1) * chunks : (row_total + 2) * chunks] = body[
        (row_total - 1) * chunks : row_total * chunks
    ]
    halo_ref[0:width] = inner_ref[...]
    halo_ref[width : 2 * width] = outer_ref[...]


def main_kernel(
    sizes, heights, halo_ref, field_ref, late_outer_ref, conduct_ref,
    sent_ref, p_ref, u_ref, v_ref, left_gain_ref, right_gain_ref, joint_ref,
    ends, links, framed, solved,
):
    rows, layers, chunks, row_total, layer_total, column_total = sizes
    width = layers * chunks
    blocks = row_total // rows
    me = lax.axis_index("wide")
    first_layer = lax.axis_index("grp") * layers
    zeta = [
        ((first_layer + k).astype(f32) + 0.5) * (1.0 / layer_total) for k in range(layers)
    ]
    half = 0.5 * weight
    own_start = pl.multiple_of(me * (rows * chunks), 8)

    def faces(start):
        h = [heights[pl.ds(start + j * chunks, chunks), :] for j in range(rows + 2)]
        out = []
        for j in range(rows + 1):
            both = h[j] + h[j + 1]
            out.append(jnp.concatenate([weight + (half * z) * both for z in zeta], 0))
        return out

    def keep_ends(b, values):
        base = pl.multiple_of(b * (4 * width), 8)
        for n, value in enumerate(values):
            ends[pl.ds(base + n * width, width), :] = value

    inv, scaled, chain, u, v = block_factors(faces(own_start))
    for j in range(rows):
        u_ref[j * width : (j + 1) * width] = u[j]
        v_ref[j * width : (j + 1) * width] = v[j]
    keep_ends(me, (u[0], v[0], u[-1], v[-1]))

    def other_block(n):
        b = lax.rem(me + 1 + n, blocks)
        keep_ends(b, block_ends(faces(pl.multiple_of(b * (rows * chunks), 8))))

    if blocks <= 8:
        for n in range(blocks - 1):
            other_block(n)
    else:
        lax.fori_loop(0, blocks - 1, lambda n, carry: (other_block(n), carry)[1], 0)

    def end(b, n):
        return ends[(4 * b + n) * width : (4 * b + n + 1) * width]

    left = jnp.zeros((width, LANES), f32)
    right = jnp.zeros((width, LANES), f32)
    for b in range(blocks):
        u_first, v_first, u_last, v_last = (end(b, n) for n in range(4))
        gain = u_last * inverse(1.0 - u_first * left)
        left_gain_ref[b * width : (b + 1) * width] = gain
        links[b * width : (b + 1) * width] = left
        left = v_last + gain * left * v_first
        b = blocks - 1 - b
        u_first, v_first, u_last, v_last = (end(b, n) for n in range(4))
        gain = v_first * inverse(1.0 - v_last * right)
        right_gain_ref[b * width : (b + 1) * width] = gain
        links[(blocks + b) * width : (blocks + b + 1) * width] = right
        right = u_first + gain * right * u_last

    own = pl.ds(pl.multiple_of(me * width, 8), width)
    left_link = links[own, :]
    right_link = links[pl.ds(pl.multiple_of((blocks + me) * width, 8), width), :]
    a = 1.0 - left_link * u[0]
    b = left_link * v[0]
    c = right_link * u[-1]
    d = 1.0 - right_link * v[-1]
    by = inverse(a * d - b * c)
    joint = (
        left_gain_ref[own, :] * left_link, right_gain_ref[own, :] * right_link,
        left_link, right_link, d * by, b * by, c * by, a * by,
    )
    for n, value in enumerate(joint):
        joint_ref[n * width : (n + 1) * width] = value

    odd = lax.rem(me, 2)
    beyond = (rows + 1) * width
    framed[width:beyond] = field_ref[...]
    framed[pl.ds(pl.multiple_of((1 - odd) * beyond, 8), width), :] = halo_ref[0:width]
    outer_rows = jnp.where(first_layer == 0, halo_ref[width : 2 * width], late_outer_ref[...])
    at_edge = (me == 0) | (me == blocks - 1)
    framed[pl.ds(pl.multiple_of(odd * beyond, 8), width), :] = jnp.where(at_edge, 0.0, outer_rows)
    lane = lax.broadcasted_iota(jnp.int32, (rows, LANES), 1)
    g, f, rhs = [], [], []
    for k in range(layers):
        g.append([])
        f.append([])
        rhs.append([])
        for c in range(chunks):
            h_low, h, h_high = (
                heights[pl.ds(own_start + s * chunks + c, rows, stride=chunks), :]
                for s in range(3)
            )
            place = c * layers + k
            f_low, f_mid, f_high = (
                framed[pl.ds(s * width + place, rows, stride=width), :] for s in range(3)
            )
            g[k].append(conduct_ref[pl.ds(place, rows, stride=width), :] * (1.0 + zeta[k] * h))
            f[k].append(f_mid)
            along = (weight + (half * zeta[k]) * (h + h_high)) * (f_high - f_mid) - (
                weight + (half * zeta[k]) * (h + h_low)
            ) * (f_mid - f_low)
            rhs[k].append(2.0 * (f_mid + along))
    for k in range(0, layers, 2):
        both = solve_x_pair(g[k : k + 2], rhs[k : k + 2], lane)
        for n in range(2):
            for c in range(chunks):
                spot = pl.ds((k + n) * chunks + c, rows, stride=width)
                solved[spot, :] = both[n][c] - 2.0 * f[k + n][c]

    def part(ref, j):
        return ref[j * width : (j + 1) * width]

    p = [part(solved, 0) * inv[0]]
    for j in range(1, rows):
        p.append(part(solved, j) * inv[j] + scaled[j] * p[-1])
    for j in range(rows - 2, -1, -1):
        p[j] = p[j] + chain[j] * p[j + 1]
    for j in range(rows):
        p_ref[j * width : (j + 1) * width] = p[j]

    upward = p[-1] + part(joint_ref, 0) * p[0]
    downward = p[0] + part(joint_ref, 1) * p[-1]
    for b in range(blocks):
        sent_ref[b * width : (b + 1) * width] = jnp.where(b > me, upward, downward)


def last_kernel(
    sizes, came_ref, left_gain_ref, right_gain_ref, joint_ref, p_ref, u_ref, v_ref, field_ref,
    out_ref,
):
    rows, layers, chunks, row_total, layer_total, column_total = sizes
    width = layers * chunks
    blocks = row_total // rows
    me = lax.axis_index("wide")

    def part(ref, b):
        return ref[b * width : (b + 1) * width]

    left = jnp.zeros((width, LANES), f32)
    right = jnp.zeros((width, LANES), f32)
    for b in range(blocks - 1):
        left = jnp.where(b < me, part(came_ref, b) + part(left_gain_ref, b) * left, left)
        b = blocks - 1 - b
        right = jnp.where(b > me, part(came_ref, b) + part(right_gain_ref, b) * right, right)

    y = left + part(joint_ref, 2) * part(p_ref, 0)
    z = right + part(joint_ref, 3) * part(p_ref, rows - 1)
    before = part(joint_ref, 4) * y + part(joint_ref, 5) * z
    after = part(joint_ref, 6) * y + part(joint_ref, 7) * z
    for j in range(rows):
        x = part(p_ref, j) + part(u_ref, j) * before + part(v_ref, j) * after
        for k in range(layers):
            spot = pl.ds(j * width + k, chunks, stride=layers)
            out_ref[spot, :] = field_ref[spot, :] + x[k * chunks : (k + 1) * chunks]


def on_device(field, conduct, mode_index, mode_amp, mode_phase, step_index):
    rows, layers, columns = field.shape
    wide_count = lax.axis_size("wide")
    row_total = rows * wide_count
    grp_count = lax.axis_size("grp")
    layer_total = layers * grp_count
    chunks = columns // LANES
    width = layers * chunks
    sizes = (rows, layers, chunks, row_total, layer_total, columns)
    limit = pltpu.CompilerParams(vmem_limit_bytes=16 * 1024 * 1024)
    hbm = pl.BlockSpec(memory_space=pltpu.HBM)

    def lines(count):
        return jax.ShapeDtypeStruct((count * width, LANES), f32)

    packed, field_lines, conduct_lines, inner, outer = pl.pallas_call(
        load_kernel,
        out_shape=(
            jax.ShapeDtypeStruct((mode_index.shape[0], 8), f32),
            lines(rows),
            lines(rows),
            lines(1),
            lines(1),
        ),
        in_specs=[pl.BlockSpec(memory_space=pltpu.SMEM)] + [hbm] * 5,
        scratch_shapes=[
            pltpu.SMEM(mode_index.shape, jnp.int32),
            pltpu.SMEM(mode_amp.shape, f32),
            pltpu.SMEM(mode_phase.shape, f32),
            pltpu.SemaphoreType.DMA((7,)),
        ],
        compiler_params=limit,
    )(
        step_index,
        *(
            pltpu.with_memory_space_constraint(a, pltpu.HBM)
            for a in (mode_index, mode_amp, mode_phase, to_lines(field), to_lines(conduct))
        ),
    )

    def swap(rows_sent, first, groups):
        pairs = []
        for g in range(grp_count):
            for i in range(wide_count):
                partner = i + 1 if (i - first) % 2 == 0 else i - 1
                if g not in groups or not 0 <= partner < wide_count:
                    partner = i
                pairs.append((g * wide_count + i, g * wide_count + partner))
        return lax.ppermute(rows_sent, ("grp", "wide"), pairs)

    inner_came = swap(inner, 0, range(grp_count))
    outer_came = swap(outer, 1, [0])
    modes = lax.all_gather(packed, "grp", axis=0, tiled=True)
    modes, outer = lax.optimization_barrier((modes, outer))
    late_outer_came = swap(outer, 1, range(1, grp_count))

    heights, halo = pl.pallas_call(
        functools.partial(height_kernel, sizes),
        out_shape=(jax.ShapeDtypeStruct(((row_total + 2) * chunks, LANES), f32), lines(2)),
        compiler_params=limit,
    )(modes, inner_came, outer_came)

    sent, p, u, v, left_gain, right_gain, joint = pl.pallas_call(
        functools.partial(main_kernel, sizes),
        out_shape=(lines(wide_count),)
        + (lines(rows),) * 3
        + (lines(wide_count),) * 2
        + (lines(8),),
        scratch_shapes=[
            pltpu.VMEM((4 * wide_count * width, LANES), f32),
            pltpu.VMEM((2 * wide_count * width, LANES), f32),
            pltpu.VMEM(((rows + 2) * width, LANES), f32),
            pltpu.VMEM((rows * width, LANES), f32),
        ],
        compiler_params=limit,
    )(heights, halo, field_lines, late_outer_came, conduct_lines)

    came = lax.all_to_all(
        sent.reshape(wide_count, width, LANES), "wide", split_axis=0, concat_axis=0
    ).reshape(wide_count * width, LANES)

    advanced = pl.pallas_call(
        functools.partial(last_kernel, sizes),
        out_shape=lines(rows),
        compiler_params=limit,
    )(came, left_gain, right_gain, joint, p, u, v, field_lines)
    return from_lines(advanced, field.shape)


def solution(mesh):
    return jax.shard_map(
        on_device,
        mesh=mesh,
        in_specs=(
            P("wide", "grp", None),
            P("wide", "grp", None),
            P("grp", None),
            P("grp"),
            P("grp"),
            P(),
        ),
        out_specs=P("wide", "grp", None),
        check_vma=False,
    )
```

```python
import functools
import math

import jax
import jax.numpy as jnp
from jax import lax
from jax.experimental import pallas as pl
from jax.experimental.pallas import tpu as pltpu
from jax.sharding import PartitionSpec as P

time_step = 600.0
implicit_weight = 0.5
weight = implicit_weight * time_step
LANES = 128
f32 = jnp.float32


def to_lines(block):
    rows, layers, columns = block.shape
    chunks = columns // LANES
    return (
        block.reshape(rows, layers, chunks, LANES)
        .transpose(0, 2, 1, 3)
        .reshape(rows * chunks * layers, LANES)
    )


def from_lines(lines, shape):
    rows, layers, columns = shape
    chunks = columns // LANES
    return (
        lines.reshape(rows, chunks, layers, LANES)
        .transpose(0, 2, 1, 3)
        .reshape(rows, layers, columns)
    )


def turns(wave, index, period):
    product = wave * index
    if period & (period - 1) == 0:
        product = product & (period - 1)
    else:
        product = lax.rem(product, jnp.int32(period))
    return product.astype(f32) * (1.0 / period)


def cos_sin(turn):
    part = turn - jnp.floor(turn + 0.5)
    square = part * part

    def series(first):
        terms = [
            (-1.0) ** n * math.pi ** (2 * n + first) / math.factorial(2 * n + first)
            for n in range(7)
        ]
        total = jnp.full_like(square, terms[-1])
        for term in terms[-2::-1]:
            total = total * square + term
        return total

    half_cos = series(0)
    half_sin = series(1) * part
    return 1.0 - 2.0 * half_sin * half_sin, 2.0 * half_sin * half_cos


def halves(values):
    high = values.astype(jnp.bfloat16)
    return high, (values - high.astype(f32)).astype(jnp.bfloat16)


def height_lines(modes, first_row, count, row_total, chunks, column_total):
    mode_count = modes.shape[0]
    wave_x = modes[:, 0:1].astype(jnp.int32)
    wave_y = modes[:, 1:2].astype(jnp.int32)
    offset = modes[:, 2:3]
    amp = modes[:, 3:4]
    spot = lax.broadcasted_iota(jnp.int32, (mode_count, count * chunks), 1)
    chunk = spot % chunks
    row = jnp.clip(first_row + spot // chunks, 0, row_total - 1)
    angle = (
        turns(wave_y, row, row_total) + turns(wave_x, chunk * LANES, column_total)
    ) + offset
    left_cos, left_sin = cos_sin(angle)
    lane = lax.broadcasted_iota(jnp.int32, (mode_count, LANES), 1)
    right_cos, right_sin = cos_sin(turns(wave_x, lane, column_total))
    left = jnp.concatenate([amp * left_cos, amp * left_sin], 0)
    right = jnp.concatenate([right_cos, -right_sin], 0)
    left_high, left_low = halves(left)
    right_high, right_low = halves(right)
    return lax.dot_general(
        jnp.concatenate([left_high, left_high, left_low], 0),
        jnp.concatenate([right_high, right_low, right_high], 0),
        (((0,), (0,)), ((), ())),
        preferred_element_type=f32,
    )


def inverse(values):
    return pl.reciprocal(values, approx=False)


def from_left(values, stride, lane):
    moved = [pltpu.roll(v, stride, 1) for v in values]
    return [jnp.where(lane < stride, moved[c - 1], moved[c]) for c in range(len(values))]


def from_right(values, stride, lane):
    count = len(values)
    moved = [pltpu.roll(v, LANES - stride, 1) for v in values]
    return [
        jnp.where(lane >= LANES - stride, moved[(c + 1) % count], moved[c]) for c in range(count)
    ]


def solve_chunks(diagonal, link, rhs):
    count = len(rhs)
    if count == 1:
        return [rhs[0] * inverse(diagonal[0])]
    inv = {i: inverse(diagonal[i]) for i in range(0, count, 2)}
    scaled = {i: inv[i] * rhs[i] for i in inv}
    odd_diagonal, odd_link, odd_rhs = [], [], []
    for i in range(1, count, 2):
        d = diagonal[i] - link[i - 1] * (link[i - 1] * inv[i - 1])
        r = rhs[i] + link[i - 1] * scaled[i - 1]
        e = None
        if i + 1 < count:
            by = link[i] * inv[i + 1]
            d = d - link[i] * by
            r = r + link[i] * scaled[i + 1]
            e = by * link[i + 1] if i + 2 < count else None
        odd_diagonal.append(d)
        odd_rhs.append(r)
        odd_link.append(e)
    odd = solve_chunks(odd_diagonal, odd_link, odd_rhs)
    out = [None] * count
    out[1::2] = odd
    for i in range(0, count, 2):
        r = rhs[i]
        if i > 0:
            r = r + link[i - 1] * out[i - 1]
        if i + 1 < count:
            r = r + link[i] * out[i + 1]
        out[i] = r * inv[i]
    return out


def reduce_lanes(diagonal, link, rhs, lane, stride):
    count = len(rhs)
    while stride < LANES:
        inv = [inverse(d) for d in diagonal]
        t = [q * r for q, r in zip(inv, rhs)]
        w = [q * e for q, e in zip(inv, link)]
        low_d = from_left([e * v for e, v in zip(link, w)], stride, lane)
        low_r = from_left([e * v for e, v in zip(link, t)], stride, lane)
        high_q = from_right(inv, stride, lane)
        high_t = from_right(t, stride, lane)
        high_w = from_right(w, stride, lane)
        diagonal = [
            diagonal[c] - low_d[c] - link[c] * (link[c] * high_q[c]) for c in range(count)
        ]
        rhs = [rhs[c] + low_r[c] + link[c] * high_t[c] for c in range(count)]
        link = [link[c] * high_w[c] for c in range(count)]
        stride *= 2
    return solve_chunks(diagonal, link, rhs)


def pack_pair(a, b, odd_lane):
    even = [jnp.where(odd_lane, pltpu.roll(x, 1, 1), y) for x, y in zip(a, b)]
    odd = [jnp.where(odd_lane, x, pltpu.roll(y, LANES - 1, 1)) for x, y in zip(a, b)]
    return even, odd


def unpack_pair(even, odd, odd_lane):
    a = [jnp.where(odd_lane, y, pltpu.roll(x, LANES - 1, 1)) for x, y in zip(even, odd)]
    b = [jnp.where(odd_lane, pltpu.roll(y, 1, 1), x) for x, y in zip(even, odd)]
    return a, b


def solve_x_pair(g_pair, rhs_pair, lane):
    odd_lane = (lane & 1) == 1
    first_cell = lane < 2
    last_cell = lane >= LANES - 2
    half = 0.5 * weight
    g_even, g_odd = pack_pair(*g_pair, odd_lane)
    r_even, r_odd = pack_pair(*rhs_pair, odd_lane)
    face = [half * (a + b) for a, b in zip(g_even, g_odd)]
    after = from_right(g_even, 2, lane)
    after[-1] = jnp.where(last_cell, g_odd[-1], after[-1])
    face_after = [half * (a + b) for a, b in zip(g_odd, after)]
    face_before = from_left(face_after, 2, lane)
    face_before[0] = jnp.where(first_cell, weight * g_even[0], face_before[0])
    inv = [inverse(1.0 + (a + b)) for a, b in zip(face_before, face)]
    d_odd = [1.0 + (a + b) for a, b in zip(face, face_after)]
    link = list(face_after)
    link[-1] = jnp.where(last_cell, 0.0, link[-1])
    link_before = list(face_before)
    link_before[0] = jnp.where(first_cell, 0.0, link_before[0])
    t = [q * r for q, r in zip(inv, r_even)]
    w = [q * e for q, e in zip(inv, face)]
    next_q = from_right(inv, 2, lane)
    next_t = from_right(t, 2, lane)
    next_w = from_right(w, 2, lane)
    diagonal = [
        d - e * v - l * (l * q) for d, e, v, l, q in zip(d_odd, face, w, link, next_q)
    ]
    rhs = [r + e * v + l * n for r, e, v, l, n in zip(r_odd, face, t, link, next_t)]
    x_odd = reduce_lanes(diagonal, [l * n for l, n in zip(link, next_w)], rhs, lane, 2)
    x_before = from_left(x_odd, 2, lane)
    x_even = [
        v + q * (l * b) + u * x for v, q, l, b, u, x in zip(t, inv, link_before, x_before, w, x_odd)
    ]
    return unpack_pair(x_even, x_odd, odd_lane)


def load_kernel(
    step_ref, index_ref, amp_ref, phase_ref, field_ref, conduct_ref,
    packed_ref, field_out, conduct_out, inner_ref, outer_ref,
    index_in, amp_in, phase_in, sems,
):
    width = inner_ref.shape[0]
    last = field_ref.shape[0] - width
    odd = lax.rem(lax.axis_index("wide"), 2)
    inner_rows = pl.ds(pl.multiple_of((1 - odd) * last, 8), width)
    outer_rows = pl.ds(pl.multiple_of(odd * last, 8), width)
    pairs = (
        (index_ref, index_in),
        (amp_ref, amp_in),
        (phase_ref, phase_in),
        (field_ref.at[inner_rows], inner_ref),
        (field_ref.at[outer_rows], outer_ref),
        (field_ref, field_out),
        (conduct_ref, conduct_out),
    )
    copies = [pltpu.make_async_copy(a, b, sems.at[n]) for n, (a, b) in enumerate(pairs)]
    for copy in copies:
        copy.start()
    for copy in copies[:3]:
        copy.wait()
    count = index_in.shape[0]
    row = lax.broadcasted_iota(jnp.int32, packed_ref.shape, 0)
    lane = lax.broadcasted_iota(jnp.int32, packed_ref.shape, 1)
    total = jnp.zeros(packed_ref.shape, f32)
    for m in range(count):
        moment = lax.rem(index_in[m, 2] * step_ref[0], jnp.int32(64)).astype(f32)
        offset = phase_in[m] * (0.5 / math.pi) + moment * (1.0 / 64.0)
        for place, value in enumerate(
            (index_in[m, 0].astype(f32), index_in[m, 1].astype(f32), offset, amp_in[m])
        ):
            total = jnp.where((row == m) & (lane == place), value, total)
    packed_ref[...] = total
    for copy in copies[3:]:
        copy.wait()


def block_factors(face):
    inv, scaled, chain, u = [], [], [], []
    rows = len(face) - 1
    rest = 1.0 + face[0]
    for j in range(rows):
        inv.append(inverse(rest + face[j + 1]))
        scaled.append(face[j] * inv[j])
        chain.append(face[j + 1] * inv[j])
        u.append(scaled[j] * u[-1] if j else scaled[j])
        rest = 1.0 + rest * chain[j]
    v = list(chain)
    for j in range(rows - 2, -1, -1):
        u[j] = u[j] + chain[j] * u[j + 1]
        v[j] = chain[j] * v[j + 1]
    return inv, scaled, chain, u, v


def block_ends(face):
    rows = len(face) - 1
    down = 1.0 + face[0]
    up = 1.0 + face[rows]
    v_first = None
    for j in range(rows):
        v_last = face[j + 1] * inverse(down + face[j + 1])
        v_first = v_last if v_first is None else v_first * v_last
        u_first = face[rows - 1 - j] * inverse(up + face[rows - 1 - j])
        if j < rows - 1:
            down = 1.0 + down * v_last
            up = 1.0 + up * u_first
    u_last = v_first * (face[0] * inverse(face[rows]))
    return u_first, v_first, u_last, v_last


def height_kernel(sizes, modes_ref, inner_ref, outer_ref, heights_ref, halo_ref):
    rows, layers, chunks, row_total, layer_total, column_total = sizes
    width = layers * chunks
    body = height_lines(modes_ref[...], 0, row_total, row_total, chunks, column_total)
    heights_ref[chunks : (row_total + 1) * chunks] = body
    heights_ref[0:chunks] = body[0:chunks]
    heights_ref[(row_total + 1) * chunks : (row_total + 2) * chunks] = body[
        (row_total - 1) * chunks : row_total * chunks
    ]
    halo_ref[0:width] = inner_ref[...]
    halo_ref[width : 2 * width] = outer_ref[...]


def main_kernel(
    sizes, heights, halo_ref, field_ref, late_outer_ref, conduct_ref,
    sent_ref, p_ref, u_ref, v_ref, left_gain_ref, right_gain_ref, joint_ref,
    ends, links, framed, solved,
):
    rows, layers, chunks, row_total, layer_total, column_total = sizes
    width = layers * chunks
    blocks = row_total // rows
    me = lax.axis_index("wide")
    first_layer = lax.axis_index("grp") * layers
    zeta = [
        ((first_layer + k).astype(f32) + 0.5) * (1.0 / layer_total) for k in range(layers)
    ]
    half = 0.5 * weight
    own_start = pl.multiple_of(me * (rows * chunks), 8)

    def faces(start):
        h = [heights[pl.ds(start + j * chunks, chunks), :] for j in range(rows + 2)]
        out = []
        for j in range(rows + 1):
            both = h[j] + h[j + 1]
            out.append(jnp.concatenate([weight + (half * z) * both for z in zeta], 0))
        return out

    def keep_ends(b, values):
        base = pl.multiple_of(b * (4 * width), 8)
        for n, value in enumerate(values):
            ends[pl.ds(base + n * width, width), :] = value

    inv, scaled, chain, u, v = block_factors(faces(own_start))
    for j in range(rows):
        u_ref[j * width : (j + 1) * width] = u[j]
        v_ref[j * width : (j + 1) * width] = v[j]
    keep_ends(me, (u[0], v[0], u[-1], v[-1]))

    def other_block(n):
        b = lax.rem(me + 1 + n, blocks)
        keep_ends(b, block_ends(faces(pl.multiple_of(b * (rows * chunks), 8))))

    if blocks <= 8:
        for n in range(blocks - 1):
            other_block(n)
    else:
        lax.fori_loop(0, blocks - 1, lambda n, carry: (other_block(n), carry)[1], 0)

    def end(b, n):
        return ends[(4 * b + n) * width : (4 * b + n + 1) * width]

    left = jnp.zeros((width, LANES), f32)
    right = jnp.zeros((width, LANES), f32)
    for b in range(blocks):
        u_first, v_first, u_last, v_last = (end(b, n) for n in range(4))
        gain = u_last * inverse(1.0 - u_first * left)
        left_gain_ref[b * width : (b + 1) * width] = gain
        links[b * width : (b + 1) * width] = left
        left = v_last + gain * left * v_first
        b = blocks - 1 - b
        u_first, v_first, u_last, v_last = (end(b, n) for n in range(4))
        gain = v_first * inverse(1.0 - v_last * right)
        right_gain_ref[b * width : (b + 1) * width] = gain
        links[(blocks + b) * width : (blocks + b + 1) * width] = right
        right = u_first + gain * right * u_last

    own = pl.ds(pl.multiple_of(me * width, 8), width)
    left_link = links[own, :]
    right_link = links[pl.ds(pl.multiple_of((blocks + me) * width, 8), width), :]
    a = 1.0 - left_link * u[0]
    b = left_link * v[0]
    c = right_link * u[-1]
    d = 1.0 - right_link * v[-1]
    by = inverse(a * d - b * c)
    joint = (
        left_gain_ref[own, :] * left_link, right_gain_ref[own, :] * right_link,
        left_link, right_link, d * by, b * by, c * by, a * by,
    )
    for n, value in enumerate(joint):
        joint_ref[n * width : (n + 1) * width] = value

    odd = lax.rem(me, 2)
    beyond = (rows + 1) * width
    framed[width:beyond] = field_ref[...]
    framed[pl.ds(pl.multiple_of((1 - odd) * beyond, 8), width), :] = halo_ref[0:width]
    outer_rows = jnp.where(first_layer == 0, halo_ref[width : 2 * width], late_outer_ref[...])
    at_edge = (me == 0) | (me == blocks - 1)
    framed[pl.ds(pl.multiple_of(odd * beyond, 8), width), :] = jnp.where(at_edge, 0.0, outer_rows)
    lane = lax.broadcasted_iota(jnp.int32, (rows, LANES), 1)
    g, f, rhs = [], [], []
    for k in range(layers):
        g.append([])
        f.append([])
        rhs.append([])
        for c in range(chunks):
            h_low, h, h_high = (
                heights[pl.ds(own_start + s * chunks + c, rows, stride=chunks), :]
                for s in range(3)
            )
            place = c * layers + k
            f_low, f_mid, f_high = (
                framed[pl.ds(s * width + place, rows, stride=width), :] for s in range(3)
            )
            g[k].append(conduct_ref[pl.ds(place, rows, stride=width), :] * (1.0 + zeta[k] * h))
            f[k].append(f_mid)
            along = (weight + (half * zeta[k]) * (h + h_high)) * (f_high - f_mid) - (
                weight + (half * zeta[k]) * (h + h_low)
            ) * (f_mid - f_low)
            rhs[k].append(2.0 * (f_mid + along))
    for k in range(0, layers, 2):
        both = solve_x_pair(g[k : k + 2], rhs[k : k + 2], lane)
        for n in range(2):
            for c in range(chunks):
                spot = pl.ds((k + n) * chunks + c, rows, stride=width)
                solved[spot, :] = both[n][c] - 2.0 * f[k + n][c]

    def part(ref, j):
        return ref[j * width : (j + 1) * width]

    p = [part(solved, 0) * inv[0]]
    for j in range(1, rows):
        p.append(part(solved, j) * inv[j] + scaled[j] * p[-1])
    for j in range(rows - 2, -1, -1):
        p[j] = p[j] + chain[j] * p[j + 1]
    for j in range(rows):
        p_ref[j * width : (j + 1) * width] = p[j]

    upward = p[-1] + part(joint_ref, 0) * p[0]
    downward = p[0] + part(joint_ref, 1) * p[-1]
    for b in range(blocks):
        sent_ref[b * width : (b + 1) * width] = jnp.where(b > me, upward, downward)


def last_kernel(
    sizes, came_ref, left_gain_ref, right_gain_ref, joint_ref, p_ref, u_ref, v_ref, field_ref,
    out_ref,
):
    rows, layers, chunks, row_total, layer_total, column_total = sizes
    width = layers * chunks
    blocks = row_total // rows
    me = lax.axis_index("wide")

    def part(ref, b):
        return ref[b * width : (b + 1) * width]

    left = jnp.zeros((width, LANES), f32)
    right = jnp.zeros((width, LANES), f32)
    for b in range(blocks - 1):
        left = jnp.where(b < me, part(came_ref, b) + part(left_gain_ref, b) * left, left)
        b = blocks - 1 - b
        right = jnp.where(b > me, part(came_ref, b) + part(right_gain_ref, b) * right, right)

    y = left + part(joint_ref, 2) * part(p_ref, 0)
    z = right + part(joint_ref, 3) * part(p_ref, rows - 1)
    before = part(joint_ref, 4) * y + part(joint_ref, 5) * z
    after = part(joint_ref, 6) * y + part(joint_ref, 7) * z
    for j in range(rows):
        x = part(p_ref, j) + part(u_ref, j) * before + part(v_ref, j) * after
        for k in range(layers):
            spot = pl.ds(j * width + k, chunks, stride=layers)
            out_ref[spot, :] = field_ref[spot, :] + x[k * chunks : (k + 1) * chunks]


def on_device(field, conduct, mode_index, mode_amp, mode_phase, step_index):
    rows, layers, columns = field.shape
    wide_count = lax.axis_size("wide")
    row_total = rows * wide_count
    grp_count = lax.axis_size("grp")
    layer_total = layers * grp_count
    chunks = columns // LANES
    width = layers * chunks
    sizes = (rows, layers, chunks, row_total, layer_total, columns)
    limit = pltpu.CompilerParams(vmem_limit_bytes=16 * 1024 * 1024)
    hbm = pl.BlockSpec(memory_space=pltpu.HBM)

    def lines(count):
        return jax.ShapeDtypeStruct((count * width, LANES), f32)

    packed, field_lines, conduct_lines, inner, outer = pl.pallas_call(
        load_kernel,
        out_shape=(
            jax.ShapeDtypeStruct((mode_index.shape[0], 8), f32),
            lines(rows),
            lines(rows),
            lines(1),
            lines(1),
        ),
        in_specs=[pl.BlockSpec(memory_space=pltpu.SMEM)] + [hbm] * 5,
        scratch_shapes=[
            pltpu.SMEM(mode_index.shape, jnp.int32),
            pltpu.SMEM(mode_amp.shape, f32),
            pltpu.SMEM(mode_phase.shape, f32),
            pltpu.SemaphoreType.DMA((7,)),
        ],
        compiler_params=limit,
    )(
        step_index,
        *(
            pltpu.with_memory_space_constraint(a, pltpu.HBM)
            for a in (mode_index, mode_amp, mode_phase, to_lines(field), to_lines(conduct))
        ),
    )

    def swap(rows_sent, first, groups):
        pairs = []
        for g in range(grp_count):
            for i in range(wide_count):
                shift = first if g in groups else 0
                partner = i + 1 if (i - shift) % 2 == 0 else i - 1
                if not 0 <= partner < wide_count:
                    continue
                pairs.append((g * wide_count + i, g * wide_count + partner))
        return lax.ppermute(rows_sent, ("grp", "wide"), pairs)

    inner_came = swap(inner, 0, range(grp_count))
    outer_came = swap(outer, 1, [0])
    modes = lax.all_gather(packed, "grp", axis=0, tiled=True)
    modes, outer = lax.optimization_barrier((modes, outer))
    late_outer_came = swap(outer, 1, range(1, grp_count))

    heights, halo = pl.pallas_call(
        functools.partial(height_kernel, sizes),
        out_shape=(jax.ShapeDtypeStruct(((row_total + 2) * chunks, LANES), f32), lines(2)),
        compiler_params=limit,
    )(modes, inner_came, outer_came)

    sent, p, u, v, left_gain, right_gain, joint = pl.pallas_call(
        functools.partial(main_kernel, sizes),
        out_shape=(lines(wide_count),)
        + (lines(rows),) * 3
        + (lines(wide_count),) * 2
        + (lines(8),),
        scratch_shapes=[
            pltpu.VMEM((4 * wide_count * width, LANES), f32),
            pltpu.VMEM((2 * wide_count * width, LANES), f32),
            pltpu.VMEM(((rows + 2) * width, LANES), f32),
            pltpu.VMEM((rows * width, LANES), f32),
        ],
        compiler_params=limit,
    )(heights, halo, field_lines, late_outer_came, conduct_lines)

    came = lax.all_to_all(
        sent.reshape(wide_count, width, LANES), "wide", split_axis=0, concat_axis=0
    ).reshape(wide_count * width, LANES)

    advanced = pl.pallas_call(
        functools.partial(last_kernel, sizes),
        out_shape=lines(rows),
        compiler_params=limit,
    )(came, left_gain, right_gain, joint, p, u, v, field_lines)
    return from_lines(advanced, field.shape)


def solution(mesh):
    return jax.shard_map(
        on_device,
        mesh=mesh,
        in_specs=(
            P("wide", "grp", None),
            P("wide", "grp", None),
            P("grp", None),
            P("grp"),
            P("grp"),
            P(),
        ),
        out_specs=P("wide", "grp", None),
        check_vma=False,
    )
```

```python
import functools
import math

import jax
import jax.numpy as jnp
from jax import lax
from jax.experimental import pallas as pl
from jax.experimental.pallas import tpu as pltpu
from jax.sharding import PartitionSpec as P

time_step = 600.0
implicit_weight = 0.5
weight = implicit_weight * time_step
LANES = 128
f32 = jnp.float32


def to_lines(block):
    rows, layers, columns = block.shape
    chunks = columns // LANES
    return (
        block.reshape(rows, layers, chunks, LANES)
        .transpose(0, 2, 1, 3)
        .reshape(rows * chunks * layers, LANES)
    )


def from_lines(lines, shape):
    rows, layers, columns = shape
    chunks = columns // LANES
    return (
        lines.reshape(rows, chunks, layers, LANES)
        .transpose(0, 2, 1, 3)
        .reshape(rows, layers, columns)
    )


def turns(wave, index, period):
    product = wave * index
    if period & (period - 1) == 0:
        product = product & (period - 1)
    else:
        product = lax.rem(product, jnp.int32(period))
    return product.astype(f32) * (1.0 / period)


def cos_sin(turn):
    part = turn - jnp.floor(turn + 0.5)
    square = part * part

    def series(first):
        terms = [
            (-1.0) ** n * math.pi ** (2 * n + first) / math.factorial(2 * n + first)
            for n in range(7)
        ]
        total = jnp.full_like(square, terms[-1])
        for term in terms[-2::-1]:
            total = total * square + term
        return total

    half_cos = series(0)
    half_sin = series(1) * part
    return 1.0 - 2.0 * half_sin * half_sin, 2.0 * half_sin * half_cos


def halves(values):
    high = values.astype(jnp.bfloat16)
    return high, (values - high.astype(f32)).astype(jnp.bfloat16)


def height_lines(modes, first_row, count, row_total, chunks, column_total):
    mode_count = modes.shape[0]
    wave_x = modes[:, 0:1].astype(jnp.int32)
    wave_y = modes[:, 1:2].astype(jnp.int32)
    offset = modes[:, 2:3]
    amp = modes[:, 3:4]
    spot = lax.broadcasted_iota(jnp.int32, (mode_count, count * chunks), 1)
    chunk = spot % chunks
    row = jnp.clip(first_row + spot // chunks, 0, row_total - 1)
    angle = (
        turns(wave_y, row, row_total) + turns(wave_x, chunk * LANES, column_total)
    ) + offset
    left_cos, left_sin = cos_sin(angle)
    lane = lax.broadcasted_iota(jnp.int32, (mode_count, LANES), 1)
    right_cos, right_sin = cos_sin(turns(wave_x, lane, column_total))
    left = jnp.concatenate([amp * left_cos, amp * left_sin], 0)
    right = jnp.concatenate([right_cos, -right_sin], 0)
    left_high, left_low = halves(left)
    right_high, right_low = halves(right)
    return lax.dot_general(
        jnp.concatenate([left_high, left_high, left_low], 0),
        jnp.concatenate([right_high, right_low, right_high], 0),
        (((0,), (0,)), ((), ())),
        preferred_element_type=f32,
    )


def inverse(values):
    return pl.reciprocal(values, approx=False)


def from_left(values, stride, lane):
    moved = [pltpu.roll(v, stride, 1) for v in values]
    return [jnp.where(lane < stride, moved[c - 1], moved[c]) for c in range(len(values))]


def from_right(values, stride, lane):
    count = len(values)
    moved = [pltpu.roll(v, LANES - stride, 1) for v in values]
    return [
        jnp.where(lane >= LANES - stride, moved[(c + 1) % count], moved[c]) for c in range(count)
    ]


def solve_chunks(diagonal, link, rhs):
    count = len(rhs)
    if count == 1:
        return [rhs[0] * inverse(diagonal[0])]
    inv = {i: inverse(diagonal[i]) for i in range(0, count, 2)}
    scaled = {i: inv[i] * rhs[i] for i in inv}
    odd_diagonal, odd_link, odd_rhs = [], [], []
    for i in range(1, count, 2):
        d = diagonal[i] - link[i - 1] * (link[i - 1] * inv[i - 1])
        r = rhs[i] + link[i - 1] * scaled[i - 1]
        e = None
        if i + 1 < count:
            by = link[i] * inv[i + 1]
            d = d - link[i] * by
            r = r + link[i] * scaled[i + 1]
            e = by * link[i + 1] if i + 2 < count else None
        odd_diagonal.append(d)
        odd_rhs.append(r)
        odd_link.append(e)
    odd = solve_chunks(odd_diagonal, odd_link, odd_rhs)
    out = [None] * count
    out[1::2] = odd
    for i in range(0, count, 2):
        r = rhs[i]
        if i > 0:
            r = r + link[i - 1] * out[i - 1]
        if i + 1 < count:
            r = r + link[i] * out[i + 1]
        out[i] = r * inv[i]
    return out


def reduce_lanes(diagonal, link, rhs, lane, stride):
    count = len(rhs)
    while stride < LANES:
        inv = [inverse(d) for d in diagonal]
        t = [q * r for q, r in zip(inv, rhs)]
        w = [q * e for q, e in zip(inv, link)]
        low_d = from_left([e * v for e, v in zip(link, w)], stride, lane)
        low_r = from_left([e * v for e, v in zip(link, t)], stride, lane)
        high_q = from_right(inv, stride, lane)
        high_t = from_right(t, stride, lane)
        high_w = from_right(w, stride, lane)
        diagonal = [
            diagonal[c] - low_d[c] - link[c] * (link[c] * high_q[c]) for c in range(count)
        ]
        rhs = [rhs[c] + low_r[c] + link[c] * high_t[c] for c in range(count)]
        link = [link[c] * high_w[c] for c in range(count)]
        stride *= 2
    return solve_chunks(diagonal, link, rhs)


def pack_pair(a, b, odd_lane):
    even = [jnp.where(odd_lane, pltpu.roll(x, 1, 1), y) for x, y in zip(a, b)]
    odd = [jnp.where(odd_lane, x, pltpu.roll(y, LANES - 1, 1)) for x, y in zip(a, b)]
    return even, odd


def unpack_pair(even, odd, odd_lane):
    a = [jnp.where(odd_lane, y, pltpu.roll(x, LANES - 1, 1)) for x, y in zip(even, odd)]
    b = [jnp.where(odd_lane, pltpu.roll(y, 1, 1), x) for x, y in zip(even, odd)]
    return a, b


def solve_x_pair(g_pair, rhs_pair, lane):
    odd_lane = (lane & 1) == 1
    first_cell = lane < 2
    last_cell = lane >= LANES - 2
    half = 0.5 * weight
    g_even, g_odd = pack_pair(*g_pair, odd_lane)
    r_even, r_odd = pack_pair(*rhs_pair, odd_lane)
    face = [half * (a + b) for a, b in zip(g_even, g_odd)]
    after = from_right(g_even, 2, lane)
    after[-1] = jnp.where(last_cell, g_odd[-1], after[-1])
    face_after = [half * (a + b) for a, b in zip(g_odd, after)]
    face_before = from_left(face_after, 2, lane)
    face_before[0] = jnp.where(first_cell, weight * g_even[0], face_before[0])
    inv = [inverse(1.0 + (a + b)) for a, b in zip(face_before, face)]
    d_odd = [1.0 + (a + b) for a, b in zip(face, face_after)]
    link = list(face_after)
    link[-1] = jnp.where(last_cell, 0.0, link[-1])
    link_before = list(face_before)
    link_before[0] = jnp.where(first_cell, 0.0, link_before[0])
    t = [q * r for q, r in zip(inv, r_even)]
    w = [q * e for q, e in zip(inv, face)]
    next_q = from_right(inv, 2, lane)
    next_t = from_right(t, 2, lane)
    next_w = from_right(w, 2, lane)
    diagonal = [
        d - e * v - l * (l * q) for d, e, v, l, q in zip(d_odd, face, w, link, next_q)
    ]
    rhs = [r + e * v + l * n for r, e, v, l, n in zip(r_odd, face, t, link, next_t)]
    x_odd = reduce_lanes(diagonal, [l * n for l, n in zip(link, next_w)], rhs, lane, 2)
    x_before = from_left(x_odd, 2, lane)
    x_even = [
        v + q * (l * b) + u * x for v, q, l, b, u, x in zip(t, inv, link_before, x_before, w, x_odd)
    ]
    return unpack_pair(x_even, x_odd, odd_lane)


def load_kernel(
    step_ref, index_ref, amp_ref, phase_ref, field_ref, conduct_ref,
    packed_ref, field_out, conduct_out, inner_ref, outer_ref,
    index_in, amp_in, phase_in, sems,
):
    width = inner_ref.shape[0]
    last = field_ref.shape[0] - width
    odd = lax.rem(lax.axis_index("wide"), 2)
    inner_rows = pl.ds(pl.multiple_of((1 - odd) * last, 8), width)
    outer_rows = pl.ds(pl.multiple_of(odd * last, 8), width)
    pairs = (
        (index_ref, index_in),
        (amp_ref, amp_in),
        (phase_ref, phase_in),
        (field_ref.at[inner_rows], inner_ref),
        (field_ref.at[outer_rows], outer_ref),
        (field_ref, field_out),
        (conduct_ref, conduct_out),
    )
    copies = [pltpu.make_async_copy(a, b, sems.at[n]) for n, (a, b) in enumerate(pairs)]
    for copy in copies:
        copy.start()
    for copy in copies[:3]:
        copy.wait()
    count = index_in.shape[0]
    row = lax.broadcasted_iota(jnp.int32, packed_ref.shape, 0)
    lane = lax.broadcasted_iota(jnp.int32, packed_ref.shape, 1)
    total = jnp.zeros(packed_ref.shape, f32)
    for m in range(count):
        moment = lax.rem(index_in[m, 2] * step_ref[0], jnp.int32(64)).astype(f32)
        offset = phase_in[m] * (0.5 / math.pi) + moment * (1.0 / 64.0)
        for place, value in enumerate(
            (index_in[m, 0].astype(f32), index_in[m, 1].astype(f32), offset, amp_in[m])
        ):
            total = jnp.where((row == m) & (lane == place), value, total)
    packed_ref[...] = total
    for copy in copies[3:]:
        copy.wait()


def block_factors(face):
    inv, scaled, chain, u = [], [], [], []
    rows = len(face) - 1
    rest = 1.0 + face[0]
    for j in range(rows):
        inv.append(inverse(rest + face[j + 1]))
        scaled.append(face[j] * inv[j])
        chain.append(face[j + 1] * inv[j])
        u.append(scaled[j] * u[-1] if j else scaled[j])
        rest = 1.0 + rest * chain[j]
    v = list(chain)
    for j in range(rows - 2, -1, -1):
        u[j] = u[j] + chain[j] * u[j + 1]
        v[j] = chain[j] * v[j + 1]
    return inv, scaled, chain, u, v


def block_ends(face):
    rows = len(face) - 1
    down = 1.0 + face[0]
    up = 1.0 + face[rows]
    v_first = None
    for j in range(rows):
        v_last = face[j + 1] * inverse(down + face[j + 1])
        v_first = v_last if v_first is None else v_first * v_last
        u_first = face[rows - 1 - j] * inverse(up + face[rows - 1 - j])
        if j < rows - 1:
            down = 1.0 + down * v_last
            up = 1.0 + up * u_first
    u_last = v_first * (face[0] * inverse(face[rows]))
    return u_first, v_first, u_last, v_last


def height_kernel(sizes, modes_ref, heights_ref):
    rows, layers, chunks, row_total, layer_total, column_total = sizes
    width = layers * chunks
    body = height_lines(modes_ref[...], 0, row_total, row_total, chunks, column_total)
    heights_ref[chunks : (row_total + 1) * chunks] = body
    heights_ref[0:chunks] = body[0:chunks]
    heights_ref[(row_total + 1) * chunks : (row_total + 2) * chunks] = body[
        (row_total - 1) * chunks : row_total * chunks
    ]


def main_kernel(
    sizes, heights, inner_ref, early_ref, late_ref, field_ref, conduct_ref,
    sent_ref, p_ref, u_ref, v_ref, left_gain_ref, right_gain_ref, joint_ref,
    ends, links, framed, solved,
):
    rows, layers, chunks, row_total, layer_total, column_total = sizes
    width = layers * chunks
    blocks = row_total // rows
    me = lax.axis_index("wide")
    first_layer = lax.axis_index("grp") * layers
    zeta = [
        ((first_layer + k).astype(f32) + 0.5) * (1.0 / layer_total) for k in range(layers)
    ]
    half = 0.5 * weight
    own_start = pl.multiple_of(me * (rows * chunks), 8)

    def faces(start):
        h = [heights[pl.ds(start + j * chunks, chunks), :] for j in range(rows + 2)]
        out = []
        for j in range(rows + 1):
            both = h[j] + h[j + 1]
            out.append(jnp.concatenate([weight + (half * z) * both for z in zeta], 0))
        return out

    def keep_ends(b, values):
        base = pl.multiple_of(b * (4 * width), 8)
        for n, value in enumerate(values):
            ends[pl.ds(base + n * width, width), :] = value

    inv, scaled, chain, u, v = block_factors(faces(own_start))
    for j in range(rows):
        u_ref[j * width : (j + 1) * width] = u[j]
        v_ref[j * width : (j + 1) * width] = v[j]
    keep_ends(me, (u[0], v[0], u[-1], v[-1]))

    def other_block(n):
        b = lax.rem(me + 1 + n, blocks)
        keep_ends(b, block_ends(faces(pl.multiple_of(b * (rows * chunks), 8))))

    if blocks <= 8:
        for n in range(blocks - 1):
            other_block(n)
    else:
        lax.fori_loop(0, blocks - 1, lambda n, carry: (other_block(n), carry)[1], 0)

    def end(b, n):
        return ends[(4 * b + n) * width : (4 * b + n + 1) * width]

    left = jnp.zeros((width, LANES), f32)
    right = jnp.zeros((width, LANES), f32)
    for b in range(blocks):
        u_first, v_first, u_last, v_last = (end(b, n) for n in range(4))
        gain = u_last * inverse(1.0 - u_first * left)
        left_gain_ref[b * width : (b + 1) * width] = gain
        links[b * width : (b + 1) * width] = left
        left = v_last + gain * left * v_first
        b = blocks - 1 - b
        u_first, v_first, u_last, v_last = (end(b, n) for n in range(4))
        gain = v_first * inverse(1.0 - v_last * right)
        right_gain_ref[b * width : (b + 1) * width] = gain
        links[(blocks + b) * width : (blocks + b + 1) * width] = right
        right = u_first + gain * right * u_last

    own = pl.ds(pl.multiple_of(me * width, 8), width)
    left_link = links[own, :]
    right_link = links[pl.ds(pl.multiple_of((blocks + me) * width, 8), width), :]
    a = 1.0 - left_link * u[0]
    b = left_link * v[0]
    c = right_link * u[-1]
    d = 1.0 - right_link * v[-1]
    by = inverse(a * d - b * c)
    joint = (
        left_gain_ref[own, :] * left_link, right_gain_ref[own, :] * right_link,
        left_link, right_link, d * by, b * by, c * by, a * by,
    )
    for n, value in enumerate(joint):
        joint_ref[n * width : (n + 1) * width] = value

    odd = lax.rem(me, 2)
    beyond = (rows + 1) * width
    framed[width:beyond] = field_ref[...]
    framed[pl.ds(pl.multiple_of((1 - odd) * beyond, 8), width), :] = inner_ref[...]
    other = pl.ds(pl.multiple_of(odd * width, 8), width)
    outer_rows = jnp.where(first_layer == 0, early_ref[other, :], late_ref[other, :])
    at_edge = (me == 0) | (me == blocks - 1)
    framed[pl.ds(pl.multiple_of(odd * beyond, 8), width), :] = jnp.where(at_edge, 0.0, outer_rows)
    lane = lax.broadcasted_iota(jnp.int32, (rows, LANES), 1)
    g, f, rhs = [], [], []
    for k in range(layers):
        g.append([])
        f.append([])
        rhs.append([])
        for c in range(chunks):
            h_low, h, h_high = (
                heights[pl.ds(own_start + s * chunks + c, rows, stride=chunks), :]
                for s in range(3)
            )
            place = c * layers + k
            f_low, f_mid, f_high = (
                framed[pl.ds(s * width + place, rows, stride=width), :] for s in range(3)
            )
            g[k].append(conduct_ref[pl.ds(place, rows, stride=width), :] * (1.0 + zeta[k] * h))
            f[k].append(f_mid)
            along = (weight + (half * zeta[k]) * (h + h_high)) * (f_high - f_mid) - (
                weight + (half * zeta[k]) * (h + h_low)
            ) * (f_mid - f_low)
            rhs[k].append(2.0 * (f_mid + along))
    for k in range(0, layers, 2):
        both = solve_x_pair(g[k : k + 2], rhs[k : k + 2], lane)
        for n in range(2):
            for c in range(chunks):
                spot = pl.ds((k + n) * chunks + c, rows, stride=width)
                solved[spot, :] = both[n][c] - 2.0 * f[k + n][c]

    def part(ref, j):
        return ref[j * width : (j + 1) * width]

    p = [part(solved, 0) * inv[0]]
    for j in range(1, rows):
        p.append(part(solved, j) * inv[j] + scaled[j] * p[-1])
    for j in range(rows - 2, -1, -1):
        p[j] = p[j] + chain[j] * p[j + 1]
    for j in range(rows):
        p_ref[j * width : (j + 1) * width] = p[j]

    upward = p[-1] + part(joint_ref, 0) * p[0]
    downward = p[0] + part(joint_ref, 1) * p[-1]
    for b in range(blocks):
        sent_ref[b * width : (b + 1) * width] = jnp.where(b > me, upward, downward)


def last_kernel(
    sizes, came_ref, left_gain_ref, right_gain_ref, joint_ref, p_ref, u_ref, v_ref, field_ref,
    out_ref,
):
    rows, layers, chunks, row_total, layer_total, column_total = sizes
    width = layers * chunks
    blocks = row_total // rows
    me = lax.axis_index("wide")

    def part(ref, b):
        return ref[b * width : (b + 1) * width]

    left = jnp.zeros((width, LANES), f32)
    right = jnp.zeros((width, LANES), f32)
    for b in range(blocks - 1):
        left = jnp.where(b < me, part(came_ref, b) + part(left_gain_ref, b) * left, left)
        b = blocks - 1 - b
        right = jnp.where(b > me, part(came_ref, b) + part(right_gain_ref, b) * right, right)

    y = left + part(joint_ref, 2) * part(p_ref, 0)
    z = right + part(joint_ref, 3) * part(p_ref, rows - 1)
    before = part(joint_ref, 4) * y + part(joint_ref, 5) * z
    after = part(joint_ref, 6) * y + part(joint_ref, 7) * z
    for j in range(rows):
        x = part(p_ref, j) + part(u_ref, j) * before + part(v_ref, j) * after
        for k in range(layers):
            spot = pl.ds(j * width + k, chunks, stride=layers)
            out_ref[spot, :] = field_ref[spot, :] + x[k * chunks : (k + 1) * chunks]


def on_device(field, conduct, mode_index, mode_amp, mode_phase, step_index):
    rows, layers, columns = field.shape
    wide_count = lax.axis_size("wide")
    row_total = rows * wide_count
    grp_count = lax.axis_size("grp")
    layer_total = layers * grp_count
    chunks = columns // LANES
    width = layers * chunks
    sizes = (rows, layers, chunks, row_total, layer_total, columns)
    limit = pltpu.CompilerParams(vmem_limit_bytes=16 * 1024 * 1024)
    hbm = pl.BlockSpec(memory_space=pltpu.HBM)

    def lines(count):
        return jax.ShapeDtypeStruct((count * width, LANES), f32)

    packed, field_lines, conduct_lines, inner, outer = pl.pallas_call(
        load_kernel,
        out_shape=(
            jax.ShapeDtypeStruct((mode_index.shape[0], 8), f32),
            lines(rows),
            lines(rows),
            lines(1),
            lines(1),
        ),
        in_specs=[pl.BlockSpec(memory_space=pltpu.SMEM)] + [hbm] * 5,
        scratch_shapes=[
            pltpu.SMEM(mode_index.shape, jnp.int32),
            pltpu.SMEM(mode_amp.shape, f32),
            pltpu.SMEM(mode_phase.shape, f32),
            pltpu.SemaphoreType.DMA((7,)),
        ],
        compiler_params=limit,
    )(
        step_index,
        *(
            pltpu.with_memory_space_constraint(a, pltpu.HBM)
            for a in (mode_index, mode_amp, mode_phase, to_lines(field), to_lines(conduct))
        ),
    )

    swaps = [(i, i ^ 1) for i in range(wide_count)]
    inner_came = lax.ppermute(inner, "wide", swaps)
    pairs = [[0, wide_count - 1]] + [[i, i + 1] for i in range(1, wide_count - 1, 2)]

    def gather_rows(rows_sent):
        return lax.all_gather(rows_sent, "wide", axis_index_groups=pairs, axis=0, tiled=True)

    def no_rows(rows_sent):
        return jnp.zeros((2 * width, LANES), f32)

    in_first = lax.axis_index("grp") == 0
    early = lax.cond(in_first, gather_rows, no_rows, outer)
    packed, early = lax.optimization_barrier((packed, early))
    modes = lax.all_gather(packed, "grp", axis=0, tiled=True)
    modes, outer = lax.optimization_barrier((modes, outer))
    late = lax.cond(in_first, no_rows, gather_rows, outer)

    heights = pl.pallas_call(
        functools.partial(height_kernel, sizes),
        out_shape=jax.ShapeDtypeStruct(((row_total + 2) * chunks, LANES), f32),
        compiler_params=limit,
    )(modes)

    sent, p, u, v, left_gain, right_gain, joint = pl.pallas_call(
        functools.partial(main_kernel, sizes),
        out_shape=(lines(wide_count),)
        + (lines(rows),) * 3
        + (lines(wide_count),) * 2
        + (lines(8),),
        scratch_shapes=[
            pltpu.VMEM((4 * wide_count * width, LANES), f32),
            pltpu.VMEM((2 * wide_count * width, LANES), f32),
            pltpu.VMEM(((rows + 2) * width, LANES), f32),
            pltpu.VMEM((rows * width, LANES), f32),
        ],
        compiler_params=limit,
    )(heights, inner_came, early, late, field_lines, conduct_lines)

    came = lax.all_to_all(
        sent.reshape(wide_count, width, LANES), "wide", split_axis=0, concat_axis=0
    ).reshape(wide_count * width, LANES)

    advanced = pl.pallas_call(
        functools.partial(last_kernel, sizes),
        out_shape=lines(rows),
        compiler_params=limit,
    )(came, left_gain, right_gain, joint, p, u, v, field_lines)
    return from_lines(advanced, field.shape)


def solution(mesh):
    return jax.shard_map(
        on_device,
        mesh=mesh,
        in_specs=(
            P("wide", "grp", None),
            P("wide", "grp", None),
            P("grp", None),
            P("grp"),
            P("grp"),
            P(),
        ),
        out_specs=P("wide", "grp", None),
        check_vma=False,
    )
```

```python
import functools
import math

import jax
import jax.numpy as jnp
from jax import lax
from jax.experimental import pallas as pl
from jax.experimental.pallas import tpu as pltpu
from jax.sharding import PartitionSpec as P

time_step = 600.0
implicit_weight = 0.5
weight = implicit_weight * time_step
LANES = 128
f32 = jnp.float32


def to_lines(block):
    rows, layers, columns = block.shape
    chunks = columns // LANES
    return (
        block.reshape(rows, layers, chunks, LANES)
        .transpose(0, 2, 1, 3)
        .reshape(rows * chunks * layers, LANES)
    )


def from_lines(lines, shape):
    rows, layers, columns = shape
    chunks = columns // LANES
    return (
        lines.reshape(rows, chunks, layers, LANES)
        .transpose(0, 2, 1, 3)
        .reshape(rows, layers, columns)
    )


def turns(wave, index, period):
    product = wave * index
    if period & (period - 1) == 0:
        product = product & (period - 1)
    else:
        product = lax.rem(product, jnp.int32(period))
    return product.astype(f32) * (1.0 / period)


def cos_sin(turn):
    part = turn - jnp.floor(turn + 0.5)
    square = part * part

    def series(first):
        terms = [
            (-1.0) ** n * math.pi ** (2 * n + first) / math.factorial(2 * n + first)
            for n in range(7)
        ]
        total = jnp.full_like(square, terms[-1])
        for term in terms[-2::-1]:
            total = total * square + term
        return total

    half_cos = series(0)
    half_sin = series(1) * part
    return 1.0 - 2.0 * half_sin * half_sin, 2.0 * half_sin * half_cos


def halves(values):
    high = values.astype(jnp.bfloat16)
    return high, (values - high.astype(f32)).astype(jnp.bfloat16)


def height_lines(modes, first_row, count, row_total, chunks, column_total):
    mode_count = modes.shape[0]
    wave_x = modes[:, 0:1].astype(jnp.int32)
    wave_y = modes[:, 1:2].astype(jnp.int32)
    offset = modes[:, 2:3]
    amp = modes[:, 3:4]
    spot = lax.broadcasted_iota(jnp.int32, (mode_count, count * chunks), 1)
    chunk = spot % chunks
    row = jnp.clip(first_row + spot // chunks, 0, row_total - 1)
    angle = (
        turns(wave_y, row, row_total) + turns(wave_x, chunk * LANES, column_total)
    ) + offset
    left_cos, left_sin = cos_sin(angle)
    lane = lax.broadcasted_iota(jnp.int32, (mode_count, LANES), 1)
    right_cos, right_sin = cos_sin(turns(wave_x, lane, column_total))
    left = jnp.concatenate([amp * left_cos, amp * left_sin], 0)
    right = jnp.concatenate([right_cos, -right_sin], 0)
    left_high, left_low = halves(left)
    right_high, right_low = halves(right)
    return lax.dot_general(
        jnp.concatenate([left_high, left_high, left_low], 0),
        jnp.concatenate([right_high, right_low, right_high], 0),
        (((0,), (0,)), ((), ())),
        preferred_element_type=f32,
    )


def inverse(values):
    return pl.reciprocal(values, approx=False)


def from_left(values, stride, lane):
    moved = [pltpu.roll(v, stride, 1) for v in values]
    return [jnp.where(lane < stride, moved[c - 1], moved[c]) for c in range(len(values))]


def from_right(values, stride, lane):
    count = len(values)
    moved = [pltpu.roll(v, LANES - stride, 1) for v in values]
    return [
        jnp.where(lane >= LANES - stride, moved[(c + 1) % count], moved[c]) for c in range(count)
    ]


def solve_chunks(diagonal, link, rhs):
    count = len(rhs)
    if count == 1:
        return [rhs[0] * inverse(diagonal[0])]
    inv = {i: inverse(diagonal[i]) for i in range(0, count, 2)}
    scaled = {i: inv[i] * rhs[i] for i in inv}
    odd_diagonal, odd_link, odd_rhs = [], [], []
    for i in range(1, count, 2):
        d = diagonal[i] - link[i - 1] * (link[i - 1] * inv[i - 1])
        r = rhs[i] + link[i - 1] * scaled[i - 1]
        e = None
        if i + 1 < count:
            by = link[i] * inv[i + 1]
            d = d - link[i] * by
            r = r + link[i] * scaled[i + 1]
            e = by * link[i + 1] if i + 2 < count else None
        odd_diagonal.append(d)
        odd_rhs.append(r)
        odd_link.append(e)
    odd = solve_chunks(odd_diagonal, odd_link, odd_rhs)
    out = [None] * count
    out[1::2] = odd
    for i in range(0, count, 2):
        r = rhs[i]
        if i > 0:
            r = r + link[i - 1] * out[i - 1]
        if i + 1 < count:
            r = r + link[i] * out[i + 1]
        out[i] = r * inv[i]
    return out


def reduce_lanes(diagonal, link, rhs, lane, stride):
    count = len(rhs)
    while stride < LANES:
        inv = [inverse(d) for d in diagonal]
        t = [q * r for q, r in zip(inv, rhs)]
        w = [q * e for q, e in zip(inv, link)]
        low_d = from_left([e * v for e, v in zip(link, w)], stride, lane)
        low_r = from_left([e * v for e, v in zip(link, t)], stride, lane)
        high_q = from_right(inv, stride, lane)
        high_t = from_right(t, stride, lane)
        high_w = from_right(w, stride, lane)
        diagonal = [
            diagonal[c] - low_d[c] - link[c] * (link[c] * high_q[c]) for c in range(count)
        ]
        rhs = [rhs[c] + low_r[c] + link[c] * high_t[c] for c in range(count)]
        link = [link[c] * high_w[c] for c in range(count)]
        stride *= 2
    return solve_chunks(diagonal, link, rhs)


def pack_pair(a, b, odd_lane):
    even = [jnp.where(odd_lane, pltpu.roll(x, 1, 1), y) for x, y in zip(a, b)]
    odd = [jnp.where(odd_lane, x, pltpu.roll(y, LANES - 1, 1)) for x, y in zip(a, b)]
    return even, odd


def unpack_pair(even, odd, odd_lane):
    a = [jnp.where(odd_lane, y, pltpu.roll(x, LANES - 1, 1)) for x, y in zip(even, odd)]
    b = [jnp.where(odd_lane, pltpu.roll(y, 1, 1), x) for x, y in zip(even, odd)]
    return a, b


def solve_x_pair(g_pair, rhs_pair, lane):
    odd_lane = (lane & 1) == 1
    first_cell = lane < 2
    last_cell = lane >= LANES - 2
    half = 0.5 * weight
    g_even, g_odd = pack_pair(*g_pair, odd_lane)
    r_even, r_odd = pack_pair(*rhs_pair, odd_lane)
    face = [half * (a + b) for a, b in zip(g_even, g_odd)]
    after = from_right(g_even, 2, lane)
    after[-1] = jnp.where(last_cell, g_odd[-1], after[-1])
    face_after = [half * (a + b) for a, b in zip(g_odd, after)]
    face_before = from_left(face_after, 2, lane)
    face_before[0] = jnp.where(first_cell, weight * g_even[0], face_before[0])
    inv = [inverse(1.0 + (a + b)) for a, b in zip(face_before, face)]
    d_odd = [1.0 + (a + b) for a, b in zip(face, face_after)]
    link = list(face_after)
    link[-1] = jnp.where(last_cell, 0.0, link[-1])
    link_before = list(face_before)
    link_before[0] = jnp.where(first_cell, 0.0, link_before[0])
    t = [q * r for q, r in zip(inv, r_even)]
    w = [q * e for q, e in zip(inv, face)]
    next_q = from_right(inv, 2, lane)
    next_t = from_right(t, 2, lane)
    next_w = from_right(w, 2, lane)
    diagonal = [
        d - e * v - l * (l * q) for d, e, v, l, q in zip(d_odd, face, w, link, next_q)
    ]
    rhs = [r + e * v + l * n for r, e, v, l, n in zip(r_odd, face, t, link, next_t)]
    x_odd = reduce_lanes(diagonal, [l * n for l, n in zip(link, next_w)], rhs, lane, 2)
    x_before = from_left(x_odd, 2, lane)
    x_even = [
        v + q * (l * b) + u * x for v, q, l, b, u, x in zip(t, inv, link_before, x_before, w, x_odd)
    ]
    return unpack_pair(x_even, x_odd, odd_lane)


def load_kernel(
    step_ref, index_ref, amp_ref, phase_ref, field_ref, conduct_ref,
    packed_ref, field_out, conduct_out, inner_ref, outer_ref,
    index_in, amp_in, phase_in, sems,
):
    width = inner_ref.shape[0]
    last = field_ref.shape[0] - width
    odd = lax.rem(lax.axis_index("wide"), 2)
    inner_rows = pl.ds(pl.multiple_of((1 - odd) * last, 8), width)
    outer_rows = pl.ds(pl.multiple_of(odd * last, 8), width)
    pairs = (
        (index_ref, index_in),
        (amp_ref, amp_in),
        (phase_ref, phase_in),
        (field_ref.at[inner_rows], inner_ref),
        (field_ref.at[outer_rows], outer_ref),
        (field_ref, field_out),
        (conduct_ref, conduct_out),
    )
    copies = [pltpu.make_async_copy(a, b, sems.at[n]) for n, (a, b) in enumerate(pairs)]
    for copy in copies:
        copy.start()
    for copy in copies[:3]:
        copy.wait()
    count = index_in.shape[0]
    row = lax.broadcasted_iota(jnp.int32, packed_ref.shape, 0)
    lane = lax.broadcasted_iota(jnp.int32, packed_ref.shape, 1)
    total = jnp.zeros(packed_ref.shape, f32)
    for m in range(count):
        moment = lax.rem(index_in[m, 2] * step_ref[0], jnp.int32(64)).astype(f32)
        offset = phase_in[m] * (0.5 / math.pi) + moment * (1.0 / 64.0)
        for place, value in enumerate(
            (index_in[m, 0].astype(f32), index_in[m, 1].astype(f32), offset, amp_in[m])
        ):
            total = jnp.where((row == m) & (lane == place), value, total)
    packed_ref[...] = total
    for copy in copies[3:]:
        copy.wait()


def block_factors(face):
    inv, scaled, chain, u = [], [], [], []
    rows = len(face) - 1
    rest = 1.0 + face[0]
    for j in range(rows):
        inv.append(inverse(rest + face[j + 1]))
        scaled.append(face[j] * inv[j])
        chain.append(face[j + 1] * inv[j])
        u.append(scaled[j] * u[-1] if j else scaled[j])
        rest = 1.0 + rest * chain[j]
    v = list(chain)
    for j in range(rows - 2, -1, -1):
        u[j] = u[j] + chain[j] * u[j + 1]
        v[j] = chain[j] * v[j + 1]
    return inv, scaled, chain, u, v


def block_ends(face):
    rows = len(face) - 1
    down = 1.0 + face[0]
    up = 1.0 + face[rows]
    v_first = None
    for j in range(rows):
        v_last = face[j + 1] * inverse(down + face[j + 1])
        v_first = v_last if v_first is None else v_first * v_last
        u_first = face[rows - 1 - j] * inverse(up + face[rows - 1 - j])
        if j < rows - 1:
            down = 1.0 + down * v_last
            up = 1.0 + up * u_first
    u_last = v_first * (face[0] * inverse(face[rows]))
    return u_first, v_first, u_last, v_last


def height_kernel(
    sizes, modes_ref, modes_came_ref, inner_ref, outer_ref, heights_ref, halo_ref
):
    rows, layers, chunks, row_total, layer_total, column_total = sizes
    width = layers * chunks
    odd = lax.rem(lax.axis_index("wide"), 2) == 1
    modes = jnp.where(odd, modes_ref[...], modes_came_ref[...])
    body = height_lines(modes, 0, row_total, row_total, chunks, column_total)
    heights_ref[chunks : (row_total + 1) * chunks] = body
    heights_ref[0:chunks] = body[0:chunks]
    heights_ref[(row_total + 1) * chunks : (row_total + 2) * chunks] = body[
        (row_total - 1) * chunks : row_total * chunks
    ]
    halo_ref[0:width] = inner_ref[...]
    halo_ref[width : 2 * width] = outer_ref[...]


def main_kernel(
    sizes, heights, halo_ref, late_ref, field_ref, conduct_ref,
    sent_ref, p_ref, u_ref, v_ref, left_gain_ref, right_gain_ref, joint_ref,
    ends, links, framed, solved,
):
    rows, layers, chunks, row_total, layer_total, column_total = sizes
    width = layers * chunks
    blocks = row_total // rows
    me = lax.axis_index("wide")
    first_layer = lax.axis_index("grp") * layers
    zeta = [
        ((first_layer + k).astype(f32) + 0.5) * (1.0 / layer_total) for k in range(layers)
    ]
    half = 0.5 * weight
    own_start = pl.multiple_of(me * (rows * chunks), 8)

    def faces(start):
        h = [heights[pl.ds(start + j * chunks, chunks), :] for j in range(rows + 2)]
        out = []
        for j in range(rows + 1):
            both = h[j] + h[j + 1]
            out.append(jnp.concatenate([weight + (half * z) * both for z in zeta], 0))
        return out

    def keep_ends(b, values):
        base = pl.multiple_of(b * (4 * width), 8)
        for n, value in enumerate(values):
            ends[pl.ds(base + n * width, width), :] = value

    inv, scaled, chain, u, v = block_factors(faces(own_start))
    for j in range(rows):
        u_ref[j * width : (j + 1) * width] = u[j]
        v_ref[j * width : (j + 1) * width] = v[j]
    keep_ends(me, (u[0], v[0], u[-1], v[-1]))

    def other_block(n):
        b = lax.rem(me + 1 + n, blocks)
        keep_ends(b, block_ends(faces(pl.multiple_of(b * (rows * chunks), 8))))

    if blocks <= 8:
        for n in range(blocks - 1):
            other_block(n)
    else:
        lax.fori_loop(0, blocks - 1, lambda n, carry: (other_block(n), carry)[1], 0)

    def end(b, n):
        return ends[(4 * b + n) * width : (4 * b + n + 1) * width]

    left = jnp.zeros((width, LANES), f32)
    right = jnp.zeros((width, LANES), f32)
    for b in range(blocks):
        u_first, v_first, u_last, v_last = (end(b, n) for n in range(4))
        gain = u_last * inverse(1.0 - u_first * left)
        left_gain_ref[b * width : (b + 1) * width] = gain
        links[b * width : (b + 1) * width] = left
        left = v_last + gain * left * v_first
        b = blocks - 1 - b
        u_first, v_first, u_last, v_last = (end(b, n) for n in range(4))
        gain = v_first * inverse(1.0 - v_last * right)
        right_gain_ref[b * width : (b + 1) * width] = gain
        links[(blocks + b) * width : (blocks + b + 1) * width] = right
        right = u_first + gain * right * u_last

    own = pl.ds(pl.multiple_of(me * width, 8), width)
    left_link = links[own, :]
    right_link = links[pl.ds(pl.multiple_of((blocks + me) * width, 8), width), :]
    a = 1.0 - left_link * u[0]
    b = left_link * v[0]
    c = right_link * u[-1]
    d = 1.0 - right_link * v[-1]
    by = inverse(a * d - b * c)
    joint = (
        left_gain_ref[own, :] * left_link, right_gain_ref[own, :] * right_link,
        left_link, right_link, d * by, b * by, c * by, a * by,
    )
    for n, value in enumerate(joint):
        joint_ref[n * width : (n + 1) * width] = value

    odd = lax.rem(me, 2)
    beyond = (rows + 1) * width
    framed[width:beyond] = field_ref[...]
    framed[pl.ds(pl.multiple_of((1 - odd) * beyond, 8), width), :] = halo_ref[0:width]
    other = pl.ds(pl.multiple_of(odd * width, 8), width)
    outer_rows = jnp.where(
        first_layer == 0, halo_ref[width : 2 * width], late_ref[other, :]
    )
    at_edge = (me == 0) | (me == blocks - 1)
    framed[pl.ds(pl.multiple_of(odd * beyond, 8), width), :] = jnp.where(at_edge, 0.0, outer_rows)
    lane = lax.broadcasted_iota(jnp.int32, (rows, LANES), 1)
    g, f, rhs = [], [], []
    for k in range(layers):
        g.append([])
        f.append([])
        rhs.append([])
        for c in range(chunks):
            h_low, h, h_high = (
                heights[pl.ds(own_start + s * chunks + c, rows, stride=chunks), :]
                for s in range(3)
            )
            place = c * layers + k
            f_low, f_mid, f_high = (
                framed[pl.ds(s * width + place, rows, stride=width), :] for s in range(3)
            )
            g[k].append(conduct_ref[pl.ds(place, rows, stride=width), :] * (1.0 + zeta[k] * h))
            f[k].append(f_mid)
            along = (weight + (half * zeta[k]) * (h + h_high)) * (f_high - f_mid) - (
                weight + (half * zeta[k]) * (h + h_low)
            ) * (f_mid - f_low)
            rhs[k].append(2.0 * (f_mid + along))
    for k in range(0, layers, 2):
        both = solve_x_pair(g[k : k + 2], rhs[k : k + 2], lane)
        for n in range(2):
            for c in range(chunks):
                spot = pl.ds((k + n) * chunks + c, rows, stride=width)
                solved[spot, :] = both[n][c] - 2.0 * f[k + n][c]

    def part(ref, j):
        return ref[j * width : (j + 1) * width]

    p = [part(solved, 0) * inv[0]]
    for j in range(1, rows):
        p.append(part(solved, j) * inv[j] + scaled[j] * p[-1])
    for j in range(rows - 2, -1, -1):
        p[j] = p[j] + chain[j] * p[j + 1]
    for j in range(rows):
        p_ref[j * width : (j + 1) * width] = p[j]

    upward = p[-1] + part(joint_ref, 0) * p[0]
    downward = p[0] + part(joint_ref, 1) * p[-1]
    for b in range(blocks):
        sent_ref[b * width : (b + 1) * width] = jnp.where(b > me, upward, downward)


def last_kernel(
    sizes, came_ref, left_gain_ref, right_gain_ref, joint_ref, p_ref, u_ref, v_ref, field_ref,
    out_ref,
):
    rows, layers, chunks, row_total, layer_total, column_total = sizes
    width = layers * chunks
    blocks = row_total // rows
    me = lax.axis_index("wide")

    def part(ref, b):
        return ref[b * width : (b + 1) * width]

    left = jnp.zeros((width, LANES), f32)
    right = jnp.zeros((width, LANES), f32)
    for b in range(blocks - 1):
        left = jnp.where(b < me, part(came_ref, b) + part(left_gain_ref, b) * left, left)
        b = blocks - 1 - b
        right = jnp.where(b > me, part(came_ref, b) + part(right_gain_ref, b) * right, right)

    y = left + part(joint_ref, 2) * part(p_ref, 0)
    z = right + part(joint_ref, 3) * part(p_ref, rows - 1)
    before = part(joint_ref, 4) * y + part(joint_ref, 5) * z
    after = part(joint_ref, 6) * y + part(joint_ref, 7) * z
    for j in range(rows):
        x = part(p_ref, j) + part(u_ref, j) * before + part(v_ref, j) * after
        for k in range(layers):
            spot = pl.ds(j * width + k, chunks, stride=layers)
            out_ref[spot, :] = field_ref[spot, :] + x[k * chunks : (k + 1) * chunks]


def on_device(field, conduct, mode_index, mode_amp, mode_phase, step_index):
    rows, layers, columns = field.shape
    wide_count = lax.axis_size("wide")
    row_total = rows * wide_count
    grp_count = lax.axis_size("grp")
    layer_total = layers * grp_count
    chunks = columns // LANES
    width = layers * chunks
    sizes = (rows, layers, chunks, row_total, layer_total, columns)
    limit = pltpu.CompilerParams(vmem_limit_bytes=16 * 1024 * 1024)
    hbm = pl.BlockSpec(memory_space=pltpu.HBM)

    def lines(count):
        return jax.ShapeDtypeStruct((count * width, LANES), f32)

    packed, field_lines, conduct_lines, inner, outer = pl.pallas_call(
        load_kernel,
        out_shape=(
            jax.ShapeDtypeStruct((mode_index.shape[0], 8), f32),
            lines(rows),
            lines(rows),
            lines(1),
            lines(1),
        ),
        in_specs=[pl.BlockSpec(memory_space=pltpu.SMEM)] + [hbm] * 5,
        scratch_shapes=[
            pltpu.SMEM(mode_index.shape, jnp.int32),
            pltpu.SMEM(mode_amp.shape, f32),
            pltpu.SMEM(mode_phase.shape, f32),
            pltpu.SemaphoreType.DMA((7,)),
        ],
        compiler_params=limit,
    )(
        step_index,
        *(
            pltpu.with_memory_space_constraint(a, pltpu.HBM)
            for a in (mode_index, mode_amp, mode_phase, to_lines(field), to_lines(conduct))
        ),
    )

    swaps = [(i, i ^ 1) for i in range(wide_count)]
    inner_came = lax.ppermute(inner, "wide", swaps)
    pairs = [[0, wide_count - 1]] + [[i, i + 1] for i in range(1, wide_count - 1, 2)]
    early_came = lax.ppermute(
        outer, ("grp", "wide"), [pair for a, b in pairs[1:] for pair in ((a, b), (b, a))]
    )

    odd = lax.axis_index("wide") % 2 == 1
    mode_shape = (grp_count * packed.shape[0], packed.shape[1])

    def gather_modes(own):
        return lax.all_gather(own, "grp", axis=0, tiled=True)

    modes = lax.cond(odd, gather_modes, lambda own: jnp.zeros(mode_shape, f32), packed)
    modes_came = lax.ppermute(modes, "wide", swaps)
    modes, modes_came, outer = lax.optimization_barrier((modes, modes_came, outer))

    def gather_rows(rows_sent):
        return lax.all_gather(rows_sent, "wide", axis_index_groups=pairs, axis=0, tiled=True)

    late_came = lax.cond(
        lax.axis_index("grp") == 0, lambda own: jnp.zeros((2 * width, LANES), f32), gather_rows, outer
    )

    heights, halo = pl.pallas_call(
        functools.partial(height_kernel, sizes),
        out_shape=(jax.ShapeDtypeStruct(((row_total + 2) * chunks, LANES), f32), lines(2)),
        compiler_params=limit,
    )(modes, modes_came, inner_came, early_came)

    sent, p, u, v, left_gain, right_gain, joint = pl.pallas_call(
        functools.partial(main_kernel, sizes),
        out_shape=(lines(wide_count),)
        + (lines(rows),) * 3
        + (lines(wide_count),) * 2
        + (lines(8),),
        scratch_shapes=[
            pltpu.VMEM((4 * wide_count * width, LANES), f32),
            pltpu.VMEM((2 * wide_count * width, LANES), f32),
            pltpu.VMEM(((rows + 2) * width, LANES), f32),
            pltpu.VMEM((rows * width, LANES), f32),
        ],
        compiler_params=limit,
    )(heights, halo, late_came, field_lines, conduct_lines)

    came = lax.all_to_all(
        sent.reshape(wide_count, width, LANES), "wide", split_axis=0, concat_axis=0
    ).reshape(wide_count * width, LANES)

    advanced = pl.pallas_call(
        functools.partial(last_kernel, sizes),
        out_shape=lines(rows),
        compiler_params=limit,
    )(came, left_gain, right_gain, joint, p, u, v, field_lines)
    return from_lines(advanced, field.shape)


def solution(mesh):
    return jax.shard_map(
        on_device,
        mesh=mesh,
        in_specs=(
            P("wide", "grp", None),
            P("wide", "grp", None),
            P("grp", None),
            P("grp"),
            P("grp"),
            P(),
        ),
        out_specs=P("wide", "grp", None),
        check_vma=False,
    )
```

```python
import functools
import math

import jax
import jax.numpy as jnp
from jax import lax
from jax.experimental import pallas as pl
from jax.experimental.pallas import tpu as pltpu
from jax.sharding import PartitionSpec as P

time_step = 600.0
implicit_weight = 0.5
weight = implicit_weight * time_step
LANES = 128
f32 = jnp.float32


def to_lines(block):
    rows, layers, columns = block.shape
    chunks = columns // LANES
    return (
        block.reshape(rows, layers, chunks, LANES)
        .transpose(0, 2, 1, 3)
        .reshape(rows * chunks * layers, LANES)
    )


def from_lines(lines, shape):
    rows, layers, columns = shape
    chunks = columns // LANES
    return (
        lines.reshape(rows, chunks, layers, LANES)
        .transpose(0, 2, 1, 3)
        .reshape(rows, layers, columns)
    )


def turns(wave, index, period):
    product = wave * index
    if period & (period - 1) == 0:
        product = product & (period - 1)
    else:
        product = lax.rem(product, jnp.int32(period))
    return product.astype(f32) * (1.0 / period)


def cos_sin(turn):
    part = turn - jnp.floor(turn + 0.5)
    square = part * part

    def series(first):
        terms = [
            (-1.0) ** n * math.pi ** (2 * n + first) / math.factorial(2 * n + first)
            for n in range(7)
        ]
        total = jnp.full_like(square, terms[-1])
        for term in terms[-2::-1]:
            total = total * square + term
        return total

    half_cos = series(0)
    half_sin = series(1) * part
    return 1.0 - 2.0 * half_sin * half_sin, 2.0 * half_sin * half_cos


def halves(values):
    high = values.astype(jnp.bfloat16)
    return high, (values - high.astype(f32)).astype(jnp.bfloat16)


def height_lines(modes, first_row, count, row_total, chunks, column_total):
    mode_count = modes.shape[0]
    wave_x = modes[:, 0:1].astype(jnp.int32)
    wave_y = modes[:, 1:2].astype(jnp.int32)
    offset = modes[:, 2:3]
    amp = modes[:, 3:4]
    spot = lax.broadcasted_iota(jnp.int32, (mode_count, count * chunks), 1)
    chunk = spot % chunks
    row = jnp.clip(first_row + spot // chunks, 0, row_total - 1)
    angle = (
        turns(wave_y, row, row_total) + turns(wave_x, chunk * LANES, column_total)
    ) + offset
    left_cos, left_sin = cos_sin(angle)
    lane = lax.broadcasted_iota(jnp.int32, (mode_count, LANES), 1)
    right_cos, right_sin = cos_sin(turns(wave_x, lane, column_total))
    left = jnp.concatenate([amp * left_cos, amp * left_sin], 0)
    right = jnp.concatenate([right_cos, -right_sin], 0)
    left_high, left_low = halves(left)
    right_high, right_low = halves(right)
    return lax.dot_general(
        jnp.concatenate([left_high, left_high, left_low], 0),
        jnp.concatenate([right_high, right_low, right_high], 0),
        (((0,), (0,)), ((), ())),
        preferred_element_type=f32,
    )


def inverse(values):
    return pl.reciprocal(values, approx=False)


def from_left(values, stride, lane):
    moved = [pltpu.roll(v, stride, 1) for v in values]
    return [jnp.where(lane < stride, moved[c - 1], moved[c]) for c in range(len(values))]


def from_right(values, stride, lane):
    count = len(values)
    moved = [pltpu.roll(v, LANES - stride, 1) for v in values]
    return [
        jnp.where(lane >= LANES - stride, moved[(c + 1) % count], moved[c]) for c in range(count)
    ]


def solve_chunks(diagonal, link, rhs):
    count = len(rhs)
    if count == 1:
        return [rhs[0] * inverse(diagonal[0])]
    inv = {i: inverse(diagonal[i]) for i in range(0, count, 2)}
    scaled = {i: inv[i] * rhs[i] for i in inv}
    odd_diagonal, odd_link, odd_rhs = [], [], []
    for i in range(1, count, 2):
        d = diagonal[i] - link[i - 1] * (link[i - 1] * inv[i - 1])
        r = rhs[i] + link[i - 1] * scaled[i - 1]
        e = None
        if i + 1 < count:
            by = link[i] * inv[i + 1]
            d = d - link[i] * by
            r = r + link[i] * scaled[i + 1]
            e = by * link[i + 1] if i + 2 < count else None
        odd_diagonal.append(d)
        odd_rhs.append(r)
        odd_link.append(e)
    odd = solve_chunks(odd_diagonal, odd_link, odd_rhs)
    out = [None] * count
    out[1::2] = odd
    for i in range(0, count, 2):
        r = rhs[i]
        if i > 0:
            r = r + link[i - 1] * out[i - 1]
        if i + 1 < count:
            r = r + link[i] * out[i + 1]
        out[i] = r * inv[i]
    return out


def reduce_lanes(diagonal, link, rhs, lane, stride):
    count = len(rhs)
    while stride < LANES:
        inv = [inverse(d) for d in diagonal]
        t = [q * r for q, r in zip(inv, rhs)]
        w = [q * e for q, e in zip(inv, link)]
        low_d = from_left([e * v for e, v in zip(link, w)], stride, lane)
        low_r = from_left([e * v for e, v in zip(link, t)], stride, lane)
        high_q = from_right(inv, stride, lane)
        high_t = from_right(t, stride, lane)
        high_w = from_right(w, stride, lane)
        diagonal = [
            diagonal[c] - low_d[c] - link[c] * (link[c] * high_q[c]) for c in range(count)
        ]
        rhs = [rhs[c] + low_r[c] + link[c] * high_t[c] for c in range(count)]
        link = [link[c] * high_w[c] for c in range(count)]
        stride *= 2
    return solve_chunks(diagonal, link, rhs)


def pack_pair(a, b, odd_lane):
    even = [jnp.where(odd_lane, pltpu.roll(x, 1, 1), y) for x, y in zip(a, b)]
    odd = [jnp.where(odd_lane, x, pltpu.roll(y, LANES - 1, 1)) for x, y in zip(a, b)]
    return even, odd


def unpack_pair(even, odd, odd_lane):
    a = [jnp.where(odd_lane, y, pltpu.roll(x, LANES - 1, 1)) for x, y in zip(even, odd)]
    b = [jnp.where(odd_lane, pltpu.roll(y, 1, 1), x) for x, y in zip(even, odd)]
    return a, b


def solve_x_pair(g_pair, rhs_pair, lane):
    odd_lane = (lane & 1) == 1
    first_cell = lane < 2
    last_cell = lane >= LANES - 2
    half = 0.5 * weight
    g_even, g_odd = pack_pair(*g_pair, odd_lane)
    r_even, r_odd = pack_pair(*rhs_pair, odd_lane)
    face = [half * (a + b) for a, b in zip(g_even, g_odd)]
    after = from_right(g_even, 2, lane)
    after[-1] = jnp.where(last_cell, g_odd[-1], after[-1])
    face_after = [half * (a + b) for a, b in zip(g_odd, after)]
    face_before = from_left(face_after, 2, lane)
    face_before[0] = jnp.where(first_cell, weight * g_even[0], face_before[0])
    inv = [inverse(1.0 + (a + b)) for a, b in zip(face_before, face)]
    d_odd = [1.0 + (a + b) for a, b in zip(face, face_after)]
    link = list(face_after)
    link[-1] = jnp.where(last_cell, 0.0, link[-1])
    link_before = list(face_before)
    link_before[0] = jnp.where(first_cell, 0.0, link_before[0])
    t = [q * r for q, r in zip(inv, r_even)]
    w = [q * e for q, e in zip(inv, face)]
    next_q = from_right(inv, 2, lane)
    next_t = from_right(t, 2, lane)
    next_w = from_right(w, 2, lane)
    diagonal = [
        d - e * v - l * (l * q) for d, e, v, l, q in zip(d_odd, face, w, link, next_q)
    ]
    rhs = [r + e * v + l * n for r, e, v, l, n in zip(r_odd, face, t, link, next_t)]
    x_odd = reduce_lanes(diagonal, [l * n for l, n in zip(link, next_w)], rhs, lane, 2)
    x_before = from_left(x_odd, 2, lane)
    x_even = [
        v + q * (l * b) + u * x for v, q, l, b, u, x in zip(t, inv, link_before, x_before, w, x_odd)
    ]
    return unpack_pair(x_even, x_odd, odd_lane)


def load_kernel(
    step_ref, index_ref, amp_ref, phase_ref, field_ref, conduct_ref,
    packed_ref, field_out, conduct_out, both_ref, outer_ref,
    index_in, amp_in, phase_in, sems,
):
    width = outer_ref.shape[0]
    last = field_ref.shape[0] - width
    odd = lax.rem(lax.axis_index("wide"), 2)
    inner_rows = pl.ds(pl.multiple_of((1 - odd) * last, 8), width)
    outer_rows = pl.ds(pl.multiple_of(odd * last, 8), width)
    pairs = (
        (index_ref, index_in),
        (amp_ref, amp_in),
        (phase_ref, phase_in),
        (field_ref.at[inner_rows], both_ref.at[pl.ds(0, width)]),
        (field_ref.at[outer_rows], both_ref.at[pl.ds(width, width)]),
        (field_ref.at[outer_rows], outer_ref),
        (field_ref, field_out),
        (conduct_ref, conduct_out),
    )
    copies = [pltpu.make_async_copy(a, b, sems.at[n]) for n, (a, b) in enumerate(pairs)]
    for copy in copies:
        copy.start()
    for copy in copies[:3]:
        copy.wait()
    count = index_in.shape[0]
    row = lax.broadcasted_iota(jnp.int32, packed_ref.shape, 0)
    lane = lax.broadcasted_iota(jnp.int32, packed_ref.shape, 1)
    total = jnp.zeros(packed_ref.shape, f32)
    for m in range(count):
        moment = lax.rem(index_in[m, 2] * step_ref[0], jnp.int32(64)).astype(f32)
        offset = phase_in[m] * (0.5 / math.pi) + moment * (1.0 / 64.0)
        for place, value in enumerate(
            (index_in[m, 0].astype(f32), index_in[m, 1].astype(f32), offset, amp_in[m])
        ):
            total = jnp.where((row == m) & (lane == place), value, total)
    packed_ref[...] = total
    for copy in copies[3:]:
        copy.wait()


def block_factors(face):
    inv, scaled, chain, u = [], [], [], []
    rows = len(face) - 1
    rest = 1.0 + face[0]
    for j in range(rows):
        inv.append(inverse(rest + face[j + 1]))
        scaled.append(face[j] * inv[j])
        chain.append(face[j + 1] * inv[j])
        u.append(scaled[j] * u[-1] if j else scaled[j])
        rest = 1.0 + rest * chain[j]
    v = list(chain)
    for j in range(rows - 2, -1, -1):
        u[j] = u[j] + chain[j] * u[j + 1]
        v[j] = chain[j] * v[j + 1]
    return inv, scaled, chain, u, v


def block_ends(face):
    rows = len(face) - 1
    down = 1.0 + face[0]
    up = 1.0 + face[rows]
    v_first = None
    for j in range(rows):
        v_last = face[j + 1] * inverse(down + face[j + 1])
        v_first = v_last if v_first is None else v_first * v_last
        u_first = face[rows - 1 - j] * inverse(up + face[rows - 1 - j])
        if j < rows - 1:
            down = 1.0 + down * v_last
            up = 1.0 + up * u_first
    u_last = v_first * (face[0] * inverse(face[rows]))
    return u_first, v_first, u_last, v_last


def height_kernel(sizes, modes_ref, modes_came_ref, heights_ref):
    rows, layers, chunks, row_total, layer_total, column_total = sizes
    odd = lax.rem(lax.axis_index("wide"), 2) == 1
    modes = jnp.where(odd, modes_ref[...], modes_came_ref[...])
    body = height_lines(modes, 0, row_total, row_total, chunks, column_total)
    heights_ref[chunks : (row_total + 1) * chunks] = body
    heights_ref[0:chunks] = body[0:chunks]
    heights_ref[(row_total + 1) * chunks : (row_total + 2) * chunks] = body[
        (row_total - 1) * chunks : row_total * chunks
    ]

def main_kernel(
    sizes, heights, both_ref, below_ref, above_ref, field_ref, conduct_ref,
    sent_ref, p_ref, u_ref, v_ref, left_gain_ref, right_gain_ref, joint_ref,
    ends, links, framed, solved,
):
    rows, layers, chunks, row_total, layer_total, column_total = sizes
    width = layers * chunks
    blocks = row_total // rows
    me = lax.axis_index("wide")
    first_layer = lax.axis_index("grp") * layers
    zeta = [
        ((first_layer + k).astype(f32) + 0.5) * (1.0 / layer_total) for k in range(layers)
    ]
    half = 0.5 * weight
    own_start = pl.multiple_of(me * (rows * chunks), 8)

    def faces(start):
        h = [heights[pl.ds(start + j * chunks, chunks), :] for j in range(rows + 2)]
        out = []
        for j in range(rows + 1):
            both = h[j] + h[j + 1]
            out.append(jnp.concatenate([weight + (half * z) * both for z in zeta], 0))
        return out

    def keep_ends(b, values):
        base = pl.multiple_of(b * (4 * width), 8)
        for n, value in enumerate(values):
            ends[pl.ds(base + n * width, width), :] = value

    inv, scaled, chain, u, v = block_factors(faces(own_start))
    for j in range(rows):
        u_ref[j * width : (j + 1) * width] = u[j]
        v_ref[j * width : (j + 1) * width] = v[j]
    keep_ends(me, (u[0], v[0], u[-1], v[-1]))

    def other_block(n):
        b = lax.rem(me + 1 + n, blocks)
        keep_ends(b, block_ends(faces(pl.multiple_of(b * (rows * chunks), 8))))

    if blocks <= 8:
        for n in range(blocks - 1):
            other_block(n)
    else:
        lax.fori_loop(0, blocks - 1, lambda n, carry: (other_block(n), carry)[1], 0)

    def end(b, n):
        return ends[(4 * b + n) * width : (4 * b + n + 1) * width]

    left = jnp.zeros((width, LANES), f32)
    right = jnp.zeros((width, LANES), f32)
    for b in range(blocks):
        u_first, v_first, u_last, v_last = (end(b, n) for n in range(4))
        gain = u_last * inverse(1.0 - u_first * left)
        left_gain_ref[b * width : (b + 1) * width] = gain
        links[b * width : (b + 1) * width] = left
        left = v_last + gain * left * v_first
        b = blocks - 1 - b
        u_first, v_first, u_last, v_last = (end(b, n) for n in range(4))
        gain = v_first * inverse(1.0 - v_last * right)
        right_gain_ref[b * width : (b + 1) * width] = gain
        links[(blocks + b) * width : (blocks + b + 1) * width] = right
        right = u_first + gain * right * u_last

    own = pl.ds(pl.multiple_of(me * width, 8), width)
    left_link = links[own, :]
    right_link = links[pl.ds(pl.multiple_of((blocks + me) * width, 8), width), :]
    a = 1.0 - left_link * u[0]
    b = left_link * v[0]
    c = right_link * u[-1]
    d = 1.0 - right_link * v[-1]
    by = inverse(a * d - b * c)
    joint = (
        left_gain_ref[own, :] * left_link, right_gain_ref[own, :] * right_link,
        left_link, right_link, d * by, b * by, c * by, a * by,
    )
    for n, value in enumerate(joint):
        joint_ref[n * width : (n + 1) * width] = value

    odd = lax.rem(me, 2)
    beyond = (rows + 1) * width
    framed[width:beyond] = field_ref[...]
    framed[pl.ds(pl.multiple_of((1 - odd) * beyond, 8), width), :] = both_ref[0:width]
    outer_rows = jnp.where(odd == 1, above_ref[...], below_ref[...])
    at_edge = (me == 0) | (me == blocks - 1)
    framed[pl.ds(pl.multiple_of(odd * beyond, 8), width), :] = jnp.where(at_edge, 0.0, outer_rows)
    lane = lax.broadcasted_iota(jnp.int32, (rows, LANES), 1)
    g, f, rhs = [], [], []
    for k in range(layers):
        g.append([])
        f.append([])
        rhs.append([])
        for c in range(chunks):
            h_low, h, h_high = (
                heights[pl.ds(own_start + s * chunks + c, rows, stride=chunks), :]
                for s in range(3)
            )
            place = c * layers + k
            f_low, f_mid, f_high = (
                framed[pl.ds(s * width + place, rows, stride=width), :] for s in range(3)
            )
            g[k].append(conduct_ref[pl.ds(place, rows, stride=width), :] * (1.0 + zeta[k] * h))
            f[k].append(f_mid)
            along = (weight + (half * zeta[k]) * (h + h_high)) * (f_high - f_mid) - (
                weight + (half * zeta[k]) * (h + h_low)
            ) * (f_mid - f_low)
            rhs[k].append(2.0 * (f_mid + along))
    for k in range(0, layers, 2):
        both = solve_x_pair(g[k : k + 2], rhs[k : k + 2], lane)
        for n in range(2):
            for c in range(chunks):
                spot = pl.ds((k + n) * chunks + c, rows, stride=width)
                solved[spot, :] = both[n][c] - 2.0 * f[k + n][c]

    def part(ref, j):
        return ref[j * width : (j + 1) * width]

    p = [part(solved, 0) * inv[0]]
    for j in range(1, rows):
        p.append(part(solved, j) * inv[j] + scaled[j] * p[-1])
    for j in range(rows - 2, -1, -1):
        p[j] = p[j] + chain[j] * p[j + 1]
    for j in range(rows):
        p_ref[j * width : (j + 1) * width] = p[j]

    upward = p[-1] + part(joint_ref, 0) * p[0]
    downward = p[0] + part(joint_ref, 1) * p[-1]
    for b in range(blocks):
        sent_ref[b * width : (b + 1) * width] = jnp.where(b > me, upward, downward)


def last_kernel(
    sizes, came_ref, left_gain_ref, right_gain_ref, joint_ref, p_ref, u_ref, v_ref, field_ref,
    out_ref,
):
    rows, layers, chunks, row_total, layer_total, column_total = sizes
    width = layers * chunks
    blocks = row_total // rows
    me = lax.axis_index("wide")

    def part(ref, b):
        return ref[b * width : (b + 1) * width]

    left = jnp.zeros((width, LANES), f32)
    right = jnp.zeros((width, LANES), f32)
    for b in range(blocks - 1):
        left = jnp.where(b < me, part(came_ref, b) + part(left_gain_ref, b) * left, left)
        b = blocks - 1 - b
        right = jnp.where(b > me, part(came_ref, b) + part(right_gain_ref, b) * right, right)

    y = left + part(joint_ref, 2) * part(p_ref, 0)
    z = right + part(joint_ref, 3) * part(p_ref, rows - 1)
    before = part(joint_ref, 4) * y + part(joint_ref, 5) * z
    after = part(joint_ref, 6) * y + part(joint_ref, 7) * z
    for j in range(rows):
        x = part(p_ref, j) + part(u_ref, j) * before + part(v_ref, j) * after
        for k in range(layers):
            spot = pl.ds(j * width + k, chunks, stride=layers)
            out_ref[spot, :] = field_ref[spot, :] + x[k * chunks : (k + 1) * chunks]


def on_device(field, conduct, mode_index, mode_amp, mode_phase, step_index):
    rows, layers, columns = field.shape
    wide_count = lax.axis_size("wide")
    row_total = rows * wide_count
    grp_count = lax.axis_size("grp")
    layer_total = layers * grp_count
    chunks = columns // LANES
    width = layers * chunks
    sizes = (rows, layers, chunks, row_total, layer_total, columns)
    limit = pltpu.CompilerParams(vmem_limit_bytes=16 * 1024 * 1024)
    hbm = pl.BlockSpec(memory_space=pltpu.HBM)

    def lines(count):
        return jax.ShapeDtypeStruct((count * width, LANES), f32)

    packed, field_lines, conduct_lines, both, outer = pl.pallas_call(
        load_kernel,
        out_shape=(
            jax.ShapeDtypeStruct((mode_index.shape[0], 8), f32),
            lines(rows),
            lines(rows),
            lines(2),
            lines(1),
        ),
        in_specs=[pl.BlockSpec(memory_space=pltpu.SMEM)] + [hbm] * 5,
        scratch_shapes=[
            pltpu.SMEM(mode_index.shape, jnp.int32),
            pltpu.SMEM(mode_amp.shape, f32),
            pltpu.SMEM(mode_phase.shape, f32),
            pltpu.SemaphoreType.DMA((8,)),
        ],
        compiler_params=limit,
    )(
        step_index,
        *(
            pltpu.with_memory_space_constraint(a, pltpu.HBM)
            for a in (mode_index, mode_amp, mode_phase, to_lines(field), to_lines(conduct))
        ),
    )

    place = lax.axis_index("wide")
    odd = place % 2 == 1
    swaps = [(i, i ^ 1) for i in range(wide_count)]
    cores = [list(range(n, wide_count, 2)) for n in range(2)]
    both_came = lax.ppermute(both, "wide", swaps)

    def gather_modes(own):
        return lax.all_gather(own, "grp", axis=0, tiled=True)

    def no_modes(own):
        return jnp.zeros((grp_count * own.shape[0], own.shape[1]), f32)

    modes = lax.cond(odd, gather_modes, no_modes, packed)
    modes, outer, both_came = lax.optimization_barrier((modes, outer, both_came))

    def gather_rows(own, came):
        rows_sent = jnp.concatenate([own, came[width:]], 0)
        rows_all = lax.all_gather(rows_sent, "wide", axis_index_groups=cores, axis=0)
        chip = place // 2
        below = lax.dynamic_index_in_dim(rows_all, jnp.maximum(chip - 1, 0), 0, False)
        above = lax.dynamic_index_in_dim(
            rows_all, jnp.minimum(chip + 1, wide_count // 2 - 1), 0, False
        )
        return below[width:], above[:width]

    def no_rows(own, came):
        return jnp.zeros_like(own), jnp.zeros_like(own)

    below, above = lax.cond(odd, no_rows, gather_rows, outer, both_came)
    above_came = lax.ppermute(above, "wide", swaps)
    modes_came = lax.ppermute(modes, "wide", swaps)

    heights = pl.pallas_call(
        functools.partial(height_kernel, sizes),
        out_shape=jax.ShapeDtypeStruct(((row_total + 2) * chunks, LANES), f32),
        compiler_params=limit,
    )(modes, modes_came)

    sent, p, u, v, left_gain, right_gain, joint = pl.pallas_call(
        functools.partial(main_kernel, sizes),
        out_shape=(lines(wide_count),)
        + (lines(rows),) * 3
        + (lines(wide_count),) * 2
        + (lines(8),),
        scratch_shapes=[
            pltpu.VMEM((4 * wide_count * width, LANES), f32),
            pltpu.VMEM((2 * wide_count * width, LANES), f32),
            pltpu.VMEM(((rows + 2) * width, LANES), f32),
            pltpu.VMEM((rows * width, LANES), f32),
        ],
        compiler_params=limit,
    )(heights, both_came, below, above_came, field_lines, conduct_lines)

    came = lax.all_to_all(
        sent.reshape(wide_count, width, LANES), "wide", split_axis=0, concat_axis=0
    ).reshape(wide_count * width, LANES)

    advanced = pl.pallas_call(
        functools.partial(last_kernel, sizes),
        out_shape=lines(rows),
        compiler_params=limit,
    )(came, left_gain, right_gain, joint, p, u, v, field_lines)
    return from_lines(advanced, field.shape)


def solution(mesh):
    return jax.shard_map(
        on_device,
        mesh=mesh,
        in_specs=(
            P("wide", "grp", None),
            P("wide", "grp", None),
            P("grp", None),
            P("grp"),
            P("grp"),
            P(),
        ),
        out_specs=P("wide", "grp", None),
        check_vma=False,
    )
```

```python
import functools
import math

import jax
import jax.numpy as jnp
from jax import lax
from jax.experimental import pallas as pl
from jax.experimental.pallas import tpu as pltpu
from jax.sharding import PartitionSpec as P

time_step = 600.0
implicit_weight = 0.5
weight = implicit_weight * time_step
LANES = 128
f32 = jnp.float32


def to_lines(block):
    rows, layers, columns = block.shape
    chunks = columns // LANES
    return (
        block.reshape(rows, layers, chunks, LANES)
        .transpose(0, 2, 1, 3)
        .reshape(rows * chunks * layers, LANES)
    )


def from_lines(lines, shape):
    rows, layers, columns = shape
    chunks = columns // LANES
    return (
        lines.reshape(rows, chunks, layers, LANES)
        .transpose(0, 2, 1, 3)
        .reshape(rows, layers, columns)
    )


def turns(wave, index, period):
    product = wave * index
    if period & (period - 1) == 0:
        product = product & (period - 1)
    else:
        product = lax.rem(product, jnp.int32(period))
    return product.astype(f32) * (1.0 / period)


def cos_sin(turn):
    part = turn - jnp.floor(turn + 0.5)
    square = part * part

    def series(first):
        terms = [
            (-1.0) ** n * math.pi ** (2 * n + first) / math.factorial(2 * n + first)
            for n in range(7)
        ]
        total = jnp.full_like(square, terms[-1])
        for term in terms[-2::-1]:
            total = total * square + term
        return total

    half_cos = series(0)
    half_sin = series(1) * part
    return 1.0 - 2.0 * half_sin * half_sin, 2.0 * half_sin * half_cos


def halves(values):
    high = values.astype(jnp.bfloat16)
    return high, (values - high.astype(f32)).astype(jnp.bfloat16)


def height_lines(modes, first_row, count, row_total, chunks, column_total):
    mode_count = modes.shape[0]
    wave_x = modes[:, 0:1].astype(jnp.int32)
    wave_y = modes[:, 1:2].astype(jnp.int32)
    offset = modes[:, 2:3]
    amp = modes[:, 3:4]
    spot = lax.broadcasted_iota(jnp.int32, (mode_count, count * chunks), 1)
    chunk = spot % chunks
    row = jnp.clip(first_row + spot // chunks, 0, row_total - 1)
    angle = (
        turns(wave_y, row, row_total) + turns(wave_x, chunk * LANES, column_total)
    ) + offset
    left_cos, left_sin = cos_sin(angle)
    lane = lax.broadcasted_iota(jnp.int32, (mode_count, LANES), 1)
    right_cos, right_sin = cos_sin(turns(wave_x, lane, column_total))
    left = jnp.concatenate([amp * left_cos, amp * left_sin], 0)
    right = jnp.concatenate([right_cos, -right_sin], 0)
    left_high, left_low = halves(left)
    right_high, right_low = halves(right)
    return lax.dot_general(
        jnp.concatenate([left_high, left_high, left_low], 0),
        jnp.concatenate([right_high, right_low, right_high], 0),
        (((0,), (0,)), ((), ())),
        preferred_element_type=f32,
    )


def inverse(values):
    return pl.reciprocal(values, approx=False)


def from_left(values, stride, lane):
    moved = [pltpu.roll(v, stride, 1) for v in values]
    return [jnp.where(lane < stride, moved[c - 1], moved[c]) for c in range(len(values))]


def from_right(values, stride, lane):
    count = len(values)
    moved = [pltpu.roll(v, LANES - stride, 1) for v in values]
    return [
        jnp.where(lane >= LANES - stride, moved[(c + 1) % count], moved[c]) for c in range(count)
    ]


def solve_chunks(diagonal, link, rhs):
    count = len(rhs)
    if count == 1:
        return [rhs[0] * inverse(diagonal[0])]
    inv = {i: inverse(diagonal[i]) for i in range(0, count, 2)}
    scaled = {i: inv[i] * rhs[i] for i in inv}
    odd_diagonal, odd_link, odd_rhs = [], [], []
    for i in range(1, count, 2):
        d = diagonal[i] - link[i - 1] * (link[i - 1] * inv[i - 1])
        r = rhs[i] + link[i - 1] * scaled[i - 1]
        e = None
        if i + 1 < count:
            by = link[i] * inv[i + 1]
            d = d - link[i] * by
            r = r + link[i] * scaled[i + 1]
            e = by * link[i + 1] if i + 2 < count else None
        odd_diagonal.append(d)
        odd_rhs.append(r)
        odd_link.append(e)
    odd = solve_chunks(odd_diagonal, odd_link, odd_rhs)
    out = [None] * count
    out[1::2] = odd
    for i in range(0, count, 2):
        r = rhs[i]
        if i > 0:
            r = r + link[i - 1] * out[i - 1]
        if i + 1 < count:
            r = r + link[i] * out[i + 1]
        out[i] = r * inv[i]
    return out


def reduce_lanes(diagonal, link, rhs, lane, stride):
    count = len(rhs)
    while stride < LANES:
        inv = [inverse(d) for d in diagonal]
        t = [q * r for q, r in zip(inv, rhs)]
        w = [q * e for q, e in zip(inv, link)]
        low_d = from_left([e * v for e, v in zip(link, w)], stride, lane)
        low_r = from_left([e * v for e, v in zip(link, t)], stride, lane)
        high_q = from_right(inv, stride, lane)
        high_t = from_right(t, stride, lane)
        high_w = from_right(w, stride, lane)
        diagonal = [
            diagonal[c] - low_d[c] - link[c] * (link[c] * high_q[c]) for c in range(count)
        ]
        rhs = [rhs[c] + low_r[c] + link[c] * high_t[c] for c in range(count)]
        link = [link[c] * high_w[c] for c in range(count)]
        stride *= 2
    return solve_chunks(diagonal, link, rhs)


def pack_pair(a, b, odd_lane):
    even = [jnp.where(odd_lane, pltpu.roll(x, 1, 1), y) for x, y in zip(a, b)]
    odd = [jnp.where(odd_lane, x, pltpu.roll(y, LANES - 1, 1)) for x, y in zip(a, b)]
    return even, odd


def unpack_pair(even, odd, odd_lane):
    a = [jnp.where(odd_lane, y, pltpu.roll(x, LANES - 1, 1)) for x, y in zip(even, odd)]
    b = [jnp.where(odd_lane, pltpu.roll(y, 1, 1), x) for x, y in zip(even, odd)]
    return a, b


def solve_x_pair(g_pair, rhs_pair, lane):
    odd_lane = (lane & 1) == 1
    first_cell = lane < 2
    last_cell = lane >= LANES - 2
    half = 0.5 * weight
    g_even, g_odd = pack_pair(*g_pair, odd_lane)
    r_even, r_odd = pack_pair(*rhs_pair, odd_lane)
    face = [half * (a + b) for a, b in zip(g_even, g_odd)]
    after = from_right(g_even, 2, lane)
    after[-1] = jnp.where(last_cell, g_odd[-1], after[-1])
    face_after = [half * (a + b) for a, b in zip(g_odd, after)]
    face_before = from_left(face_after, 2, lane)
    face_before[0] = jnp.where(first_cell, weight * g_even[0], face_before[0])
    inv = [inverse(1.0 + (a + b)) for a, b in zip(face_before, face)]
    d_odd = [1.0 + (a + b) for a, b in zip(face, face_after)]
    link = list(face_after)
    link[-1] = jnp.where(last_cell, 0.0, link[-1])
    link_before = list(face_before)
    link_before[0] = jnp.where(first_cell, 0.0, link_before[0])
    t = [q * r for q, r in zip(inv, r_even)]
    w = [q * e for q, e in zip(inv, face)]
    next_q = from_right(inv, 2, lane)
    next_t = from_right(t, 2, lane)
    next_w = from_right(w, 2, lane)
    diagonal = [
        d - e * v - l * (l * q) for d, e, v, l, q in zip(d_odd, face, w, link, next_q)
    ]
    rhs = [r + e * v + l * n for r, e, v, l, n in zip(r_odd, face, t, link, next_t)]
    x_odd = reduce_lanes(diagonal, [l * n for l, n in zip(link, next_w)], rhs, lane, 2)
    x_before = from_left(x_odd, 2, lane)
    x_even = [
        v + q * (l * b) + u * x for v, q, l, b, u, x in zip(t, inv, link_before, x_before, w, x_odd)
    ]
    return unpack_pair(x_even, x_odd, odd_lane)


def load_kernel(
    step_ref, index_ref, amp_ref, phase_ref, field_ref, conduct_ref,
    packed_ref, field_out, conduct_out, both_ref, outer_ref,
    index_in, amp_in, phase_in, sems,
):
    width = outer_ref.shape[0]
    last = field_ref.shape[0] - width
    odd = lax.rem(lax.axis_index("wide"), 2)
    inner_rows = pl.ds(pl.multiple_of((1 - odd) * last, 8), width)
    outer_rows = pl.ds(pl.multiple_of(odd * last, 8), width)
    pairs = (
        (index_ref, index_in),
        (amp_ref, amp_in),
        (phase_ref, phase_in),
        (field_ref.at[inner_rows], both_ref.at[pl.ds(0, width)]),
        (field_ref.at[outer_rows], both_ref.at[pl.ds(width, width)]),
        (field_ref.at[outer_rows], outer_ref),
        (field_ref, field_out),
        (conduct_ref, conduct_out),
    )
    copies = [pltpu.make_async_copy(a, b, sems.at[n]) for n, (a, b) in enumerate(pairs)]
    for copy in copies:
        copy.start()
    for copy in copies[:3]:
        copy.wait()
    count = index_in.shape[0]
    row = lax.broadcasted_iota(jnp.int32, packed_ref.shape, 0)
    lane = lax.broadcasted_iota(jnp.int32, packed_ref.shape, 1)
    total = jnp.zeros(packed_ref.shape, f32)
    for m in range(count):
        moment = lax.rem(index_in[m, 2] * step_ref[0], jnp.int32(64)).astype(f32)
        offset = phase_in[m] * (0.5 / math.pi) + moment * (1.0 / 64.0)
        for place, value in enumerate(
            (index_in[m, 0].astype(f32), index_in[m, 1].astype(f32), offset, amp_in[m])
        ):
            total = jnp.where((row == m) & (lane == place), value, total)
    packed_ref[...] = total
    for copy in copies[3:]:
        copy.wait()


def block_factors(face):
    inv, scaled, chain, u = [], [], [], []
    rows = len(face) - 1
    rest = 1.0 + face[0]
    for j in range(rows):
        inv.append(inverse(rest + face[j + 1]))
        scaled.append(face[j] * inv[j])
        chain.append(face[j + 1] * inv[j])
        u.append(scaled[j] * u[-1] if j else scaled[j])
        rest = 1.0 + rest * chain[j]
    v = list(chain)
    for j in range(rows - 2, -1, -1):
        u[j] = u[j] + chain[j] * u[j + 1]
        v[j] = chain[j] * v[j + 1]
    return inv, scaled, chain, u, v


def block_ends(faces):
    rows = len(faces[0]) - 1
    down = [1.0 + face[0] for face in faces]
    up = [1.0 + face[rows] for face in faces]
    v_first = None
    for j in range(rows):
        v_last = [f[j + 1] * inverse(d + f[j + 1]) for f, d in zip(faces, down)]
        u_first = [f[rows - 1 - j] * inverse(d + f[rows - 1 - j]) for f, d in zip(faces, up)]
        v_first = [a * b for a, b in zip(v_first, v_last)] if j else v_last
        if j < rows - 1:
            down = [1.0 + d * v for d, v in zip(down, v_last)]
            up = [1.0 + d * u for d, u in zip(up, u_first)]
    u_last = [v * (f[0] * inverse(f[rows])) for f, v in zip(faces, v_first)]
    return list(zip(u_first, v_first, u_last, v_last))


def main_kernel(
    sizes, modes_ref, modes_came_ref, both_ref, below_ref, above_ref, field_ref, conduct_ref,
    sent_ref, p_ref, u_ref, v_ref, left_gain_ref, right_gain_ref, joint_ref,
    heights, ends, links, framed, solved,
):
    rows, layers, chunks, row_total, layer_total, column_total = sizes
    width = layers * chunks
    blocks = row_total // rows
    me = lax.axis_index("wide")
    first_layer = lax.axis_index("grp") * layers
    zeta = [
        ((first_layer + k).astype(f32) + 0.5) * (1.0 / layer_total) for k in range(layers)
    ]
    half = 0.5 * weight
    odd = lax.rem(me, 2)
    modes = jnp.where(odd == 1, modes_ref[...], modes_came_ref[...])
    body = height_lines(modes, 0, row_total, row_total, chunks, column_total)
    heights[chunks : (row_total + 1) * chunks] = body
    heights[0:chunks] = body[0:chunks]
    heights[(row_total + 1) * chunks : (row_total + 2) * chunks] = body[
        (row_total - 1) * chunks : row_total * chunks
    ]
    own_start = pl.multiple_of(me * (rows * chunks), 8)

    def faces(start):
        h = [heights[pl.ds(start + j * chunks, chunks), :] for j in range(rows + 2)]
        out = []
        for j in range(rows + 1):
            both = h[j] + h[j + 1]
            out.append(jnp.concatenate([weight + (half * z) * both for z in zeta], 0))
        return out

    def keep_ends(b, values):
        base = pl.multiple_of(b * (4 * width), 8)
        for n, value in enumerate(values):
            ends[pl.ds(base + n * width, width), :] = value

    inv, scaled, chain, u, v = block_factors(faces(own_start))
    for j in range(rows):
        u_ref[j * width : (j + 1) * width] = u[j]
        v_ref[j * width : (j + 1) * width] = v[j]
    keep_ends(me, (u[0], v[0], u[-1], v[-1]))

    def other_blocks(first, count):
        spots = [lax.rem(me + 1 + first + n, blocks) for n in range(count)]
        starts = [pl.multiple_of(b * (rows * chunks), 8) for b in spots]
        for b, values in zip(spots, block_ends([faces(start) for start in starts])):
            keep_ends(b, values)

    group = 4
    if blocks <= 8:
        for first in range(0, blocks - 1, group):
            other_blocks(first, min(group, blocks - 1 - first))
    else:
        lax.fori_loop(0, blocks - 1, lambda n, carry: (other_blocks(n, 1), carry)[1], 0)

    def end(b, n):
        return ends[(4 * b + n) * width : (4 * b + n + 1) * width]

    left = jnp.zeros((width, LANES), f32)
    right = jnp.zeros((width, LANES), f32)
    for b in range(blocks):
        u_first, v_first, u_last, v_last = (end(b, n) for n in range(4))
        gain = u_last * inverse(1.0 - u_first * left)
        left_gain_ref[b * width : (b + 1) * width] = gain
        links[b * width : (b + 1) * width] = left
        left = v_last + gain * left * v_first
        b = blocks - 1 - b
        u_first, v_first, u_last, v_last = (end(b, n) for n in range(4))
        gain = v_first * inverse(1.0 - v_last * right)
        right_gain_ref[b * width : (b + 1) * width] = gain
        links[(blocks + b) * width : (blocks + b + 1) * width] = right
        right = u_first + gain * right * u_last

    own = pl.ds(pl.multiple_of(me * width, 8), width)
    left_link = links[own, :]
    right_link = links[pl.ds(pl.multiple_of((blocks + me) * width, 8), width), :]
    a = 1.0 - left_link * u[0]
    b = left_link * v[0]
    c = right_link * u[-1]
    d = 1.0 - right_link * v[-1]
    by = inverse(a * d - b * c)
    joint = (
        left_gain_ref[own, :] * left_link, right_gain_ref[own, :] * right_link,
        left_link, right_link, d * by, b * by, c * by, a * by,
    )
    for n, value in enumerate(joint):
        joint_ref[n * width : (n + 1) * width] = value

    beyond = (rows + 1) * width
    framed[width:beyond] = field_ref[...]
    framed[pl.ds(pl.multiple_of((1 - odd) * beyond, 8), width), :] = both_ref[0:width]
    outer_rows = jnp.where(odd == 1, above_ref[...], below_ref[...])
    at_edge = (me == 0) | (me == blocks - 1)
    framed[pl.ds(pl.multiple_of(odd * beyond, 8), width), :] = jnp.where(at_edge, 0.0, outer_rows)
    lane = lax.broadcasted_iota(jnp.int32, (rows, LANES), 1)
    g, f, rhs = [], [], []
    for k in range(layers):
        g.append([])
        f.append([])
        rhs.append([])
        for c in range(chunks):
            h_low, h, h_high = (
                heights[pl.ds(own_start + s * chunks + c, rows, stride=chunks), :]
                for s in range(3)
            )
            place = c * layers + k
            f_low, f_mid, f_high = (
                framed[pl.ds(s * width + place, rows, stride=width), :] for s in range(3)
            )
            g[k].append(conduct_ref[pl.ds(place, rows, stride=width), :] * (1.0 + zeta[k] * h))
            f[k].append(f_mid)
            along = (weight + (half * zeta[k]) * (h + h_high)) * (f_high - f_mid) - (
                weight + (half * zeta[k]) * (h + h_low)
            ) * (f_mid - f_low)
            rhs[k].append(2.0 * (f_mid + along))
    for k in range(0, layers, 2):
        both = solve_x_pair(g[k : k + 2], rhs[k : k + 2], lane)
        for n in range(2):
            for c in range(chunks):
                spot = pl.ds((k + n) * chunks + c, rows, stride=width)
                solved[spot, :] = both[n][c] - 2.0 * f[k + n][c]

    def part(ref, j):
        return ref[j * width : (j + 1) * width]

    p = [part(solved, 0) * inv[0]]
    for j in range(1, rows):
        p.append(part(solved, j) * inv[j] + scaled[j] * p[-1])
    for j in range(rows - 2, -1, -1):
        p[j] = p[j] + chain[j] * p[j + 1]
    for j in range(rows):
        p_ref[j * width : (j + 1) * width] = p[j]

    upward = p[-1] + part(joint_ref, 0) * p[0]
    downward = p[0] + part(joint_ref, 1) * p[-1]
    for b in range(blocks):
        sent_ref[b * width : (b + 1) * width] = jnp.where(b > me, upward, downward)


def last_kernel(
    sizes, came_ref, left_gain_ref, right_gain_ref, joint_ref, p_ref, u_ref, v_ref, field_ref,
    out_ref, done, sems,
):
    rows, layers, chunks, row_total, layer_total, column_total = sizes
    width = layers * chunks
    blocks = row_total // rows
    me = lax.axis_index("wide")

    def part(ref, b):
        return ref[b * width : (b + 1) * width]

    left = jnp.zeros((width, LANES), f32)
    right = jnp.zeros((width, LANES), f32)
    for b in range(blocks - 1):
        left = jnp.where(b < me, part(came_ref, b) + part(left_gain_ref, b) * left, left)
        b = blocks - 1 - b
        right = jnp.where(b > me, part(came_ref, b) + part(right_gain_ref, b) * right, right)

    y = left + part(joint_ref, 2) * part(p_ref, 0)
    z = right + part(joint_ref, 3) * part(p_ref, rows - 1)
    before = part(joint_ref, 4) * y + part(joint_ref, 5) * z
    after = part(joint_ref, 6) * y + part(joint_ref, 7) * z
    copies = []
    for j in range(rows):
        x = part(p_ref, j) + part(u_ref, j) * before + part(v_ref, j) * after
        for k in range(layers):
            spot = pl.ds(j * width + k, chunks, stride=layers)
            done[spot, :] = field_ref[spot, :] + x[k * chunks : (k + 1) * chunks]
        if j % 2 == 1:
            slab = pl.ds((j - 1) * width, 2 * width)
            copies.append(pltpu.make_async_copy(done.at[slab], out_ref.at[slab], sems.at[j // 2]))
            copies[-1].start()
    for copy in copies:
        copy.wait()


def on_device(field, conduct, mode_index, mode_amp, mode_phase, step_index):
    rows, layers, columns = field.shape
    wide_count = lax.axis_size("wide")
    row_total = rows * wide_count
    grp_count = lax.axis_size("grp")
    layer_total = layers * grp_count
    chunks = columns // LANES
    width = layers * chunks
    sizes = (rows, layers, chunks, row_total, layer_total, columns)
    limit = pltpu.CompilerParams(vmem_limit_bytes=16 * 1024 * 1024)
    hbm = pl.BlockSpec(memory_space=pltpu.HBM)

    def lines(count):
        return jax.ShapeDtypeStruct((count * width, LANES), f32)

    packed, field_lines, conduct_lines, both, outer = pl.pallas_call(
        load_kernel,
        out_shape=(
            jax.ShapeDtypeStruct((mode_index.shape[0], 8), f32),
            lines(rows),
            lines(rows),
            lines(2),
            lines(1),
        ),
        in_specs=[pl.BlockSpec(memory_space=pltpu.SMEM)] + [hbm] * 5,
        scratch_shapes=[
            pltpu.SMEM(mode_index.shape, jnp.int32),
            pltpu.SMEM(mode_amp.shape, f32),
            pltpu.SMEM(mode_phase.shape, f32),
            pltpu.SemaphoreType.DMA((8,)),
        ],
        compiler_params=limit,
    )(
        step_index,
        *(
            pltpu.with_memory_space_constraint(a, pltpu.HBM)
            for a in (mode_index, mode_amp, mode_phase, to_lines(field), to_lines(conduct))
        ),
    )

    place = lax.axis_index("wide")
    odd = place % 2 == 1
    swaps = [(i, i ^ 1) for i in range(wide_count)]
    cores = [list(range(n, wide_count, 2)) for n in range(2)]
    both_came = lax.ppermute(both, "wide", swaps)

    def gather_modes(own):
        return lax.all_gather(own, "grp", axis=0, tiled=True)

    def no_modes(own):
        return jnp.zeros((grp_count * own.shape[0], own.shape[1]), f32)

    modes = lax.cond(odd, gather_modes, no_modes, packed)
    modes, outer, both_came = lax.optimization_barrier((modes, outer, both_came))

    def gather_rows(own, came):
        rows_sent = jnp.concatenate([own, came[width:]], 0)
        rows_all = lax.all_gather(rows_sent, "wide", axis_index_groups=cores, axis=0)
        chip = place // 2
        below = lax.dynamic_index_in_dim(rows_all, jnp.maximum(chip - 1, 0), 0, False)
        above = lax.dynamic_index_in_dim(
            rows_all, jnp.minimum(chip + 1, wide_count // 2 - 1), 0, False
        )
        return below[width:], above[:width]

    def no_rows(own, came):
        return jnp.zeros_like(own), jnp.zeros_like(own)

    below, above = lax.cond(odd, no_rows, gather_rows, outer, both_came)
    above_came = lax.ppermute(above, "wide", swaps)
    modes_came = lax.ppermute(modes, "wide", swaps)

    sent, p, u, v, left_gain, right_gain, joint = pl.pallas_call(
        functools.partial(main_kernel, sizes),
        out_shape=(lines(wide_count),)
        + (lines(rows),) * 3
        + (lines(wide_count),) * 2
        + (lines(8),),
        scratch_shapes=[
            pltpu.VMEM(((row_total + 2) * chunks, LANES), f32),
            pltpu.VMEM((4 * wide_count * width, LANES), f32),
            pltpu.VMEM((2 * wide_count * width, LANES), f32),
            pltpu.VMEM(((rows + 2) * width, LANES), f32),
            pltpu.VMEM((rows * width, LANES), f32),
        ],
        compiler_params=limit,
    )(modes, modes_came, both_came, below, above_came, field_lines, conduct_lines)

    came = lax.all_to_all(
        sent.reshape(wide_count, width, LANES), "wide", split_axis=0, concat_axis=0
    ).reshape(wide_count * width, LANES)

    advanced = pl.pallas_call(
        functools.partial(last_kernel, sizes),
        out_shape=lines(rows),
        out_specs=hbm,
        scratch_shapes=[
            pltpu.VMEM((rows * width, LANES), f32),
            pltpu.SemaphoreType.DMA((rows // 2,)),
        ],
        compiler_params=limit,
    )(came, left_gain, right_gain, joint, p, u, v, field_lines)
    return from_lines(advanced, field.shape)


def solution(mesh):
    return jax.shard_map(
        on_device,
        mesh=mesh,
        in_specs=(
            P("wide", "grp", None),
            P("wide", "grp", None),
            P("grp", None),
            P("grp"),
            P("grp"),
            P(),
        ),
        out_specs=P("wide", "grp", None),
        check_vma=False,
    )
```

```python
import functools
import math

import jax
import jax.numpy as jnp
from jax import lax
from jax.experimental import pallas as pl
from jax.experimental.pallas import tpu as pltpu
from jax.sharding import PartitionSpec as P

time_step = 600.0
implicit_weight = 0.5
weight = implicit_weight * time_step
LANES = 128
f32 = jnp.float32


def to_lines(block):
    rows, layers, columns = block.shape
    chunks = columns // LANES
    return (
        block.reshape(rows, layers, chunks, LANES)
        .transpose(0, 2, 1, 3)
        .reshape(rows * chunks * layers, LANES)
    )


def from_lines(lines, shape):
    rows, layers, columns = shape
    chunks = columns // LANES
    return (
        lines.reshape(rows, chunks, layers, LANES)
        .transpose(0, 2, 1, 3)
        .reshape(rows, layers, columns)
    )


def turns(wave, index, period):
    product = wave * index
    if period & (period - 1) == 0:
        product = product & (period - 1)
    else:
        product = lax.rem(product, jnp.int32(period))
    return product.astype(f32) * (1.0 / period)


def cos_sin(turn):
    part = turn - jnp.floor(turn + 0.5)
    square = part * part

    def series(first):
        terms = [
            (-1.0) ** n * math.pi ** (2 * n + first) / math.factorial(2 * n + first)
            for n in range(7)
        ]
        total = jnp.full_like(square, terms[-1])
        for term in terms[-2::-1]:
            total = total * square + term
        return total

    half_cos = series(0)
    half_sin = series(1) * part
    return 1.0 - 2.0 * half_sin * half_sin, 2.0 * half_sin * half_cos


def halves(values):
    high = values.astype(jnp.bfloat16)
    return high, (values - high.astype(f32)).astype(jnp.bfloat16)


def height_lines(modes, first_row, count, row_total, chunks, column_total):
    mode_count = modes.shape[0]
    wave_x = modes[:, 0:1].astype(jnp.int32)
    wave_y = modes[:, 1:2].astype(jnp.int32)
    offset = modes[:, 2:3]
    amp = modes[:, 3:4]
    spot = lax.broadcasted_iota(jnp.int32, (mode_count, count * chunks), 1)
    chunk = spot % chunks
    row = jnp.clip(first_row + spot // chunks, 0, row_total - 1)
    angle = (
        turns(wave_y, row, row_total) + turns(wave_x, chunk * LANES, column_total)
    ) + offset
    left_cos, left_sin = cos_sin(angle)
    lane = lax.broadcasted_iota(jnp.int32, (mode_count, LANES), 1)
    right_cos, right_sin = cos_sin(turns(wave_x, lane, column_total))
    left = jnp.concatenate([amp * left_cos, amp * left_sin], 0)
    right = jnp.concatenate([right_cos, -right_sin], 0)
    left_high, left_low = halves(left)
    right_high, right_low = halves(right)
    return lax.dot_general(
        jnp.concatenate([left_high, left_high, left_low], 0),
        jnp.concatenate([right_high, right_low, right_high], 0),
        (((0,), (0,)), ((), ())),
        preferred_element_type=f32,
    )


def inverse(values):
    return pl.reciprocal(values, approx=False)


def from_left(values, stride, lane):
    moved = [pltpu.roll(v, stride, 1) for v in values]
    return [jnp.where(lane < stride, moved[c - 1], moved[c]) for c in range(len(values))]


def from_right(values, stride, lane):
    count = len(values)
    moved = [pltpu.roll(v, LANES - stride, 1) for v in values]
    return [
        jnp.where(lane >= LANES - stride, moved[(c + 1) % count], moved[c]) for c in range(count)
    ]


def solve_chunks(diagonal, link, rhs):
    count = len(rhs)
    if count == 1:
        return [rhs[0] * inverse(diagonal[0])]
    inv = {i: inverse(diagonal[i]) for i in range(0, count, 2)}
    scaled = {i: inv[i] * rhs[i] for i in inv}
    odd_diagonal, odd_link, odd_rhs = [], [], []
    for i in range(1, count, 2):
        d = diagonal[i] - link[i - 1] * (link[i - 1] * inv[i - 1])
        r = rhs[i] + link[i - 1] * scaled[i - 1]
        e = None
        if i + 1 < count:
            by = link[i] * inv[i + 1]
            d = d - link[i] * by
            r = r + link[i] * scaled[i + 1]
            e = by * link[i + 1] if i + 2 < count else None
        odd_diagonal.append(d)
        odd_rhs.append(r)
        odd_link.append(e)
    odd = solve_chunks(odd_diagonal, odd_link, odd_rhs)
    out = [None] * count
    out[1::2] = odd
    for i in range(0, count, 2):
        r = rhs[i]
        if i > 0:
            r = r + link[i - 1] * out[i - 1]
        if i + 1 < count:
            r = r + link[i] * out[i + 1]
        out[i] = r * inv[i]
    return out


def reduce_lanes(diagonal, link, rhs, lane, stride):
    count = len(rhs)
    while stride < LANES:
        inv = [inverse(d) for d in diagonal]
        t = [q * r for q, r in zip(inv, rhs)]
        w = [q * e for q, e in zip(inv, link)]
        low_d = from_left([e * v for e, v in zip(link, w)], stride, lane)
        low_r = from_left([e * v for e, v in zip(link, t)], stride, lane)
        high_q = from_right(inv, stride, lane)
        high_t = from_right(t, stride, lane)
        high_w = from_right(w, stride, lane)
        diagonal = [
            diagonal[c] - low_d[c] - link[c] * (link[c] * high_q[c]) for c in range(count)
        ]
        rhs = [rhs[c] + low_r[c] + link[c] * high_t[c] for c in range(count)]
        link = [link[c] * high_w[c] for c in range(count)]
        stride *= 2
    return solve_chunks(diagonal, link, rhs)


def pack_pair(a, b, odd_lane):
    even = [jnp.where(odd_lane, pltpu.roll(x, 1, 1), y) for x, y in zip(a, b)]
    odd = [jnp.where(odd_lane, x, pltpu.roll(y, LANES - 1, 1)) for x, y in zip(a, b)]
    return even, odd


def unpack_pair(even, odd, odd_lane):
    a = [jnp.where(odd_lane, y, pltpu.roll(x, LANES - 1, 1)) for x, y in zip(even, odd)]
    b = [jnp.where(odd_lane, pltpu.roll(y, 1, 1), x) for x, y in zip(even, odd)]
    return a, b


def solve_x_pair(g_pair, rhs_pair, lane):
    odd_lane = (lane & 1) == 1
    first_cell = lane < 2
    last_cell = lane >= LANES - 2
    half = 0.5 * weight
    g_even, g_odd = pack_pair(*g_pair, odd_lane)
    r_even, r_odd = pack_pair(*rhs_pair, odd_lane)
    face = [half * (a + b) for a, b in zip(g_even, g_odd)]
    after = from_right(g_even, 2, lane)
    after[-1] = jnp.where(last_cell, g_odd[-1], after[-1])
    face_after = [half * (a + b) for a, b in zip(g_odd, after)]
    face_before = from_left(face_after, 2, lane)
    face_before[0] = jnp.where(first_cell, weight * g_even[0], face_before[0])
    inv = [inverse(1.0 + (a + b)) for a, b in zip(face_before, face)]
    d_odd = [1.0 + (a + b) for a, b in zip(face, face_after)]
    link = list(face_after)
    link[-1] = jnp.where(last_cell, 0.0, link[-1])
    link_before = list(face_before)
    link_before[0] = jnp.where(first_cell, 0.0, link_before[0])
    t = [q * r for q, r in zip(inv, r_even)]
    w = [q * e for q, e in zip(inv, face)]
    next_q = from_right(inv, 2, lane)
    next_t = from_right(t, 2, lane)
    next_w = from_right(w, 2, lane)
    diagonal = [
        d - e * v - l * (l * q) for d, e, v, l, q in zip(d_odd, face, w, link, next_q)
    ]
    rhs = [r + e * v + l * n for r, e, v, l, n in zip(r_odd, face, t, link, next_t)]
    x_odd = reduce_lanes(diagonal, [l * n for l, n in zip(link, next_w)], rhs, lane, 2)
    x_before = from_left(x_odd, 2, lane)
    x_even = [
        v + q * (l * b) + u * x for v, q, l, b, u, x in zip(t, inv, link_before, x_before, w, x_odd)
    ]
    return unpack_pair(x_even, x_odd, odd_lane)


def load_kernel(
    step_ref, index_ref, amp_ref, phase_ref, field_ref, conduct_ref,
    packed_ref, field_out, conduct_out, both_ref, outer_ref,
    index_in, amp_in, phase_in, sems,
):
    width = outer_ref.shape[0]
    last = field_ref.shape[0] - width
    odd = lax.rem(lax.axis_index("wide"), 2)
    inner_rows = pl.ds(pl.multiple_of((1 - odd) * last, 8), width)
    outer_rows = pl.ds(pl.multiple_of(odd * last, 8), width)
    pairs = (
        (index_ref, index_in),
        (amp_ref, amp_in),
        (phase_ref, phase_in),
        (field_ref.at[inner_rows], both_ref.at[pl.ds(0, width)]),
        (field_ref.at[outer_rows], both_ref.at[pl.ds(width, width)]),
        (field_ref.at[outer_rows], outer_ref),
        (field_ref, field_out),
        (conduct_ref, conduct_out),
    )
    copies = [pltpu.make_async_copy(a, b, sems.at[n]) for n, (a, b) in enumerate(pairs)]
    for copy in copies:
        copy.start()
    for copy in copies[:3]:
        copy.wait()
    count = index_in.shape[0]
    row = lax.broadcasted_iota(jnp.int32, packed_ref.shape, 0)
    lane = lax.broadcasted_iota(jnp.int32, packed_ref.shape, 1)
    total = jnp.zeros(packed_ref.shape, f32)
    for m in range(count):
        moment = lax.rem(index_in[m, 2] * step_ref[0], jnp.int32(64)).astype(f32)
        offset = phase_in[m] * (0.5 / math.pi) + moment * (1.0 / 64.0)
        for place, value in enumerate(
            (index_in[m, 0].astype(f32), index_in[m, 1].astype(f32), offset, amp_in[m])
        ):
            total = jnp.where((row == m) & (lane == place), value, total)
    packed_ref[...] = total
    for copy in copies[3:]:
        copy.wait()


def block_factors(face):
    inv, scaled, chain, u = [], [], [], []
    rows = len(face) - 1
    rest = 1.0 + face[0]
    for j in range(rows):
        inv.append(inverse(rest + face[j + 1]))
        scaled.append(face[j] * inv[j])
        chain.append(face[j + 1] * inv[j])
        u.append(scaled[j] * u[-1] if j else scaled[j])
        rest = 1.0 + rest * chain[j]
    v = list(chain)
    for j in range(rows - 2, -1, -1):
        u[j] = u[j] + chain[j] * u[j + 1]
        v[j] = chain[j] * v[j + 1]
    return inv, scaled, chain, u, v


def block_ends(face):
    rows = len(face) - 1
    down = 1.0 + face[0]
    up = 1.0 + face[rows]
    v_first = None
    for j in range(rows):
        v_last = face[j + 1] * inverse(down + face[j + 1])
        v_first = v_last if v_first is None else v_first * v_last
        u_first = face[rows - 1 - j] * inverse(up + face[rows - 1 - j])
        if j < rows - 1:
            down = 1.0 + down * v_last
            up = 1.0 + up * u_first
    u_last = v_first * (face[0] * inverse(face[rows]))
    return u_first, v_first, u_last, v_last


def height_kernel(sizes, modes_ref, modes_came_ref, heights_ref):
    rows, layers, chunks, row_total, layer_total, column_total = sizes
    odd = lax.rem(lax.axis_index("wide"), 2) == 1
    modes = jnp.where(odd, modes_ref[...], modes_came_ref[...])
    body = height_lines(modes, 0, row_total, row_total, chunks, column_total)
    heights_ref[chunks : (row_total + 1) * chunks] = body
    heights_ref[0:chunks] = body[0:chunks]
    heights_ref[(row_total + 1) * chunks : (row_total + 2) * chunks] = body[
        (row_total - 1) * chunks : row_total * chunks
    ]

def main_kernel(
    sizes, heights, both_ref, below_ref, above_ref, field_ref, conduct_ref,
    sent_ref, p_ref, u_ref, v_ref, left_gain_ref, right_gain_ref, joint_ref,
    ends, links, halo, solved,
):
    rows, layers, chunks, row_total, layer_total, column_total = sizes
    width = layers * chunks
    blocks = row_total // rows
    me = lax.axis_index("wide")
    first_layer = lax.axis_index("grp") * layers
    zeta = [
        ((first_layer + k).astype(f32) + 0.5) * (1.0 / layer_total) for k in range(layers)
    ]
    half = 0.5 * weight
    own_start = pl.multiple_of(me * (rows * chunks), 8)

    def faces(start):
        h = [heights[pl.ds(start + j * chunks, chunks), :] for j in range(rows + 2)]
        out = []
        for j in range(rows + 1):
            both = h[j] + h[j + 1]
            out.append(jnp.concatenate([weight + (half * z) * both for z in zeta], 0))
        return out

    def keep_ends(b, values):
        base = pl.multiple_of(b * (4 * width), 8)
        for n, value in enumerate(values):
            ends[pl.ds(base + n * width, width), :] = value

    inv, scaled, chain, u, v = block_factors(faces(own_start))
    for j in range(rows):
        u_ref[j * width : (j + 1) * width] = u[j]
        v_ref[j * width : (j + 1) * width] = v[j]
    keep_ends(me, (u[0], v[0], u[-1], v[-1]))

    def other_block(n):
        b = lax.rem(me + 1 + n, blocks)
        keep_ends(b, block_ends(faces(pl.multiple_of(b * (rows * chunks), 8))))

    if blocks <= 8:
        for n in range(blocks - 1):
            other_block(n)
    else:
        lax.fori_loop(0, blocks - 1, lambda n, carry: (other_block(n), carry)[1], 0)

    def end(b, n):
        return ends[(4 * b + n) * width : (4 * b + n + 1) * width]

    left = jnp.zeros((width, LANES), f32)
    right = jnp.zeros((width, LANES), f32)
    for b in range(blocks):
        u_first, v_first, u_last, v_last = (end(b, n) for n in range(4))
        gain = u_last * inverse(1.0 - u_first * left)
        left_gain_ref[b * width : (b + 1) * width] = gain
        links[b * width : (b + 1) * width] = left
        left = v_last + gain * left * v_first
        b = blocks - 1 - b
        u_first, v_first, u_last, v_last = (end(b, n) for n in range(4))
        gain = v_first * inverse(1.0 - v_last * right)
        right_gain_ref[b * width : (b + 1) * width] = gain
        links[(blocks + b) * width : (blocks + b + 1) * width] = right
        right = u_first + gain * right * u_last

    own = pl.ds(pl.multiple_of(me * width, 8), width)
    left_link = links[own, :]
    right_link = links[pl.ds(pl.multiple_of((blocks + me) * width, 8), width), :]
    a = 1.0 - left_link * u[0]
    b = left_link * v[0]
    c = right_link * u[-1]
    d = 1.0 - right_link * v[-1]
    by = inverse(a * d - b * c)
    joint = (
        left_gain_ref[own, :] * left_link, right_gain_ref[own, :] * right_link,
        left_link, right_link, d * by, b * by, c * by, a * by,
    )
    for n, value in enumerate(joint):
        joint_ref[n * width : (n + 1) * width] = value

    odd = lax.rem(me, 2) == 1
    inner = both_ref[0:width]
    below = jnp.where(odd, inner, below_ref[...])
    above = jnp.where(odd, above_ref[...], inner)
    halo[0:width] = jnp.where(me == 0, 0.0, below)
    halo[width : 2 * width] = jnp.where(me == blocks - 1, 0.0, above)
    lane = lax.broadcasted_iota(jnp.int32, (rows, LANES), 1)
    row = lax.broadcasted_iota(jnp.int32, (rows, LANES), 0)

    def neighbours(values, low, high):
        return (
            jnp.where(row == 0, low, pltpu.roll(values, 1, 0)),
            jnp.where(row == rows - 1, high, pltpu.roll(values, rows - 1, 0)),
        )

    g = [[] for _ in range(layers)]
    f = [[] for _ in range(layers)]
    rhs = [[] for _ in range(layers)]
    for c in range(chunks):
        h = heights[pl.ds(own_start + chunks + c, rows, stride=chunks), :]
        h_low, h_high = neighbours(
            h,
            heights[pl.ds(own_start + c, 1), :],
            heights[pl.ds(own_start + (rows + 1) * chunks + c, 1), :],
        )
        low_sum, high_sum = h + h_low, h + h_high
        for k in range(layers):
            place = c * layers + k
            f_mid = field_ref[pl.ds(place, rows, stride=width), :]
            f_low, f_high = neighbours(
                f_mid, halo[pl.ds(place, 1), :], halo[pl.ds(width + place, 1), :]
            )
            g[k].append(conduct_ref[pl.ds(place, rows, stride=width), :] * (1.0 + zeta[k] * h))
            f[k].append(f_mid)
            along = (weight + (half * zeta[k]) * high_sum) * (f_high - f_mid) - (
                weight + (half * zeta[k]) * low_sum
            ) * (f_mid - f_low)
            rhs[k].append(2.0 * (f_mid + along))
    for k in range(0, layers, 2):
        both = solve_x_pair(g[k : k + 2], rhs[k : k + 2], lane)
        for n in range(2):
            for c in range(chunks):
                spot = pl.ds((k + n) * chunks + c, rows, stride=width)
                solved[spot, :] = both[n][c] - 2.0 * f[k + n][c]

    def part(ref, j):
        return ref[j * width : (j + 1) * width]

    p = [part(solved, 0) * inv[0]]
    for j in range(1, rows):
        p.append(part(solved, j) * inv[j] + scaled[j] * p[-1])
    for j in range(rows - 2, -1, -1):
        p[j] = p[j] + chain[j] * p[j + 1]
    for j in range(rows):
        p_ref[j * width : (j + 1) * width] = p[j]

    upward = p[-1] + part(joint_ref, 0) * p[0]
    downward = p[0] + part(joint_ref, 1) * p[-1]
    for b in range(blocks):
        sent_ref[b * width : (b + 1) * width] = jnp.where(b > me, upward, downward)


def last_kernel(
    sizes, came_ref, left_gain_ref, right_gain_ref, joint_ref, p_ref, u_ref, v_ref, field_ref,
    out_ref,
):
    rows, layers, chunks, row_total, layer_total, column_total = sizes
    width = layers * chunks
    blocks = row_total // rows
    me = lax.axis_index("wide")

    def part(ref, b):
        return ref[b * width : (b + 1) * width]

    left = jnp.zeros((width, LANES), f32)
    right = jnp.zeros((width, LANES), f32)
    for b in range(blocks - 1):
        left = jnp.where(b < me, part(came_ref, b) + part(left_gain_ref, b) * left, left)
        b = blocks - 1 - b
        right = jnp.where(b > me, part(came_ref, b) + part(right_gain_ref, b) * right, right)

    y = left + part(joint_ref, 2) * part(p_ref, 0)
    z = right + part(joint_ref, 3) * part(p_ref, rows - 1)
    before = part(joint_ref, 4) * y + part(joint_ref, 5) * z
    after = part(joint_ref, 6) * y + part(joint_ref, 7) * z
    for j in range(rows):
        x = part(p_ref, j) + part(u_ref, j) * before + part(v_ref, j) * after
        for k in range(layers):
            spot = pl.ds(j * width + k, chunks, stride=layers)
            out_ref[spot, :] = field_ref[spot, :] + x[k * chunks : (k + 1) * chunks]


def on_device(field, conduct, mode_index, mode_amp, mode_phase, step_index):
    rows, layers, columns = field.shape
    wide_count = lax.axis_size("wide")
    row_total = rows * wide_count
    grp_count = lax.axis_size("grp")
    layer_total = layers * grp_count
    chunks = columns // LANES
    width = layers * chunks
    sizes = (rows, layers, chunks, row_total, layer_total, columns)
    limit = pltpu.CompilerParams(vmem_limit_bytes=16 * 1024 * 1024)
    hbm = pl.BlockSpec(memory_space=pltpu.HBM)

    def lines(count):
        return jax.ShapeDtypeStruct((count * width, LANES), f32)

    packed, field_lines, conduct_lines, both, outer = pl.pallas_call(
        load_kernel,
        out_shape=(
            jax.ShapeDtypeStruct((mode_index.shape[0], 8), f32),
            lines(rows),
            lines(rows),
            lines(2),
            lines(1),
        ),
        in_specs=[pl.BlockSpec(memory_space=pltpu.SMEM)] + [hbm] * 5,
        scratch_shapes=[
            pltpu.SMEM(mode_index.shape, jnp.int32),
            pltpu.SMEM(mode_amp.shape, f32),
            pltpu.SMEM(mode_phase.shape, f32),
            pltpu.SemaphoreType.DMA((8,)),
        ],
        compiler_params=limit,
    )(
        step_index,
        *(
            pltpu.with_memory_space_constraint(a, pltpu.HBM)
            for a in (mode_index, mode_amp, mode_phase, to_lines(field), to_lines(conduct))
        ),
    )

    place = lax.axis_index("wide")
    odd = place % 2 == 1
    swaps = [(i, i ^ 1) for i in range(wide_count)]
    cores = [list(range(n, wide_count, 2)) for n in range(2)]
    both_came = lax.ppermute(both, "wide", swaps)

    def gather_modes(own):
        return lax.all_gather(own, "grp", axis=0, tiled=True)

    def no_modes(own):
        return jnp.zeros((grp_count * own.shape[0], own.shape[1]), f32)

    modes = lax.cond(odd, gather_modes, no_modes, packed)
    modes, outer, both_came = lax.optimization_barrier((modes, outer, both_came))

    def gather_rows(own, came):
        rows_sent = jnp.concatenate([own, came[width:]], 0)
        rows_all = lax.all_gather(rows_sent, "wide", axis_index_groups=cores, axis=0)
        chip = place // 2
        below = lax.dynamic_index_in_dim(rows_all, jnp.maximum(chip - 1, 0), 0, False)
        above = lax.dynamic_index_in_dim(
            rows_all, jnp.minimum(chip + 1, wide_count // 2 - 1), 0, False
        )
        return below[width:], above[:width]

    def no_rows(own, came):
        return jnp.zeros_like(own), jnp.zeros_like(own)

    below, above = lax.cond(odd, no_rows, gather_rows, outer, both_came)
    above_came = lax.ppermute(above, "wide", swaps)
    modes_came = lax.ppermute(modes, "wide", swaps)

    heights = pl.pallas_call(
        functools.partial(height_kernel, sizes),
        out_shape=jax.ShapeDtypeStruct(((row_total + 2) * chunks, LANES), f32),
        compiler_params=limit,
    )(modes, modes_came)

    sent, p, u, v, left_gain, right_gain, joint = pl.pallas_call(
        functools.partial(main_kernel, sizes),
        out_shape=(lines(wide_count),)
        + (lines(rows),) * 3
        + (lines(wide_count),) * 2
        + (lines(8),),
        scratch_shapes=[
            pltpu.VMEM((4 * wide_count * width, LANES), f32),
            pltpu.VMEM((2 * wide_count * width, LANES), f32),
            pltpu.VMEM((2 * width, LANES), f32),
            pltpu.VMEM((rows * width, LANES), f32),
        ],
        compiler_params=limit,
    )(heights, both_came, below, above_came, field_lines, conduct_lines)

    came = lax.all_to_all(
        sent.reshape(wide_count, width, LANES), "wide", split_axis=0, concat_axis=0
    ).reshape(wide_count * width, LANES)

    advanced = pl.pallas_call(
        functools.partial(last_kernel, sizes),
        out_shape=lines(rows),
        compiler_params=limit,
    )(came, left_gain, right_gain, joint, p, u, v, field_lines)
    return from_lines(advanced, field.shape)


def solution(mesh):
    return jax.shard_map(
        on_device,
        mesh=mesh,
        in_specs=(
            P("wide", "grp", None),
            P("wide", "grp", None),
            P("grp", None),
            P("grp"),
            P("grp"),
            P(),
        ),
        out_specs=P("wide", "grp", None),
        check_vma=False,
    )
```

```python
import functools
import math

import jax
import jax.numpy as jnp
from jax import lax
from jax.experimental import pallas as pl
from jax.experimental.pallas import tpu as pltpu
from jax.sharding import PartitionSpec as P

time_step = 600.0
implicit_weight = 0.5
weight = implicit_weight * time_step
LANES = 128
f32 = jnp.float32


def to_lines(block):
    rows, layers, columns = block.shape
    chunks = columns // LANES
    return (
        block.reshape(rows, layers, chunks, LANES)
        .transpose(0, 2, 1, 3)
        .reshape(rows * chunks * layers, LANES)
    )


def from_lines(lines, shape):
    rows, layers, columns = shape
    chunks = columns // LANES
    return (
        lines.reshape(rows, chunks, layers, LANES)
        .transpose(0, 2, 1, 3)
        .reshape(rows, layers, columns)
    )


def turns(wave, index, period):
    product = wave * index
    if period & (period - 1) == 0:
        product = product & (period - 1)
    else:
        product = lax.rem(product, jnp.int32(period))
    return product.astype(f32) * (1.0 / period)


def cos_sin(turn):
    part = turn - jnp.floor(turn + 0.5)
    square = part * part

    def series(first):
        terms = [
            (-1.0) ** n * math.pi ** (2 * n + first) / math.factorial(2 * n + first)
            for n in range(7)
        ]
        total = jnp.full_like(square, terms[-1])
        for term in terms[-2::-1]:
            total = total * square + term
        return total

    half_cos = series(0)
    half_sin = series(1) * part
    return 1.0 - 2.0 * half_sin * half_sin, 2.0 * half_sin * half_cos


def halves(values):
    high = values.astype(jnp.bfloat16)
    return high, (values - high.astype(f32)).astype(jnp.bfloat16)


def height_lines(modes, first_row, count, row_total, chunks, column_total):
    mode_count = modes.shape[0]
    wave_x = modes[:, 0:1].astype(jnp.int32)
    wave_y = modes[:, 1:2].astype(jnp.int32)
    offset = modes[:, 2:3]
    amp = modes[:, 3:4]
    spot = lax.broadcasted_iota(jnp.int32, (mode_count, count * chunks), 1)
    chunk = spot % chunks
    row = jnp.clip(first_row + spot // chunks, 0, row_total - 1)
    angle = (
        turns(wave_y, row, row_total) + turns(wave_x, chunk * LANES, column_total)
    ) + offset
    left_cos, left_sin = cos_sin(angle)
    lane = lax.broadcasted_iota(jnp.int32, (mode_count, LANES), 1)
    right_cos, right_sin = cos_sin(turns(wave_x, lane, column_total))
    left = jnp.concatenate([amp * left_cos, amp * left_sin], 0)
    right = jnp.concatenate([right_cos, -right_sin], 0)
    left_high, left_low = halves(left)
    right_high, right_low = halves(right)
    return lax.dot_general(
        jnp.concatenate([left_high, left_high, left_low], 0),
        jnp.concatenate([right_high, right_low, right_high], 0),
        (((0,), (0,)), ((), ())),
        preferred_element_type=f32,
    )


def inverse(values):
    return pl.reciprocal(values, approx=False)


def from_left(values, stride, lane):
    moved = [pltpu.roll(v, stride, 1) for v in values]
    return [jnp.where(lane < stride, moved[c - 1], moved[c]) for c in range(len(values))]


def from_right(values, stride, lane):
    count = len(values)
    moved = [pltpu.roll(v, LANES - stride, 1) for v in values]
    return [
        jnp.where(lane >= LANES - stride, moved[(c + 1) % count], moved[c]) for c in range(count)
    ]


def solve_chunks(diagonal, link, rhs):
    count = len(rhs)
    if count == 1:
        return [rhs[0] * inverse(diagonal[0])]
    inv = {i: inverse(diagonal[i]) for i in range(0, count, 2)}
    scaled = {i: inv[i] * rhs[i] for i in inv}
    odd_diagonal, odd_link, odd_rhs = [], [], []
    for i in range(1, count, 2):
        d = diagonal[i] - link[i - 1] * (link[i - 1] * inv[i - 1])
        r = rhs[i] + link[i - 1] * scaled[i - 1]
        e = None
        if i + 1 < count:
            by = link[i] * inv[i + 1]
            d = d - link[i] * by
            r = r + link[i] * scaled[i + 1]
            e = by * link[i + 1] if i + 2 < count else None
        odd_diagonal.append(d)
        odd_rhs.append(r)
        odd_link.append(e)
    odd = solve_chunks(odd_diagonal, odd_link, odd_rhs)
    out = [None] * count
    out[1::2] = odd
    for i in range(0, count, 2):
        r = rhs[i]
        if i > 0:
            r = r + link[i - 1] * out[i - 1]
        if i + 1 < count:
            r = r + link[i] * out[i + 1]
        out[i] = r * inv[i]
    return out


def reduce_lanes(diagonal, link, rhs, lane, stride):
    count = len(rhs)
    while stride < LANES:
        inv = [inverse(d) for d in diagonal]
        t = [q * r for q, r in zip(inv, rhs)]
        w = [q * e for q, e in zip(inv, link)]
        low_d = from_left([e * v for e, v in zip(link, w)], stride, lane)
        low_r = from_left([e * v for e, v in zip(link, t)], stride, lane)
        high_q = from_right(inv, stride, lane)
        high_t = from_right(t, stride, lane)
        high_w = from_right(w, stride, lane)
        diagonal = [
            diagonal[c] - low_d[c] - link[c] * (link[c] * high_q[c]) for c in range(count)
        ]
        rhs = [rhs[c] + low_r[c] + link[c] * high_t[c] for c in range(count)]
        link = [link[c] * high_w[c] for c in range(count)]
        stride *= 2
    return solve_chunks(diagonal, link, rhs)


def pack_pair(a, b, odd_lane):
    even = [jnp.where(odd_lane, pltpu.roll(x, 1, 1), y) for x, y in zip(a, b)]
    odd = [jnp.where(odd_lane, x, pltpu.roll(y, LANES - 1, 1)) for x, y in zip(a, b)]
    return even, odd


def unpack_pair(even, odd, odd_lane):
    a = [jnp.where(odd_lane, y, pltpu.roll(x, LANES - 1, 1)) for x, y in zip(even, odd)]
    b = [jnp.where(odd_lane, pltpu.roll(y, 1, 1), x) for x, y in zip(even, odd)]
    return a, b


def solve_x_pair(g_pair, rhs_pair, lane):
    odd_lane = (lane & 1) == 1
    first_cell = lane < 2
    last_cell = lane >= LANES - 2
    half = 0.5 * weight
    g_even, g_odd = pack_pair(*g_pair, odd_lane)
    r_even, r_odd = pack_pair(*rhs_pair, odd_lane)
    face = [half * (a + b) for a, b in zip(g_even, g_odd)]
    after = from_right(g_even, 2, lane)
    after[-1] = jnp.where(last_cell, g_odd[-1], after[-1])
    face_after = [half * (a + b) for a, b in zip(g_odd, after)]
    face_before = from_left(face_after, 2, lane)
    face_before[0] = jnp.where(first_cell, weight * g_even[0], face_before[0])
    inv = [inverse(1.0 + (a + b)) for a, b in zip(face_before, face)]
    d_odd = [1.0 + (a + b) for a, b in zip(face, face_after)]
    link = list(face_after)
    link[-1] = jnp.where(last_cell, 0.0, link[-1])
    link_before = list(face_before)
    link_before[0] = jnp.where(first_cell, 0.0, link_before[0])
    t = [q * r for q, r in zip(inv, r_even)]
    w = [q * e for q, e in zip(inv, face)]
    next_q = from_right(inv, 2, lane)
    next_t = from_right(t, 2, lane)
    next_w = from_right(w, 2, lane)
    diagonal = [
        d - e * v - l * (l * q) for d, e, v, l, q in zip(d_odd, face, w, link, next_q)
    ]
    rhs = [r + e * v + l * n for r, e, v, l, n in zip(r_odd, face, t, link, next_t)]
    x_odd = reduce_lanes(diagonal, [l * n for l, n in zip(link, next_w)], rhs, lane, 2)
    x_before = from_left(x_odd, 2, lane)
    x_even = [
        v + q * (l * b) + u * x for v, q, l, b, u, x in zip(t, inv, link_before, x_before, w, x_odd)
    ]
    return unpack_pair(x_even, x_odd, odd_lane)


def pack_kernel(
    step_ref, index_ref, amp_ref, phase_ref, field_ref,
    packed_ref, both_ref, outer_ref,
    index_in, amp_in, phase_in, sems,
):
    width = outer_ref.shape[0]
    last = field_ref.shape[0] - width
    odd = lax.rem(lax.axis_index("wide"), 2)
    inner_rows = pl.ds(pl.multiple_of((1 - odd) * last, 8), width)
    outer_rows = pl.ds(pl.multiple_of(odd * last, 8), width)
    pairs = (
        (index_ref, index_in),
        (amp_ref, amp_in),
        (phase_ref, phase_in),
        (field_ref.at[inner_rows], both_ref.at[pl.ds(0, width)]),
        (field_ref.at[outer_rows], both_ref.at[pl.ds(width, width)]),
        (field_ref.at[outer_rows], outer_ref),
    )
    copies = [pltpu.make_async_copy(a, b, sems.at[n]) for n, (a, b) in enumerate(pairs)]
    for copy in copies:
        copy.start()
    for copy in copies[:3]:
        copy.wait()
    count = index_in.shape[0]
    row = lax.broadcasted_iota(jnp.int32, packed_ref.shape, 0)
    lane = lax.broadcasted_iota(jnp.int32, packed_ref.shape, 1)
    total = jnp.zeros(packed_ref.shape, f32)
    for m in range(count):
        moment = lax.rem(index_in[m, 2] * step_ref[0], jnp.int32(64)).astype(f32)
        offset = phase_in[m] * (0.5 / math.pi) + moment * (1.0 / 64.0)
        for place, value in enumerate(
            (index_in[m, 0].astype(f32), index_in[m, 1].astype(f32), offset, amp_in[m])
        ):
            total = jnp.where((row == m) & (lane == place), value, total)
    packed_ref[...] = total
    for copy in copies[3:]:
        copy.wait()


def load_kernel(sizes, field_ref, conduct_ref, field_out, turned_ref, conduct_in, sems):
    rows, layers, chunks, row_total, layer_total, column_total = sizes
    width = layers * chunks
    copies = (
        pltpu.make_async_copy(field_ref, field_out, sems.at[0]),
        pltpu.make_async_copy(conduct_ref, conduct_in, sems.at[1]),
    )
    for copy in copies:
        copy.start()
    for n, (copy, ref) in enumerate(zip(copies, (field_out, conduct_in))):
        copy.wait()
        for place in range(width):
            spot = (n * width + place) * rows
            turned_ref[spot : spot + rows] = ref[pl.ds(place, rows, stride=width), :]


def block_factors(face):
    inv, scaled, chain, u = [], [], [], []
    rows = len(face) - 1
    rest = 1.0 + face[0]
    for j in range(rows):
        inv.append(inverse(rest + face[j + 1]))
        scaled.append(face[j] * inv[j])
        chain.append(face[j + 1] * inv[j])
        u.append(scaled[j] * u[-1] if j else scaled[j])
        rest = 1.0 + rest * chain[j]
    v = list(chain)
    for j in range(rows - 2, -1, -1):
        u[j] = u[j] + chain[j] * u[j + 1]
        v[j] = chain[j] * v[j + 1]
    return inv, scaled, chain, u, v


def block_ends(face):
    rows = len(face) - 1
    down = 1.0 + face[0]
    up = 1.0 + face[rows]
    v_first = None
    for j in range(rows):
        v_last = face[j + 1] * inverse(down + face[j + 1])
        v_first = v_last if v_first is None else v_first * v_last
        u_first = face[rows - 1 - j] * inverse(up + face[rows - 1 - j])
        if j < rows - 1:
            down = 1.0 + down * v_last
            up = 1.0 + up * u_first
    u_last = v_first * (face[0] * inverse(face[rows]))
    return u_first, v_first, u_last, v_last


def height_kernel(sizes, handed_ref, came_ref, heights_ref):
    rows, layers, chunks, row_total, layer_total, column_total = sizes
    odd = lax.rem(lax.axis_index("wide"), 2) == 1
    modes = jnp.where(odd, handed_ref[layers * chunks :], came_ref[layers * chunks :])
    body = height_lines(modes, 0, row_total, row_total, chunks, column_total)
    heights_ref[chunks : (row_total + 1) * chunks] = body
    heights_ref[0:chunks] = body[0:chunks]
    heights_ref[(row_total + 1) * chunks : (row_total + 2) * chunks] = body[
        (row_total - 1) * chunks : row_total * chunks
    ]

def main_kernel(
    sizes, heights, both_ref, below_ref, came_ref, turned_ref,
    sent_ref, p_ref, u_ref, v_ref, left_gain_ref, right_gain_ref, joint_ref,
    ends, links, halo, solved,
):
    rows, layers, chunks, row_total, layer_total, column_total = sizes
    width = layers * chunks
    blocks = row_total // rows
    me = lax.axis_index("wide")
    first_layer = lax.axis_index("grp") * layers
    zeta = [
        ((first_layer + k).astype(f32) + 0.5) * (1.0 / layer_total) for k in range(layers)
    ]
    half = 0.5 * weight
    own_start = pl.multiple_of(me * (rows * chunks), 8)

    def faces(start):
        h = [heights[pl.ds(start + j * chunks, chunks), :] for j in range(rows + 2)]
        out = []
        for j in range(rows + 1):
            both = h[j] + h[j + 1]
            out.append(jnp.concatenate([weight + (half * z) * both for z in zeta], 0))
        return out

    def keep_ends(b, values):
        base = pl.multiple_of(b * (4 * width), 8)
        for n, value in enumerate(values):
            ends[pl.ds(base + n * width, width), :] = value

    inv, scaled, chain, u, v = block_factors(faces(own_start))
    for j in range(rows):
        u_ref[j * width : (j + 1) * width] = u[j]
        v_ref[j * width : (j + 1) * width] = v[j]
    keep_ends(me, (u[0], v[0], u[-1], v[-1]))

    def other_block(n):
        b = lax.rem(me + 1 + n, blocks)
        keep_ends(b, block_ends(faces(pl.multiple_of(b * (rows * chunks), 8))))

    if blocks <= 8:
        for n in range(blocks - 1):
            other_block(n)
    else:
        lax.fori_loop(0, blocks - 1, lambda n, carry: (other_block(n), carry)[1], 0)

    def end(b, n):
        return ends[(4 * b + n) * width : (4 * b + n + 1) * width]

    left = jnp.zeros((width, LANES), f32)
    right = jnp.zeros((width, LANES), f32)
    for b in range(blocks):
        u_first, v_first, u_last, v_last = (end(b, n) for n in range(4))
        gain = u_last * inverse(1.0 - u_first * left)
        left_gain_ref[b * width : (b + 1) * width] = gain
        links[b * width : (b + 1) * width] = left
        left = v_last + gain * left * v_first
        b = blocks - 1 - b
        u_first, v_first, u_last, v_last = (end(b, n) for n in range(4))
        gain = v_first * inverse(1.0 - v_last * right)
        right_gain_ref[b * width : (b + 1) * width] = gain
        links[(blocks + b) * width : (blocks + b + 1) * width] = right
        right = u_first + gain * right * u_last

    own = pl.ds(pl.multiple_of(me * width, 8), width)
    left_link = links[own, :]
    right_link = links[pl.ds(pl.multiple_of((blocks + me) * width, 8), width), :]
    a = 1.0 - left_link * u[0]
    b = left_link * v[0]
    c = right_link * u[-1]
    d = 1.0 - right_link * v[-1]
    by = inverse(a * d - b * c)
    joint = (
        left_gain_ref[own, :] * left_link, right_gain_ref[own, :] * right_link,
        left_link, right_link, d * by, b * by, c * by, a * by,
    )
    for n, value in enumerate(joint):
        joint_ref[n * width : (n + 1) * width] = value

    odd = lax.rem(me, 2) == 1
    inner = both_ref[0:width]
    below = jnp.where(odd, inner, below_ref[...])
    above = jnp.where(odd, came_ref[0:width], inner)
    halo[0:width] = jnp.where(me == 0, 0.0, below)
    halo[width : 2 * width] = jnp.where(me == blocks - 1, 0.0, above)
    lane = lax.broadcasted_iota(jnp.int32, (rows, LANES), 1)
    row = lax.broadcasted_iota(jnp.int32, (rows, LANES), 0)

    def neighbours(values, low, high):
        return (
            jnp.where(row == 0, low, pltpu.roll(values, 1, 0)),
            jnp.where(row == rows - 1, high, pltpu.roll(values, rows - 1, 0)),
        )

    g = [[] for _ in range(layers)]
    f = [[] for _ in range(layers)]
    rhs = [[] for _ in range(layers)]
    for c in range(chunks):
        h = heights[pl.ds(own_start + chunks + c, rows, stride=chunks), :]
        h_low, h_high = neighbours(
            h,
            heights[pl.ds(own_start + c, 1), :],
            heights[pl.ds(own_start + (rows + 1) * chunks + c, 1), :],
        )
        low_sum, high_sum = h + h_low, h + h_high
        for k in range(layers):
            place = c * layers + k
            f_mid = turned_ref[place * rows : (place + 1) * rows]
            f_low, f_high = neighbours(
                f_mid, halo[pl.ds(place, 1), :], halo[pl.ds(width + place, 1), :]
            )
            g[k].append(
                turned_ref[(width + place) * rows : (width + place + 1) * rows] * (1.0 + zeta[k] * h)
            )
            f[k].append(f_mid)
            along = (weight + (half * zeta[k]) * high_sum) * (f_high - f_mid) - (
                weight + (half * zeta[k]) * low_sum
            ) * (f_mid - f_low)
            rhs[k].append(2.0 * (f_mid + along))
    for k in range(0, layers, 2):
        both = solve_x_pair(g[k : k + 2], rhs[k : k + 2], lane)
        for n in range(2):
            for c in range(chunks):
                spot = pl.ds((k + n) * chunks + c, rows, stride=width)
                solved[spot, :] = both[n][c] - 2.0 * f[k + n][c]

    def part(ref, j):
        return ref[j * width : (j + 1) * width]

    p = [part(solved, 0) * inv[0]]
    for j in range(1, rows):
        p.append(part(solved, j) * inv[j] + scaled[j] * p[-1])
    for j in range(rows - 2, -1, -1):
        p[j] = p[j] + chain[j] * p[j + 1]
    for j in range(rows):
        p_ref[j * width : (j + 1) * width] = p[j]

    upward = p[-1] + part(joint_ref, 0) * p[0]
    downward = p[0] + part(joint_ref, 1) * p[-1]
    for b in range(blocks):
        sent_ref[b * width : (b + 1) * width] = jnp.where(b > me, upward, downward)


def last_kernel(
    sizes, came_ref, left_gain_ref, right_gain_ref, joint_ref, p_ref, u_ref, v_ref, field_ref,
    out_ref,
):
    rows, layers, chunks, row_total, layer_total, column_total = sizes
    width = layers * chunks
    blocks = row_total // rows
    me = lax.axis_index("wide")

    def part(ref, b):
        return ref[b * width : (b + 1) * width]

    left = jnp.zeros((width, LANES), f32)
    right = jnp.zeros((width, LANES), f32)
    for b in range(blocks - 1):
        left = jnp.where(b < me, part(came_ref, b) + part(left_gain_ref, b) * left, left)
        b = blocks - 1 - b
        right = jnp.where(b > me, part(came_ref, b) + part(right_gain_ref, b) * right, right)

    y = left + part(joint_ref, 2) * part(p_ref, 0)
    z = right + part(joint_ref, 3) * part(p_ref, rows - 1)
    before = part(joint_ref, 4) * y + part(joint_ref, 5) * z
    after = part(joint_ref, 6) * y + part(joint_ref, 7) * z
    for j in range(rows):
        x = part(p_ref, j) + part(u_ref, j) * before + part(v_ref, j) * after
        for k in range(layers):
            spot = pl.ds(j * width + k, chunks, stride=layers)
            out_ref[spot, :] = field_ref[spot, :] + x[k * chunks : (k + 1) * chunks]


def on_device(field, conduct, mode_index, mode_amp, mode_phase, step_index):
    rows, layers, columns = field.shape
    wide_count = lax.axis_size("wide")
    row_total = rows * wide_count
    grp_count = lax.axis_size("grp")
    layer_total = layers * grp_count
    chunks = columns // LANES
    width = layers * chunks
    sizes = (rows, layers, chunks, row_total, layer_total, columns)
    limit = pltpu.CompilerParams(vmem_limit_bytes=16 * 1024 * 1024)
    hbm = pl.BlockSpec(memory_space=pltpu.HBM)

    def lines(count):
        return jax.ShapeDtypeStruct((count * width, LANES), f32)

    step_index, mode_index, mode_amp, mode_phase, field_lines, conduct_lines = (
        step_index,
        *(
            pltpu.with_memory_space_constraint(a, pltpu.HBM)
            for a in (mode_index, mode_amp, mode_phase, to_lines(field), to_lines(conduct))
        ),
    )
    packed, both, outer = pl.pallas_call(
        pack_kernel,
        out_shape=(
            jax.ShapeDtypeStruct((mode_index.shape[0], LANES), f32),
            lines(2),
            lines(1),
        ),
        in_specs=[pl.BlockSpec(memory_space=pltpu.SMEM)] + [hbm] * 4,
        scratch_shapes=[
            pltpu.SMEM(mode_index.shape, jnp.int32),
            pltpu.SMEM(mode_amp.shape, f32),
            pltpu.SMEM(mode_phase.shape, f32),
            pltpu.SemaphoreType.DMA((6,)),
        ],
        compiler_params=limit,
    )(step_index, mode_index, mode_amp, mode_phase, field_lines)

    place = lax.axis_index("wide")
    odd = place % 2 == 1
    swaps = [(i, i ^ 1) for i in range(wide_count)]
    cores = [list(range(n, wide_count, 2)) for n in range(2)]
    both_came = lax.ppermute(both, "wide", swaps)

    def gather_modes(own):
        return lax.all_gather(own, "grp", axis=0, tiled=True)

    def no_modes(own):
        return jnp.zeros((grp_count * own.shape[0], own.shape[1]), f32)

    modes = lax.cond(odd, gather_modes, no_modes, packed)
    modes, outer, both_came = lax.optimization_barrier((modes, outer, both_came))

    def gather_rows(own, came):
        rows_sent = jnp.concatenate([own, came[width:]], 0)
        rows_all = lax.all_gather(rows_sent, "wide", axis_index_groups=cores, axis=0)
        chip = place // 2
        below = lax.dynamic_index_in_dim(rows_all, jnp.maximum(chip - 1, 0), 0, False)
        above = lax.dynamic_index_in_dim(
            rows_all, jnp.minimum(chip + 1, wide_count // 2 - 1), 0, False
        )
        return below[width:], above[:width]

    def no_rows(own, came):
        return jnp.zeros_like(own), jnp.zeros_like(own)

    below, above = lax.cond(odd, no_rows, gather_rows, outer, both_came)
    handed = jnp.concatenate([above, modes], 0)
    came = lax.ppermute(handed, "wide", swaps)
    handed, field, conduct = lax.optimization_barrier((handed, field, conduct))
    field_lines, turned = pl.pallas_call(
        functools.partial(load_kernel, sizes),
        out_shape=(lines(rows), lines(2 * rows)),
        in_specs=[hbm] * 2,
        scratch_shapes=[
            pltpu.VMEM((rows * width, LANES), f32),
            pltpu.SemaphoreType.DMA((2,)),
        ],
        compiler_params=limit,
    )(
        *(
            pltpu.with_memory_space_constraint(to_lines(a), pltpu.HBM)
            for a in (field, conduct)
        )
    )
    heights = pl.pallas_call(
        functools.partial(height_kernel, sizes),
        out_shape=jax.ShapeDtypeStruct(((row_total + 2) * chunks, LANES), f32),
        compiler_params=limit,
    )(handed, came)

    sent, p, u, v, left_gain, right_gain, joint = pl.pallas_call(
        functools.partial(main_kernel, sizes),
        out_shape=(lines(wide_count),)
        + (lines(rows),) * 3
        + (lines(wide_count),) * 2
        + (lines(8),),
        scratch_shapes=[
            pltpu.VMEM((4 * wide_count * width, LANES), f32),
            pltpu.VMEM((2 * wide_count * width, LANES), f32),
            pltpu.VMEM((2 * width, LANES), f32),
            pltpu.VMEM((rows * width, LANES), f32),
        ],
        compiler_params=limit,
    )(heights, both_came, below, came, turned)

    came = lax.all_to_all(
        sent.reshape(wide_count, width, LANES), "wide", split_axis=0, concat_axis=0
    ).reshape(wide_count * width, LANES)

    advanced = pl.pallas_call(
        functools.partial(last_kernel, sizes),
        out_shape=lines(rows),
        compiler_params=limit,
    )(came, left_gain, right_gain, joint, p, u, v, field_lines)
    return from_lines(advanced, field.shape)


def solution(mesh):
    return jax.shard_map(
        on_device,
        mesh=mesh,
        in_specs=(
            P("wide", "grp", None),
            P("wide", "grp", None),
            P("grp", None),
            P("grp"),
            P("grp"),
            P(),
        ),
        out_specs=P("wide", "grp", None),
        check_vma=False,
    )
```

```python
import functools
import math

import jax
import jax.numpy as jnp
from jax import lax
from jax.experimental import pallas as pl
from jax.experimental.pallas import tpu as pltpu
from jax.sharding import PartitionSpec as P

time_step = 600.0
implicit_weight = 0.5
weight = implicit_weight * time_step
LANES = 128
f32 = jnp.float32


def to_lines(block):
    rows, layers, columns = block.shape
    chunks = columns // LANES
    return (
        block.reshape(rows, layers, chunks, LANES)
        .transpose(0, 2, 1, 3)
        .reshape(rows * chunks * layers, LANES)
    )


def from_lines(lines, shape):
    rows, layers, columns = shape
    chunks = columns // LANES
    return (
        lines.reshape(rows, chunks, layers, LANES)
        .transpose(0, 2, 1, 3)
        .reshape(rows, layers, columns)
    )


def turns(wave, index, period):
    product = wave * index
    if period & (period - 1) == 0:
        product = product & (period - 1)
    else:
        product = lax.rem(product, jnp.int32(period))
    return product.astype(f32) * (1.0 / period)


def cos_sin(turn):
    part = turn - jnp.floor(turn + 0.5)
    square = part * part

    def series(first):
        terms = [
            (-1.0) ** n * math.pi ** (2 * n + first) / math.factorial(2 * n + first)
            for n in range(7)
        ]
        total = jnp.full_like(square, terms[-1])
        for term in terms[-2::-1]:
            total = total * square + term
        return total

    half_cos = series(0)
    half_sin = series(1) * part
    return 1.0 - 2.0 * half_sin * half_sin, 2.0 * half_sin * half_cos


def halves(values):
    high = values.astype(jnp.bfloat16)
    return high, (values - high.astype(f32)).astype(jnp.bfloat16)


def height_lines(modes, first_row, count, row_total, chunks, column_total):
    mode_count = modes.shape[0]
    wave_x = modes[:, 0:1].astype(jnp.int32)
    wave_y = modes[:, 1:2].astype(jnp.int32)
    offset = modes[:, 2:3]
    amp = modes[:, 3:4]
    spot = lax.broadcasted_iota(jnp.int32, (mode_count, count * chunks), 1)
    chunk = spot % chunks
    row = jnp.clip(first_row + spot // chunks, 0, row_total - 1)
    angle = (
        turns(wave_y, row, row_total) + turns(wave_x, chunk * LANES, column_total)
    ) + offset
    left_cos, left_sin = cos_sin(angle)
    lane = lax.broadcasted_iota(jnp.int32, (mode_count, LANES), 1)
    right_cos, right_sin = cos_sin(turns(wave_x, lane, column_total))
    left = jnp.concatenate([amp * left_cos, amp * left_sin], 0)
    right = jnp.concatenate([right_cos, -right_sin], 0)
    left_high, left_low = halves(left)
    right_high, right_low = halves(right)
    return lax.dot_general(
        jnp.concatenate([left_high, left_high, left_low], 0),
        jnp.concatenate([right_high, right_low, right_high], 0),
        (((0,), (0,)), ((), ())),
        preferred_element_type=f32,
    )


def inverse(values):
    return pl.reciprocal(values, approx=False)


def from_left(values, stride, lane):
    moved = [pltpu.roll(v, stride, 1) for v in values]
    return [jnp.where(lane < stride, moved[c - 1], moved[c]) for c in range(len(values))]


def from_right(values, stride, lane):
    count = len(values)
    moved = [pltpu.roll(v, LANES - stride, 1) for v in values]
    return [
        jnp.where(lane >= LANES - stride, moved[(c + 1) % count], moved[c]) for c in range(count)
    ]


def solve_chunks(diagonal, link, rhs):
    count = len(rhs)
    if count == 1:
        return [rhs[0] * inverse(diagonal[0])]
    inv = {i: inverse(diagonal[i]) for i in range(0, count, 2)}
    scaled = {i: inv[i] * rhs[i] for i in inv}
    odd_diagonal, odd_link, odd_rhs = [], [], []
    for i in range(1, count, 2):
        d = diagonal[i] - link[i - 1] * (link[i - 1] * inv[i - 1])
        r = rhs[i] + link[i - 1] * scaled[i - 1]
        e = None
        if i + 1 < count:
            by = link[i] * inv[i + 1]
            d = d - link[i] * by
            r = r + link[i] * scaled[i + 1]
            e = by * link[i + 1] if i + 2 < count else None
        odd_diagonal.append(d)
        odd_rhs.append(r)
        odd_link.append(e)
    odd = solve_chunks(odd_diagonal, odd_link, odd_rhs)
    out = [None] * count
    out[1::2] = odd
    for i in range(0, count, 2):
        r = rhs[i]
        if i > 0:
            r = r + link[i - 1] * out[i - 1]
        if i + 1 < count:
            r = r + link[i] * out[i + 1]
        out[i] = r * inv[i]
    return out


def reduce_lanes(diagonal, link, rhs, lane, stride):
    count = len(rhs)
    while stride < LANES:
        inv = [inverse(d) for d in diagonal]
        t = [q * r for q, r in zip(inv, rhs)]
        w = [q * e for q, e in zip(inv, link)]
        low_d = from_left([e * v for e, v in zip(link, w)], stride, lane)
        low_r = from_left([e * v for e, v in zip(link, t)], stride, lane)
        high_q = from_right(inv, stride, lane)
        high_t = from_right(t, stride, lane)
        high_w = from_right(w, stride, lane)
        diagonal = [
            diagonal[c] - low_d[c] - link[c] * (link[c] * high_q[c]) for c in range(count)
        ]
        rhs = [rhs[c] + low_r[c] + link[c] * high_t[c] for c in range(count)]
        link = [link[c] * high_w[c] for c in range(count)]
        stride *= 2
    return solve_chunks(diagonal, link, rhs)


def pack_pair(a, b, odd_lane):
    even = [jnp.where(odd_lane, pltpu.roll(x, 1, 1), y) for x, y in zip(a, b)]
    odd = [jnp.where(odd_lane, x, pltpu.roll(y, LANES - 1, 1)) for x, y in zip(a, b)]
    return even, odd


def unpack_pair(even, odd, odd_lane):
    a = [jnp.where(odd_lane, y, pltpu.roll(x, LANES - 1, 1)) for x, y in zip(even, odd)]
    b = [jnp.where(odd_lane, pltpu.roll(y, 1, 1), x) for x, y in zip(even, odd)]
    return a, b


def solve_x_pair(g_pair, rhs_pair, lane):
    odd_lane = (lane & 1) == 1
    first_cell = lane < 2
    last_cell = lane >= LANES - 2
    half = 0.5 * weight
    g_even, g_odd = pack_pair(*g_pair, odd_lane)
    r_even, r_odd = pack_pair(*rhs_pair, odd_lane)
    face = [half * (a + b) for a, b in zip(g_even, g_odd)]
    after = from_right(g_even, 2, lane)
    after[-1] = jnp.where(last_cell, g_odd[-1], after[-1])
    face_after = [half * (a + b) for a, b in zip(g_odd, after)]
    face_before = from_left(face_after, 2, lane)
    face_before[0] = jnp.where(first_cell, weight * g_even[0], face_before[0])
    inv = [inverse(1.0 + (a + b)) for a, b in zip(face_before, face)]
    d_odd = [1.0 + (a + b) for a, b in zip(face, face_after)]
    link = list(face_after)
    link[-1] = jnp.where(last_cell, 0.0, link[-1])
    link_before = list(face_before)
    link_before[0] = jnp.where(first_cell, 0.0, link_before[0])
    t = [q * r for q, r in zip(inv, r_even)]
    w = [q * e for q, e in zip(inv, face)]
    next_q = from_right(inv, 2, lane)
    next_t = from_right(t, 2, lane)
    next_w = from_right(w, 2, lane)
    diagonal = [
        d - e * v - l * (l * q) for d, e, v, l, q in zip(d_odd, face, w, link, next_q)
    ]
    rhs = [r + e * v + l * n for r, e, v, l, n in zip(r_odd, face, t, link, next_t)]
    x_odd = reduce_lanes(diagonal, [l * n for l, n in zip(link, next_w)], rhs, lane, 2)
    x_before = from_left(x_odd, 2, lane)
    x_even = [
        v + q * (l * b) + u * x for v, q, l, b, u, x in zip(t, inv, link_before, x_before, w, x_odd)
    ]
    return unpack_pair(x_even, x_odd, odd_lane)


def pack_kernel(
    step_ref, index_ref, amp_ref, phase_ref, field_ref,
    packed_ref, both_ref, outer_ref,
    index_in, amp_in, phase_in, sems,
):
    width = outer_ref.shape[0]
    last = field_ref.shape[0] - width
    odd = lax.rem(lax.axis_index("wide"), 2)
    inner_rows = pl.ds(pl.multiple_of((1 - odd) * last, 8), width)
    outer_rows = pl.ds(pl.multiple_of(odd * last, 8), width)
    pairs = (
        (index_ref, index_in),
        (amp_ref, amp_in),
        (phase_ref, phase_in),
        (field_ref.at[inner_rows], both_ref.at[pl.ds(0, width)]),
        (field_ref.at[outer_rows], both_ref.at[pl.ds(width, width)]),
        (field_ref.at[outer_rows], outer_ref),
    )
    copies = [pltpu.make_async_copy(a, b, sems.at[n]) for n, (a, b) in enumerate(pairs)]
    for copy in copies:
        copy.start()
    for copy in copies[:3]:
        copy.wait()
    count = index_in.shape[0]
    row = lax.broadcasted_iota(jnp.int32, packed_ref.shape, 0)
    lane = lax.broadcasted_iota(jnp.int32, packed_ref.shape, 1)
    total = jnp.zeros(packed_ref.shape, f32)
    for m in range(count):
        moment = lax.rem(index_in[m, 2] * step_ref[0], jnp.int32(64)).astype(f32)
        offset = phase_in[m] * (0.5 / math.pi) + moment * (1.0 / 64.0)
        for place, value in enumerate(
            (index_in[m, 0].astype(f32), index_in[m, 1].astype(f32), offset, amp_in[m])
        ):
            total = jnp.where((row == m) & (lane == place), value, total)
    packed_ref[...] = total
    for copy in copies[3:]:
        copy.wait()


def load_kernel(sizes, field_ref, conduct_ref, field_out, turned_ref, conduct_in, sems):
    rows, layers, chunks, row_total, layer_total, column_total = sizes
    width = layers * chunks
    copies = (
        pltpu.make_async_copy(field_ref, field_out, sems.at[0]),
        pltpu.make_async_copy(conduct_ref, conduct_in, sems.at[1]),
    )
    for copy in copies:
        copy.start()
    for n, (copy, ref) in enumerate(zip(copies, (field_out, conduct_in))):
        copy.wait()
        for place in range(width):
            spot = (n * width + place) * rows
            turned_ref[spot : spot + rows] = ref[pl.ds(place, rows, stride=width), :]


def block_factors(face):
    inv, scaled, chain, u = [], [], [], []
    rows = len(face) - 1
    rest = 1.0 + face[0]
    for j in range(rows):
        inv.append(inverse(rest + face[j + 1]))
        scaled.append(face[j] * inv[j])
        chain.append(face[j + 1] * inv[j])
        u.append(scaled[j] * u[-1] if j else scaled[j])
        rest = 1.0 + rest * chain[j]
    v = list(chain)
    for j in range(rows - 2, -1, -1):
        u[j] = u[j] + chain[j] * u[j + 1]
        v[j] = chain[j] * v[j + 1]
    return inv, scaled, chain, u, v


def block_ends(face):
    rows = len(face) - 1
    rest = 1.0 + face[0]
    chain = None
    for j in range(rows):
        inv = inverse(rest + face[j + 1])
        v_last = face[j + 1] * inv
        corner = corner + chain * (chain * inv) if j else inv
        chain = chain * v_last if j else v_last
        if j < rows - 1:
            rest = 1.0 + rest * v_last
    return face[0] * corner, chain, chain * (face[0] * inverse(face[rows])), v_last


def height_kernel(sizes, handed_ref, came_ref, heights_ref):
    rows, layers, chunks, row_total, layer_total, column_total = sizes
    odd = lax.rem(lax.axis_index("wide"), 2) == 1
    modes = jnp.where(odd, handed_ref[layers * chunks :], came_ref[layers * chunks :])
    body = height_lines(modes, 0, row_total, row_total, chunks, column_total)
    heights_ref[chunks : (row_total + 1) * chunks] = body
    heights_ref[0:chunks] = body[0:chunks]
    heights_ref[(row_total + 1) * chunks : (row_total + 2) * chunks] = body[
        (row_total - 1) * chunks : row_total * chunks
    ]

def main_kernel(
    sizes, heights, both_ref, below_ref, came_ref, turned_ref,
    sent_ref, p_ref, u_ref, v_ref, left_gain_ref, right_gain_ref, joint_ref,
    ends, links, halo, solved,
):
    rows, layers, chunks, row_total, layer_total, column_total = sizes
    width = layers * chunks
    blocks = row_total // rows
    me = lax.axis_index("wide")
    first_layer = lax.axis_index("grp") * layers
    zeta = [
        ((first_layer + k).astype(f32) + 0.5) * (1.0 / layer_total) for k in range(layers)
    ]
    half = 0.5 * weight
    own_start = pl.multiple_of(me * (rows * chunks), 8)

    odd = lax.rem(me, 2) == 1
    inner = both_ref[0:width]
    below = jnp.where(odd, inner, below_ref[...])
    above = jnp.where(odd, came_ref[0:width], inner)
    halo[0:width] = jnp.where(me == 0, 0.0, below)
    halo[width : 2 * width] = jnp.where(me == blocks - 1, 0.0, above)
    lane = lax.broadcasted_iota(jnp.int32, (rows, LANES), 1)
    row = lax.broadcasted_iota(jnp.int32, (rows, LANES), 0)

    def neighbours(values, low, high):
        return (
            jnp.where(row == 0, low, pltpu.roll(values, 1, 0)),
            jnp.where(row == rows - 1, high, pltpu.roll(values, rows - 1, 0)),
        )

    g = [[] for _ in range(layers)]
    f = [[] for _ in range(layers)]
    rhs = [[] for _ in range(layers)]
    for c in range(chunks):
        h = heights[pl.ds(own_start + chunks + c, rows, stride=chunks), :]
        h_low, h_high = neighbours(
            h,
            heights[pl.ds(own_start + c, 1), :],
            heights[pl.ds(own_start + (rows + 1) * chunks + c, 1), :],
        )
        low_sum, high_sum = h + h_low, h + h_high
        for k in range(layers):
            place = c * layers + k
            f_mid = turned_ref[place * rows : (place + 1) * rows]
            f_low, f_high = neighbours(
                f_mid, halo[pl.ds(place, 1), :], halo[pl.ds(width + place, 1), :]
            )
            g[k].append(
                turned_ref[(width + place) * rows : (width + place + 1) * rows] * (1.0 + zeta[k] * h)
            )
            f[k].append(f_mid)
            along = (weight + (half * zeta[k]) * high_sum) * (f_high - f_mid) - (
                weight + (half * zeta[k]) * low_sum
            ) * (f_mid - f_low)
            rhs[k].append(2.0 * (f_mid + along))
    for k in range(0, layers, 2):
        both = solve_x_pair(g[k : k + 2], rhs[k : k + 2], lane)
        for n in range(2):
            for c in range(chunks):
                spot = pl.ds((k + n) * chunks + c, rows, stride=width)
                solved[spot, :] = both[n][c] - 2.0 * f[k + n][c]

    def faces(start):
        h = [heights[pl.ds(start + j * chunks, chunks), :] for j in range(rows + 2)]
        out = []
        for j in range(rows + 1):
            both = h[j] + h[j + 1]
            out.append(jnp.concatenate([weight + (half * z) * both for z in zeta], 0))
        return out

    def keep_ends(b, values):
        base = pl.multiple_of(b * (4 * width), 8)
        for n, value in enumerate(values):
            ends[pl.ds(base + n * width, width), :] = value

    inv, scaled, chain, u, v = block_factors(faces(own_start))
    for j in range(rows):
        u_ref[j * width : (j + 1) * width] = u[j]
        v_ref[j * width : (j + 1) * width] = v[j]
    keep_ends(me, (u[0], v[0], u[-1], v[-1]))

    def other_block(n):
        b = lax.rem(me + 1 + n, blocks)
        keep_ends(b, block_ends(faces(pl.multiple_of(b * (rows * chunks), 8))))

    if blocks <= 8:
        for n in range(blocks - 1):
            other_block(n)
    else:
        lax.fori_loop(0, blocks - 1, lambda n, carry: (other_block(n), carry)[1], 0)

    def end(b, n):
        return ends[(4 * b + n) * width : (4 * b + n + 1) * width]

    left = jnp.zeros((width, LANES), f32)
    right = jnp.zeros((width, LANES), f32)
    for b in range(blocks):
        u_first, v_first, u_last, v_last = (end(b, n) for n in range(4))
        gain = u_last * inverse(1.0 - u_first * left)
        left_gain_ref[b * width : (b + 1) * width] = gain
        links[b * width : (b + 1) * width] = left
        left = v_last + gain * left * v_first
        b = blocks - 1 - b
        u_first, v_first, u_last, v_last = (end(b, n) for n in range(4))
        gain = v_first * inverse(1.0 - v_last * right)
        right_gain_ref[b * width : (b + 1) * width] = gain
        links[(blocks + b) * width : (blocks + b + 1) * width] = right
        right = u_first + gain * right * u_last

    own = pl.ds(pl.multiple_of(me * width, 8), width)
    left_link = links[own, :]
    right_link = links[pl.ds(pl.multiple_of((blocks + me) * width, 8), width), :]
    a = 1.0 - left_link * u[0]
    b = left_link * v[0]
    c = right_link * u[-1]
    d = 1.0 - right_link * v[-1]
    by = inverse(a * d - b * c)
    joint = (
        left_gain_ref[own, :] * left_link, right_gain_ref[own, :] * right_link,
        left_link, right_link, d * by, b * by, c * by, a * by,
    )
    for n, value in enumerate(joint):
        joint_ref[n * width : (n + 1) * width] = value

    def part(ref, j):
        return ref[j * width : (j + 1) * width]

    p = [part(solved, 0) * inv[0]]
    for j in range(1, rows):
        p.append(part(solved, j) * inv[j] + scaled[j] * p[-1])
    for j in range(rows - 2, -1, -1):
        p[j] = p[j] + chain[j] * p[j + 1]
    for j in range(rows):
        p_ref[j * width : (j + 1) * width] = p[j]

    upward = p[-1] + part(joint_ref, 0) * p[0]
    downward = p[0] + part(joint_ref, 1) * p[-1]
    for b in range(blocks):
        sent_ref[b * width : (b + 1) * width] = jnp.where(b > me, upward, downward)


def last_kernel(
    sizes, came_ref, left_gain_ref, right_gain_ref, joint_ref, p_ref, u_ref, v_ref, field_ref,
    out_ref,
):
    rows, layers, chunks, row_total, layer_total, column_total = sizes
    width = layers * chunks
    blocks = row_total // rows
    me = lax.axis_index("wide")

    def part(ref, b):
        return ref[b * width : (b + 1) * width]

    left = jnp.zeros((width, LANES), f32)
    right = jnp.zeros((width, LANES), f32)
    for b in range(blocks - 1):
        left = jnp.where(b < me, part(came_ref, b) + part(left_gain_ref, b) * left, left)
        b = blocks - 1 - b
        right = jnp.where(b > me, part(came_ref, b) + part(right_gain_ref, b) * right, right)

    y = left + part(joint_ref, 2) * part(p_ref, 0)
    z = right + part(joint_ref, 3) * part(p_ref, rows - 1)
    before = part(joint_ref, 4) * y + part(joint_ref, 5) * z
    after = part(joint_ref, 6) * y + part(joint_ref, 7) * z
    for j in range(rows):
        x = part(p_ref, j) + part(u_ref, j) * before + part(v_ref, j) * after
        for k in range(layers):
            spot = pl.ds(j * width + k, chunks, stride=layers)
            out_ref[spot, :] = field_ref[spot, :] + x[k * chunks : (k + 1) * chunks]


def on_device(field, conduct, mode_index, mode_amp, mode_phase, step_index):
    rows, layers, columns = field.shape
    wide_count = lax.axis_size("wide")
    row_total = rows * wide_count
    grp_count = lax.axis_size("grp")
    layer_total = layers * grp_count
    chunks = columns // LANES
    width = layers * chunks
    sizes = (rows, layers, chunks, row_total, layer_total, columns)
    limit = pltpu.CompilerParams(vmem_limit_bytes=16 * 1024 * 1024)
    hbm = pl.BlockSpec(memory_space=pltpu.HBM)

    def lines(count):
        return jax.ShapeDtypeStruct((count * width, LANES), f32)

    step_index, mode_index, mode_amp, mode_phase, field_lines, conduct_lines = (
        step_index,
        *(
            pltpu.with_memory_space_constraint(a, pltpu.HBM)
            for a in (mode_index, mode_amp, mode_phase, to_lines(field), to_lines(conduct))
        ),
    )
    packed, both, outer = pl.pallas_call(
        pack_kernel,
        out_shape=(
            jax.ShapeDtypeStruct((mode_index.shape[0], LANES), f32),
            lines(2),
            lines(1),
        ),
        in_specs=[pl.BlockSpec(memory_space=pltpu.SMEM)] + [hbm] * 4,
        scratch_shapes=[
            pltpu.SMEM(mode_index.shape, jnp.int32),
            pltpu.SMEM(mode_amp.shape, f32),
            pltpu.SMEM(mode_phase.shape, f32),
            pltpu.SemaphoreType.DMA((6,)),
        ],
        compiler_params=limit,
    )(step_index, mode_index, mode_amp, mode_phase, field_lines)

    place = lax.axis_index("wide")
    odd = place % 2 == 1
    swaps = [(i, i ^ 1) for i in range(wide_count)]
    cores = [list(range(n, wide_count, 2)) for n in range(2)]
    both_came = lax.ppermute(both, "wide", swaps)

    def gather_modes(own):
        return lax.all_gather(own, "grp", axis=0, tiled=True)

    def no_modes(own):
        return jnp.zeros((grp_count * own.shape[0], own.shape[1]), f32)

    modes = lax.cond(odd, gather_modes, no_modes, packed)
    modes, outer, both_came = lax.optimization_barrier((modes, outer, both_came))

    def gather_rows(own, came):
        rows_sent = jnp.concatenate([own, came[width:]], 0)
        rows_all = lax.all_gather(rows_sent, "wide", axis_index_groups=cores, axis=0)
        chip = place // 2
        below = lax.dynamic_index_in_dim(rows_all, jnp.maximum(chip - 1, 0), 0, False)
        above = lax.dynamic_index_in_dim(
            rows_all, jnp.minimum(chip + 1, wide_count // 2 - 1), 0, False
        )
        return below[width:], above[:width]

    def no_rows(own, came):
        return jnp.zeros_like(own), jnp.zeros_like(own)

    below, above = lax.cond(odd, no_rows, gather_rows, outer, both_came)
    handed = jnp.concatenate([above, modes], 0)
    came = lax.ppermute(handed, "wide", swaps)
    handed, field, conduct = lax.optimization_barrier((handed, field, conduct))
    field_lines, turned = pl.pallas_call(
        functools.partial(load_kernel, sizes),
        out_shape=(lines(rows), lines(2 * rows)),
        in_specs=[hbm] * 2,
        scratch_shapes=[
            pltpu.VMEM((rows * width, LANES), f32),
            pltpu.SemaphoreType.DMA((2,)),
        ],
        compiler_params=limit,
    )(
        *(
            pltpu.with_memory_space_constraint(to_lines(a), pltpu.HBM)
            for a in (field, conduct)
        )
    )
    heights = pl.pallas_call(
        functools.partial(height_kernel, sizes),
        out_shape=jax.ShapeDtypeStruct(((row_total + 2) * chunks, LANES), f32),
        compiler_params=limit,
    )(handed, came)

    sent, p, u, v, left_gain, right_gain, joint = pl.pallas_call(
        functools.partial(main_kernel, sizes),
        out_shape=(lines(wide_count),)
        + (lines(rows),) * 3
        + (lines(wide_count),) * 2
        + (lines(8),),
        scratch_shapes=[
            pltpu.VMEM((4 * wide_count * width, LANES), f32),
            pltpu.VMEM((2 * wide_count * width, LANES), f32),
            pltpu.VMEM((2 * width, LANES), f32),
            pltpu.VMEM((rows * width, LANES), f32),
        ],
        compiler_params=limit,
    )(heights, both_came, below, came, turned)

    came = lax.all_to_all(
        sent.reshape(wide_count, width, LANES), "wide", split_axis=0, concat_axis=0
    ).reshape(wide_count * width, LANES)

    advanced = pl.pallas_call(
        functools.partial(last_kernel, sizes),
        out_shape=lines(rows),
        compiler_params=limit,
    )(came, left_gain, right_gain, joint, p, u, v, field_lines)
    return from_lines(advanced, field.shape)


def solution(mesh):
    return jax.shard_map(
        on_device,
        mesh=mesh,
        in_specs=(
            P("wide", "grp", None),
            P("wide", "grp", None),
            P("grp", None),
            P("grp"),
            P("grp"),
            P(),
        ),
        out_specs=P("wide", "grp", None),
        check_vma=False,
    )
```

```python
import functools
import math

import jax
import jax.numpy as jnp
from jax import lax
from jax.experimental import pallas as pl
from jax.experimental.pallas import tpu as pltpu
from jax.sharding import PartitionSpec as P

time_step = 600.0
implicit_weight = 0.5
weight = implicit_weight * time_step
LANES = 128
f32 = jnp.float32


def to_lines(block):
    rows, layers, columns = block.shape
    chunks = columns // LANES
    return (
        block.reshape(rows, layers, chunks, LANES)
        .transpose(0, 2, 1, 3)
        .reshape(rows * chunks * layers, LANES)
    )


def from_lines(lines, shape):
    rows, layers, columns = shape
    chunks = columns // LANES
    return (
        lines.reshape(rows, chunks, layers, LANES)
        .transpose(0, 2, 1, 3)
        .reshape(rows, layers, columns)
    )


def turns(wave, index, period):
    product = wave * index
    if period & (period - 1) == 0:
        product = product & (period - 1)
    else:
        product = lax.rem(product, jnp.int32(period))
    return product.astype(f32) * (1.0 / period)


def cos_sin(turn):
    part = turn - jnp.floor(turn + 0.5)
    square = part * part

    def series(first):
        terms = [
            (-1.0) ** n * math.pi ** (2 * n + first) / math.factorial(2 * n + first)
            for n in range(7)
        ]
        total = jnp.full_like(square, terms[-1])
        for term in terms[-2::-1]:
            total = total * square + term
        return total

    half_cos = series(0)
    half_sin = series(1) * part
    return 1.0 - 2.0 * half_sin * half_sin, 2.0 * half_sin * half_cos


def halves(values):
    high = values.astype(jnp.bfloat16)
    return high, (values - high.astype(f32)).astype(jnp.bfloat16)


def height_lines(modes, first_row, count, row_total, chunks, column_total):
    mode_count = modes.shape[0]
    wave_x = modes[:, 0:1].astype(jnp.int32)
    wave_y = modes[:, 1:2].astype(jnp.int32)
    offset = modes[:, 2:3]
    amp = modes[:, 3:4]
    spot = lax.broadcasted_iota(jnp.int32, (mode_count, count * chunks), 1)
    chunk = spot % chunks
    row = jnp.clip(first_row + spot // chunks, 0, row_total - 1)
    angle = (
        turns(wave_y, row, row_total) + turns(wave_x, chunk * LANES, column_total)
    ) + offset
    left_cos, left_sin = cos_sin(angle)
    lane = lax.broadcasted_iota(jnp.int32, (mode_count, LANES), 1)
    right_cos, right_sin = cos_sin(turns(wave_x, lane, column_total))
    left = jnp.concatenate([amp * left_cos, amp * left_sin], 0)
    right = jnp.concatenate([right_cos, -right_sin], 0)
    left_high, left_low = halves(left)
    right_high, right_low = halves(right)
    return lax.dot_general(
        jnp.concatenate([left_high, left_high, left_low], 0),
        jnp.concatenate([right_high, right_low, right_high], 0),
        (((0,), (0,)), ((), ())),
        preferred_element_type=f32,
    )


def inverse(values):
    return pl.reciprocal(values, approx=False)


def from_left(values, stride, lane):
    moved = [pltpu.roll(v, stride, 1) for v in values]
    return [jnp.where(lane < stride, moved[c - 1], moved[c]) for c in range(len(values))]


def from_right(values, stride, lane):
    count = len(values)
    moved = [pltpu.roll(v, LANES - stride, 1) for v in values]
    return [
        jnp.where(lane >= LANES - stride, moved[(c + 1) % count], moved[c]) for c in range(count)
    ]


def solve_chunks(diagonal, link, rhs, tick):
    count = len(rhs)
    if count == 1:
        return [rhs[0] * inverse(diagonal[0])]
    inv = {i: inverse(diagonal[i]) for i in range(0, count, 2)}
    scaled = {i: inv[i] * rhs[i] for i in inv}
    odd_diagonal, odd_link, odd_rhs = [], [], []
    for i in range(1, count, 2):
        d = diagonal[i] - link[i - 1] * (link[i - 1] * inv[i - 1])
        r = rhs[i] + link[i - 1] * scaled[i - 1]
        e = None
        if i + 1 < count:
            by = link[i] * inv[i + 1]
            d = d - link[i] * by
            r = r + link[i] * scaled[i + 1]
            e = by * link[i + 1] if i + 2 < count else None
        odd_diagonal.append(d)
        odd_rhs.append(r)
        odd_link.append(e)
    tick()
    odd = solve_chunks(odd_diagonal, odd_link, odd_rhs, tick)
    tick()
    out = [None] * count
    out[1::2] = odd
    for i in range(0, count, 2):
        r = rhs[i]
        if i > 0:
            r = r + link[i - 1] * out[i - 1]
        if i + 1 < count:
            r = r + link[i] * out[i + 1]
        out[i] = r * inv[i]
    return out


def reduce_lanes(diagonal, link, rhs, lane, stride, tick):
    count = len(rhs)
    while stride < LANES:
        inv = [inverse(d) for d in diagonal]
        t = [q * r for q, r in zip(inv, rhs)]
        w = [q * e for q, e in zip(inv, link)]
        tick()
        low_d = from_left([e * v for e, v in zip(link, w)], stride, lane)
        low_r = from_left([e * v for e, v in zip(link, t)], stride, lane)
        high_q = from_right(inv, stride, lane)
        high_t = from_right(t, stride, lane)
        high_w = from_right(w, stride, lane)
        tick()
        diagonal = [
            diagonal[c] - low_d[c] - link[c] * (link[c] * high_q[c]) for c in range(count)
        ]
        rhs = [rhs[c] + low_r[c] + link[c] * high_t[c] for c in range(count)]
        link = [link[c] * high_w[c] for c in range(count)]
        stride *= 2
        tick()
    return solve_chunks(diagonal, link, rhs, tick)


def pack_pair(a, b, odd_lane):
    even = [jnp.where(odd_lane, pltpu.roll(x, 1, 1), y) for x, y in zip(a, b)]
    odd = [jnp.where(odd_lane, x, pltpu.roll(y, LANES - 1, 1)) for x, y in zip(a, b)]
    return even, odd


def unpack_pair(even, odd, odd_lane):
    a = [jnp.where(odd_lane, y, pltpu.roll(x, LANES - 1, 1)) for x, y in zip(even, odd)]
    b = [jnp.where(odd_lane, pltpu.roll(y, 1, 1), x) for x, y in zip(even, odd)]
    return a, b


def solve_x_pair(g_pair, rhs_pair, lane, tick):
    odd_lane = (lane & 1) == 1
    first_cell = lane < 2
    last_cell = lane >= LANES - 2
    half = 0.5 * weight
    g_even, g_odd = pack_pair(*g_pair, odd_lane)
    r_even, r_odd = pack_pair(*rhs_pair, odd_lane)
    face = [half * (a + b) for a, b in zip(g_even, g_odd)]
    after = from_right(g_even, 2, lane)
    after[-1] = jnp.where(last_cell, g_odd[-1], after[-1])
    face_after = [half * (a + b) for a, b in zip(g_odd, after)]
    face_before = from_left(face_after, 2, lane)
    face_before[0] = jnp.where(first_cell, weight * g_even[0], face_before[0])
    inv = [inverse(1.0 + (a + b)) for a, b in zip(face_before, face)]
    d_odd = [1.0 + (a + b) for a, b in zip(face, face_after)]
    link = list(face_after)
    link[-1] = jnp.where(last_cell, 0.0, link[-1])
    link_before = list(face_before)
    link_before[0] = jnp.where(first_cell, 0.0, link_before[0])
    tick()
    t = [q * r for q, r in zip(inv, r_even)]
    w = [q * e for q, e in zip(inv, face)]
    next_q = from_right(inv, 2, lane)
    next_t = from_right(t, 2, lane)
    next_w = from_right(w, 2, lane)
    tick()
    diagonal = [
        d - e * v - l * (l * q) for d, e, v, l, q in zip(d_odd, face, w, link, next_q)
    ]
    rhs = [r + e * v + l * n for r, e, v, l, n in zip(r_odd, face, t, link, next_t)]
    x_odd = reduce_lanes(diagonal, [l * n for l, n in zip(link, next_w)], rhs, lane, 2, tick)
    x_before = from_left(x_odd, 2, lane)
    x_even = [
        v + q * (l * b) + u * x for v, q, l, b, u, x in zip(t, inv, link_before, x_before, w, x_odd)
    ]
    return unpack_pair(x_even, x_odd, odd_lane)


def pack_kernel(
    step_ref, index_ref, amp_ref, phase_ref, field_ref,
    packed_ref, both_ref, outer_ref,
    index_in, amp_in, phase_in, sems,
):
    width = outer_ref.shape[0]
    last = field_ref.shape[0] - width
    odd = lax.rem(lax.axis_index("wide"), 2)
    inner_rows = pl.ds(pl.multiple_of((1 - odd) * last, 8), width)
    outer_rows = pl.ds(pl.multiple_of(odd * last, 8), width)
    pairs = (
        (index_ref, index_in),
        (amp_ref, amp_in),
        (phase_ref, phase_in),
        (field_ref.at[inner_rows], both_ref.at[pl.ds(0, width)]),
        (field_ref.at[outer_rows], both_ref.at[pl.ds(width, width)]),
        (field_ref.at[outer_rows], outer_ref),
    )
    copies = [pltpu.make_async_copy(a, b, sems.at[n]) for n, (a, b) in enumerate(pairs)]
    for copy in copies:
        copy.start()
    for copy in copies[:3]:
        copy.wait()
    count = index_in.shape[0]
    row = lax.broadcasted_iota(jnp.int32, packed_ref.shape, 0)
    lane = lax.broadcasted_iota(jnp.int32, packed_ref.shape, 1)
    total = jnp.zeros(packed_ref.shape, f32)
    for m in range(count):
        moment = lax.rem(index_in[m, 2] * step_ref[0], jnp.int32(64)).astype(f32)
        offset = phase_in[m] * (0.5 / math.pi) + moment * (1.0 / 64.0)
        for place, value in enumerate(
            (index_in[m, 0].astype(f32), index_in[m, 1].astype(f32), offset, amp_in[m])
        ):
            total = jnp.where((row == m) & (lane == place), value, total)
    packed_ref[...] = total
    for copy in copies[3:]:
        copy.wait()


def load_kernel(sizes, field_ref, conduct_ref, field_out, turned_ref, conduct_in, sems):
    rows, layers, chunks, row_total, layer_total, column_total = sizes
    width = layers * chunks
    copies = (
        pltpu.make_async_copy(field_ref, field_out, sems.at[0]),
        pltpu.make_async_copy(conduct_ref, conduct_in, sems.at[1]),
    )
    for copy in copies:
        copy.start()
    for n, (copy, ref) in enumerate(zip(copies, (field_out, conduct_in))):
        copy.wait()
        for place in range(width):
            spot = (n * width + place) * rows
            turned_ref[spot : spot + rows] = ref[pl.ds(place, rows, stride=width), :]


def block_factors(face):
    inv, scaled, chain, u = [], [], [], []
    rows = len(face) - 1
    rest = 1.0 + face[0]
    for j in range(rows):
        inv.append(inverse(rest + face[j + 1]))
        scaled.append(face[j] * inv[j])
        chain.append(face[j + 1] * inv[j])
        u.append(scaled[j] * u[-1] if j else scaled[j])
        rest = 1.0 + rest * chain[j]
        yield
    v = list(chain)
    for j in range(rows - 2, -1, -1):
        u[j] = u[j] + chain[j] * u[j + 1]
        v[j] = chain[j] * v[j + 1]
    return inv, scaled, chain, u, v


def block_ends(face, rows):
    rest = [1.0 + f for f in face(0)]
    chain, corner = None, None
    for j in range(rows):
        after = face(j + 1)
        inv = [inverse(r + f) for r, f in zip(rest, after)]
        v_last = [f * q for f, q in zip(after, inv)]
        corner = [a + b * (b * q) for a, b, q in zip(corner, chain, inv)] if j else inv
        chain = [b * v for b, v in zip(chain, v_last)] if j else v_last
        if j < rows - 1:
            rest = [1.0 + r * v for r, v in zip(rest, v_last)]
        yield
    return [
        (f * a, b, b * (f * inverse(g)), v)
        for f, g, a, b, v in zip(face(0), after, corner, chain, v_last)
    ]


def height_kernel(sizes, handed_ref, came_ref, heights_ref):
    rows, layers, chunks, row_total, layer_total, column_total = sizes
    odd = lax.rem(lax.axis_index("wide"), 2) == 1
    modes = jnp.where(odd, handed_ref[layers * chunks :], came_ref[layers * chunks :])
    body = height_lines(modes, 0, row_total, row_total, chunks, column_total)
    heights_ref[chunks : (row_total + 1) * chunks] = body
    heights_ref[0:chunks] = body[0:chunks]
    heights_ref[(row_total + 1) * chunks : (row_total + 2) * chunks] = body[
        (row_total - 1) * chunks : row_total * chunks
    ]

def main_kernel(
    sizes, heights, both_ref, below_ref, came_ref, turned_ref,
    sent_ref, p_ref, u_ref, v_ref, left_gain_ref, right_gain_ref, joint_ref,
    ends, links, halo, solved,
):
    rows, layers, chunks, row_total, layer_total, column_total = sizes
    width = layers * chunks
    blocks = row_total // rows
    me = lax.axis_index("wide")
    first_layer = lax.axis_index("grp") * layers
    zeta = [
        ((first_layer + k).astype(f32) + 0.5) * (1.0 / layer_total) for k in range(layers)
    ]
    half = 0.5 * weight
    own_start = pl.multiple_of(me * (rows * chunks), 8)

    def face(start, j):
        both = heights[pl.ds(start + j * chunks, 2 * chunks), :]
        both = both[:chunks] + both[chunks:]
        return jnp.concatenate([weight + (half * z) * both for z in zeta], 0)

    def keep_ends(b, values):
        base = pl.multiple_of(b * (4 * width), 8)
        for n, value in enumerate(values):
            ends[pl.ds(base + n * width, width), :] = value

    factors = []

    def other_blocks(first, count):
        spots = [lax.rem(me + 1 + first + n, blocks) for n in range(count)]
        starts = [pl.multiple_of(b * (rows * chunks), 8) for b in spots]
        values = yield from block_ends(lambda j: [face(start, j) for start in starts], rows)
        for b, ends_of_one in zip(spots, values):
            keep_ends(b, ends_of_one)

    def end(b, n):
        return ends[(4 * b + n) * width : (4 * b + n + 1) * width]

    def scan_steps(group):
        for first in range(0, blocks - 1, group) if group else ():
            yield from other_blocks(first, min(group, blocks - 1 - first))
        inv, scaled, chain, u, v = yield from block_factors([face(own_start, j) for j in range(rows + 1)])
        factors.extend((inv, scaled, chain))
        for j in range(rows):
            u_ref[j * width : (j + 1) * width] = u[j]
            v_ref[j * width : (j + 1) * width] = v[j]
        keep_ends(me, (u[0], v[0], u[-1], v[-1]))
        left = jnp.zeros((width, LANES), f32)
        right = jnp.zeros((width, LANES), f32)
        for b in range(blocks):
            u_first, v_first, u_last, v_last = (end(b, n) for n in range(4))
            gain = u_last * inverse(1.0 - u_first * left)
            left_gain_ref[b * width : (b + 1) * width] = gain
            links[b * width : (b + 1) * width] = left
            left = v_last + gain * left * v_first
            b = blocks - 1 - b
            u_first, v_first, u_last, v_last = (end(b, n) for n in range(4))
            gain = v_first * inverse(1.0 - v_last * right)
            right_gain_ref[b * width : (b + 1) * width] = gain
            links[(blocks + b) * width : (blocks + b + 1) * width] = right
            right = u_first + gain * right * u_last
            yield
        own = pl.ds(pl.multiple_of(me * width, 8), width)
        left_link = links[own, :]
        right_link = links[pl.ds(pl.multiple_of((blocks + me) * width, 8), width), :]
        a = 1.0 - left_link * u[0]
        b = left_link * v[0]
        c = right_link * u[-1]
        d = 1.0 - right_link * v[-1]
        by = inverse(a * d - b * c)
        joint = (
            left_gain_ref[own, :] * left_link, right_gain_ref[own, :] * right_link,
            left_link, right_link, d * by, b * by, c * by, a * by,
        )
        for n, value in enumerate(joint):
            joint_ref[n * width : (n + 1) * width] = value

    if blocks <= 8:
        steps = scan_steps(4)
    else:
        def one_block(n, carry):
            for _ in other_blocks(n, 1):
                pass
            return carry

        lax.fori_loop(0, blocks - 1, one_block, 0)
        steps = scan_steps(0)

    def tick():
        next(steps, None)

    odd = lax.rem(me, 2) == 1
    inner = both_ref[0:width]
    below = jnp.where(odd, inner, below_ref[...])
    above = jnp.where(odd, came_ref[0:width], inner)
    halo[0:width] = jnp.where(me == 0, 0.0, below)
    halo[width : 2 * width] = jnp.where(me == blocks - 1, 0.0, above)
    lane = lax.broadcasted_iota(jnp.int32, (rows, LANES), 1)
    row = lax.broadcasted_iota(jnp.int32, (rows, LANES), 0)

    def neighbours(values, low, high):
        return (
            jnp.where(row == 0, low, pltpu.roll(values, 1, 0)),
            jnp.where(row == rows - 1, high, pltpu.roll(values, rows - 1, 0)),
        )

    g = [[] for _ in range(layers)]
    f = [[] for _ in range(layers)]
    rhs = [[] for _ in range(layers)]
    for c in range(chunks):
        h = heights[pl.ds(own_start + chunks + c, rows, stride=chunks), :]
        h_low, h_high = neighbours(
            h,
            heights[pl.ds(own_start + c, 1), :],
            heights[pl.ds(own_start + (rows + 1) * chunks + c, 1), :],
        )
        low_sum, high_sum = h + h_low, h + h_high
        for k in range(layers):
            place = c * layers + k
            f_mid = turned_ref[place * rows : (place + 1) * rows]
            f_low, f_high = neighbours(
                f_mid, halo[pl.ds(place, 1), :], halo[pl.ds(width + place, 1), :]
            )
            g[k].append(
                turned_ref[(width + place) * rows : (width + place + 1) * rows] * (1.0 + zeta[k] * h)
            )
            f[k].append(f_mid)
            along = (weight + (half * zeta[k]) * high_sum) * (f_high - f_mid) - (
                weight + (half * zeta[k]) * low_sum
            ) * (f_mid - f_low)
            rhs[k].append(2.0 * (f_mid + along))
    for k in range(0, layers, 2):
        both = solve_x_pair(g[k : k + 2], rhs[k : k + 2], lane, tick)
        for n in range(2):
            for c in range(chunks):
                spot = pl.ds((k + n) * chunks + c, rows, stride=width)
                solved[spot, :] = both[n][c] - 2.0 * f[k + n][c]

    for _ in steps:
        pass
    inv, scaled, chain = factors

    def part(ref, j):
        return ref[j * width : (j + 1) * width]

    p = [part(solved, 0) * inv[0]]
    for j in range(1, rows):
        p.append(part(solved, j) * inv[j] + scaled[j] * p[-1])
    for j in range(rows - 2, -1, -1):
        p[j] = p[j] + chain[j] * p[j + 1]
    for j in range(rows):
        p_ref[j * width : (j + 1) * width] = p[j]

    upward = p[-1] + part(joint_ref, 0) * p[0]
    downward = p[0] + part(joint_ref, 1) * p[-1]
    for b in range(blocks):
        sent_ref[b * width : (b + 1) * width] = jnp.where(b > me, upward, downward)


def last_kernel(
    sizes, came_ref, left_gain_ref, right_gain_ref, joint_ref, p_ref, u_ref, v_ref, field_ref,
    out_ref,
):
    rows, layers, chunks, row_total, layer_total, column_total = sizes
    width = layers * chunks
    blocks = row_total // rows
    me = lax.axis_index("wide")

    def part(ref, b):
        return ref[b * width : (b + 1) * width]

    left = jnp.zeros((width, LANES), f32)
    right = jnp.zeros((width, LANES), f32)
    for b in range(blocks - 1):
        left = jnp.where(b < me, part(came_ref, b) + part(left_gain_ref, b) * left, left)
        b = blocks - 1 - b
        right = jnp.where(b > me, part(came_ref, b) + part(right_gain_ref, b) * right, right)

    y = left + part(joint_ref, 2) * part(p_ref, 0)
    z = right + part(joint_ref, 3) * part(p_ref, rows - 1)
    before = part(joint_ref, 4) * y + part(joint_ref, 5) * z
    after = part(joint_ref, 6) * y + part(joint_ref, 7) * z
    for j in range(rows):
        x = part(p_ref, j) + part(u_ref, j) * before + part(v_ref, j) * after
        for k in range(layers):
            spot = pl.ds(j * width + k, chunks, stride=layers)
            out_ref[spot, :] = field_ref[spot, :] + x[k * chunks : (k + 1) * chunks]


def on_device(field, conduct, mode_index, mode_amp, mode_phase, step_index):
    rows, layers, columns = field.shape
    wide_count = lax.axis_size("wide")
    row_total = rows * wide_count
    grp_count = lax.axis_size("grp")
    layer_total = layers * grp_count
    chunks = columns // LANES
    width = layers * chunks
    sizes = (rows, layers, chunks, row_total, layer_total, columns)
    limit = pltpu.CompilerParams(vmem_limit_bytes=16 * 1024 * 1024)
    hbm = pl.BlockSpec(memory_space=pltpu.HBM)

    def lines(count):
        return jax.ShapeDtypeStruct((count * width, LANES), f32)

    step_index, mode_index, mode_amp, mode_phase, field_lines, conduct_lines = (
        step_index,
        *(
            pltpu.with_memory_space_constraint(a, pltpu.HBM)
            for a in (mode_index, mode_amp, mode_phase, to_lines(field), to_lines(conduct))
        ),
    )
    packed, both, outer = pl.pallas_call(
        pack_kernel,
        out_shape=(
            jax.ShapeDtypeStruct((mode_index.shape[0], LANES), f32),
            lines(2),
            lines(1),
        ),
        in_specs=[pl.BlockSpec(memory_space=pltpu.SMEM)] + [hbm] * 4,
        scratch_shapes=[
            pltpu.SMEM(mode_index.shape, jnp.int32),
            pltpu.SMEM(mode_amp.shape, f32),
            pltpu.SMEM(mode_phase.shape, f32),
            pltpu.SemaphoreType.DMA((6,)),
        ],
        compiler_params=limit,
    )(step_index, mode_index, mode_amp, mode_phase, field_lines)

    place = lax.axis_index("wide")
    odd = place % 2 == 1
    swaps = [(i, i ^ 1) for i in range(wide_count)]
    cores = [list(range(n, wide_count, 2)) for n in range(2)]
    both_came = lax.ppermute(both, "wide", swaps)

    def gather_modes(own):
        return lax.all_gather(own, "grp", axis=0, tiled=True)

    def no_modes(own):
        return jnp.zeros((grp_count * own.shape[0], own.shape[1]), f32)

    modes = lax.cond(odd, gather_modes, no_modes, packed)
    modes, outer, both_came = lax.optimization_barrier((modes, outer, both_came))

    def gather_rows(own, came):
        rows_sent = jnp.concatenate([own, came[width:]], 0)
        rows_all = lax.all_gather(rows_sent, "wide", axis_index_groups=cores, axis=0)
        chip = place // 2
        below = lax.dynamic_index_in_dim(rows_all, jnp.maximum(chip - 1, 0), 0, False)
        above = lax.dynamic_index_in_dim(
            rows_all, jnp.minimum(chip + 1, wide_count // 2 - 1), 0, False
        )
        return below[width:], above[:width]

    def no_rows(own, came):
        return jnp.zeros_like(own), jnp.zeros_like(own)

    below, above = lax.cond(odd, no_rows, gather_rows, outer, both_came)
    handed = jnp.concatenate([above, modes], 0)
    came = lax.ppermute(handed, "wide", swaps)
    handed, field, conduct = lax.optimization_barrier((handed, field, conduct))
    field_lines, turned = pl.pallas_call(
        functools.partial(load_kernel, sizes),
        out_shape=(lines(rows), lines(2 * rows)),
        in_specs=[hbm] * 2,
        scratch_shapes=[
            pltpu.VMEM((rows * width, LANES), f32),
            pltpu.SemaphoreType.DMA((2,)),
        ],
        compiler_params=limit,
    )(
        *(
            pltpu.with_memory_space_constraint(to_lines(a), pltpu.HBM)
            for a in (field, conduct)
        )
    )
    heights = pl.pallas_call(
        functools.partial(height_kernel, sizes),
        out_shape=jax.ShapeDtypeStruct(((row_total + 2) * chunks, LANES), f32),
        compiler_params=limit,
    )(handed, came)

    sent, p, u, v, left_gain, right_gain, joint = pl.pallas_call(
        functools.partial(main_kernel, sizes),
        out_shape=(lines(wide_count),)
        + (lines(rows),) * 3
        + (lines(wide_count),) * 2
        + (lines(8),),
        scratch_shapes=[
            pltpu.VMEM((4 * wide_count * width, LANES), f32),
            pltpu.VMEM((2 * wide_count * width, LANES), f32),
            pltpu.VMEM((2 * width, LANES), f32),
            pltpu.VMEM((rows * width, LANES), f32),
        ],
        compiler_params=limit,
    )(heights, both_came, below, came, turned)

    came = lax.all_to_all(
        sent.reshape(wide_count, width, LANES), "wide", split_axis=0, concat_axis=0
    ).reshape(wide_count * width, LANES)

    advanced = pl.pallas_call(
        functools.partial(last_kernel, sizes),
        out_shape=lines(rows),
        compiler_params=limit,
    )(came, left_gain, right_gain, joint, p, u, v, field_lines)
    return from_lines(advanced, field.shape)


def solution(mesh):
    return jax.shard_map(
        on_device,
        mesh=mesh,
        in_specs=(
            P("wide", "grp", None),
            P("wide", "grp", None),
            P("grp", None),
            P("grp"),
            P("grp"),
            P(),
        ),
        out_specs=P("wide", "grp", None),
        check_vma=False,
    )
```

```python
import functools
import math

import jax
import jax.numpy as jnp
from jax import lax
from jax.experimental import pallas as pl
from jax.experimental.pallas import tpu as pltpu
from jax.sharding import PartitionSpec as P

time_step = 600.0
implicit_weight = 0.5
weight = implicit_weight * time_step
LANES = 128
f32 = jnp.float32


def to_lines(block):
    rows, layers, columns = block.shape
    chunks = columns // LANES
    return (
        block.reshape(rows, layers, chunks, LANES)
        .transpose(0, 2, 1, 3)
        .reshape(rows * chunks * layers, LANES)
    )


def from_lines(lines, shape):
    rows, layers, columns = shape
    chunks = columns // LANES
    return (
        lines.reshape(rows, chunks, layers, LANES)
        .transpose(0, 2, 1, 3)
        .reshape(rows, layers, columns)
    )


def turns(wave, index, period):
    product = wave * index
    if period & (period - 1) == 0:
        product = product & (period - 1)
    else:
        product = lax.rem(product, jnp.int32(period))
    return product.astype(f32) * (1.0 / period)


def cos_sin(turn):
    part = turn - jnp.floor(turn + 0.5)
    square = part * part

    def series(first):
        terms = [
            (-1.0) ** n * math.pi ** (2 * n + first) / math.factorial(2 * n + first)
            for n in range(7)
        ]
        total = jnp.full_like(square, terms[-1])
        for term in terms[-2::-1]:
            total = total * square + term
        return total

    half_cos = series(0)
    half_sin = series(1) * part
    return 1.0 - 2.0 * half_sin * half_sin, 2.0 * half_sin * half_cos


def halves(values):
    high = values.astype(jnp.bfloat16)
    return high, (values - high.astype(f32)).astype(jnp.bfloat16)


def height_lines(modes, first_row, count, row_total, chunks, column_total):
    mode_count = modes.shape[0]
    wave_x = modes[:, 0:1].astype(jnp.int32)
    wave_y = modes[:, 1:2].astype(jnp.int32)
    offset = modes[:, 2:3]
    amp = modes[:, 3:4]
    spot = lax.broadcasted_iota(jnp.int32, (mode_count, count * chunks), 1)
    chunk = spot % chunks
    row = jnp.clip(first_row + spot // chunks, 0, row_total - 1)
    angle = (
        turns(wave_y, row, row_total) + turns(wave_x, chunk * LANES, column_total)
    ) + offset
    left_cos, left_sin = cos_sin(angle)
    lane = lax.broadcasted_iota(jnp.int32, (mode_count, LANES), 1)
    right_cos, right_sin = cos_sin(turns(wave_x, lane, column_total))
    left = jnp.concatenate([amp * left_cos, amp * left_sin], 0)
    right = jnp.concatenate([right_cos, -right_sin], 0)
    left_high, left_low = halves(left)
    right_high, right_low = halves(right)
    return lax.dot_general(
        jnp.concatenate([left_high, left_high, left_low], 0),
        jnp.concatenate([right_high, right_low, right_high], 0),
        (((0,), (0,)), ((), ())),
        preferred_element_type=f32,
    )


def inverse(values):
    return pl.reciprocal(values, approx=False)


def from_left(values, stride, lane):
    moved = [pltpu.roll(v, stride, 1) for v in values]
    return [jnp.where(lane < stride, moved[c - 1], moved[c]) for c in range(len(values))]


def from_right(values, stride, lane):
    count = len(values)
    moved = [pltpu.roll(v, LANES - stride, 1) for v in values]
    return [
        jnp.where(lane >= LANES - stride, moved[(c + 1) % count], moved[c]) for c in range(count)
    ]


def solve_chunks(diagonal, link, rhs):
    count = len(rhs)
    if count == 1:
        return [rhs[0] * inverse(diagonal[0])]
    inv = {i: inverse(diagonal[i]) for i in range(0, count, 2)}
    scaled = {i: inv[i] * rhs[i] for i in inv}
    odd_diagonal, odd_link, odd_rhs = [], [], []
    for i in range(1, count, 2):
        d = diagonal[i] - link[i - 1] * (link[i - 1] * inv[i - 1])
        r = rhs[i] + link[i - 1] * scaled[i - 1]
        e = None
        if i + 1 < count:
            by = link[i] * inv[i + 1]
            d = d - link[i] * by
            r = r + link[i] * scaled[i + 1]
            e = by * link[i + 1] if i + 2 < count else None
        odd_diagonal.append(d)
        odd_rhs.append(r)
        odd_link.append(e)
    odd = solve_chunks(odd_diagonal, odd_link, odd_rhs)
    out = [None] * count
    out[1::2] = odd
    for i in range(0, count, 2):
        r = rhs[i]
        if i > 0:
            r = r + link[i - 1] * out[i - 1]
        if i + 1 < count:
            r = r + link[i] * out[i + 1]
        out[i] = r * inv[i]
    return out


def reduce_lanes(diagonal, link, rhs, lane, stride):
    count = len(rhs)
    while stride < LANES:
        inv = [inverse(d) for d in diagonal]
        t = [q * r for q, r in zip(inv, rhs)]
        w = [q * e for q, e in zip(inv, link)]
        low_d = from_left([e * v for e, v in zip(link, w)], stride, lane)
        low_r = from_left([e * v for e, v in zip(link, t)], stride, lane)
        high_q = from_right(inv, stride, lane)
        high_t = from_right(t, stride, lane)
        high_w = from_right(w, stride, lane)
        diagonal = [
            diagonal[c] - low_d[c] - link[c] * (link[c] * high_q[c]) for c in range(count)
        ]
        rhs = [rhs[c] + low_r[c] + link[c] * high_t[c] for c in range(count)]
        link = [link[c] * high_w[c] for c in range(count)]
        stride *= 2
    return solve_chunks(diagonal, link, rhs)


def pack_pair(a, b, odd_lane):
    even = [jnp.where(odd_lane, pltpu.roll(x, 1, 1), y) for x, y in zip(a, b)]
    odd = [jnp.where(odd_lane, x, pltpu.roll(y, LANES - 1, 1)) for x, y in zip(a, b)]
    return even, odd


def unpack_pair(even, odd, odd_lane):
    a = [jnp.where(odd_lane, y, pltpu.roll(x, LANES - 1, 1)) for x, y in zip(even, odd)]
    b = [jnp.where(odd_lane, pltpu.roll(y, 1, 1), x) for x, y in zip(even, odd)]
    return a, b


def solve_x_pair(g_pair, rhs_pair, lane):
    odd_lane = (lane & 1) == 1
    first_cell = lane < 2
    last_cell = lane >= LANES - 2
    half = 0.5 * weight
    g_even, g_odd = pack_pair(*g_pair, odd_lane)
    r_even, r_odd = pack_pair(*rhs_pair, odd_lane)
    face = [half * (a + b) for a, b in zip(g_even, g_odd)]
    after = from_right(g_even, 2, lane)
    after[-1] = jnp.where(last_cell, g_odd[-1], after[-1])
    face_after = [half * (a + b) for a, b in zip(g_odd, after)]
    face_before = from_left(face_after, 2, lane)
    face_before[0] = jnp.where(first_cell, weight * g_even[0], face_before[0])
    inv = [inverse(1.0 + (a + b)) for a, b in zip(face_before, face)]
    d_odd = [1.0 + (a + b) for a, b in zip(face, face_after)]
    link = list(face_after)
    link[-1] = jnp.where(last_cell, 0.0, link[-1])
    link_before = list(face_before)
    link_before[0] = jnp.where(first_cell, 0.0, link_before[0])
    t = [q * r for q, r in zip(inv, r_even)]
    w = [q * e for q, e in zip(inv, face)]
    next_q = from_right(inv, 2, lane)
    next_t = from_right(t, 2, lane)
    next_w = from_right(w, 2, lane)
    diagonal = [
        d - e * v - l * (l * q) for d, e, v, l, q in zip(d_odd, face, w, link, next_q)
    ]
    rhs = [r + e * v + l * n for r, e, v, l, n in zip(r_odd, face, t, link, next_t)]
    x_odd = reduce_lanes(diagonal, [l * n for l, n in zip(link, next_w)], rhs, lane, 2)
    x_before = from_left(x_odd, 2, lane)
    x_even = [
        v + q * (l * b) + u * x for v, q, l, b, u, x in zip(t, inv, link_before, x_before, w, x_odd)
    ]
    return unpack_pair(x_even, x_odd, odd_lane)


def pack_kernel(
    step_ref, index_ref, amp_ref, phase_ref, field_ref,
    packed_ref, both_ref, outer_ref,
    index_in, amp_in, phase_in, sems,
):
    width = outer_ref.shape[0]
    last = field_ref.shape[0] - width
    odd = lax.rem(lax.axis_index("wide"), 2)
    inner_rows = pl.ds(pl.multiple_of((1 - odd) * last, 8), width)
    outer_rows = pl.ds(pl.multiple_of(odd * last, 8), width)
    pairs = (
        (index_ref, index_in),
        (amp_ref, amp_in),
        (phase_ref, phase_in),
        (field_ref.at[inner_rows], both_ref.at[pl.ds(0, width)]),
        (field_ref.at[outer_rows], both_ref.at[pl.ds(width, width)]),
        (field_ref.at[outer_rows], outer_ref),
    )
    copies = [pltpu.make_async_copy(a, b, sems.at[n]) for n, (a, b) in enumerate(pairs)]
    for copy in copies:
        copy.start()
    for copy in copies[:3]:
        copy.wait()
    count = index_in.shape[0]
    row = lax.broadcasted_iota(jnp.int32, packed_ref.shape, 0)
    lane = lax.broadcasted_iota(jnp.int32, packed_ref.shape, 1)
    total = jnp.zeros(packed_ref.shape, f32)
    for m in range(count):
        moment = lax.rem(index_in[m, 2] * step_ref[0], jnp.int32(64)).astype(f32)
        offset = phase_in[m] * (0.5 / math.pi) + moment * (1.0 / 64.0)
        for place, value in enumerate(
            (index_in[m, 0].astype(f32), index_in[m, 1].astype(f32), offset, amp_in[m])
        ):
            total = jnp.where((row == m) & (lane == place), value, total)
    packed_ref[...] = total
    for copy in copies[3:]:
        copy.wait()


def load_kernel(sizes, field_ref, conduct_ref, field_out, turned_ref, conduct_in, sems):
    rows, layers, chunks, row_total, layer_total, column_total = sizes
    width = layers * chunks
    copies = (
        pltpu.make_async_copy(field_ref, field_out, sems.at[0]),
        pltpu.make_async_copy(conduct_ref, conduct_in, sems.at[1]),
    )
    for copy in copies:
        copy.start()
    for n, (copy, ref) in enumerate(zip(copies, (field_out, conduct_in))):
        copy.wait()
        for place in range(width):
            spot = (n * width + place) * rows
            turned_ref[spot : spot + rows] = ref[pl.ds(place, rows, stride=width), :]


def block_factors(face):
    inv, scaled, chain, u = [], [], [], []
    rows = len(face) - 1
    rest = 1.0 + face[0]
    for j in range(rows):
        inv.append(inverse(rest + face[j + 1]))
        scaled.append(face[j] * inv[j])
        chain.append(face[j + 1] * inv[j])
        u.append(scaled[j] * u[-1] if j else scaled[j])
        rest = 1.0 + rest * chain[j]
    v = list(chain)
    for j in range(rows - 2, -1, -1):
        u[j] = u[j] + chain[j] * u[j + 1]
        v[j] = chain[j] * v[j + 1]
    return inv, scaled, chain, u, v


def block_ends(face):
    rows = len(face) - 1
    down = 1.0 + face[0]
    up = 1.0 + face[rows]
    v_first = None
    for j in range(rows):
        v_last = face[j + 1] * inverse(down + face[j + 1])
        v_first = v_last if v_first is None else v_first * v_last
        u_first = face[rows - 1 - j] * inverse(up + face[rows - 1 - j])
        if j < rows - 1:
            down = 1.0 + down * v_last
            up = 1.0 + up * u_first
    u_last = v_first * (face[0] * inverse(face[rows]))
    return u_first, v_first, u_last, v_last


def height_kernel(sizes, handed_ref, came_ref, heights_ref):
    rows, layers, chunks, row_total, layer_total, column_total = sizes
    odd = lax.rem(lax.axis_index("wide"), 2) == 1
    modes = jnp.where(odd, handed_ref[layers * chunks :], came_ref[layers * chunks :])
    body = height_lines(modes, 0, row_total, row_total, chunks, column_total)
    heights_ref[chunks : (row_total + 1) * chunks] = body
    heights_ref[0:chunks] = body[0:chunks]
    heights_ref[(row_total + 1) * chunks : (row_total + 2) * chunks] = body[
        (row_total - 1) * chunks : row_total * chunks
    ]

def main_kernel(
    sizes, heights, inner_ref, below_ref, late_ref, came_ref, turned_ref,
    sent_ref, p_ref, u_ref, v_ref, left_gain_ref, right_gain_ref, joint_ref,
    ends, links, halo, solved,
):
    rows, layers, chunks, row_total, layer_total, column_total = sizes
    width = layers * chunks
    blocks = row_total // rows
    me = lax.axis_index("wide")
    first_layer = lax.axis_index("grp") * layers
    zeta = [
        ((first_layer + k).astype(f32) + 0.5) * (1.0 / layer_total) for k in range(layers)
    ]
    half = 0.5 * weight
    own_start = pl.multiple_of(me * (rows * chunks), 8)

    def faces(start):
        h = [heights[pl.ds(start + j * chunks, chunks), :] for j in range(rows + 2)]
        out = []
        for j in range(rows + 1):
            both = h[j] + h[j + 1]
            out.append(jnp.concatenate([weight + (half * z) * both for z in zeta], 0))
        return out

    def keep_ends(b, values):
        base = pl.multiple_of(b * (4 * width), 8)
        for n, value in enumerate(values):
            ends[pl.ds(base + n * width, width), :] = value

    inv, scaled, chain, u, v = block_factors(faces(own_start))
    for j in range(rows):
        u_ref[j * width : (j + 1) * width] = u[j]
        v_ref[j * width : (j + 1) * width] = v[j]
    keep_ends(me, (u[0], v[0], u[-1], v[-1]))

    def other_block(n):
        b = lax.rem(me + 1 + n, blocks)
        keep_ends(b, block_ends(faces(pl.multiple_of(b * (rows * chunks), 8))))

    if blocks <= 8:
        for n in range(blocks - 1):
            other_block(n)
    else:
        lax.fori_loop(0, blocks - 1, lambda n, carry: (other_block(n), carry)[1], 0)

    def end(b, n):
        return ends[(4 * b + n) * width : (4 * b + n + 1) * width]

    left = jnp.zeros((width, LANES), f32)
    right = jnp.zeros((width, LANES), f32)
    for b in range(blocks):
        u_first, v_first, u_last, v_last = (end(b, n) for n in range(4))
        gain = u_last * inverse(1.0 - u_first * left)
        left_gain_ref[b * width : (b + 1) * width] = gain
        links[b * width : (b + 1) * width] = left
        left = v_last + gain * left * v_first
        b = blocks - 1 - b
        u_first, v_first, u_last, v_last = (end(b, n) for n in range(4))
        gain = v_first * inverse(1.0 - v_last * right)
        right_gain_ref[b * width : (b + 1) * width] = gain
        links[(blocks + b) * width : (blocks + b + 1) * width] = right
        right = u_first + gain * right * u_last

    own = pl.ds(pl.multiple_of(me * width, 8), width)
    left_link = links[own, :]
    right_link = links[pl.ds(pl.multiple_of((blocks + me) * width, 8), width), :]
    a = 1.0 - left_link * u[0]
    b = left_link * v[0]
    c = right_link * u[-1]
    d = 1.0 - right_link * v[-1]
    by = inverse(a * d - b * c)
    joint = (
        left_gain_ref[own, :] * left_link, right_gain_ref[own, :] * right_link,
        left_link, right_link, d * by, b * by, c * by, a * by,
    )
    for n, value in enumerate(joint):
        joint_ref[n * width : (n + 1) * width] = value

    odd = lax.rem(me, 2) == 1
    in_first = first_layer == 0
    other = pl.ds(pl.multiple_of(lax.rem(me, 2) * width, 8), width)
    came = came_ref[0:width]
    inner = jnp.where(in_first, inner_ref[...], came)
    outer = jnp.where(in_first, jnp.where(odd, came, below_ref[...]), late_ref[other, :])
    below = jnp.where(odd, inner, outer)
    above = jnp.where(odd, outer, inner)
    halo[0:width] = jnp.where(me == 0, 0.0, below)
    halo[width : 2 * width] = jnp.where(me == blocks - 1, 0.0, above)
    lane = lax.broadcasted_iota(jnp.int32, (rows, LANES), 1)
    row = lax.broadcasted_iota(jnp.int32, (rows, LANES), 0)

    def neighbours(values, low, high):
        return (
            jnp.where(row == 0, low, pltpu.roll(values, 1, 0)),
            jnp.where(row == rows - 1, high, pltpu.roll(values, rows - 1, 0)),
        )

    g = [[] for _ in range(layers)]
    f = [[] for _ in range(layers)]
    rhs = [[] for _ in range(layers)]
    for c in range(chunks):
        h = heights[pl.ds(own_start + chunks + c, rows, stride=chunks), :]
        h_low, h_high = neighbours(
            h,
            heights[pl.ds(own_start + c, 1), :],
            heights[pl.ds(own_start + (rows + 1) * chunks + c, 1), :],
        )
        low_sum, high_sum = h + h_low, h + h_high
        for k in range(layers):
            place = c * layers + k
            f_mid = turned_ref[place * rows : (place + 1) * rows]
            f_low, f_high = neighbours(
                f_mid, halo[pl.ds(place, 1), :], halo[pl.ds(width + place, 1), :]
            )
            g[k].append(
                turned_ref[(width + place) * rows : (width + place + 1) * rows] * (1.0 + zeta[k] * h)
            )
            f[k].append(f_mid)
            along = (weight + (half * zeta[k]) * high_sum) * (f_high - f_mid) - (
                weight + (half * zeta[k]) * low_sum
            ) * (f_mid - f_low)
            rhs[k].append(2.0 * (f_mid + along))
    for k in range(0, layers, 2):
        both = solve_x_pair(g[k : k + 2], rhs[k : k + 2], lane)
        for n in range(2):
            for c in range(chunks):
                spot = pl.ds((k + n) * chunks + c, rows, stride=width)
                solved[spot, :] = both[n][c] - 2.0 * f[k + n][c]

    def part(ref, j):
        return ref[j * width : (j + 1) * width]

    p = [part(solved, 0) * inv[0]]
    for j in range(1, rows):
        p.append(part(solved, j) * inv[j] + scaled[j] * p[-1])
    for j in range(rows - 2, -1, -1):
        p[j] = p[j] + chain[j] * p[j + 1]
    for j in range(rows):
        p_ref[j * width : (j + 1) * width] = p[j]

    upward = p[-1] + part(joint_ref, 0) * p[0]
    downward = p[0] + part(joint_ref, 1) * p[-1]
    for b in range(blocks):
        sent_ref[b * width : (b + 1) * width] = jnp.where(b > me, upward, downward)


def last_kernel(
    sizes, came_ref, left_gain_ref, right_gain_ref, joint_ref, p_ref, u_ref, v_ref, field_ref,
    out_ref,
):
    rows, layers, chunks, row_total, layer_total, column_total = sizes
    width = layers * chunks
    blocks = row_total // rows
    me = lax.axis_index("wide")

    def part(ref, b):
        return ref[b * width : (b + 1) * width]

    left = jnp.zeros((width, LANES), f32)
    right = jnp.zeros((width, LANES), f32)
    for b in range(blocks - 1):
        left = jnp.where(b < me, part(came_ref, b) + part(left_gain_ref, b) * left, left)
        b = blocks - 1 - b
        right = jnp.where(b > me, part(came_ref, b) + part(right_gain_ref, b) * right, right)

    y = left + part(joint_ref, 2) * part(p_ref, 0)
    z = right + part(joint_ref, 3) * part(p_ref, rows - 1)
    before = part(joint_ref, 4) * y + part(joint_ref, 5) * z
    after = part(joint_ref, 6) * y + part(joint_ref, 7) * z
    for j in range(rows):
        x = part(p_ref, j) + part(u_ref, j) * before + part(v_ref, j) * after
        for k in range(layers):
            spot = pl.ds(j * width + k, chunks, stride=layers)
            out_ref[spot, :] = field_ref[spot, :] + x[k * chunks : (k + 1) * chunks]


def on_device(field, conduct, mode_index, mode_amp, mode_phase, step_index):
    rows, layers, columns = field.shape
    wide_count = lax.axis_size("wide")
    row_total = rows * wide_count
    grp_count = lax.axis_size("grp")
    layer_total = layers * grp_count
    chunks = columns // LANES
    width = layers * chunks
    sizes = (rows, layers, chunks, row_total, layer_total, columns)
    limit = pltpu.CompilerParams(vmem_limit_bytes=16 * 1024 * 1024)
    hbm = pl.BlockSpec(memory_space=pltpu.HBM)

    def lines(count):
        return jax.ShapeDtypeStruct((count * width, LANES), f32)

    step_index, mode_index, mode_amp, mode_phase, field_lines, conduct_lines = (
        step_index,
        *(
            pltpu.with_memory_space_constraint(a, pltpu.HBM)
            for a in (mode_index, mode_amp, mode_phase, to_lines(field), to_lines(conduct))
        ),
    )
    packed, both, outer = pl.pallas_call(
        pack_kernel,
        out_shape=(
            jax.ShapeDtypeStruct((mode_index.shape[0], LANES), f32),
            lines(2),
            lines(1),
        ),
        in_specs=[pl.BlockSpec(memory_space=pltpu.SMEM)] + [hbm] * 4,
        scratch_shapes=[
            pltpu.SMEM(mode_index.shape, jnp.int32),
            pltpu.SMEM(mode_amp.shape, f32),
            pltpu.SMEM(mode_phase.shape, f32),
            pltpu.SemaphoreType.DMA((6,)),
        ],
        compiler_params=limit,
    )(step_index, mode_index, mode_amp, mode_phase, field_lines)

    place = lax.axis_index("wide")
    odd = place % 2 == 1
    in_first = lax.axis_index("grp") == 0
    swaps = [(i, i ^ 1) for i in range(wide_count)]
    cores = [list(range(n, wide_count, 2)) for n in range(2)]
    pairs = [[0, wide_count - 1]] + [[i, i + 1] for i in range(1, wide_count - 1, 2)]

    def gather_rows(own, came):
        rows_sent = jnp.concatenate([own, came[width:]], 0)
        rows_all = lax.all_gather(rows_sent, "wide", axis_index_groups=cores, axis=0)
        chip = place // 2
        below = lax.dynamic_index_in_dim(rows_all, jnp.maximum(chip - 1, 0), 0, False)
        above = lax.dynamic_index_in_dim(
            rows_all, jnp.minimum(chip + 1, wide_count // 2 - 1), 0, False
        )
        return below[width:], above[:width]

    def no_rows(own, came):
        return jnp.zeros_like(own), jnp.zeros_like(own)

    def early_rows(own, mine):
        came = lax.ppermute(mine, "wide", swaps)
        return (came[:width],) + lax.cond(odd, no_rows, gather_rows, own, came)

    def no_early_rows(own, mine):
        return jnp.zeros_like(own), jnp.zeros_like(own), mine[:width]

    inner_came, below, to_other = lax.cond(in_first, early_rows, no_early_rows, outer, both)
    packed, to_other = lax.optimization_barrier((packed, to_other))

    def gather_modes(own):
        return lax.all_gather(own, "grp", axis=0, tiled=True)

    def no_modes(own):
        return jnp.zeros((grp_count * own.shape[0], own.shape[1]), f32)

    modes = lax.cond(odd, gather_modes, no_modes, packed)
    handed = jnp.concatenate([to_other, modes], 0)
    came = lax.ppermute(handed, "wide", swaps)
    handed, field, conduct = lax.optimization_barrier((handed, field, conduct))
    field_lines, turned = pl.pallas_call(
        functools.partial(load_kernel, sizes),
        out_shape=(lines(rows), lines(2 * rows)),
        in_specs=[hbm] * 2,
        scratch_shapes=[
            pltpu.VMEM((rows * width, LANES), f32),
            pltpu.SemaphoreType.DMA((2,)),
        ],
        compiler_params=limit,
    )(
        *(
            pltpu.with_memory_space_constraint(to_lines(a), pltpu.HBM)
            for a in (field, conduct)
        )
    )
    field_lines, turned, outer = lax.optimization_barrier((field_lines, turned, outer))

    def gather_pairs(rows_sent):
        return lax.all_gather(rows_sent, "wide", axis_index_groups=pairs, axis=0, tiled=True)

    def no_pairs(rows_sent):
        return jnp.zeros((2 * width, LANES), f32)

    late = lax.cond(in_first, no_pairs, gather_pairs, outer)
    heights = pl.pallas_call(
        functools.partial(height_kernel, sizes),
        out_shape=jax.ShapeDtypeStruct(((row_total + 2) * chunks, LANES), f32),
        compiler_params=limit,
    )(handed, came)

    sent, p, u, v, left_gain, right_gain, joint = pl.pallas_call(
        functools.partial(main_kernel, sizes),
        out_shape=(lines(wide_count),)
        + (lines(rows),) * 3
        + (lines(wide_count),) * 2
        + (lines(8),),
        scratch_shapes=[
            pltpu.VMEM((4 * wide_count * width, LANES), f32),
            pltpu.VMEM((2 * wide_count * width, LANES), f32),
            pltpu.VMEM((2 * width, LANES), f32),
            pltpu.VMEM((rows * width, LANES), f32),
        ],
        compiler_params=limit,
    )(heights, inner_came, below, late, came, turned)

    came = lax.all_to_all(
        sent.reshape(wide_count, width, LANES), "wide", split_axis=0, concat_axis=0
    ).reshape(wide_count * width, LANES)

    advanced = pl.pallas_call(
        functools.partial(last_kernel, sizes),
        out_shape=lines(rows),
        compiler_params=limit,
    )(came, left_gain, right_gain, joint, p, u, v, field_lines)
    return from_lines(advanced, field.shape)


def solution(mesh):
    return jax.shard_map(
        on_device,
        mesh=mesh,
        in_specs=(
            P("wide", "grp", None),
            P("wide", "grp", None),
            P("grp", None),
            P("grp"),
            P("grp"),
            P(),
        ),
        out_specs=P("wide", "grp", None),
        check_vma=False,
    )
```

```python
import functools
import math

import jax
import jax.numpy as jnp
from jax import lax
from jax.experimental import pallas as pl
from jax.experimental.pallas import tpu as pltpu
from jax.sharding import PartitionSpec as P

time_step = 600.0
implicit_weight = 0.5
weight = implicit_weight * time_step
LANES = 128
f32 = jnp.float32


def to_lines(block):
    rows, layers, columns = block.shape
    chunks = columns // LANES
    return (
        block.reshape(rows, layers, chunks, LANES)
        .transpose(0, 2, 1, 3)
        .reshape(rows * chunks * layers, LANES)
    )


def from_lines(lines, shape):
    rows, layers, columns = shape
    chunks = columns // LANES
    return (
        lines.reshape(rows, chunks, layers, LANES)
        .transpose(0, 2, 1, 3)
        .reshape(rows, layers, columns)
    )


def turns(wave, index, period):
    product = wave * index
    if period & (period - 1) == 0:
        product = product & (period - 1)
    else:
        product = lax.rem(product, jnp.int32(period))
    return product.astype(f32) * (1.0 / period)


def cos_sin(turn):
    part = turn - jnp.floor(turn + 0.5)
    square = part * part

    def series(first):
        terms = [
            (-1.0) ** n * math.pi ** (2 * n + first) / math.factorial(2 * n + first)
            for n in range(7)
        ]
        total = jnp.full_like(square, terms[-1])
        for term in terms[-2::-1]:
            total = total * square + term
        return total

    half_cos = series(0)
    half_sin = series(1) * part
    return 1.0 - 2.0 * half_sin * half_sin, 2.0 * half_sin * half_cos


def halves(values):
    high = values.astype(jnp.bfloat16)
    return high, (values - high.astype(f32)).astype(jnp.bfloat16)


def height_lines(modes, first_row, count, row_total, chunks, column_total):
    mode_count = modes.shape[0]
    wave_x = modes[:, 0:1].astype(jnp.int32)
    wave_y = modes[:, 1:2].astype(jnp.int32)
    offset = modes[:, 2:3]
    amp = modes[:, 3:4]
    spot = lax.broadcasted_iota(jnp.int32, (mode_count, count * chunks), 1)
    chunk = spot % chunks
    row = jnp.clip(first_row + spot // chunks, 0, row_total - 1)
    angle = (
        turns(wave_y, row, row_total) + turns(wave_x, chunk * LANES, column_total)
    ) + offset
    left_cos, left_sin = cos_sin(angle)
    lane = lax.broadcasted_iota(jnp.int32, (mode_count, LANES), 1)
    right_cos, right_sin = cos_sin(turns(wave_x, lane, column_total))
    left = jnp.concatenate([amp * left_cos, amp * left_sin], 0)
    right = jnp.concatenate([right_cos, -right_sin], 0)
    left_high, left_low = halves(left)
    right_high, right_low = halves(right)
    return lax.dot_general(
        jnp.concatenate([left_high, left_high, left_low], 0),
        jnp.concatenate([right_high, right_low, right_high], 0),
        (((0,), (0,)), ((), ())),
        preferred_element_type=f32,
    )


def inverse(values):
    return pl.reciprocal(values, approx=False)


def from_left(values, stride, lane):
    moved = [pltpu.roll(v, stride, 1) for v in values]
    return [jnp.where(lane < stride, moved[c - 1], moved[c]) for c in range(len(values))]


def from_right(values, stride, lane):
    count = len(values)
    moved = [pltpu.roll(v, LANES - stride, 1) for v in values]
    return [
        jnp.where(lane >= LANES - stride, moved[(c + 1) % count], moved[c]) for c in range(count)
    ]


def solve_chunks(diagonal, link, rhs):
    count = len(rhs)
    if count == 1:
        return [rhs[0] * inverse(diagonal[0])]
    inv = {i: inverse(diagonal[i]) for i in range(0, count, 2)}
    scaled = {i: inv[i] * rhs[i] for i in inv}
    odd_diagonal, odd_link, odd_rhs = [], [], []
    for i in range(1, count, 2):
        d = diagonal[i] - link[i - 1] * (link[i - 1] * inv[i - 1])
        r = rhs[i] + link[i - 1] * scaled[i - 1]
        e = None
        if i + 1 < count:
            by = link[i] * inv[i + 1]
            d = d - link[i] * by
            r = r + link[i] * scaled[i + 1]
            e = by * link[i + 1] if i + 2 < count else None
        odd_diagonal.append(d)
        odd_rhs.append(r)
        odd_link.append(e)
    odd = solve_chunks(odd_diagonal, odd_link, odd_rhs)
    out = [None] * count
    out[1::2] = odd
    for i in range(0, count, 2):
        r = rhs[i]
        if i > 0:
            r = r + link[i - 1] * out[i - 1]
        if i + 1 < count:
            r = r + link[i] * out[i + 1]
        out[i] = r * inv[i]
    return out


def reduce_lanes(diagonal, link, rhs, lane, stride):
    count = len(rhs)
    while stride < LANES:
        inv = [inverse(d) for d in diagonal]
        t = [q * r for q, r in zip(inv, rhs)]
        w = [q * e for q, e in zip(inv, link)]
        low_d = from_left([e * v for e, v in zip(link, w)], stride, lane)
        low_r = from_left([e * v for e, v in zip(link, t)], stride, lane)
        high_q = from_right(inv, stride, lane)
        high_t = from_right(t, stride, lane)
        high_w = from_right(w, stride, lane)
        diagonal = [
            diagonal[c] - low_d[c] - link[c] * (link[c] * high_q[c]) for c in range(count)
        ]
        rhs = [rhs[c] + low_r[c] + link[c] * high_t[c] for c in range(count)]
        link = [link[c] * high_w[c] for c in range(count)]
        stride *= 2
    return solve_chunks(diagonal, link, rhs)


def pack_pair(a, b, odd_lane):
    even = [jnp.where(odd_lane, pltpu.roll(x, 1, 1), y) for x, y in zip(a, b)]
    odd = [jnp.where(odd_lane, x, pltpu.roll(y, LANES - 1, 1)) for x, y in zip(a, b)]
    return even, odd


def unpack_pair(even, odd, odd_lane):
    a = [jnp.where(odd_lane, y, pltpu.roll(x, LANES - 1, 1)) for x, y in zip(even, odd)]
    b = [jnp.where(odd_lane, pltpu.roll(y, 1, 1), x) for x, y in zip(even, odd)]
    return a, b


def solve_x_pair(g_pair, rhs_pair, lane):
    odd_lane = (lane & 1) == 1
    first_cell = lane < 2
    last_cell = lane >= LANES - 2
    half = 0.5 * weight
    g_even, g_odd = pack_pair(*g_pair, odd_lane)
    r_even, r_odd = pack_pair(*rhs_pair, odd_lane)
    face = [half * (a + b) for a, b in zip(g_even, g_odd)]
    after = from_right(g_even, 2, lane)
    after[-1] = jnp.where(last_cell, g_odd[-1], after[-1])
    face_after = [half * (a + b) for a, b in zip(g_odd, after)]
    face_before = from_left(face_after, 2, lane)
    face_before[0] = jnp.where(first_cell, weight * g_even[0], face_before[0])
    inv = [inverse(1.0 + (a + b)) for a, b in zip(face_before, face)]
    d_odd = [1.0 + (a + b) for a, b in zip(face, face_after)]
    link = list(face_after)
    link[-1] = jnp.where(last_cell, 0.0, link[-1])
    link_before = list(face_before)
    link_before[0] = jnp.where(first_cell, 0.0, link_before[0])
    t = [q * r for q, r in zip(inv, r_even)]
    w = [q * e for q, e in zip(inv, face)]
    next_q = from_right(inv, 2, lane)
    next_t = from_right(t, 2, lane)
    next_w = from_right(w, 2, lane)
    diagonal = [
        d - e * v - l * (l * q) for d, e, v, l, q in zip(d_odd, face, w, link, next_q)
    ]
    rhs = [r + e * v + l * n for r, e, v, l, n in zip(r_odd, face, t, link, next_t)]
    x_odd = reduce_lanes(diagonal, [l * n for l, n in zip(link, next_w)], rhs, lane, 2)
    x_before = from_left(x_odd, 2, lane)
    x_even = [
        v + q * (l * b) + u * x for v, q, l, b, u, x in zip(t, inv, link_before, x_before, w, x_odd)
    ]
    return unpack_pair(x_even, x_odd, odd_lane)


def pack_kernel(
    step_ref, index_ref, amp_ref, phase_ref, field_ref,
    packed_ref, both_ref, inner_ref, outer_ref, late_ref,
    index_in, amp_in, phase_in, sems,
):
    width = outer_ref.shape[0]
    last = field_ref.shape[0] - width
    odd = lax.rem(lax.axis_index("wide"), 2)
    inner_rows = pl.ds(pl.multiple_of((1 - odd) * last, 8), width)
    outer_rows = pl.ds(pl.multiple_of(odd * last, 8), width)
    pairs = (
        (index_ref, index_in),
        (amp_ref, amp_in),
        (phase_ref, phase_in),
        (field_ref.at[inner_rows], both_ref.at[pl.ds(0, width)]),
        (field_ref.at[outer_rows], both_ref.at[pl.ds(width, width)]),
        (field_ref.at[inner_rows], inner_ref),
        (field_ref.at[outer_rows], outer_ref),
        (field_ref.at[outer_rows], late_ref),
    )
    copies = [pltpu.make_async_copy(a, b, sems.at[n]) for n, (a, b) in enumerate(pairs)]
    for copy in copies:
        copy.start()
    for copy in copies[:3]:
        copy.wait()
    count = index_in.shape[0]
    row = lax.broadcasted_iota(jnp.int32, packed_ref.shape, 0)
    lane = lax.broadcasted_iota(jnp.int32, packed_ref.shape, 1)
    total = jnp.zeros(packed_ref.shape, f32)
    for m in range(count):
        moment = lax.rem(index_in[m, 2] * step_ref[0], jnp.int32(64)).astype(f32)
        offset = phase_in[m] * (0.5 / math.pi) + moment * (1.0 / 64.0)
        for place, value in enumerate(
            (index_in[m, 0].astype(f32), index_in[m, 1].astype(f32), offset, amp_in[m])
        ):
            total = jnp.where((row == m) & (lane == place), value, total)
    packed_ref[...] = total
    for copy in copies[3:]:
        copy.wait()


def load_kernel(sizes, field_ref, conduct_ref, field_out, turned_ref, conduct_in, sems):
    rows, layers, chunks, row_total, layer_total, column_total = sizes
    width = layers * chunks
    copies = (
        pltpu.make_async_copy(field_ref, field_out, sems.at[0]),
        pltpu.make_async_copy(conduct_ref, conduct_in, sems.at[1]),
    )
    for copy in copies:
        copy.start()
    for n, (copy, ref) in enumerate(zip(copies, (field_out, conduct_in))):
        copy.wait()
        for place in range(width):
            spot = (n * width + place) * rows
            turned_ref[spot : spot + rows] = ref[pl.ds(place, rows, stride=width), :]


def block_factors(face):
    inv, scaled, chain, u = [], [], [], []
    rows = len(face) - 1
    rest = 1.0 + face[0]
    for j in range(rows):
        inv.append(inverse(rest + face[j + 1]))
        scaled.append(face[j] * inv[j])
        chain.append(face[j + 1] * inv[j])
        u.append(scaled[j] * u[-1] if j else scaled[j])
        rest = 1.0 + rest * chain[j]
    v = list(chain)
    for j in range(rows - 2, -1, -1):
        u[j] = u[j] + chain[j] * u[j + 1]
        v[j] = chain[j] * v[j + 1]
    return inv, scaled, chain, u, v


def block_ends(face):
    rows = len(face) - 1
    down = 1.0 + face[0]
    up = 1.0 + face[rows]
    v_first = None
    for j in range(rows):
        v_last = face[j + 1] * inverse(down + face[j + 1])
        v_first = v_last if v_first is None else v_first * v_last
        u_first = face[rows - 1 - j] * inverse(up + face[rows - 1 - j])
        if j < rows - 1:
            down = 1.0 + down * v_last
            up = 1.0 + up * u_first
    u_last = v_first * (face[0] * inverse(face[rows]))
    return u_first, v_first, u_last, v_last


def height_kernel(sizes, handed_ref, came_ref, heights_ref):
    rows, layers, chunks, row_total, layer_total, column_total = sizes
    odd = lax.rem(lax.axis_index("wide"), 2) == 1
    modes = jnp.where(odd, handed_ref[layers * chunks :], came_ref[layers * chunks :])
    body = height_lines(modes, 0, row_total, row_total, chunks, column_total)
    heights_ref[chunks : (row_total + 1) * chunks] = body
    heights_ref[0:chunks] = body[0:chunks]
    heights_ref[(row_total + 1) * chunks : (row_total + 2) * chunks] = body[
        (row_total - 1) * chunks : row_total * chunks
    ]

def main_kernel(
    sizes, heights, rows_ref, came_ref, turned_ref,
    sent_ref, p_ref, u_ref, v_ref, left_gain_ref, right_gain_ref, joint_ref,
    ends, links, halo, solved,
):
    rows, layers, chunks, row_total, layer_total, column_total = sizes
    width = layers * chunks
    blocks = row_total // rows
    me = lax.axis_index("wide")
    first_layer = lax.axis_index("grp") * layers
    zeta = [
        ((first_layer + k).astype(f32) + 0.5) * (1.0 / layer_total) for k in range(layers)
    ]
    half = 0.5 * weight
    own_start = pl.multiple_of(me * (rows * chunks), 8)

    def faces(start):
        h = [heights[pl.ds(start + j * chunks, chunks), :] for j in range(rows + 2)]
        out = []
        for j in range(rows + 1):
            both = h[j] + h[j + 1]
            out.append(jnp.concatenate([weight + (half * z) * both for z in zeta], 0))
        return out

    def keep_ends(b, values):
        base = pl.multiple_of(b * (4 * width), 8)
        for n, value in enumerate(values):
            ends[pl.ds(base + n * width, width), :] = value

    inv, scaled, chain, u, v = block_factors(faces(own_start))
    for j in range(rows):
        u_ref[j * width : (j + 1) * width] = u[j]
        v_ref[j * width : (j + 1) * width] = v[j]
    keep_ends(me, (u[0], v[0], u[-1], v[-1]))

    def other_block(n):
        b = lax.rem(me + 1 + n, blocks)
        keep_ends(b, block_ends(faces(pl.multiple_of(b * (rows * chunks), 8))))

    if blocks <= 8:
        for n in range(blocks - 1):
            other_block(n)
    else:
        lax.fori_loop(0, blocks - 1, lambda n, carry: (other_block(n), carry)[1], 0)

    def end(b, n):
        return ends[(4 * b + n) * width : (4 * b + n + 1) * width]

    left = jnp.zeros((width, LANES), f32)
    right = jnp.zeros((width, LANES), f32)
    for b in range(blocks):
        u_first, v_first, u_last, v_last = (end(b, n) for n in range(4))
        gain = u_last * inverse(1.0 - u_first * left)
        left_gain_ref[b * width : (b + 1) * width] = gain
        links[b * width : (b + 1) * width] = left
        left = v_last + gain * left * v_first
        b = blocks - 1 - b
        u_first, v_first, u_last, v_last = (end(b, n) for n in range(4))
        gain = v_first * inverse(1.0 - v_last * right)
        right_gain_ref[b * width : (b + 1) * width] = gain
        links[(blocks + b) * width : (blocks + b + 1) * width] = right
        right = u_first + gain * right * u_last

    own = pl.ds(pl.multiple_of(me * width, 8), width)
    left_link = links[own, :]
    right_link = links[pl.ds(pl.multiple_of((blocks + me) * width, 8), width), :]
    a = 1.0 - left_link * u[0]
    b = left_link * v[0]
    c = right_link * u[-1]
    d = 1.0 - right_link * v[-1]
    by = inverse(a * d - b * c)
    joint = (
        left_gain_ref[own, :] * left_link, right_gain_ref[own, :] * right_link,
        left_link, right_link, d * by, b * by, c * by, a * by,
    )
    for n, value in enumerate(joint):
        joint_ref[n * width : (n + 1) * width] = value

    odd = lax.rem(me, 2) == 1
    in_first = first_layer == 0
    other = pl.ds(pl.multiple_of(lax.rem(me, 2) * width, 8), width)
    came = came_ref[0:width]
    inner = jnp.where(in_first, rows_ref[0:width], came)
    outer = jnp.where(
        in_first, jnp.where(odd, came, rows_ref[width : 2 * width]), rows_ref[other, :]
    )
    below = jnp.where(odd, inner, outer)
    above = jnp.where(odd, outer, inner)
    halo[0:width] = jnp.where(me == 0, 0.0, below)
    halo[width : 2 * width] = jnp.where(me == blocks - 1, 0.0, above)
    lane = lax.broadcasted_iota(jnp.int32, (rows, LANES), 1)
    row = lax.broadcasted_iota(jnp.int32, (rows, LANES), 0)

    def neighbours(values, low, high):
        return (
            jnp.where(row == 0, low, pltpu.roll(values, 1, 0)),
            jnp.where(row == rows - 1, high, pltpu.roll(values, rows - 1, 0)),
        )

    g = [[] for _ in range(layers)]
    f = [[] for _ in range(layers)]
    rhs = [[] for _ in range(layers)]
    for c in range(chunks):
        h = heights[pl.ds(own_start + chunks + c, rows, stride=chunks), :]
        h_low, h_high = neighbours(
            h,
            heights[pl.ds(own_start + c, 1), :],
            heights[pl.ds(own_start + (rows + 1) * chunks + c, 1), :],
        )
        low_sum, high_sum = h + h_low, h + h_high
        for k in range(layers):
            place = c * layers + k
            f_mid = turned_ref[place * rows : (place + 1) * rows]
            f_low, f_high = neighbours(
                f_mid, halo[pl.ds(place, 1), :], halo[pl.ds(width + place, 1), :]
            )
            g[k].append(
                turned_ref[(width + place) * rows : (width + place + 1) * rows] * (1.0 + zeta[k] * h)
            )
            f[k].append(f_mid)
            along = (weight + (half * zeta[k]) * high_sum) * (f_high - f_mid) - (
                weight + (half * zeta[k]) * low_sum
            ) * (f_mid - f_low)
            rhs[k].append(2.0 * (f_mid + along))
    for k in range(0, layers, 2):
        both = solve_x_pair(g[k : k + 2], rhs[k : k + 2], lane)
        for n in range(2):
            for c in range(chunks):
                spot = pl.ds((k + n) * chunks + c, rows, stride=width)
                solved[spot, :] = both[n][c] - 2.0 * f[k + n][c]

    def part(ref, j):
        return ref[j * width : (j + 1) * width]

    p = [part(solved, 0) * inv[0]]
    for j in range(1, rows):
        p.append(part(solved, j) * inv[j] + scaled[j] * p[-1])
    for j in range(rows - 2, -1, -1):
        p[j] = p[j] + chain[j] * p[j + 1]
    for j in range(rows):
        p_ref[j * width : (j + 1) * width] = p[j]

    upward = p[-1] + part(joint_ref, 0) * p[0]
    downward = p[0] + part(joint_ref, 1) * p[-1]
    for b in range(blocks):
        sent_ref[b * width : (b + 1) * width] = jnp.where(b > me, upward, downward)


def last_kernel(
    sizes, came_ref, left_gain_ref, right_gain_ref, joint_ref, p_ref, u_ref, v_ref, field_ref,
    out_ref,
):
    rows, layers, chunks, row_total, layer_total, column_total = sizes
    width = layers * chunks
    blocks = row_total // rows
    me = lax.axis_index("wide")

    def part(ref, b):
        return ref[b * width : (b + 1) * width]

    left = jnp.zeros((width, LANES), f32)
    right = jnp.zeros((width, LANES), f32)
    for b in range(blocks - 1):
        left = jnp.where(b < me, part(came_ref, b) + part(left_gain_ref, b) * left, left)
        b = blocks - 1 - b
        right = jnp.where(b > me, part(came_ref, b) + part(right_gain_ref, b) * right, right)

    y = left + part(joint_ref, 2) * part(p_ref, 0)
    z = right + part(joint_ref, 3) * part(p_ref, rows - 1)
    before = part(joint_ref, 4) * y + part(joint_ref, 5) * z
    after = part(joint_ref, 6) * y + part(joint_ref, 7) * z
    for j in range(rows):
        x = part(p_ref, j) + part(u_ref, j) * before + part(v_ref, j) * after
        for k in range(layers):
            spot = pl.ds(j * width + k, chunks, stride=layers)
            out_ref[spot, :] = field_ref[spot, :] + x[k * chunks : (k + 1) * chunks]


def on_device(field, conduct, mode_index, mode_amp, mode_phase, step_index):
    rows, layers, columns = field.shape
    wide_count = lax.axis_size("wide")
    row_total = rows * wide_count
    grp_count = lax.axis_size("grp")
    layer_total = layers * grp_count
    chunks = columns // LANES
    width = layers * chunks
    sizes = (rows, layers, chunks, row_total, layer_total, columns)
    limit = pltpu.CompilerParams(vmem_limit_bytes=16 * 1024 * 1024)
    hbm = pl.BlockSpec(memory_space=pltpu.HBM)

    def lines(count):
        return jax.ShapeDtypeStruct((count * width, LANES), f32)

    step_index, mode_index, mode_amp, mode_phase, field_lines, conduct_lines = (
        step_index,
        *(
            pltpu.with_memory_space_constraint(a, pltpu.HBM)
            for a in (mode_index, mode_amp, mode_phase, to_lines(field), to_lines(conduct))
        ),
    )
    packed, both, inner, outer, outer_late = pl.pallas_call(
        pack_kernel,
        out_shape=(
            jax.ShapeDtypeStruct((mode_index.shape[0], LANES), f32),
            lines(2),
            lines(1),
            lines(1),
            lines(1),
        ),
        in_specs=[pl.BlockSpec(memory_space=pltpu.SMEM)] + [hbm] * 4,
        scratch_shapes=[
            pltpu.SMEM(mode_index.shape, jnp.int32),
            pltpu.SMEM(mode_amp.shape, f32),
            pltpu.SMEM(mode_phase.shape, f32),
            pltpu.SemaphoreType.DMA((8,)),
        ],
        compiler_params=limit,
    )(step_index, mode_index, mode_amp, mode_phase, field_lines)

    place = lax.axis_index("wide")
    odd = place % 2 == 1
    in_first = lax.axis_index("grp") == 0
    swaps = [(i, i ^ 1) for i in range(wide_count)]
    cores = [list(range(n, wide_count, 2)) for n in range(2)]
    pairs = [[0, wide_count - 1]] + [[i, i + 1] for i in range(1, wide_count - 1, 2)]

    def gather_rows(own, came):
        rows_sent = jnp.concatenate([own, came[width:]], 0)
        rows_all = lax.all_gather(rows_sent, "wide", axis_index_groups=cores, axis=0)
        chip = place // 2
        below = lax.dynamic_index_in_dim(rows_all, jnp.maximum(chip - 1, 0), 0, False)
        above = lax.dynamic_index_in_dim(
            rows_all, jnp.minimum(chip + 1, wide_count // 2 - 1), 0, False
        )
        return below[width:], above[:width]

    mode_shape = (grp_count * packed.shape[0], LANES)

    def gather_modes(own, outer_own, inner_own, both_other):
        modes = lax.all_gather(own, "grp", axis=0, tiled=True)
        return jnp.concatenate([inner_own, modes], 0), jnp.zeros_like(outer_own)

    def early_rows(own, outer_own, inner_own, both_other):
        below, above = gather_rows(outer_own, both_other)
        return jnp.concatenate([above, jnp.zeros(mode_shape, f32)], 0), below

    def no_early_rows(own, outer_own, inner_own, both_other):
        return (
            jnp.concatenate([inner_own, jnp.zeros(mode_shape, f32)], 0),
            jnp.zeros_like(outer_own),
        )

    def even_core(*operands):
        return lax.cond(in_first, early_rows, no_early_rows, *operands)

    both_came = lax.cond(
        in_first,
        lambda mine: lax.ppermute(mine, "wide", swaps),
        lambda mine: jnp.zeros_like(mine),
        both,
    )
    handed, below = lax.cond(odd, gather_modes, even_core, packed, outer, inner, both_came)
    came = lax.ppermute(handed, "wide", swaps)
    handed, field, conduct = lax.optimization_barrier((handed, field, conduct))
    field_lines, turned = pl.pallas_call(
        functools.partial(load_kernel, sizes),
        out_shape=(lines(rows), lines(2 * rows)),
        in_specs=[hbm] * 2,
        scratch_shapes=[
            pltpu.VMEM((rows * width, LANES), f32),
            pltpu.SemaphoreType.DMA((2,)),
        ],
        compiler_params=limit,
    )(
        *(
            pltpu.with_memory_space_constraint(to_lines(a), pltpu.HBM)
            for a in (field, conduct)
        )
    )
    field_lines, turned, outer_late = lax.optimization_barrier((field_lines, turned, outer_late))

    def gather_pairs(rows_sent, both_other, below):
        return lax.all_gather(rows_sent, "wide", axis_index_groups=pairs, axis=0, tiled=True)

    def pass_rows(rows_sent, both_other, below):
        return jnp.concatenate([both_other[:width], below], 0)

    rows_came = lax.cond(in_first, pass_rows, gather_pairs, outer_late, both_came, below)
    heights = pl.pallas_call(
        functools.partial(height_kernel, sizes),
        out_shape=jax.ShapeDtypeStruct(((row_total + 2) * chunks, LANES), f32),
        compiler_params=limit,
    )(handed, came)

    sent, p, u, v, left_gain, right_gain, joint = pl.pallas_call(
        functools.partial(main_kernel, sizes),
        out_shape=(lines(wide_count),)
        + (lines(rows),) * 3
        + (lines(wide_count),) * 2
        + (lines(8),),
        scratch_shapes=[
            pltpu.VMEM((4 * wide_count * width, LANES), f32),
            pltpu.VMEM((2 * wide_count * width, LANES), f32),
            pltpu.VMEM((2 * width, LANES), f32),
            pltpu.VMEM((rows * width, LANES), f32),
        ],
        compiler_params=limit,
    )(heights, rows_came, came, turned)

    came = lax.all_to_all(
        sent.reshape(wide_count, width, LANES), "wide", split_axis=0, concat_axis=0
    ).reshape(wide_count * width, LANES)

    advanced = pl.pallas_call(
        functools.partial(last_kernel, sizes),
        out_shape=lines(rows),
        compiler_params=limit,
    )(came, left_gain, right_gain, joint, p, u, v, field_lines)
    return from_lines(advanced, field.shape)


def solution(mesh):
    return jax.shard_map(
        on_device,
        mesh=mesh,
        in_specs=(
            P("wide", "grp", None),
            P("wide", "grp", None),
            P("grp", None),
            P("grp"),
            P("grp"),
            P(),
        ),
        out_specs=P("wide", "grp", None),
        check_vma=False,
    )
```

```python
import functools
import math

import jax
import jax.numpy as jnp
from jax import lax
from jax.experimental import pallas as pl
from jax.experimental.pallas import tpu as pltpu
from jax.sharding import PartitionSpec as P

time_step = 600.0
implicit_weight = 0.5
weight = implicit_weight * time_step
LANES = 128
f32 = jnp.float32


def to_lines(block):
    rows, layers, columns = block.shape
    chunks = columns // LANES
    return (
        block.reshape(rows, layers, chunks, LANES)
        .transpose(0, 2, 1, 3)
        .reshape(rows * chunks * layers, LANES)
    )


def from_lines(lines, shape):
    rows, layers, columns = shape
    chunks = columns // LANES
    return (
        lines.reshape(rows, chunks, layers, LANES)
        .transpose(0, 2, 1, 3)
        .reshape(rows, layers, columns)
    )


def turns(wave, index, period):
    product = wave * index
    if period & (period - 1) == 0:
        product = product & (period - 1)
    else:
        product = lax.rem(product, jnp.int32(period))
    return product.astype(f32) * (1.0 / period)


def cos_sin(turn):
    part = turn - jnp.floor(turn + 0.5)
    square = part * part

    def series(first):
        terms = [
            (-1.0) ** n * math.pi ** (2 * n + first) / math.factorial(2 * n + first)
            for n in range(7)
        ]
        total = jnp.full_like(square, terms[-1])
        for term in terms[-2::-1]:
            total = total * square + term
        return total

    half_cos = series(0)
    half_sin = series(1) * part
    return 1.0 - 2.0 * half_sin * half_sin, 2.0 * half_sin * half_cos


def halves(values):
    high = values.astype(jnp.bfloat16)
    return high, (values - high.astype(f32)).astype(jnp.bfloat16)


def height_lines(modes, first_row, count, row_total, chunks, column_total):
    mode_count = modes.shape[0]
    wave_x = modes[:, 0:1].astype(jnp.int32)
    wave_y = modes[:, 1:2].astype(jnp.int32)
    offset = modes[:, 2:3]
    amp = modes[:, 3:4]
    spot = lax.broadcasted_iota(jnp.int32, (mode_count, count * chunks), 1)
    chunk = spot % chunks
    row = jnp.clip(first_row + spot // chunks, 0, row_total - 1)
    angle = (
        turns(wave_y, row, row_total) + turns(wave_x, chunk * LANES, column_total)
    ) + offset
    left_cos, left_sin = cos_sin(angle)
    lane = lax.broadcasted_iota(jnp.int32, (mode_count, LANES), 1)
    right_cos, right_sin = cos_sin(turns(wave_x, lane, column_total))
    left = jnp.concatenate([amp * left_cos, amp * left_sin], 0)
    right = jnp.concatenate([right_cos, -right_sin], 0)
    left_high, left_low = halves(left)
    right_high, right_low = halves(right)
    return lax.dot_general(
        jnp.concatenate([left_high, left_high, left_low], 0),
        jnp.concatenate([right_high, right_low, right_high], 0),
        (((0,), (0,)), ((), ())),
        preferred_element_type=f32,
    )


def inverse(values):
    return pl.reciprocal(values, approx=False)


def from_left(values, stride, lane):
    moved = [pltpu.roll(v, stride, 1) for v in values]
    return [jnp.where(lane < stride, moved[c - 1], moved[c]) for c in range(len(values))]


def from_right(values, stride, lane):
    count = len(values)
    moved = [pltpu.roll(v, LANES - stride, 1) for v in values]
    return [
        jnp.where(lane >= LANES - stride, moved[(c + 1) % count], moved[c]) for c in range(count)
    ]


def solve_chunks(diagonal, link, rhs):
    count = len(rhs)
    if count == 1:
        return [rhs[0] * inverse(diagonal[0])]
    inv = {i: inverse(diagonal[i]) for i in range(0, count, 2)}
    scaled = {i: inv[i] * rhs[i] for i in inv}
    odd_diagonal, odd_link, odd_rhs = [], [], []
    for i in range(1, count, 2):
        d = diagonal[i] - link[i - 1] * (link[i - 1] * inv[i - 1])
        r = rhs[i] + link[i - 1] * scaled[i - 1]
        e = None
        if i + 1 < count:
            by = link[i] * inv[i + 1]
            d = d - link[i] * by
            r = r + link[i] * scaled[i + 1]
            e = by * link[i + 1] if i + 2 < count else None
        odd_diagonal.append(d)
        odd_rhs.append(r)
        odd_link.append(e)
    odd = solve_chunks(odd_diagonal, odd_link, odd_rhs)
    out = [None] * count
    out[1::2] = odd
    for i in range(0, count, 2):
        r = rhs[i]
        if i > 0:
            r = r + link[i - 1] * out[i - 1]
        if i + 1 < count:
            r = r + link[i] * out[i + 1]
        out[i] = r * inv[i]
    return out


def reduce_lanes(diagonal, link, rhs, lane, stride):
    count = len(rhs)
    while stride < LANES:
        high_r = from_right(rhs, stride, lane)
        high_e = from_right(link, stride, lane)
        inv = [inverse(d) for d in diagonal]
        w = [q * e for q, e in zip(inv, link)]
        low_d = from_left([e * v for e, v in zip(link, w)], stride, lane)
        low_r = from_left([r * v for r, v in zip(rhs, w)], stride, lane)
        by = [e * q for e, q in zip(link, from_right(inv, stride, lane))]
        diagonal = [diagonal[c] - low_d[c] - link[c] * by[c] for c in range(count)]
        rhs = [rhs[c] + low_r[c] + by[c] * high_r[c] for c in range(count)]
        link = [by[c] * high_e[c] for c in range(count)]
        stride *= 2
    return solve_chunks(diagonal, link, rhs)


def pack_pair(a, b, odd_lane):
    even = [jnp.where(odd_lane, pltpu.roll(x, 1, 1), y) for x, y in zip(a, b)]
    odd = [jnp.where(odd_lane, x, pltpu.roll(y, LANES - 1, 1)) for x, y in zip(a, b)]
    return even, odd


def unpack_pair(even, odd, odd_lane):
    a = [jnp.where(odd_lane, y, pltpu.roll(x, LANES - 1, 1)) for x, y in zip(even, odd)]
    b = [jnp.where(odd_lane, pltpu.roll(y, 1, 1), x) for x, y in zip(even, odd)]
    return a, b


def solve_x_pair(g_pair, rhs_pair, lane):
    odd_lane = (lane & 1) == 1
    first_cell = lane < 2
    last_cell = lane >= LANES - 2
    half = 0.5 * weight
    g_even, g_odd = pack_pair(*g_pair, odd_lane)
    r_even, r_odd = pack_pair(*rhs_pair, odd_lane)
    face = [half * (a + b) for a, b in zip(g_even, g_odd)]
    after = from_right(g_even, 2, lane)
    after[-1] = jnp.where(last_cell, g_odd[-1], after[-1])
    face_after = [half * (a + b) for a, b in zip(g_odd, after)]
    face_before = from_left(face_after, 2, lane)
    face_before[0] = jnp.where(first_cell, weight * g_even[0], face_before[0])
    inv = [inverse(1.0 + (a + b)) for a, b in zip(face_before, face)]
    d_odd = [1.0 + (a + b) for a, b in zip(face, face_after)]
    link = list(face_after)
    link[-1] = jnp.where(last_cell, 0.0, link[-1])
    link_before = list(face_before)
    link_before[0] = jnp.where(first_cell, 0.0, link_before[0])
    t = [q * r for q, r in zip(inv, r_even)]
    w = [q * e for q, e in zip(inv, face)]
    next_q = from_right(inv, 2, lane)
    next_t = from_right(t, 2, lane)
    next_w = from_right(w, 2, lane)
    diagonal = [
        d - e * v - l * (l * q) for d, e, v, l, q in zip(d_odd, face, w, link, next_q)
    ]
    rhs = [r + e * v + l * n for r, e, v, l, n in zip(r_odd, face, t, link, next_t)]
    x_odd = reduce_lanes(diagonal, [l * n for l, n in zip(link, next_w)], rhs, lane, 2)
    x_before = from_left(x_odd, 2, lane)
    x_even = [
        v + q * (l * b) + u * x for v, q, l, b, u, x in zip(t, inv, link_before, x_before, w, x_odd)
    ]
    return unpack_pair(x_even, x_odd, odd_lane)


def pack_kernel(
    step_ref, index_ref, amp_ref, phase_ref, field_ref,
    packed_ref, both_ref, outer_ref,
    index_in, amp_in, phase_in, sems,
):
    width = outer_ref.shape[0]
    last = field_ref.shape[0] - width
    odd = lax.rem(lax.axis_index("wide"), 2)
    inner_rows = pl.ds(pl.multiple_of((1 - odd) * last, 8), width)
    outer_rows = pl.ds(pl.multiple_of(odd * last, 8), width)
    pairs = (
        (index_ref, index_in),
        (amp_ref, amp_in),
        (phase_ref, phase_in),
        (field_ref.at[inner_rows], both_ref.at[pl.ds(0, width)]),
        (field_ref.at[outer_rows], both_ref.at[pl.ds(width, width)]),
        (field_ref.at[outer_rows], outer_ref),
    )
    copies = [pltpu.make_async_copy(a, b, sems.at[n]) for n, (a, b) in enumerate(pairs)]
    for copy in copies:
        copy.start()
    for copy in copies[:3]:
        copy.wait()
    count = index_in.shape[0]
    row = lax.broadcasted_iota(jnp.int32, packed_ref.shape, 0)
    lane = lax.broadcasted_iota(jnp.int32, packed_ref.shape, 1)
    total = jnp.zeros(packed_ref.shape, f32)
    for m in range(count):
        moment = lax.rem(index_in[m, 2] * step_ref[0], jnp.int32(64)).astype(f32)
        offset = phase_in[m] * (0.5 / math.pi) + moment * (1.0 / 64.0)
        for place, value in enumerate(
            (index_in[m, 0].astype(f32), index_in[m, 1].astype(f32), offset, amp_in[m])
        ):
            total = jnp.where((row == m) & (lane == place), value, total)
    packed_ref[...] = total
    for copy in copies[3:]:
        copy.wait()


def load_kernel(sizes, field_ref, conduct_ref, field_out, turned_ref, conduct_in, sems):
    rows, layers, chunks, row_total, layer_total, column_total = sizes
    width = layers * chunks
    copies = (
        pltpu.make_async_copy(field_ref, field_out, sems.at[0]),
        pltpu.make_async_copy(conduct_ref, conduct_in, sems.at[1]),
    )
    for copy in copies:
        copy.start()
    for n, (copy, ref) in enumerate(zip(copies, (field_out, conduct_in))):
        copy.wait()
        for place in range(width):
            spot = (n * width + place) * rows
            turned_ref[spot : spot + rows] = ref[pl.ds(place, rows, stride=width), :]


def block_factors(face):
    inv, scaled, chain, u = [], [], [], []
    rows = len(face) - 1
    rest = 1.0 + face[0]
    for j in range(rows):
        inv.append(inverse(rest + face[j + 1]))
        scaled.append(face[j] * inv[j])
        chain.append(face[j + 1] * inv[j])
        u.append(scaled[j] * u[-1] if j else scaled[j])
        rest = 1.0 + rest * chain[j]
    v = list(chain)
    for j in range(rows - 2, -1, -1):
        u[j] = u[j] + chain[j] * u[j + 1]
        v[j] = chain[j] * v[j + 1]
    return inv, scaled, chain, u, v


def height_kernel(sizes, handed_ref, came_ref, heights_ref):
    rows, layers, chunks, row_total, layer_total, column_total = sizes
    odd = lax.rem(lax.axis_index("wide"), 2) == 1
    modes = jnp.where(odd, handed_ref[layers * chunks :], came_ref[layers * chunks :])
    body = height_lines(modes, 0, row_total, row_total, chunks, column_total)
    heights_ref[chunks : (row_total + 1) * chunks] = body
    heights_ref[0:chunks] = body[0:chunks]
    heights_ref[(row_total + 1) * chunks : (row_total + 2) * chunks] = body[
        (row_total - 1) * chunks : row_total * chunks
    ]

def main_kernel(
    sizes, heights, both_ref, below_ref, came_ref, turned_ref,
    sent_ref, p_ref, u_ref, v_ref, gain_ref, joint_ref,
    halo, solved,
):
    rows, layers, chunks, row_total, layer_total, column_total = sizes
    width = layers * chunks
    blocks = row_total // rows
    me = lax.axis_index("wide")
    first_layer = lax.axis_index("grp") * layers
    zeta = [
        ((first_layer + k).astype(f32) + 0.5) * (1.0 / layer_total) for k in range(layers)
    ]
    half = 0.5 * weight
    own_start = pl.multiple_of(me * (rows * chunks), 8)

    def face(low, high):
        both = heights[pl.ds(low, chunks), :] + heights[pl.ds(high, chunks), :]
        return jnp.concatenate([weight + (half * z) * both for z in zeta], 0)

    def aligned(index):
        return pl.multiple_of(index, 8)

    inv, scaled, chain, u, v = block_factors(
        [face(own_start + j * chunks, own_start + (j + 1) * chunks) for j in range(rows + 1)]
    )
    for j in range(rows):
        u_ref[j * width : (j + 1) * width] = u[j]
        v_ref[j * width : (j + 1) * width] = v[j]

    def one_block(n, carry):
        rest, link, left_link = carry
        upward = n < me
        b = jnp.where(upward, n, blocks - 1 - (n - me))
        start = b * (rows * chunks) + jnp.where(upward, 0, (rows + 1) * chunks)
        step = jnp.where(upward, chunks, -chunks)
        places = [aligned(start + j * step) for j in range(rows + 2)]
        first = face(places[0], places[1])
        anew = (n == 0) | (n == me)
        left_link = jnp.where(n == me, link, left_link)
        rest = jnp.where(anew, 1.0 + first, rest)
        for j in range(rows):
            after = face(places[j + 1], places[j + 2])
            link = after * inverse(rest + after)
            through = through * link if j else link
            rest = 1.0 + rest * link
        gain_ref[pl.ds(aligned(b * width), width), :] = through * (first * inverse(after))
        return rest, link, left_link

    gain_ref[pl.ds(aligned(me * width), width), :] = u[-1]
    nothing = 0.0 * u[0]
    carry = (nothing, nothing, nothing)
    if blocks <= 8:
        for n in range(blocks - 1):
            carry = one_block(n, carry)
    else:
        carry = lax.fori_loop(0, blocks - 1, one_block, carry)
    _, link, left_link = carry
    left_link = jnp.where(me == blocks - 1, link, left_link)
    right_link = jnp.where(me == blocks - 1, 0.0, link)

    a = 1.0 - left_link * u[0]
    b = left_link * v[0]
    c = right_link * u[-1]
    d = 1.0 - right_link * v[-1]
    by = inverse(a * d - b * c)
    joint = (
        u[-1] * inverse(a) * left_link, v[0] * inverse(d) * right_link,
        left_link, right_link, d * by, b * by, c * by, a * by,
    )
    for n, value in enumerate(joint):
        joint_ref[n * width : (n + 1) * width] = value

    odd = lax.rem(me, 2) == 1
    inner = both_ref[0:width]
    below = jnp.where(odd, inner, below_ref[...])
    above = jnp.where(odd, came_ref[0:width], inner)
    halo[0:width] = jnp.where(me == 0, 0.0, below)
    halo[width : 2 * width] = jnp.where(me == blocks - 1, 0.0, above)
    lane = lax.broadcasted_iota(jnp.int32, (rows, LANES), 1)
    row = lax.broadcasted_iota(jnp.int32, (rows, LANES), 0)

    def neighbours(values, low, high):
        return (
            jnp.where(row == 0, low, pltpu.roll(values, 1, 0)),
            jnp.where(row == rows - 1, high, pltpu.roll(values, rows - 1, 0)),
        )

    g = [[] for _ in range(layers)]
    f = [[] for _ in range(layers)]
    rhs = [[] for _ in range(layers)]
    for c in range(chunks):
        h = heights[pl.ds(own_start + chunks + c, rows, stride=chunks), :]
        h_low, h_high = neighbours(
            h,
            heights[pl.ds(own_start + c, 1), :],
            heights[pl.ds(own_start + (rows + 1) * chunks + c, 1), :],
        )
        low_sum, high_sum = h + h_low, h + h_high
        for k in range(layers):
            place = c * layers + k
            f_mid = turned_ref[place * rows : (place + 1) * rows]
            f_low, f_high = neighbours(
                f_mid, halo[pl.ds(place, 1), :], halo[pl.ds(width + place, 1), :]
            )
            g[k].append(
                turned_ref[(width + place) * rows : (width + place + 1) * rows] * (1.0 + zeta[k] * h)
            )
            f[k].append(f_mid)
            along = (weight + (half * zeta[k]) * high_sum) * (f_high - f_mid) - (
                weight + (half * zeta[k]) * low_sum
            ) * (f_mid - f_low)
            rhs[k].append(2.0 * (f_mid + along))
    for k in range(0, layers, 2):
        both = solve_x_pair(g[k : k + 2], rhs[k : k + 2], lane)
        for n in range(2):
            for c in range(chunks):
                spot = pl.ds((k + n) * chunks + c, rows, stride=width)
                solved[spot, :] = both[n][c] - 2.0 * f[k + n][c]

    def part(ref, j):
        return ref[j * width : (j + 1) * width]

    p = [part(solved, 0) * inv[0]]
    for j in range(1, rows):
        p.append(part(solved, j) * inv[j] + scaled[j] * p[-1])
    for j in range(rows - 2, -1, -1):
        p[j] = p[j] + chain[j] * p[j + 1]
    for j in range(rows):
        p_ref[j * width : (j + 1) * width] = p[j]

    upward = p[-1] + part(joint_ref, 0) * p[0]
    downward = p[0] + part(joint_ref, 1) * p[-1]
    for b in range(blocks):
        sent_ref[b * width : (b + 1) * width] = jnp.where(b > me, upward, downward)


def last_kernel(
    sizes, came_ref, gain_ref, joint_ref, p_ref, u_ref, v_ref, field_ref,
    out_ref,
):
    rows, layers, chunks, row_total, layer_total, column_total = sizes
    width = layers * chunks
    blocks = row_total // rows
    me = lax.axis_index("wide")

    def part(ref, b):
        return ref[b * width : (b + 1) * width]

    left = jnp.zeros((width, LANES), f32)
    right = jnp.zeros((width, LANES), f32)
    for b in range(blocks - 1):
        left = jnp.where(b < me, part(came_ref, b) + part(gain_ref, b) * left, left)
        b = blocks - 1 - b
        right = jnp.where(b > me, part(came_ref, b) + part(gain_ref, b) * right, right)

    y = left + part(joint_ref, 2) * part(p_ref, 0)
    z = right + part(joint_ref, 3) * part(p_ref, rows - 1)
    before = part(joint_ref, 4) * y + part(joint_ref, 5) * z
    after = part(joint_ref, 6) * y + part(joint_ref, 7) * z
    for j in range(rows):
        x = part(p_ref, j) + part(u_ref, j) * before + part(v_ref, j) * after
        for k in range(layers):
            spot = pl.ds(j * width + k, chunks, stride=layers)
            out_ref[spot, :] = field_ref[spot, :] + x[k * chunks : (k + 1) * chunks]


def on_device(field, conduct, mode_index, mode_amp, mode_phase, step_index):
    rows, layers, columns = field.shape
    wide_count = lax.axis_size("wide")
    row_total = rows * wide_count
    grp_count = lax.axis_size("grp")
    layer_total = layers * grp_count
    chunks = columns // LANES
    width = layers * chunks
    sizes = (rows, layers, chunks, row_total, layer_total, columns)
    limit = pltpu.CompilerParams(vmem_limit_bytes=16 * 1024 * 1024)
    hbm = pl.BlockSpec(memory_space=pltpu.HBM)

    def lines(count):
        return jax.ShapeDtypeStruct((count * width, LANES), f32)

    step_index, mode_index, mode_amp, mode_phase, field_lines, conduct_lines = (
        step_index,
        *(
            pltpu.with_memory_space_constraint(a, pltpu.HBM)
            for a in (mode_index, mode_amp, mode_phase, to_lines(field), to_lines(conduct))
        ),
    )
    packed, both, outer = pl.pallas_call(
        pack_kernel,
        out_shape=(
            jax.ShapeDtypeStruct((mode_index.shape[0], LANES), f32),
            lines(2),
            lines(1),
        ),
        in_specs=[pl.BlockSpec(memory_space=pltpu.SMEM)] + [hbm] * 4,
        scratch_shapes=[
            pltpu.SMEM(mode_index.shape, jnp.int32),
            pltpu.SMEM(mode_amp.shape, f32),
            pltpu.SMEM(mode_phase.shape, f32),
            pltpu.SemaphoreType.DMA((6,)),
        ],
        compiler_params=limit,
    )(step_index, mode_index, mode_amp, mode_phase, field_lines)

    place = lax.axis_index("wide")
    odd = place % 2 == 1
    swaps = [(i, i ^ 1) for i in range(wide_count)]
    cores = [list(range(n, wide_count, 2)) for n in range(2)]
    both_came = lax.ppermute(both, "wide", swaps)

    def gather_modes(own):
        return lax.all_gather(own, "grp", axis=0, tiled=True)

    def no_modes(own):
        return jnp.zeros((grp_count * own.shape[0], own.shape[1]), f32)

    modes = lax.cond(odd, gather_modes, no_modes, packed)
    modes, outer, both_came = lax.optimization_barrier((modes, outer, both_came))

    def gather_rows(own, came):
        rows_sent = jnp.concatenate([own, came[width:]], 0)
        rows_all = lax.all_gather(rows_sent, "wide", axis_index_groups=cores, axis=0)
        chip = place // 2
        below = lax.dynamic_index_in_dim(rows_all, jnp.maximum(chip - 1, 0), 0, False)
        above = lax.dynamic_index_in_dim(
            rows_all, jnp.minimum(chip + 1, wide_count // 2 - 1), 0, False
        )
        return below[width:], above[:width]

    def no_rows(own, came):
        return jnp.zeros_like(own), jnp.zeros_like(own)

    below, above = lax.cond(odd, no_rows, gather_rows, outer, both_came)
    handed = jnp.concatenate([above, modes], 0)
    came = lax.ppermute(handed, "wide", swaps)
    handed, field, conduct = lax.optimization_barrier((handed, field, conduct))
    field_lines, turned = pl.pallas_call(
        functools.partial(load_kernel, sizes),
        out_shape=(lines(rows), lines(2 * rows)),
        in_specs=[hbm] * 2,
        scratch_shapes=[
            pltpu.VMEM((rows * width, LANES), f32),
            pltpu.SemaphoreType.DMA((2,)),
        ],
        compiler_params=limit,
    )(
        *(
            pltpu.with_memory_space_constraint(to_lines(a), pltpu.HBM)
            for a in (field, conduct)
        )
    )
    heights = pl.pallas_call(
        functools.partial(height_kernel, sizes),
        out_shape=jax.ShapeDtypeStruct(((row_total + 2) * chunks, LANES), f32),
        compiler_params=limit,
    )(handed, came)

    sent, p, u, v, gain, joint = pl.pallas_call(
        functools.partial(main_kernel, sizes),
        out_shape=(lines(wide_count),)
        + (lines(rows),) * 3
        + (lines(wide_count), lines(8)),
        scratch_shapes=[
            pltpu.VMEM((2 * width, LANES), f32),
            pltpu.VMEM((rows * width, LANES), f32),
        ],
        compiler_params=limit,
    )(heights, both_came, below, came, turned)

    came = lax.all_to_all(
        sent.reshape(wide_count, width, LANES), "wide", split_axis=0, concat_axis=0
    ).reshape(wide_count * width, LANES)

    advanced = pl.pallas_call(
        functools.partial(last_kernel, sizes),
        out_shape=lines(rows),
        compiler_params=limit,
    )(came, gain, joint, p, u, v, field_lines)
    return from_lines(advanced, field.shape)


def solution(mesh):
    return jax.shard_map(
        on_device,
        mesh=mesh,
        in_specs=(
            P("wide", "grp", None),
            P("wide", "grp", None),
            P("grp", None),
            P("grp"),
            P("grp"),
            P(),
        ),
        out_specs=P("wide", "grp", None),
        check_vma=False,
    )
```

```python
import functools
import math

import jax
import jax.numpy as jnp
from jax import lax
from jax.experimental import pallas as pl
from jax.experimental.pallas import tpu as pltpu
from jax.sharding import PartitionSpec as P

time_step = 600.0
implicit_weight = 0.5
weight = implicit_weight * time_step
LANES = 128
f32 = jnp.float32


def to_lines(block):
    rows, layers, columns = block.shape
    chunks = columns // LANES
    return (
        block.reshape(rows, layers, chunks, LANES)
        .transpose(0, 2, 1, 3)
        .reshape(rows * chunks * layers, LANES)
    )


def from_lines(lines, shape):
    rows, layers, columns = shape
    chunks = columns // LANES
    return (
        lines.reshape(rows, chunks, layers, LANES)
        .transpose(0, 2, 1, 3)
        .reshape(rows, layers, columns)
    )


def turns(wave, index, period):
    product = wave * index
    if period & (period - 1) == 0:
        product = product & (period - 1)
    else:
        product = lax.rem(product, jnp.int32(period))
    return product.astype(f32) * (1.0 / period)


def cos_sin(turn):
    part = turn - jnp.floor(turn + 0.5)
    square = part * part

    def series(first):
        terms = [
            (-1.0) ** n * math.pi ** (2 * n + first) / math.factorial(2 * n + first)
            for n in range(7)
        ]
        total = jnp.full_like(square, terms[-1])
        for term in terms[-2::-1]:
            total = total * square + term
        return total

    half_cos = series(0)
    half_sin = series(1) * part
    return 1.0 - 2.0 * half_sin * half_sin, 2.0 * half_sin * half_cos


def halves(values):
    high = values.astype(jnp.bfloat16)
    return high, (values - high.astype(f32)).astype(jnp.bfloat16)


def height_lines(modes, first_row, count, row_total, chunks, column_total):
    mode_count = modes.shape[0]
    wave_x = modes[:, 0:1].astype(jnp.int32)
    wave_y = modes[:, 1:2].astype(jnp.int32)
    offset = modes[:, 2:3]
    amp = modes[:, 3:4]
    spot = lax.broadcasted_iota(jnp.int32, (mode_count, count * chunks), 1)
    chunk = spot % chunks
    row = jnp.clip(first_row + spot // chunks, 0, row_total - 1)
    angle = (
        turns(wave_y, row, row_total) + turns(wave_x, chunk * LANES, column_total)
    ) + offset
    left_cos, left_sin = cos_sin(angle)
    lane = lax.broadcasted_iota(jnp.int32, (mode_count, LANES), 1)
    right_cos, right_sin = cos_sin(turns(wave_x, lane, column_total))
    left = jnp.concatenate([amp * left_cos, amp * left_sin], 0)
    right = jnp.concatenate([right_cos, -right_sin], 0)
    left_high, left_low = halves(left)
    right_high, right_low = halves(right)
    return lax.dot_general(
        jnp.concatenate([left_high, left_high, left_low], 0),
        jnp.concatenate([right_high, right_low, right_high], 0),
        (((0,), (0,)), ((), ())),
        preferred_element_type=f32,
    )


def inverse(values):
    return pl.reciprocal(values, approx=False)


def from_left(values, stride, lane):
    moved = [pltpu.roll(v, stride, 1) for v in values]
    return [jnp.where(lane < stride, moved[c - 1], moved[c]) for c in range(len(values))]


def from_right(values, stride, lane):
    count = len(values)
    moved = [pltpu.roll(v, LANES - stride, 1) for v in values]
    return [
        jnp.where(lane >= LANES - stride, moved[(c + 1) % count], moved[c]) for c in range(count)
    ]


def solve_chunks(diagonal, link, rhs):
    count = len(rhs)
    if count == 1:
        return [rhs[0] * inverse(diagonal[0])]
    inv = {i: inverse(diagonal[i]) for i in range(0, count, 2)}
    scaled = {i: inv[i] * rhs[i] for i in inv}
    odd_diagonal, odd_link, odd_rhs = [], [], []
    for i in range(1, count, 2):
        d = diagonal[i] - link[i - 1] * (link[i - 1] * inv[i - 1])
        r = rhs[i] + link[i - 1] * scaled[i - 1]
        e = None
        if i + 1 < count:
            by = link[i] * inv[i + 1]
            d = d - link[i] * by
            r = r + link[i] * scaled[i + 1]
            e = by * link[i + 1] if i + 2 < count else None
        odd_diagonal.append(d)
        odd_rhs.append(r)
        odd_link.append(e)
    odd = solve_chunks(odd_diagonal, odd_link, odd_rhs)
    out = [None] * count
    out[1::2] = odd
    for i in range(0, count, 2):
        r = rhs[i]
        if i > 0:
            r = r + link[i - 1] * out[i - 1]
        if i + 1 < count:
            r = r + link[i] * out[i + 1]
        out[i] = r * inv[i]
    return out


def reduce_lanes(diagonal, link, rhs, lane, stride):
    count = len(rhs)
    while stride < LANES:
        high_r = from_right(rhs, stride, lane)
        high_e = from_right(link, stride, lane)
        inv = [inverse(d) for d in diagonal]
        w = [q * e for q, e in zip(inv, link)]
        low_d = from_left([e * v for e, v in zip(link, w)], stride, lane)
        low_r = from_left([r * v for r, v in zip(rhs, w)], stride, lane)
        by = [e * q for e, q in zip(link, from_right(inv, stride, lane))]
        diagonal = [diagonal[c] - low_d[c] - link[c] * by[c] for c in range(count)]
        rhs = [rhs[c] + low_r[c] + by[c] * high_r[c] for c in range(count)]
        link = [by[c] * high_e[c] for c in range(count)]
        stride *= 2
    return solve_chunks(diagonal, link, rhs)


def pack_pair(a, b, odd_lane):
    even = [jnp.where(odd_lane, pltpu.roll(x, 1, 1), y) for x, y in zip(a, b)]
    odd = [jnp.where(odd_lane, x, pltpu.roll(y, LANES - 1, 1)) for x, y in zip(a, b)]
    return even, odd


def unpack_pair(even, odd, odd_lane):
    a = [jnp.where(odd_lane, y, pltpu.roll(x, LANES - 1, 1)) for x, y in zip(even, odd)]
    b = [jnp.where(odd_lane, pltpu.roll(y, 1, 1), x) for x, y in zip(even, odd)]
    return a, b


def solve_x_pair(g_pair, rhs_pair, lane):
    odd_lane = (lane & 1) == 1
    first_cell = lane < 2
    last_cell = lane >= LANES - 2
    half = 0.5 * weight
    g_even, g_odd = pack_pair(*g_pair, odd_lane)
    r_even, r_odd = pack_pair(*rhs_pair, odd_lane)
    face = [half * (a + b) for a, b in zip(g_even, g_odd)]
    after = from_right(g_even, 2, lane)
    after[-1] = jnp.where(last_cell, g_odd[-1], after[-1])
    face_after = [half * (a + b) for a, b in zip(g_odd, after)]
    face_before = from_left(face_after, 2, lane)
    face_before[0] = jnp.where(first_cell, weight * g_even[0], face_before[0])
    inv = [inverse(1.0 + (a + b)) for a, b in zip(face_before, face)]
    d_odd = [1.0 + (a + b) for a, b in zip(face, face_after)]
    link = list(face_after)
    link[-1] = jnp.where(last_cell, 0.0, link[-1])
    link_before = list(face_before)
    link_before[0] = jnp.where(first_cell, 0.0, link_before[0])
    t = [q * r for q, r in zip(inv, r_even)]
    w = [q * e for q, e in zip(inv, face)]
    next_q = from_right(inv, 2, lane)
    next_t = from_right(t, 2, lane)
    next_w = from_right(w, 2, lane)
    diagonal = [
        d - e * v - l * (l * q) for d, e, v, l, q in zip(d_odd, face, w, link, next_q)
    ]
    rhs = [r + e * v + l * n for r, e, v, l, n in zip(r_odd, face, t, link, next_t)]
    x_odd = reduce_lanes(diagonal, [l * n for l, n in zip(link, next_w)], rhs, lane, 2)
    x_before = from_left(x_odd, 2, lane)
    x_even = [
        v + q * (l * b) + u * x for v, q, l, b, u, x in zip(t, inv, link_before, x_before, w, x_odd)
    ]
    return unpack_pair(x_even, x_odd, odd_lane)


def pack_kernel(
    step_ref, index_ref, amp_ref, phase_ref, field_ref,
    packed_ref, both_ref, outer_ref,
    index_in, amp_in, phase_in, sems,
):
    width = outer_ref.shape[0]
    last = field_ref.shape[0] - width
    odd = lax.rem(lax.axis_index("wide"), 2)
    inner_rows = pl.ds(pl.multiple_of((1 - odd) * last, 8), width)
    outer_rows = pl.ds(pl.multiple_of(odd * last, 8), width)
    pairs = (
        (index_ref, index_in),
        (amp_ref, amp_in),
        (phase_ref, phase_in),
        (field_ref.at[inner_rows], both_ref.at[pl.ds(0, width)]),
        (field_ref.at[outer_rows], both_ref.at[pl.ds(width, width)]),
        (field_ref.at[outer_rows], outer_ref),
    )
    copies = [pltpu.make_async_copy(a, b, sems.at[n]) for n, (a, b) in enumerate(pairs)]
    for copy in copies:
        copy.start()
    for copy in copies[:3]:
        copy.wait()
    count = index_in.shape[0]
    row = lax.broadcasted_iota(jnp.int32, packed_ref.shape, 0)
    lane = lax.broadcasted_iota(jnp.int32, packed_ref.shape, 1)
    total = jnp.zeros(packed_ref.shape, f32)
    for m in range(count):
        moment = lax.rem(index_in[m, 2] * step_ref[0], jnp.int32(64)).astype(f32)
        offset = phase_in[m] * (0.5 / math.pi) + moment * (1.0 / 64.0)
        for place, value in enumerate(
            (index_in[m, 0].astype(f32), index_in[m, 1].astype(f32), offset, amp_in[m])
        ):
            total = jnp.where((row == m) & (lane == place), value, total)
    packed_ref[...] = total
    for copy in copies[3:]:
        copy.wait()


def load_kernel(sizes, field_ref, conduct_ref, field_out, turned_ref, conduct_in, sems):
    rows, layers, chunks, row_total, layer_total, column_total = sizes
    width = layers * chunks
    copies = (
        pltpu.make_async_copy(field_ref, field_out, sems.at[0]),
        pltpu.make_async_copy(conduct_ref, conduct_in, sems.at[1]),
    )
    for copy in copies:
        copy.start()
    for n, (copy, ref) in enumerate(zip(copies, (field_out, conduct_in))):
        copy.wait()
        for place in range(width):
            spot = (n * width + place) * rows
            turned_ref[spot : spot + rows] = ref[pl.ds(place, rows, stride=width), :]


def block_factors(face):
    inv, scaled, chain, u = [], [], [], []
    rows = len(face) - 1
    rest = 1.0 + face[0]
    for j in range(rows):
        inv.append(inverse(rest + face[j + 1]))
        scaled.append(face[j] * inv[j])
        chain.append(face[j + 1] * inv[j])
        u.append(scaled[j] * u[-1] if j else scaled[j])
        rest = 1.0 + rest * chain[j]
    v = list(chain)
    for j in range(rows - 2, -1, -1):
        u[j] = u[j] + chain[j] * u[j + 1]
        v[j] = chain[j] * v[j + 1]
    return inv, scaled, chain, u, v


def height_kernel(sizes, handed_ref, came_ref, heights_ref):
    rows, layers, chunks, row_total, layer_total, column_total = sizes
    odd = lax.rem(lax.axis_index("wide"), 2) == 1
    modes = jnp.where(odd, handed_ref[layers * chunks :], came_ref[layers * chunks :])
    body = height_lines(modes, 0, row_total, row_total, chunks, column_total)
    heights_ref[chunks : (row_total + 1) * chunks] = body
    heights_ref[0:chunks] = body[0:chunks]
    heights_ref[(row_total + 1) * chunks : (row_total + 2) * chunks] = body[
        (row_total - 1) * chunks : row_total * chunks
    ]

def main_kernel(
    sizes, heights, both_ref, below_ref, came_ref, turned_ref,
    sent_ref, p_ref, u_ref, v_ref, gain_ref, joint_ref,
    halo, solved,
):
    rows, layers, chunks, row_total, layer_total, column_total = sizes
    width = layers * chunks
    blocks = row_total // rows
    me = lax.axis_index("wide")
    first_layer = lax.axis_index("grp") * layers
    zeta = [
        ((first_layer + k).astype(f32) + 0.5) * (1.0 / layer_total) for k in range(layers)
    ]
    half = 0.5 * weight
    own_start = pl.multiple_of(me * (rows * chunks), 8)

    def face(low, high):
        both = heights[pl.ds(low, chunks), :] + heights[pl.ds(high, chunks), :]
        return jnp.concatenate([weight + (half * z) * both for z in zeta], 0)

    def aligned(index):
        return pl.multiple_of(index, 8)

    own_inv, scaled, chain, u, v = block_factors(
        [face(own_start + j * chunks, own_start + (j + 1) * chunks) for j in range(rows + 1)]
    )
    for j in range(rows):
        u_ref[j * width : (j + 1) * width] = u[j]
        v_ref[j * width : (j + 1) * width] = v[j]

    def one_block(n, carry):
        passed, link, left_link = carry
        upward = n < me
        b = jnp.where(upward, n, blocks - 1 - (n - me))
        start = b * (rows * chunks) + jnp.where(upward, 0, (rows + 1) * chunks)
        step = jnp.where(upward, chunks, -chunks)
        places = [aligned(start + j * step) for j in range(rows + 2)]
        first = face(places[0], places[1])
        anew = (n == 0) | (n == me)
        left_link = jnp.where(n == me, link, left_link)
        passed = jnp.where(anew, first, passed)
        for j in range(rows):
            after = face(places[j + 1], places[j + 2])
            inv = inverse(passed + (1.0 + after))
            link = after * inv
            through = through * link if j else link
            passed = ((1.0 + passed) * after) * inv
        gain_ref[pl.ds(aligned(b * width), width), :] = through * (first * inverse(after))
        return passed, link, left_link

    gain_ref[pl.ds(aligned(me * width), width), :] = u[-1]
    nothing = 0.0 * u[0]
    carry = (nothing, nothing, nothing)
    if blocks <= 8:
        for n in range(blocks - 1):
            carry = one_block(n, carry)
    else:
        carry = lax.fori_loop(0, blocks - 1, one_block, carry)
    _, link, left_link = carry
    left_link = jnp.where(me == blocks - 1, link, left_link)
    right_link = jnp.where(me == blocks - 1, 0.0, link)

    a = 1.0 - left_link * u[0]
    b = left_link * v[0]
    c = right_link * u[-1]
    d = 1.0 - right_link * v[-1]
    by = inverse(a * d - b * c)
    joint = (
        u[-1] * inverse(a) * left_link, v[0] * inverse(d) * right_link,
        left_link, right_link, d * by, b * by, c * by, a * by,
    )
    for n, value in enumerate(joint):
        joint_ref[n * width : (n + 1) * width] = value

    odd = lax.rem(me, 2) == 1
    inner = both_ref[0:width]
    below = jnp.where(odd, inner, below_ref[...])
    above = jnp.where(odd, came_ref[0:width], inner)
    halo[0:width] = jnp.where(me == 0, 0.0, below)
    halo[width : 2 * width] = jnp.where(me == blocks - 1, 0.0, above)
    lane = lax.broadcasted_iota(jnp.int32, (rows, LANES), 1)
    row = lax.broadcasted_iota(jnp.int32, (rows, LANES), 0)

    def neighbours(values, low, high):
        return (
            jnp.where(row == 0, low, pltpu.roll(values, 1, 0)),
            jnp.where(row == rows - 1, high, pltpu.roll(values, rows - 1, 0)),
        )

    g = [[] for _ in range(layers)]
    f = [[] for _ in range(layers)]
    rhs = [[] for _ in range(layers)]
    for c in range(chunks):
        h = heights[pl.ds(own_start + chunks + c, rows, stride=chunks), :]
        h_low, h_high = neighbours(
            h,
            heights[pl.ds(own_start + c, 1), :],
            heights[pl.ds(own_start + (rows + 1) * chunks + c, 1), :],
        )
        low_sum, high_sum = h + h_low, h + h_high
        for k in range(layers):
            place = c * layers + k
            f_mid = turned_ref[place * rows : (place + 1) * rows]
            f_low, f_high = neighbours(
                f_mid, halo[pl.ds(place, 1), :], halo[pl.ds(width + place, 1), :]
            )
            g[k].append(
                turned_ref[(width + place) * rows : (width + place + 1) * rows] * (1.0 + zeta[k] * h)
            )
            f[k].append(f_mid)
            along = (weight + (half * zeta[k]) * high_sum) * (f_high - f_mid) - (
                weight + (half * zeta[k]) * low_sum
            ) * (f_mid - f_low)
            rhs[k].append(2.0 * (f_mid + along))
    for k in range(0, layers, 2):
        both = solve_x_pair(g[k : k + 2], rhs[k : k + 2], lane)
        for n in range(2):
            for c in range(chunks):
                spot = pl.ds((k + n) * chunks + c, rows, stride=width)
                solved[spot, :] = both[n][c] - 2.0 * f[k + n][c]

    def part(ref, j):
        return ref[j * width : (j + 1) * width]

    p = [part(solved, 0) * own_inv[0]]
    for j in range(1, rows):
        p.append(part(solved, j) * own_inv[j] + scaled[j] * p[-1])
    for j in range(rows - 2, -1, -1):
        p[j] = p[j] + chain[j] * p[j + 1]
    for j in range(rows):
        p_ref[j * width : (j + 1) * width] = p[j]

    upward = p[-1] + part(joint_ref, 0) * p[0]
    downward = p[0] + part(joint_ref, 1) * p[-1]
    for b in range(blocks):
        sent_ref[b * width : (b + 1) * width] = jnp.where(b > me, upward, downward)


def last_kernel(
    sizes, came_ref, gain_ref, joint_ref, p_ref, u_ref, v_ref, field_ref,
    out_ref,
):
    rows, layers, chunks, row_total, layer_total, column_total = sizes
    width = layers * chunks
    blocks = row_total // rows
    me = lax.axis_index("wide")

    def part(ref, b):
        return ref[b * width : (b + 1) * width]

    left = jnp.zeros((width, LANES), f32)
    right = jnp.zeros((width, LANES), f32)
    for b in range(blocks - 1):
        left = jnp.where(b < me, part(came_ref, b) + part(gain_ref, b) * left, left)
        b = blocks - 1 - b
        right = jnp.where(b > me, part(came_ref, b) + part(gain_ref, b) * right, right)

    y = left + part(joint_ref, 2) * part(p_ref, 0)
    z = right + part(joint_ref, 3) * part(p_ref, rows - 1)
    before = part(joint_ref, 4) * y + part(joint_ref, 5) * z
    after = part(joint_ref, 6) * y + part(joint_ref, 7) * z
    for j in range(rows):
        x = part(p_ref, j) + part(u_ref, j) * before + part(v_ref, j) * after
        for k in range(layers):
            spot = pl.ds(j * width + k, chunks, stride=layers)
            out_ref[spot, :] = field_ref[spot, :] + x[k * chunks : (k + 1) * chunks]


def on_device(field, conduct, mode_index, mode_amp, mode_phase, step_index):
    rows, layers, columns = field.shape
    wide_count = lax.axis_size("wide")
    row_total = rows * wide_count
    grp_count = lax.axis_size("grp")
    layer_total = layers * grp_count
    chunks = columns // LANES
    width = layers * chunks
    sizes = (rows, layers, chunks, row_total, layer_total, columns)
    limit = pltpu.CompilerParams(vmem_limit_bytes=16 * 1024 * 1024)
    hbm = pl.BlockSpec(memory_space=pltpu.HBM)

    def lines(count):
        return jax.ShapeDtypeStruct((count * width, LANES), f32)

    step_index, mode_index, mode_amp, mode_phase, field_lines, conduct_lines = (
        step_index,
        *(
            pltpu.with_memory_space_constraint(a, pltpu.HBM)
            for a in (mode_index, mode_amp, mode_phase, to_lines(field), to_lines(conduct))
        ),
    )
    packed, both, outer = pl.pallas_call(
        pack_kernel,
        out_shape=(
            jax.ShapeDtypeStruct((mode_index.shape[0], LANES), f32),
            lines(2),
            lines(1),
        ),
        in_specs=[pl.BlockSpec(memory_space=pltpu.SMEM)] + [hbm] * 4,
        scratch_shapes=[
            pltpu.SMEM(mode_index.shape, jnp.int32),
            pltpu.SMEM(mode_amp.shape, f32),
            pltpu.SMEM(mode_phase.shape, f32),
            pltpu.SemaphoreType.DMA((6,)),
        ],
        compiler_params=limit,
    )(step_index, mode_index, mode_amp, mode_phase, field_lines)

    place = lax.axis_index("wide")
    odd = place % 2 == 1
    swaps = [(i, i ^ 1) for i in range(wide_count)]
    cores = [list(range(n, wide_count, 2)) for n in range(2)]
    both_came = lax.ppermute(both, "wide", swaps)

    def gather_modes(own):
        return lax.all_gather(own, "grp", axis=0, tiled=True)

    def no_modes(own):
        return jnp.zeros((grp_count * own.shape[0], own.shape[1]), f32)

    modes = lax.cond(odd, gather_modes, no_modes, packed)
    modes, outer, both_came = lax.optimization_barrier((modes, outer, both_came))

    def gather_rows(own, came):
        rows_sent = jnp.concatenate([own, came[width:]], 0)
        rows_all = lax.all_gather(rows_sent, "wide", axis_index_groups=cores, axis=0)
        chip = place // 2
        below = lax.dynamic_index_in_dim(rows_all, jnp.maximum(chip - 1, 0), 0, False)
        above = lax.dynamic_index_in_dim(
            rows_all, jnp.minimum(chip + 1, wide_count // 2 - 1), 0, False
        )
        return below[width:], above[:width]

    def no_rows(own, came):
        return jnp.zeros_like(own), jnp.zeros_like(own)

    below, above = lax.cond(odd, no_rows, gather_rows, outer, both_came)
    handed = jnp.concatenate([above, modes], 0)
    came = lax.ppermute(handed, "wide", swaps)
    handed, field, conduct = lax.optimization_barrier((handed, field, conduct))
    field_lines, turned = pl.pallas_call(
        functools.partial(load_kernel, sizes),
        out_shape=(lines(rows), lines(2 * rows)),
        in_specs=[hbm] * 2,
        scratch_shapes=[
            pltpu.VMEM((rows * width, LANES), f32),
            pltpu.SemaphoreType.DMA((2,)),
        ],
        compiler_params=limit,
    )(
        *(
            pltpu.with_memory_space_constraint(to_lines(a), pltpu.HBM)
            for a in (field, conduct)
        )
    )
    heights = pl.pallas_call(
        functools.partial(height_kernel, sizes),
        out_shape=jax.ShapeDtypeStruct(((row_total + 2) * chunks, LANES), f32),
        compiler_params=limit,
    )(handed, came)

    sent, p, u, v, gain, joint = pl.pallas_call(
        functools.partial(main_kernel, sizes),
        out_shape=(lines(wide_count),)
        + (lines(rows),) * 3
        + (lines(wide_count), lines(8)),
        scratch_shapes=[
            pltpu.VMEM((2 * width, LANES), f32),
            pltpu.VMEM((rows * width, LANES), f32),
        ],
        compiler_params=limit,
    )(heights, both_came, below, came, turned)

    came = lax.all_to_all(
        sent.reshape(wide_count, width, LANES), "wide", split_axis=0, concat_axis=0
    ).reshape(wide_count * width, LANES)

    advanced = pl.pallas_call(
        functools.partial(last_kernel, sizes),
        out_shape=lines(rows),
        compiler_params=limit,
    )(came, gain, joint, p, u, v, field_lines)
    return from_lines(advanced, field.shape)


def solution(mesh):
    return jax.shard_map(
        on_device,
        mesh=mesh,
        in_specs=(
            P("wide", "grp", None),
            P("wide", "grp", None),
            P("grp", None),
            P("grp"),
            P("grp"),
            P(),
        ),
        out_specs=P("wide", "grp", None),
        check_vma=False,
    )
```

```python
import functools
import math

import jax
import jax.numpy as jnp
from jax import lax
from jax.experimental import pallas as pl
from jax.experimental.pallas import tpu as pltpu
from jax.sharding import PartitionSpec as P

time_step = 600.0
implicit_weight = 0.5
weight = implicit_weight * time_step
LANES = 128
f32 = jnp.float32


def to_lines(block):
    rows, layers, columns = block.shape
    chunks = columns // LANES
    return (
        block.reshape(rows, layers, chunks, LANES)
        .transpose(0, 2, 1, 3)
        .reshape(rows * chunks * layers, LANES)
    )


def from_lines(lines, shape):
    rows, layers, columns = shape
    chunks = columns // LANES
    return (
        lines.reshape(rows, chunks, layers, LANES)
        .transpose(0, 2, 1, 3)
        .reshape(rows, layers, columns)
    )


def turns(wave, index, period):
    product = wave * index
    if period & (period - 1) == 0:
        product = product & (period - 1)
    else:
        product = lax.rem(product, jnp.int32(period))
    return product.astype(f32) * (1.0 / period)


def cos_sin(turn):
    part = turn - jnp.floor(turn + 0.5)
    square = part * part

    def series(first):
        terms = [
            (-1.0) ** n * math.pi ** (2 * n + first) / math.factorial(2 * n + first)
            for n in range(7)
        ]
        total = jnp.full_like(square, terms[-1])
        for term in terms[-2::-1]:
            total = total * square + term
        return total

    half_cos = series(0)
    half_sin = series(1) * part
    return 1.0 - 2.0 * half_sin * half_sin, 2.0 * half_sin * half_cos


def halves(values):
    high = values.astype(jnp.bfloat16)
    return high, (values - high.astype(f32)).astype(jnp.bfloat16)


def height_lines(modes, first_row, count, row_total, chunks, column_total):
    mode_count = modes.shape[0]
    wave_x = modes[:, 0:1].astype(jnp.int32)
    wave_y = modes[:, 1:2].astype(jnp.int32)
    offset = modes[:, 2:3]
    amp = modes[:, 3:4]
    spot = lax.broadcasted_iota(jnp.int32, (mode_count, count * chunks), 1)
    chunk = spot % chunks
    row = jnp.clip(first_row + spot // chunks, 0, row_total - 1)
    angle = (
        turns(wave_y, row, row_total) + turns(wave_x, chunk * LANES, column_total)
    ) + offset
    left_cos, left_sin = cos_sin(angle)
    lane = lax.broadcasted_iota(jnp.int32, (mode_count, LANES), 1)
    right_cos, right_sin = cos_sin(turns(wave_x, lane, column_total))
    left = jnp.concatenate([amp * left_cos, amp * left_sin], 0)
    right = jnp.concatenate([right_cos, -right_sin], 0)
    left_high, left_low = halves(left)
    right_high, right_low = halves(right)
    return lax.dot_general(
        jnp.concatenate([left_high, left_high, left_low], 0),
        jnp.concatenate([right_high, right_low, right_high], 0),
        (((0,), (0,)), ((), ())),
        preferred_element_type=f32,
    )


def inverse(values):
    return pl.reciprocal(values, approx=False)


def from_left(values, stride, lane):
    moved = [pltpu.roll(v, stride, 1) for v in values]
    return [jnp.where(lane < stride, moved[c - 1], moved[c]) for c in range(len(values))]


def from_right(values, stride, lane):
    count = len(values)
    moved = [pltpu.roll(v, LANES - stride, 1) for v in values]
    return [
        jnp.where(lane >= LANES - stride, moved[(c + 1) % count], moved[c]) for c in range(count)
    ]


def solve_chunks(diagonal, link, rhs):
    count = len(rhs)
    if count == 1:
        return [rhs[0] * inverse(diagonal[0])]
    inv = {i: inverse(diagonal[i]) for i in range(0, count, 2)}
    scaled = {i: inv[i] * rhs[i] for i in inv}
    odd_diagonal, odd_link, odd_rhs = [], [], []
    for i in range(1, count, 2):
        d = diagonal[i] - link[i - 1] * (link[i - 1] * inv[i - 1])
        r = rhs[i] + link[i - 1] * scaled[i - 1]
        e = None
        if i + 1 < count:
            by = link[i] * inv[i + 1]
            d = d - link[i] * by
            r = r + link[i] * scaled[i + 1]
            e = by * link[i + 1] if i + 2 < count else None
        odd_diagonal.append(d)
        odd_rhs.append(r)
        odd_link.append(e)
    odd = solve_chunks(odd_diagonal, odd_link, odd_rhs)
    out = [None] * count
    out[1::2] = odd
    for i in range(0, count, 2):
        r = rhs[i]
        if i > 0:
            r = r + link[i - 1] * out[i - 1]
        if i + 1 < count:
            r = r + link[i] * out[i + 1]
        out[i] = r * inv[i]
    return out


def reduce_lanes(diagonal, link, rhs, lane, stride):
    count = len(rhs)
    while stride < LANES:
        high_r = from_right(rhs, stride, lane)
        high_e = from_right(link, stride, lane)
        inv = [inverse(d) for d in diagonal]
        w = [q * e for q, e in zip(inv, link)]
        low_d = from_left([e * v for e, v in zip(link, w)], stride, lane)
        low_r = from_left([r * v for r, v in zip(rhs, w)], stride, lane)
        by = [e * q for e, q in zip(link, from_right(inv, stride, lane))]
        diagonal = [diagonal[c] - low_d[c] - link[c] * by[c] for c in range(count)]
        rhs = [rhs[c] + low_r[c] + by[c] * high_r[c] for c in range(count)]
        link = [by[c] * high_e[c] for c in range(count)]
        stride *= 2
    return solve_chunks(diagonal, link, rhs)


def pack_pair(a, b, odd_lane):
    even = [jnp.where(odd_lane, pltpu.roll(x, 1, 1), y) for x, y in zip(a, b)]
    odd = [jnp.where(odd_lane, x, pltpu.roll(y, LANES - 1, 1)) for x, y in zip(a, b)]
    return even, odd


def unpack_pair(even, odd, odd_lane):
    a = [jnp.where(odd_lane, y, pltpu.roll(x, LANES - 1, 1)) for x, y in zip(even, odd)]
    b = [jnp.where(odd_lane, pltpu.roll(y, 1, 1), x) for x, y in zip(even, odd)]
    return a, b


def solve_x_pair(g_pair, rhs_pair, lane):
    odd_lane = (lane & 1) == 1
    first_cell = lane < 2
    last_cell = lane >= LANES - 2
    half = 0.5 * weight
    g_even, g_odd = pack_pair(*g_pair, odd_lane)
    r_even, r_odd = pack_pair(*rhs_pair, odd_lane)
    face = [half * (a + b) for a, b in zip(g_even, g_odd)]
    after = from_right(g_even, 2, lane)
    after[-1] = jnp.where(last_cell, g_odd[-1], after[-1])
    face_after = [half * (a + b) for a, b in zip(g_odd, after)]
    face_before = from_left(face_after, 2, lane)
    face_before[0] = jnp.where(first_cell, weight * g_even[0], face_before[0])
    inv = [inverse(1.0 + (a + b)) for a, b in zip(face_before, face)]
    d_odd = [1.0 + (a + b) for a, b in zip(face, face_after)]
    link = list(face_after)
    link[-1] = jnp.where(last_cell, 0.0, link[-1])
    link_before = list(face_before)
    link_before[0] = jnp.where(first_cell, 0.0, link_before[0])
    t = [q * r for q, r in zip(inv, r_even)]
    w = [q * e for q, e in zip(inv, face)]
    next_q = from_right(inv, 2, lane)
    next_t = from_right(t, 2, lane)
    next_w = from_right(w, 2, lane)
    diagonal = [
        d - e * v - l * (l * q) for d, e, v, l, q in zip(d_odd, face, w, link, next_q)
    ]
    rhs = [r + e * v + l * n for r, e, v, l, n in zip(r_odd, face, t, link, next_t)]
    x_odd = reduce_lanes(diagonal, [l * n for l, n in zip(link, next_w)], rhs, lane, 2)
    x_before = from_left(x_odd, 2, lane)
    x_even = [
        v + q * (l * b) + u * x for v, q, l, b, u, x in zip(t, inv, link_before, x_before, w, x_odd)
    ]
    return unpack_pair(x_even, x_odd, odd_lane)


def row_copies(field_ref, both_ref, outer_ref, sems):
    width = outer_ref.shape[0]
    last = field_ref.shape[0] - width
    odd = lax.rem(lax.axis_index("wide"), 2)
    inner_rows = pl.ds(pl.multiple_of((1 - odd) * last, 8), width)
    outer_rows = pl.ds(pl.multiple_of(odd * last, 8), width)
    pairs = (
        (field_ref.at[inner_rows], both_ref.at[pl.ds(0, width)]),
        (field_ref.at[outer_rows], both_ref.at[pl.ds(width, width)]),
        (field_ref.at[outer_rows], outer_ref),
    )
    return [pltpu.make_async_copy(a, b, sems.at[n]) for n, (a, b) in enumerate(pairs)]


def row_kernel(field_ref, packed_ref, both_ref, outer_ref, row_sems):
    copies = row_copies(field_ref, both_ref, outer_ref, row_sems)
    for copy in copies:
        copy.start()
    packed_ref[...] = jnp.zeros(packed_ref.shape, f32)
    for copy in copies:
        copy.wait()


def pack_kernel(
    field_ref, step_ref, index_ref, amp_ref, phase_ref,
    packed_ref, both_ref, outer_ref,
    row_sems, step_in, index_in, amp_in, phase_in, mode_sems,
):
    pairs = (
        (step_ref, step_in), (index_ref, index_in), (amp_ref, amp_in), (phase_ref, phase_in)
    )
    mode_copies = [
        pltpu.make_async_copy(a, b, mode_sems.at[n]) for n, (a, b) in enumerate(pairs)
    ]
    copies = row_copies(field_ref, both_ref, outer_ref, row_sems)
    for copy in mode_copies + copies:
        copy.start()
    for copy in mode_copies:
        copy.wait()
    count = index_in.shape[0]
    row = lax.broadcasted_iota(jnp.int32, packed_ref.shape, 0)
    lane = lax.broadcasted_iota(jnp.int32, packed_ref.shape, 1)
    total = jnp.zeros(packed_ref.shape, f32)
    for m in range(count):
        moment = lax.rem(index_in[m, 2] * step_in[0], jnp.int32(64)).astype(f32)
        offset = phase_in[m] * (0.5 / math.pi) + moment * (1.0 / 64.0)
        for place, value in enumerate(
            (index_in[m, 0].astype(f32), index_in[m, 1].astype(f32), offset, amp_in[m])
        ):
            total = jnp.where((row == m) & (lane == place), value, total)
    packed_ref[...] = total
    for copy in copies:
        copy.wait()


def load_kernel(sizes, field_ref, conduct_ref, field_out, turned_ref, conduct_in, sems):
    rows, layers, chunks, row_total, layer_total, column_total = sizes
    width = layers * chunks
    copies = (
        pltpu.make_async_copy(field_ref, field_out, sems.at[0]),
        pltpu.make_async_copy(conduct_ref, conduct_in, sems.at[1]),
    )
    for copy in copies:
        copy.start()
    for n, (copy, ref) in enumerate(zip(copies, (field_out, conduct_in))):
        copy.wait()
        for place in range(width):
            spot = (n * width + place) * rows
            turned_ref[spot : spot + rows] = ref[pl.ds(place, rows, stride=width), :]


def block_factors(face):
    inv, scaled, chain, u = [], [], [], []
    rows = len(face) - 1
    rest = 1.0 + face[0]
    for j in range(rows):
        inv.append(inverse(rest + face[j + 1]))
        scaled.append(face[j] * inv[j])
        chain.append(face[j + 1] * inv[j])
        u.append(scaled[j] * u[-1] if j else scaled[j])
        rest = 1.0 + rest * chain[j]
    v = list(chain)
    for j in range(rows - 2, -1, -1):
        u[j] = u[j] + chain[j] * u[j + 1]
        v[j] = chain[j] * v[j + 1]
    return inv, scaled, chain, u, v


def height_kernel(sizes, handed_ref, came_ref, heights_ref):
    rows, layers, chunks, row_total, layer_total, column_total = sizes
    odd = lax.rem(lax.axis_index("wide"), 2) == 1
    modes = jnp.where(odd, handed_ref[layers * chunks :], came_ref[layers * chunks :])
    body = height_lines(modes, 0, row_total, row_total, chunks, column_total)
    heights_ref[chunks : (row_total + 1) * chunks] = body
    heights_ref[0:chunks] = body[0:chunks]
    heights_ref[(row_total + 1) * chunks : (row_total + 2) * chunks] = body[
        (row_total - 1) * chunks : row_total * chunks
    ]

def main_kernel(
    sizes, heights, both_ref, below_ref, came_ref, turned_ref,
    sent_ref, p_ref, u_ref, v_ref, gain_ref, joint_ref,
    halo, solved,
):
    rows, layers, chunks, row_total, layer_total, column_total = sizes
    width = layers * chunks
    blocks = row_total // rows
    me = lax.axis_index("wide")
    first_layer = lax.axis_index("grp") * layers
    zeta = [
        ((first_layer + k).astype(f32) + 0.5) * (1.0 / layer_total) for k in range(layers)
    ]
    half = 0.5 * weight
    own_start = pl.multiple_of(me * (rows * chunks), 8)

    def face(low, high):
        both = heights[pl.ds(low, chunks), :] + heights[pl.ds(high, chunks), :]
        return jnp.concatenate([weight + (half * z) * both for z in zeta], 0)

    def aligned(index):
        return pl.multiple_of(index, 8)

    inv, scaled, chain, u, v = block_factors(
        [face(own_start + j * chunks, own_start + (j + 1) * chunks) for j in range(rows + 1)]
    )
    for j in range(rows):
        u_ref[j * width : (j + 1) * width] = u[j]
        v_ref[j * width : (j + 1) * width] = v[j]

    def one_block(n, carry):
        rest, link, left_link = carry
        upward = n < me
        b = jnp.where(upward, n, blocks - 1 - (n - me))
        start = b * (rows * chunks) + jnp.where(upward, 0, (rows + 1) * chunks)
        step = jnp.where(upward, chunks, -chunks)
        places = [aligned(start + j * step) for j in range(rows + 2)]
        first = face(places[0], places[1])
        anew = (n == 0) | (n == me)
        left_link = jnp.where(n == me, link, left_link)
        rest = jnp.where(anew, 1.0 + first, rest)
        for j in range(rows):
            after = face(places[j + 1], places[j + 2])
            link = after * inverse(rest + after)
            through = through * link if j else link
            rest = 1.0 + rest * link
        gain_ref[pl.ds(aligned(b * width), width), :] = through * (first * inverse(after))
        return rest, link, left_link

    gain_ref[pl.ds(aligned(me * width), width), :] = u[-1]
    nothing = 0.0 * u[0]
    carry = (nothing, nothing, nothing)
    if blocks <= 8:
        for n in range(blocks - 1):
            carry = one_block(n, carry)
    else:
        carry = lax.fori_loop(0, blocks - 1, one_block, carry)
    _, link, left_link = carry
    left_link = jnp.where(me == blocks - 1, link, left_link)
    right_link = jnp.where(me == blocks - 1, 0.0, link)

    a = 1.0 - left_link * u[0]
    b = left_link * v[0]
    c = right_link * u[-1]
    d = 1.0 - right_link * v[-1]
    by = inverse(a * d - b * c)
    joint = (
        u[-1] * inverse(a) * left_link, v[0] * inverse(d) * right_link,
        left_link, right_link, d * by, b * by, c * by, a * by,
    )
    for n, value in enumerate(joint):
        joint_ref[n * width : (n + 1) * width] = value

    odd = lax.rem(me, 2) == 1
    inner = both_ref[0:width]
    below = jnp.where(odd, inner, below_ref[...])
    above = jnp.where(odd, came_ref[0:width], inner)
    halo[0:width] = jnp.where(me == 0, 0.0, below)
    halo[width : 2 * width] = jnp.where(me == blocks - 1, 0.0, above)
    lane = lax.broadcasted_iota(jnp.int32, (rows, LANES), 1)
    row = lax.broadcasted_iota(jnp.int32, (rows, LANES), 0)

    def neighbours(values, low, high):
        return (
            jnp.where(row == 0, low, pltpu.roll(values, 1, 0)),
            jnp.where(row == rows - 1, high, pltpu.roll(values, rows - 1, 0)),
        )

    g = [[] for _ in range(layers)]
    f = [[] for _ in range(layers)]
    rhs = [[] for _ in range(layers)]
    for c in range(chunks):
        h = heights[pl.ds(own_start + chunks + c, rows, stride=chunks), :]
        h_low, h_high = neighbours(
            h,
            heights[pl.ds(own_start + c, 1), :],
            heights[pl.ds(own_start + (rows + 1) * chunks + c, 1), :],
        )
        low_sum, high_sum = h + h_low, h + h_high
        for k in range(layers):
            place = c * layers + k
            f_mid = turned_ref[place * rows : (place + 1) * rows]
            f_low, f_high = neighbours(
                f_mid, halo[pl.ds(place, 1), :], halo[pl.ds(width + place, 1), :]
            )
            g[k].append(
                turned_ref[(width + place) * rows : (width + place + 1) * rows] * (1.0 + zeta[k] * h)
            )
            f[k].append(f_mid)
            along = (weight + (half * zeta[k]) * high_sum) * (f_high - f_mid) - (
                weight + (half * zeta[k]) * low_sum
            ) * (f_mid - f_low)
            rhs[k].append(2.0 * (f_mid + along))
    for k in range(0, layers, 2):
        both = solve_x_pair(g[k : k + 2], rhs[k : k + 2], lane)
        for n in range(2):
            for c in range(chunks):
                spot = pl.ds((k + n) * chunks + c, rows, stride=width)
                solved[spot, :] = both[n][c] - 2.0 * f[k + n][c]

    def part(ref, j):
        return ref[j * width : (j + 1) * width]

    p = [part(solved, 0) * inv[0]]
    for j in range(1, rows):
        p.append(part(solved, j) * inv[j] + scaled[j] * p[-1])
    for j in range(rows - 2, -1, -1):
        p[j] = p[j] + chain[j] * p[j + 1]
    for j in range(rows):
        p_ref[j * width : (j + 1) * width] = p[j]

    upward = p[-1] + part(joint_ref, 0) * p[0]
    downward = p[0] + part(joint_ref, 1) * p[-1]
    for b in range(blocks):
        sent_ref[b * width : (b + 1) * width] = jnp.where(b > me, upward, downward)


def last_kernel(
    sizes, came_ref, gain_ref, joint_ref, p_ref, u_ref, v_ref, field_ref,
    out_ref,
):
    rows, layers, chunks, row_total, layer_total, column_total = sizes
    width = layers * chunks
    blocks = row_total // rows
    me = lax.axis_index("wide")

    def part(ref, b):
        return ref[b * width : (b + 1) * width]

    left = jnp.zeros((width, LANES), f32)
    right = jnp.zeros((width, LANES), f32)
    for b in range(blocks - 1):
        left = jnp.where(b < me, part(came_ref, b) + part(gain_ref, b) * left, left)
        b = blocks - 1 - b
        right = jnp.where(b > me, part(came_ref, b) + part(gain_ref, b) * right, right)

    y = left + part(joint_ref, 2) * part(p_ref, 0)
    z = right + part(joint_ref, 3) * part(p_ref, rows - 1)
    before = part(joint_ref, 4) * y + part(joint_ref, 5) * z
    after = part(joint_ref, 6) * y + part(joint_ref, 7) * z
    for j in range(rows):
        x = part(p_ref, j) + part(u_ref, j) * before + part(v_ref, j) * after
        for k in range(layers):
            spot = pl.ds(j * width + k, chunks, stride=layers)
            out_ref[spot, :] = field_ref[spot, :] + x[k * chunks : (k + 1) * chunks]


def on_device(field, conduct, mode_index, mode_amp, mode_phase, step_index):
    rows, layers, columns = field.shape
    wide_count = lax.axis_size("wide")
    row_total = rows * wide_count
    grp_count = lax.axis_size("grp")
    layer_total = layers * grp_count
    chunks = columns // LANES
    width = layers * chunks
    sizes = (rows, layers, chunks, row_total, layer_total, columns)
    limit = pltpu.CompilerParams(vmem_limit_bytes=16 * 1024 * 1024)
    hbm = pl.BlockSpec(memory_space=pltpu.HBM)

    def lines(count):
        return jax.ShapeDtypeStruct((count * width, LANES), f32)

    place = lax.axis_index("wide")
    odd = place % 2 == 1
    first_shapes = (
        jax.ShapeDtypeStruct((mode_index.shape[0], LANES), f32),
        lines(2),
        lines(1),
    )
    row_sems = pltpu.SemaphoreType.DMA((3,))

    def pack_modes_and_rows(field_lines, *mode_arrays):
        return pl.pallas_call(
            pack_kernel,
            out_shape=first_shapes,
            in_specs=[hbm] * 5,
            scratch_shapes=[row_sems]
            + [pltpu.SMEM(a.shape, a.dtype) for a in mode_arrays]
            + [pltpu.SemaphoreType.DMA((4,))],
            compiler_params=limit,
        )(*(pltpu.with_memory_space_constraint(a, pltpu.HBM) for a in (field_lines, *mode_arrays)))

    def pack_rows(field_lines, *mode_arrays):
        return pl.pallas_call(
            row_kernel,
            out_shape=first_shapes,
            in_specs=[hbm],
            scratch_shapes=[row_sems],
            compiler_params=limit,
        )(pltpu.with_memory_space_constraint(field_lines, pltpu.HBM))

    packed, both, outer = lax.cond(
        odd, pack_modes_and_rows, pack_rows,
        to_lines(field), step_index, mode_index, mode_amp, mode_phase,
    )

    swaps = [(i, i ^ 1) for i in range(wide_count)]
    cores = [list(range(n, wide_count, 2)) for n in range(2)]
    both_came = lax.ppermute(both, "wide", swaps)

    def gather_modes(own):
        return lax.all_gather(own, "grp", axis=0, tiled=True)

    def no_modes(own):
        return jnp.zeros((grp_count * own.shape[0], own.shape[1]), f32)

    modes = lax.cond(odd, gather_modes, no_modes, packed)
    modes, outer, both_came = lax.optimization_barrier((modes, outer, both_came))

    def gather_rows(own, came):
        rows_sent = jnp.concatenate([own, came[width:]], 0)
        rows_all = lax.all_gather(rows_sent, "wide", axis_index_groups=cores, axis=0)
        chip = place // 2
        below = lax.dynamic_index_in_dim(rows_all, jnp.maximum(chip - 1, 0), 0, False)
        above = lax.dynamic_index_in_dim(
            rows_all, jnp.minimum(chip + 1, wide_count // 2 - 1), 0, False
        )
        return below[width:], above[:width]

    def no_rows(own, came):
        return jnp.zeros_like(own), jnp.zeros_like(own)

    below, above = lax.cond(odd, no_rows, gather_rows, outer, both_came)
    handed = jnp.concatenate([above, modes], 0)
    came = lax.ppermute(handed, "wide", swaps)
    handed, field, conduct = lax.optimization_barrier((handed, field, conduct))
    field_lines, turned = pl.pallas_call(
        functools.partial(load_kernel, sizes),
        out_shape=(lines(rows), lines(2 * rows)),
        in_specs=[hbm] * 2,
        scratch_shapes=[
            pltpu.VMEM((rows * width, LANES), f32),
            pltpu.SemaphoreType.DMA((2,)),
        ],
        compiler_params=limit,
    )(
        *(
            pltpu.with_memory_space_constraint(to_lines(a), pltpu.HBM)
            for a in (field, conduct)
        )
    )
    heights = pl.pallas_call(
        functools.partial(height_kernel, sizes),
        out_shape=jax.ShapeDtypeStruct(((row_total + 2) * chunks, LANES), f32),
        compiler_params=limit,
    )(handed, came)

    sent, p, u, v, gain, joint = pl.pallas_call(
        functools.partial(main_kernel, sizes),
        out_shape=(lines(wide_count),)
        + (lines(rows),) * 3
        + (lines(wide_count), lines(8)),
        scratch_shapes=[
            pltpu.VMEM((2 * width, LANES), f32),
            pltpu.VMEM((rows * width, LANES), f32),
        ],
        compiler_params=limit,
    )(heights, both_came, below, came, turned)

    came = lax.all_to_all(
        sent.reshape(wide_count, width, LANES), "wide", split_axis=0, concat_axis=0
    ).reshape(wide_count * width, LANES)

    advanced = pl.pallas_call(
        functools.partial(last_kernel, sizes),
        out_shape=lines(rows),
        compiler_params=limit,
    )(came, gain, joint, p, u, v, field_lines)
    return from_lines(advanced, field.shape)


def solution(mesh):
    return jax.shard_map(
        on_device,
        mesh=mesh,
        in_specs=(
            P("wide", "grp", None),
            P("wide", "grp", None),
            P("grp", None),
            P("grp"),
            P("grp"),
            P(),
        ),
        out_specs=P("wide", "grp", None),
        check_vma=False,
    )
```

```python
import functools
import math

import jax
import jax.numpy as jnp
from jax import lax
from jax.experimental import pallas as pl
from jax.experimental.pallas import tpu as pltpu
from jax.sharding import PartitionSpec as P

time_step = 600.0
implicit_weight = 0.5
weight = implicit_weight * time_step
LANES = 128
f32 = jnp.float32


def to_lines(block):
    rows, layers, columns = block.shape
    chunks = columns // LANES
    return (
        block.reshape(rows, layers, chunks, LANES)
        .transpose(0, 2, 1, 3)
        .reshape(rows * chunks * layers, LANES)
    )


def from_lines(lines, shape):
    rows, layers, columns = shape
    chunks = columns // LANES
    return (
        lines.reshape(rows, chunks, layers, LANES)
        .transpose(0, 2, 1, 3)
        .reshape(rows, layers, columns)
    )


def turns(wave, index, period):
    product = wave * index
    if period & (period - 1) == 0:
        product = product & (period - 1)
    else:
        product = lax.rem(product, jnp.int32(period))
    return product.astype(f32) * (1.0 / period)


def cos_sin(turn):
    part = turn - jnp.floor(turn + 0.5)
    square = part * part

    def series(first):
        terms = [
            (-1.0) ** n * math.pi ** (2 * n + first) / math.factorial(2 * n + first)
            for n in range(7)
        ]
        total = jnp.full_like(square, terms[-1])
        for term in terms[-2::-1]:
            total = total * square + term
        return total

    half_cos = series(0)
    half_sin = series(1) * part
    return 1.0 - 2.0 * half_sin * half_sin, 2.0 * half_sin * half_cos


def halves(values):
    high = values.astype(jnp.bfloat16)
    return high, (values - high.astype(f32)).astype(jnp.bfloat16)


def height_lines(modes, step, first_row, count, row_total, chunks, column_total):
    mode_count = modes.shape[0]
    wave_x = modes[:, 0:1].astype(jnp.int32)
    wave_y = modes[:, 1:2].astype(jnp.int32)
    moment = modes[:, 2:3] * step * (1.0 / 64.0)
    offset = modes[:, 3:4] * (0.5 / math.pi) + (moment - jnp.floor(moment))
    amp = modes[:, 4:5]
    spot = lax.broadcasted_iota(jnp.int32, (mode_count, count * chunks), 1)
    chunk = spot % chunks
    row = jnp.clip(first_row + spot // chunks, 0, row_total - 1)
    angle = (
        turns(wave_y, row, row_total) + turns(wave_x, chunk * LANES, column_total)
    ) + offset
    left_cos, left_sin = cos_sin(angle)
    lane = lax.broadcasted_iota(jnp.int32, (mode_count, LANES), 1)
    right_cos, right_sin = cos_sin(turns(wave_x, lane, column_total))
    left = jnp.concatenate([amp * left_cos, amp * left_sin], 0)
    right = jnp.concatenate([right_cos, -right_sin], 0)
    left_high, left_low = halves(left)
    right_high, right_low = halves(right)
    return lax.dot_general(
        jnp.concatenate([left_high, left_high, left_low], 0),
        jnp.concatenate([right_high, right_low, right_high], 0),
        (((0,), (0,)), ((), ())),
        preferred_element_type=f32,
    )


def inverse(values):
    return pl.reciprocal(values, approx=False)


def from_left(values, stride, lane):
    moved = [pltpu.roll(v, stride, 1) for v in values]
    return [jnp.where(lane < stride, moved[c - 1], moved[c]) for c in range(len(values))]


def from_right(values, stride, lane):
    count = len(values)
    moved = [pltpu.roll(v, LANES - stride, 1) for v in values]
    return [
        jnp.where(lane >= LANES - stride, moved[(c + 1) % count], moved[c]) for c in range(count)
    ]


def solve_chunks(diagonal, link, rhs):
    count = len(rhs)
    if count == 1:
        return [rhs[0] * inverse(diagonal[0])]
    inv = {i: inverse(diagonal[i]) for i in range(0, count, 2)}
    scaled = {i: inv[i] * rhs[i] for i in inv}
    odd_diagonal, odd_link, odd_rhs = [], [], []
    for i in range(1, count, 2):
        d = diagonal[i] - link[i - 1] * (link[i - 1] * inv[i - 1])
        r = rhs[i] + link[i - 1] * scaled[i - 1]
        e = None
        if i + 1 < count:
            by = link[i] * inv[i + 1]
            d = d - link[i] * by
            r = r + link[i] * scaled[i + 1]
            e = by * link[i + 1] if i + 2 < count else None
        odd_diagonal.append(d)
        odd_rhs.append(r)
        odd_link.append(e)
    odd = solve_chunks(odd_diagonal, odd_link, odd_rhs)
    out = [None] * count
    out[1::2] = odd
    for i in range(0, count, 2):
        r = rhs[i]
        if i > 0:
            r = r + link[i - 1] * out[i - 1]
        if i + 1 < count:
            r = r + link[i] * out[i + 1]
        out[i] = r * inv[i]
    return out


def reduce_lanes(diagonal, link, rhs, lane, stride):
    count = len(rhs)
    while stride < LANES:
        high_r = from_right(rhs, stride, lane)
        high_e = from_right(link, stride, lane)
        inv = [inverse(d) for d in diagonal]
        w = [q * e for q, e in zip(inv, link)]
        low_d = from_left([e * v for e, v in zip(link, w)], stride, lane)
        low_r = from_left([r * v for r, v in zip(rhs, w)], stride, lane)
        by = [e * q for e, q in zip(link, from_right(inv, stride, lane))]
        diagonal = [diagonal[c] - low_d[c] - link[c] * by[c] for c in range(count)]
        rhs = [rhs[c] + low_r[c] + by[c] * high_r[c] for c in range(count)]
        link = [by[c] * high_e[c] for c in range(count)]
        stride *= 2
    return solve_chunks(diagonal, link, rhs)


def pack_pair(a, b, odd_lane):
    even = [jnp.where(odd_lane, pltpu.roll(x, 1, 1), y) for x, y in zip(a, b)]
    odd = [jnp.where(odd_lane, x, pltpu.roll(y, LANES - 1, 1)) for x, y in zip(a, b)]
    return even, odd


def unpack_pair(even, odd, odd_lane):
    a = [jnp.where(odd_lane, y, pltpu.roll(x, LANES - 1, 1)) for x, y in zip(even, odd)]
    b = [jnp.where(odd_lane, pltpu.roll(y, 1, 1), x) for x, y in zip(even, odd)]
    return a, b


def solve_x_pair(g_pair, rhs_pair, lane):
    odd_lane = (lane & 1) == 1
    first_cell = lane < 2
    last_cell = lane >= LANES - 2
    half = 0.5 * weight
    g_even, g_odd = pack_pair(*g_pair, odd_lane)
    r_even, r_odd = pack_pair(*rhs_pair, odd_lane)
    face = [half * (a + b) for a, b in zip(g_even, g_odd)]
    after = from_right(g_even, 2, lane)
    after[-1] = jnp.where(last_cell, g_odd[-1], after[-1])
    face_after = [half * (a + b) for a, b in zip(g_odd, after)]
    face_before = from_left(face_after, 2, lane)
    face_before[0] = jnp.where(first_cell, weight * g_even[0], face_before[0])
    inv = [inverse(1.0 + (a + b)) for a, b in zip(face_before, face)]
    d_odd = [1.0 + (a + b) for a, b in zip(face, face_after)]
    link = list(face_after)
    link[-1] = jnp.where(last_cell, 0.0, link[-1])
    link_before = list(face_before)
    link_before[0] = jnp.where(first_cell, 0.0, link_before[0])
    t = [q * r for q, r in zip(inv, r_even)]
    w = [q * e for q, e in zip(inv, face)]
    next_q = from_right(inv, 2, lane)
    next_t = from_right(t, 2, lane)
    next_w = from_right(w, 2, lane)
    diagonal = [
        d - e * v - l * (l * q) for d, e, v, l, q in zip(d_odd, face, w, link, next_q)
    ]
    rhs = [r + e * v + l * n for r, e, v, l, n in zip(r_odd, face, t, link, next_t)]
    x_odd = reduce_lanes(diagonal, [l * n for l, n in zip(link, next_w)], rhs, lane, 2)
    x_before = from_left(x_odd, 2, lane)
    x_even = [
        v + q * (l * b) + u * x for v, q, l, b, u, x in zip(t, inv, link_before, x_before, w, x_odd)
    ]
    return unpack_pair(x_even, x_odd, odd_lane)


def pack_kernel(
    field_ref, index_ref, amp_ref, phase_ref,
    packed_ref, both_ref,
    index_in, amp_in, phase_in, sems,
):
    width = both_ref.shape[0] // 2
    last = field_ref.shape[0] - width
    pairs = (
        (index_ref, index_in),
        (amp_ref, amp_in),
        (phase_ref, phase_in),
        (field_ref.at[pl.ds(0, width)], both_ref.at[pl.ds(0, width)]),
        (field_ref.at[pl.ds(last, width)], both_ref.at[pl.ds(width, width)]),
    )
    copies = [pltpu.make_async_copy(a, b, sems.at[n]) for n, (a, b) in enumerate(pairs)]
    for copy in copies:
        copy.start()
    for copy in copies[:3]:
        copy.wait()
    row = lax.broadcasted_iota(jnp.int32, packed_ref.shape, 0)
    lane = lax.broadcasted_iota(jnp.int32, packed_ref.shape, 1)
    total = jnp.zeros(packed_ref.shape, f32)
    for m in range(index_in.shape[0]):
        waves = [index_in[m, n].astype(f32) for n in range(3)]
        for place, value in enumerate((*waves, phase_in[m], amp_in[m])):
            total = jnp.where((row == m) & (lane == place), value, total)
    packed_ref[...] = total
    for copy in copies[3:]:
        copy.wait()


def row_kernel(field_ref, step_ref, table_ref, inner_ref, outer_ref, step_in, sems):
    width = inner_ref.shape[0]
    pairs = (
        (step_ref, step_in),
        (field_ref.at[pl.ds(field_ref.shape[0] - width, width)], inner_ref),
        (field_ref.at[pl.ds(0, width)], outer_ref),
    )
    copies = [pltpu.make_async_copy(a, b, sems.at[n]) for n, (a, b) in enumerate(pairs)]
    for copy in copies:
        copy.start()
    for copy in copies:
        copy.wait()
    table_ref[...] = jnp.full(table_ref.shape, step_in[0].astype(f32), f32)


def load_kernel(sizes, field_ref, conduct_ref, field_out, turned_ref, conduct_in, sems):
    rows, layers, chunks, row_total, layer_total, column_total = sizes
    width = layers * chunks
    copies = (
        pltpu.make_async_copy(field_ref, field_out, sems.at[0]),
        pltpu.make_async_copy(conduct_ref, conduct_in, sems.at[1]),
    )
    for copy in copies:
        copy.start()
    for n, (copy, ref) in enumerate(zip(copies, (field_out, conduct_in))):
        copy.wait()
        for place in range(width):
            spot = (n * width + place) * rows
            turned_ref[spot : spot + rows] = ref[pl.ds(place, rows, stride=width), :]


def block_factors(face):
    inv, scaled, chain, u = [], [], [], []
    rows = len(face) - 1
    rest = 1.0 + face[0]
    for j in range(rows):
        inv.append(inverse(rest + face[j + 1]))
        scaled.append(face[j] * inv[j])
        chain.append(face[j + 1] * inv[j])
        u.append(scaled[j] * u[-1] if j else scaled[j])
        rest = 1.0 + rest * chain[j]
    v = list(chain)
    for j in range(rows - 2, -1, -1):
        u[j] = u[j] + chain[j] * u[j + 1]
        v[j] = chain[j] * v[j + 1]
    return inv, scaled, chain, u, v


def height_kernel(sizes, handed_ref, came_ref, heights_ref):
    rows, layers, chunks, row_total, layer_total, column_total = sizes
    odd = lax.rem(lax.axis_index("wide"), 2) == 1
    first = 2 * layers * chunks
    own, other = handed_ref[first:], came_ref[first:]
    modes = jnp.where(odd, own, other)
    step = jnp.where(odd, other, own)[:, 0:1]
    body = height_lines(modes, step, 0, row_total, row_total, chunks, column_total)
    heights_ref[chunks : (row_total + 1) * chunks] = body
    heights_ref[0:chunks] = body[0:chunks]
    heights_ref[(row_total + 1) * chunks : (row_total + 2) * chunks] = body[
        (row_total - 1) * chunks : row_total * chunks
    ]

def main_kernel(
    sizes, heights, both_ref, below_ref, came_ref, turned_ref,
    sent_ref, p_ref, u_ref, v_ref, gain_ref, joint_ref,
    halo, solved,
):
    rows, layers, chunks, row_total, layer_total, column_total = sizes
    width = layers * chunks
    blocks = row_total // rows
    me = lax.axis_index("wide")
    first_layer = lax.axis_index("grp") * layers
    zeta = [
        ((first_layer + k).astype(f32) + 0.5) * (1.0 / layer_total) for k in range(layers)
    ]
    half = 0.5 * weight
    own_start = pl.multiple_of(me * (rows * chunks), 8)

    def face(low, high):
        both = heights[pl.ds(low, chunks), :] + heights[pl.ds(high, chunks), :]
        return jnp.concatenate([weight + (half * z) * both for z in zeta], 0)

    def aligned(index):
        return pl.multiple_of(index, 8)

    inv, scaled, chain, u, v = block_factors(
        [face(own_start + j * chunks, own_start + (j + 1) * chunks) for j in range(rows + 1)]
    )
    for j in range(rows):
        u_ref[j * width : (j + 1) * width] = u[j]
        v_ref[j * width : (j + 1) * width] = v[j]

    def one_block(n, carry):
        rest, link, left_link = carry
        upward = n < me
        b = jnp.where(upward, n, blocks - 1 - (n - me))
        start = b * (rows * chunks) + jnp.where(upward, 0, (rows + 1) * chunks)
        step = jnp.where(upward, chunks, -chunks)
        places = [aligned(start + j * step) for j in range(rows + 2)]
        first = face(places[0], places[1])
        anew = (n == 0) | (n == me)
        left_link = jnp.where(n == me, link, left_link)
        rest = jnp.where(anew, 1.0 + first, rest)
        for j in range(rows):
            after = face(places[j + 1], places[j + 2])
            link = after * inverse(rest + after)
            through = through * link if j else link
            rest = 1.0 + rest * link
        gain_ref[pl.ds(aligned(b * width), width), :] = through * (first * inverse(after))
        return rest, link, left_link

    gain_ref[pl.ds(aligned(me * width), width), :] = u[-1]
    nothing = 0.0 * u[0]
    carry = (nothing, nothing, nothing)
    if blocks <= 8:
        for n in range(blocks - 1):
            carry = one_block(n, carry)
    else:
        carry = lax.fori_loop(0, blocks - 1, one_block, carry)
    _, link, left_link = carry
    left_link = jnp.where(me == blocks - 1, link, left_link)
    right_link = jnp.where(me == blocks - 1, 0.0, link)

    a = 1.0 - left_link * u[0]
    b = left_link * v[0]
    c = right_link * u[-1]
    d = 1.0 - right_link * v[-1]
    by = inverse(a * d - b * c)
    joint = (
        u[-1] * inverse(a) * left_link, v[0] * inverse(d) * right_link,
        left_link, right_link, d * by, b * by, c * by, a * by,
    )
    for n, value in enumerate(joint):
        joint_ref[n * width : (n + 1) * width] = value

    odd = lax.rem(me, 2) == 1
    below = jnp.where(odd, came_ref[width : 2 * width], below_ref[...])
    above = jnp.where(odd, came_ref[0:width], both_ref[0:width])
    halo[0:width] = jnp.where(me == 0, 0.0, below)
    halo[width : 2 * width] = jnp.where(me == blocks - 1, 0.0, above)
    lane = lax.broadcasted_iota(jnp.int32, (rows, LANES), 1)
    row = lax.broadcasted_iota(jnp.int32, (rows, LANES), 0)

    def neighbours(values, low, high):
        return (
            jnp.where(row == 0, low, pltpu.roll(values, 1, 0)),
            jnp.where(row == rows - 1, high, pltpu.roll(values, rows - 1, 0)),
        )

    g = [[] for _ in range(layers)]
    f = [[] for _ in range(layers)]
    rhs = [[] for _ in range(layers)]
    for c in range(chunks):
        h = heights[pl.ds(own_start + chunks + c, rows, stride=chunks), :]
        h_low, h_high = neighbours(
            h,
            heights[pl.ds(own_start + c, 1), :],
            heights[pl.ds(own_start + (rows + 1) * chunks + c, 1), :],
        )
        low_sum, high_sum = h + h_low, h + h_high
        for k in range(layers):
            place = c * layers + k
            f_mid = turned_ref[place * rows : (place + 1) * rows]
            f_low, f_high = neighbours(
                f_mid, halo[pl.ds(place, 1), :], halo[pl.ds(width + place, 1), :]
            )
            g[k].append(
                turned_ref[(width + place) * rows : (width + place + 1) * rows] * (1.0 + zeta[k] * h)
            )
            f[k].append(f_mid)
            along = (weight + (half * zeta[k]) * high_sum) * (f_high - f_mid) - (
                weight + (half * zeta[k]) * low_sum
            ) * (f_mid - f_low)
            rhs[k].append(2.0 * (f_mid + along))
    for k in range(0, layers, 2):
        both = solve_x_pair(g[k : k + 2], rhs[k : k + 2], lane)
        for n in range(2):
            for c in range(chunks):
                spot = pl.ds((k + n) * chunks + c, rows, stride=width)
                solved[spot, :] = both[n][c] - 2.0 * f[k + n][c]

    def part(ref, j):
        return ref[j * width : (j + 1) * width]

    p = [part(solved, 0) * inv[0]]
    for j in range(1, rows):
        p.append(part(solved, j) * inv[j] + scaled[j] * p[-1])
    for j in range(rows - 2, -1, -1):
        p[j] = p[j] + chain[j] * p[j + 1]
    for j in range(rows):
        p_ref[j * width : (j + 1) * width] = p[j]

    upward = p[-1] + part(joint_ref, 0) * p[0]
    downward = p[0] + part(joint_ref, 1) * p[-1]
    for b in range(blocks):
        sent_ref[b * width : (b + 1) * width] = jnp.where(b > me, upward, downward)


def last_kernel(
    sizes, came_ref, gain_ref, joint_ref, p_ref, u_ref, v_ref, field_ref,
    out_ref,
):
    rows, layers, chunks, row_total, layer_total, column_total = sizes
    width = layers * chunks
    blocks = row_total // rows
    me = lax.axis_index("wide")

    def part(ref, b):
        return ref[b * width : (b + 1) * width]

    left = jnp.zeros((width, LANES), f32)
    right = jnp.zeros((width, LANES), f32)
    for b in range(blocks - 1):
        left = jnp.where(b < me, part(came_ref, b) + part(gain_ref, b) * left, left)
        b = blocks - 1 - b
        right = jnp.where(b > me, part(came_ref, b) + part(gain_ref, b) * right, right)

    y = left + part(joint_ref, 2) * part(p_ref, 0)
    z = right + part(joint_ref, 3) * part(p_ref, rows - 1)
    before = part(joint_ref, 4) * y + part(joint_ref, 5) * z
    after = part(joint_ref, 6) * y + part(joint_ref, 7) * z
    for j in range(rows):
        x = part(p_ref, j) + part(u_ref, j) * before + part(v_ref, j) * after
        for k in range(layers):
            spot = pl.ds(j * width + k, chunks, stride=layers)
            out_ref[spot, :] = field_ref[spot, :] + x[k * chunks : (k + 1) * chunks]


def on_device(field, conduct, mode_index, mode_amp, mode_phase, step_index):
    rows, layers, columns = field.shape
    wide_count = lax.axis_size("wide")
    row_total = rows * wide_count
    grp_count = lax.axis_size("grp")
    layer_total = layers * grp_count
    chunks = columns // LANES
    width = layers * chunks
    sizes = (rows, layers, chunks, row_total, layer_total, columns)
    limit = pltpu.CompilerParams(vmem_limit_bytes=16 * 1024 * 1024)
    hbm = pl.BlockSpec(memory_space=pltpu.HBM)

    def lines(count):
        return jax.ShapeDtypeStruct((count * width, LANES), f32)

    place = lax.axis_index("wide")
    odd = place % 2 == 1
    swaps = [(i, i ^ 1) for i in range(wide_count)]
    cores = [list(range(n, wide_count, 2)) for n in range(2)]
    table_shape = (grp_count * mode_index.shape[0], LANES)
    packed_shape = (mode_index.shape[0], LANES)
    in_hbm = lambda arrays: [pltpu.with_memory_space_constraint(a, pltpu.HBM) for a in arrays]

    def pack_modes(*arrays):
        return pl.pallas_call(
            pack_kernel,
            out_shape=(jax.ShapeDtypeStruct(packed_shape, f32), lines(2)),
            in_specs=[hbm] * 4,
            scratch_shapes=[pltpu.SMEM(a.shape, a.dtype) for a in arrays[1:]]
            + [pltpu.SemaphoreType.DMA((5,))],
            compiler_params=limit,
        )(*in_hbm(arrays))

    def pack_nothing(*arrays):
        return jnp.zeros(packed_shape, f32), jnp.zeros((2 * width, LANES), f32)

    packed, both = lax.cond(
        odd, pack_modes, pack_nothing, to_lines(field), mode_index, mode_amp, mode_phase
    )
    both_came = lax.ppermute(both, "wide", swaps)

    def gather_modes(own, *arrays):
        empty = jnp.zeros((width, LANES), f32)
        return lax.all_gather(own, "grp", axis=0, tiled=True), empty, empty

    def load_rows(own, *arrays):
        return pl.pallas_call(
            row_kernel,
            out_shape=(jax.ShapeDtypeStruct(table_shape, f32), lines(1), lines(1)),
            in_specs=[hbm] * 2,
            scratch_shapes=[
                pltpu.SMEM(step_index.shape, step_index.dtype),
                pltpu.SemaphoreType.DMA((3,)),
            ],
            compiler_params=limit,
        )(*in_hbm(arrays))

    table, inner, outer = lax.cond(
        odd, gather_modes, load_rows, packed, to_lines(field), step_index
    )
    table, inner, outer, both_came = lax.optimization_barrier((table, inner, outer, both_came))

    def gather_rows(own, came):
        rows_sent = jnp.concatenate([own, came[width:]], 0)
        rows_all = lax.all_gather(rows_sent, "wide", axis_index_groups=cores, axis=0)
        chip = place // 2
        below = lax.dynamic_index_in_dim(rows_all, jnp.maximum(chip - 1, 0), 0, False)
        above = lax.dynamic_index_in_dim(
            rows_all, jnp.minimum(chip + 1, wide_count // 2 - 1), 0, False
        )
        return below[width:], above[:width]

    def no_rows(own, came):
        return jnp.zeros_like(own), jnp.zeros_like(own)

    below, above = lax.cond(odd, no_rows, gather_rows, outer, both_came)
    handed = jnp.concatenate([above, inner, table], 0)
    came = lax.ppermute(handed, "wide", swaps)
    handed, field, conduct = lax.optimization_barrier((handed, field, conduct))
    field_lines, turned = pl.pallas_call(
        functools.partial(load_kernel, sizes),
        out_shape=(lines(rows), lines(2 * rows)),
        in_specs=[hbm] * 2,
        scratch_shapes=[
            pltpu.VMEM((rows * width, LANES), f32),
            pltpu.SemaphoreType.DMA((2,)),
        ],
        compiler_params=limit,
    )(
        *(
            pltpu.with_memory_space_constraint(to_lines(a), pltpu.HBM)
            for a in (field, conduct)
        )
    )
    heights = pl.pallas_call(
        functools.partial(height_kernel, sizes),
        out_shape=jax.ShapeDtypeStruct(((row_total + 2) * chunks, LANES), f32),
        compiler_params=limit,
    )(handed, came)

    sent, p, u, v, gain, joint = pl.pallas_call(
        functools.partial(main_kernel, sizes),
        out_shape=(lines(wide_count),)
        + (lines(rows),) * 3
        + (lines(wide_count), lines(8)),
        scratch_shapes=[
            pltpu.VMEM((2 * width, LANES), f32),
            pltpu.VMEM((rows * width, LANES), f32),
        ],
        compiler_params=limit,
    )(heights, both_came, below, came, turned)

    came = lax.all_to_all(
        sent.reshape(wide_count, width, LANES), "wide", split_axis=0, concat_axis=0
    ).reshape(wide_count * width, LANES)

    advanced = pl.pallas_call(
        functools.partial(last_kernel, sizes),
        out_shape=lines(rows),
        compiler_params=limit,
    )(came, gain, joint, p, u, v, field_lines)
    return from_lines(advanced, field.shape)


def solution(mesh):
    return jax.shard_map(
        on_device,
        mesh=mesh,
        in_specs=(
            P("wide", "grp", None),
            P("wide", "grp", None),
            P("grp", None),
            P("grp"),
            P("grp"),
            P(),
        ),
        out_specs=P("wide", "grp", None),
        check_vma=False,
    )
```

```python
import functools
import math

import jax
import jax.numpy as jnp
from jax import lax
from jax.experimental import pallas as pl
from jax.experimental.pallas import tpu as pltpu
from jax.sharding import PartitionSpec as P

time_step = 600.0
implicit_weight = 0.5
weight = implicit_weight * time_step
LANES = 128
f32 = jnp.float32


def to_lines(block):
    rows, layers, columns = block.shape
    chunks = columns // LANES
    return (
        block.reshape(rows, layers, chunks, LANES)
        .transpose(0, 2, 1, 3)
        .reshape(rows * chunks * layers, LANES)
    )


def from_lines(lines, shape):
    rows, layers, columns = shape
    chunks = columns // LANES
    return (
        lines.reshape(rows, chunks, layers, LANES)
        .transpose(0, 2, 1, 3)
        .reshape(rows, layers, columns)
    )


def turns(wave, index, period):
    product = wave * index
    if period & (period - 1) == 0:
        product = product & (period - 1)
    else:
        product = lax.rem(product, jnp.int32(period))
    return product.astype(f32) * (1.0 / period)


def cos_sin(turn):
    part = turn - jnp.floor(turn + 0.5)
    square = part * part

    def series(first):
        terms = [
            (-1.0) ** n * math.pi ** (2 * n + first) / math.factorial(2 * n + first)
            for n in range(7)
        ]
        total = jnp.full_like(square, terms[-1])
        for term in terms[-2::-1]:
            total = total * square + term
        return total

    half_cos = series(0)
    half_sin = series(1) * part
    return 1.0 - 2.0 * half_sin * half_sin, 2.0 * half_sin * half_cos


def halves(values):
    high = values.astype(jnp.bfloat16)
    return high, (values - high.astype(f32)).astype(jnp.bfloat16)


def height_lines(modes, step, first_row, count, row_total, chunks, column_total):
    mode_count = modes.shape[0]
    wave_x = modes[:, 0:1].astype(jnp.int32)
    wave_y = modes[:, 1:2].astype(jnp.int32)
    moment = modes[:, 2:3] * (step * (1.0 / 64.0))
    offset = modes[:, 3:4] * (0.5 / math.pi) + (moment - jnp.floor(moment))
    offset = jnp.concatenate([offset] * (count * chunks // LANES), 1)
    amp = modes[:, 4:5]
    spot = lax.broadcasted_iota(jnp.int32, (mode_count, count * chunks), 1)
    chunk = spot % chunks
    row = jnp.clip(first_row + spot // chunks, 0, row_total - 1)
    angle = (
        turns(wave_y, row, row_total) + turns(wave_x, chunk * LANES, column_total)
    ) + offset
    left_cos, left_sin = cos_sin(angle)
    lane = lax.broadcasted_iota(jnp.int32, (mode_count, LANES), 1)
    right_cos, right_sin = cos_sin(turns(wave_x, lane, column_total))
    left = jnp.concatenate([amp * left_cos, amp * left_sin], 0)
    right = jnp.concatenate([right_cos, -right_sin], 0)
    left_high, left_low = halves(left)
    right_high, right_low = halves(right)
    return lax.dot_general(
        jnp.concatenate([left_high, left_high, left_low], 0),
        jnp.concatenate([right_high, right_low, right_high], 0),
        (((0,), (0,)), ((), ())),
        preferred_element_type=f32,
    )


def inverse(values):
    return pl.reciprocal(values, approx=False)


def from_left(values, stride, lane):
    moved = [pltpu.roll(v, stride, 1) for v in values]
    return [jnp.where(lane < stride, moved[c - 1], moved[c]) for c in range(len(values))]


def from_right(values, stride, lane):
    count = len(values)
    moved = [pltpu.roll(v, LANES - stride, 1) for v in values]
    return [
        jnp.where(lane >= LANES - stride, moved[(c + 1) % count], moved[c]) for c in range(count)
    ]


def solve_chunks(diagonal, link, rhs):
    count = len(rhs)
    if count == 1:
        return [rhs[0] * inverse(diagonal[0])]
    inv = {i: inverse(diagonal[i]) for i in range(0, count, 2)}
    scaled = {i: inv[i] * rhs[i] for i in inv}
    odd_diagonal, odd_link, odd_rhs = [], [], []
    for i in range(1, count, 2):
        d = diagonal[i] - link[i - 1] * (link[i - 1] * inv[i - 1])
        r = rhs[i] + link[i - 1] * scaled[i - 1]
        e = None
        if i + 1 < count:
            by = link[i] * inv[i + 1]
            d = d - link[i] * by
            r = r + link[i] * scaled[i + 1]
            e = by * link[i + 1] if i + 2 < count else None
        odd_diagonal.append(d)
        odd_rhs.append(r)
        odd_link.append(e)
    odd = solve_chunks(odd_diagonal, odd_link, odd_rhs)
    out = [None] * count
    out[1::2] = odd
    for i in range(0, count, 2):
        r = rhs[i]
        if i > 0:
            r = r + link[i - 1] * out[i - 1]
        if i + 1 < count:
            r = r + link[i] * out[i + 1]
        out[i] = r * inv[i]
    return out


def reduce_lanes(diagonal, link, rhs, lane, stride):
    count = len(rhs)
    while stride < LANES:
        high_r = from_right(rhs, stride, lane)
        high_e = from_right(link, stride, lane)
        inv = [inverse(d) for d in diagonal]
        w = [q * e for q, e in zip(inv, link)]
        low_d = from_left([e * v for e, v in zip(link, w)], stride, lane)
        low_r = from_left([r * v for r, v in zip(rhs, w)], stride, lane)
        by = [e * q for e, q in zip(link, from_right(inv, stride, lane))]
        diagonal = [diagonal[c] - low_d[c] - link[c] * by[c] for c in range(count)]
        rhs = [rhs[c] + low_r[c] + by[c] * high_r[c] for c in range(count)]
        link = [by[c] * high_e[c] for c in range(count)]
        stride *= 2
    return solve_chunks(diagonal, link, rhs)


def pack_pair(a, b, odd_lane):
    even = [jnp.where(odd_lane, pltpu.roll(x, 1, 1), y) for x, y in zip(a, b)]
    odd = [jnp.where(odd_lane, x, pltpu.roll(y, LANES - 1, 1)) for x, y in zip(a, b)]
    return even, odd


def unpack_pair(even, odd, odd_lane):
    a = [jnp.where(odd_lane, y, pltpu.roll(x, LANES - 1, 1)) for x, y in zip(even, odd)]
    b = [jnp.where(odd_lane, pltpu.roll(y, 1, 1), x) for x, y in zip(even, odd)]
    return a, b


def solve_x_pair(g_pair, rhs_pair, lane):
    odd_lane = (lane & 1) == 1
    first_cell = lane < 2
    last_cell = lane >= LANES - 2
    half = 0.5 * weight
    g_even, g_odd = pack_pair(*g_pair, odd_lane)
    r_even, r_odd = pack_pair(*rhs_pair, odd_lane)
    face = [half * (a + b) for a, b in zip(g_even, g_odd)]
    after = from_right(g_even, 2, lane)
    after[-1] = jnp.where(last_cell, g_odd[-1], after[-1])
    face_after = [half * (a + b) for a, b in zip(g_odd, after)]
    face_before = from_left(face_after, 2, lane)
    face_before[0] = jnp.where(first_cell, weight * g_even[0], face_before[0])
    inv = [inverse(1.0 + (a + b)) for a, b in zip(face_before, face)]
    d_odd = [1.0 + (a + b) for a, b in zip(face, face_after)]
    link = list(face_after)
    link[-1] = jnp.where(last_cell, 0.0, link[-1])
    link_before = list(face_before)
    link_before[0] = jnp.where(first_cell, 0.0, link_before[0])
    t = [q * r for q, r in zip(inv, r_even)]
    w = [q * e for q, e in zip(inv, face)]
    next_q = from_right(inv, 2, lane)
    next_t = from_right(t, 2, lane)
    next_w = from_right(w, 2, lane)
    diagonal = [
        d - e * v - l * (l * q) for d, e, v, l, q in zip(d_odd, face, w, link, next_q)
    ]
    rhs = [r + e * v + l * n for r, e, v, l, n in zip(r_odd, face, t, link, next_t)]
    x_odd = reduce_lanes(diagonal, [l * n for l, n in zip(link, next_w)], rhs, lane, 2)
    x_before = from_left(x_odd, 2, lane)
    x_even = [
        v + q * (l * b) + u * x for v, q, l, b, u, x in zip(t, inv, link_before, x_before, w, x_odd)
    ]
    return unpack_pair(x_even, x_odd, odd_lane)


def pack_kernel(
    field_ref, index_ref, amp_ref, phase_ref,
    packed_ref, both_ref,
    index_in, amp_in, phase_in, sems,
):
    width = both_ref.shape[0] // 2
    last = field_ref.shape[0] - width
    pairs = (
        (index_ref, index_in),
        (amp_ref, amp_in),
        (phase_ref, phase_in),
        (field_ref.at[pl.ds(0, width)], both_ref.at[pl.ds(0, width)]),
        (field_ref.at[pl.ds(last, width)], both_ref.at[pl.ds(width, width)]),
    )
    copies = [pltpu.make_async_copy(a, b, sems.at[n]) for n, (a, b) in enumerate(pairs)]
    for copy in copies:
        copy.start()
    for copy in copies[:3]:
        copy.wait()
    row = lax.broadcasted_iota(jnp.int32, packed_ref.shape, 0)
    lane = lax.broadcasted_iota(jnp.int32, packed_ref.shape, 1)
    total = jnp.zeros(packed_ref.shape, f32)
    for m in range(index_in.shape[0]):
        waves = [index_in[m, n].astype(f32) for n in range(3)]
        for place, value in enumerate((*waves, phase_in[m], amp_in[m])):
            total = jnp.where((row == m) & (lane == place), value, total)
    packed_ref[...] = total
    for copy in copies[3:]:
        copy.wait()


def row_kernel(field_ref, step_ref, table_ref, inner_ref, outer_ref, step_in, sems):
    width = inner_ref.shape[0]
    pairs = (
        (step_ref, step_in),
        (field_ref.at[pl.ds(field_ref.shape[0] - width, width)], inner_ref),
        (field_ref.at[pl.ds(0, width)], outer_ref),
    )
    copies = [pltpu.make_async_copy(a, b, sems.at[n]) for n, (a, b) in enumerate(pairs)]
    for copy in copies:
        copy.start()
    for copy in copies:
        copy.wait()
    step = step_in[...].astype(f32).reshape(1, 1)
    table_ref[...] = jnp.broadcast_to(step, table_ref.shape)


def load_kernel(sizes, field_ref, conduct_ref, field_out, turned_ref, conduct_in, sems):
    rows, layers, chunks, row_total, layer_total, column_total = sizes
    width = layers * chunks
    copies = (
        pltpu.make_async_copy(field_ref, field_out, sems.at[0]),
        pltpu.make_async_copy(conduct_ref, conduct_in, sems.at[1]),
    )
    for copy in copies:
        copy.start()
    for n, (copy, ref) in enumerate(zip(copies, (field_out, conduct_in))):
        copy.wait()
        for place in range(width):
            spot = (n * width + place) * rows
            turned_ref[spot : spot + rows] = ref[pl.ds(place, rows, stride=width), :]


def block_factors(face):
    inv, scaled, chain, u = [], [], [], []
    rows = len(face) - 1
    rest = 1.0 + face[0]
    for j in range(rows):
        inv.append(inverse(rest + face[j + 1]))
        scaled.append(face[j] * inv[j])
        chain.append(face[j + 1] * inv[j])
        u.append(scaled[j] * u[-1] if j else scaled[j])
        rest = 1.0 + rest * chain[j]
    v = list(chain)
    for j in range(rows - 2, -1, -1):
        u[j] = u[j] + chain[j] * u[j + 1]
        v[j] = chain[j] * v[j + 1]
    return inv, scaled, chain, u, v


def height_kernel(sizes, handed_ref, came_ref, heights_ref):
    rows, layers, chunks, row_total, layer_total, column_total = sizes
    odd = lax.rem(lax.axis_index("wide"), 2) == 1
    first = 2 * layers * chunks
    own, other = handed_ref[first:], came_ref[first:]
    modes = jnp.where(odd, own, other)
    step = jnp.where(odd, other, own)
    body = height_lines(modes, step, 0, row_total, row_total, chunks, column_total)
    heights_ref[chunks : (row_total + 1) * chunks] = body
    heights_ref[0:chunks] = body[0:chunks]
    heights_ref[(row_total + 1) * chunks : (row_total + 2) * chunks] = body[
        (row_total - 1) * chunks : row_total * chunks
    ]

def main_kernel(
    sizes, heights, both_ref, below_ref, came_ref, turned_ref,
    sent_ref, p_ref, u_ref, v_ref, gain_ref, joint_ref,
    halo, solved,
):
    rows, layers, chunks, row_total, layer_total, column_total = sizes
    width = layers * chunks
    blocks = row_total // rows
    me = lax.axis_index("wide")
    first_layer = lax.axis_index("grp") * layers
    zeta = [
        ((first_layer + k).astype(f32) + 0.5) * (1.0 / layer_total) for k in range(layers)
    ]
    half = 0.5 * weight
    own_start = pl.multiple_of(me * (rows * chunks), 8)

    def face(low, high):
        both = heights[pl.ds(low, chunks), :] + heights[pl.ds(high, chunks), :]
        return jnp.concatenate([weight + (half * z) * both for z in zeta], 0)

    def aligned(index):
        return pl.multiple_of(index, 8)

    inv, scaled, chain, u, v = block_factors(
        [face(own_start + j * chunks, own_start + (j + 1) * chunks) for j in range(rows + 1)]
    )
    for j in range(rows):
        u_ref[j * width : (j + 1) * width] = u[j]
        v_ref[j * width : (j + 1) * width] = v[j]

    def one_block(n, carry):
        rest, link, left_link = carry
        upward = n < me
        b = jnp.where(upward, n, blocks - 1 - (n - me))
        start = b * (rows * chunks) + jnp.where(upward, 0, (rows + 1) * chunks)
        step = jnp.where(upward, chunks, -chunks)
        places = [aligned(start + j * step) for j in range(rows + 2)]
        first = face(places[0], places[1])
        anew = (n == 0) | (n == me)
        left_link = jnp.where(n == me, link, left_link)
        rest = jnp.where(anew, 1.0 + first, rest)
        for j in range(rows):
            after = face(places[j + 1], places[j + 2])
            link = after * inverse(rest + after)
            through = through * link if j else link
            rest = 1.0 + rest * link
        gain_ref[pl.ds(aligned(b * width), width), :] = through * (first * inverse(after))
        return rest, link, left_link

    gain_ref[pl.ds(aligned(me * width), width), :] = u[-1]
    nothing = 0.0 * u[0]
    carry = (nothing, nothing, nothing)
    if blocks <= 8:
        for n in range(blocks - 1):
            carry = one_block(n, carry)
    else:
        carry = lax.fori_loop(0, blocks - 1, one_block, carry)
    _, link, left_link = carry
    left_link = jnp.where(me == blocks - 1, link, left_link)
    right_link = jnp.where(me == blocks - 1, 0.0, link)

    a = 1.0 - left_link * u[0]
    b = left_link * v[0]
    c = right_link * u[-1]
    d = 1.0 - right_link * v[-1]
    by = inverse(a * d - b * c)
    joint = (
        u[-1] * inverse(a) * left_link, v[0] * inverse(d) * right_link,
        left_link, right_link, d * by, b * by, c * by, a * by,
    )
    for n, value in enumerate(joint):
        joint_ref[n * width : (n + 1) * width] = value

    odd = lax.rem(me, 2) == 1
    below = jnp.where(odd, came_ref[width : 2 * width], below_ref[...])
    above = jnp.where(odd, came_ref[0:width], both_ref[0:width])
    halo[0:width] = jnp.where(me == 0, 0.0, below)
    halo[width : 2 * width] = jnp.where(me == blocks - 1, 0.0, above)
    lane = lax.broadcasted_iota(jnp.int32, (rows, LANES), 1)
    row = lax.broadcasted_iota(jnp.int32, (rows, LANES), 0)

    def neighbours(values, low, high):
        return (
            jnp.where(row == 0, low, pltpu.roll(values, 1, 0)),
            jnp.where(row == rows - 1, high, pltpu.roll(values, rows - 1, 0)),
        )

    g = [[] for _ in range(layers)]
    f = [[] for _ in range(layers)]
    rhs = [[] for _ in range(layers)]
    for c in range(chunks):
        h = heights[pl.ds(own_start + chunks + c, rows, stride=chunks), :]
        h_low, h_high = neighbours(
            h,
            heights[pl.ds(own_start + c, 1), :],
            heights[pl.ds(own_start + (rows + 1) * chunks + c, 1), :],
        )
        low_sum, high_sum = h + h_low, h + h_high
        for k in range(layers):
            place = c * layers + k
            f_mid = turned_ref[place * rows : (place + 1) * rows]
            f_low, f_high = neighbours(
                f_mid, halo[pl.ds(place, 1), :], halo[pl.ds(width + place, 1), :]
            )
            g[k].append(
                turned_ref[(width + place) * rows : (width + place + 1) * rows] * (1.0 + zeta[k] * h)
            )
            f[k].append(f_mid)
            along = (weight + (half * zeta[k]) * high_sum) * (f_high - f_mid) - (
                weight + (half * zeta[k]) * low_sum
            ) * (f_mid - f_low)
            rhs[k].append(2.0 * (f_mid + along))
    for k in range(0, layers, 2):
        both = solve_x_pair(g[k : k + 2], rhs[k : k + 2], lane)
        for n in range(2):
            for c in range(chunks):
                spot = pl.ds((k + n) * chunks + c, rows, stride=width)
                solved[spot, :] = both[n][c] - 2.0 * f[k + n][c]

    def part(ref, j):
        return ref[j * width : (j + 1) * width]

    p = [part(solved, 0) * inv[0]]
    for j in range(1, rows):
        p.append(part(solved, j) * inv[j] + scaled[j] * p[-1])
    for j in range(rows - 2, -1, -1):
        p[j] = p[j] + chain[j] * p[j + 1]
    for j in range(rows):
        p_ref[j * width : (j + 1) * width] = p[j]

    upward = p[-1] + part(joint_ref, 0) * p[0]
    downward = p[0] + part(joint_ref, 1) * p[-1]
    for b in range(blocks):
        sent_ref[b * width : (b + 1) * width] = jnp.where(b > me, upward, downward)


def last_kernel(
    sizes, came_ref, gain_ref, joint_ref, p_ref, u_ref, v_ref, field_ref,
    out_ref,
):
    rows, layers, chunks, row_total, layer_total, column_total = sizes
    width = layers * chunks
    blocks = row_total // rows
    me = lax.axis_index("wide")

    def part(ref, b):
        return ref[b * width : (b + 1) * width]

    left = jnp.zeros((width, LANES), f32)
    right = jnp.zeros((width, LANES), f32)
    for b in range(blocks - 1):
        left = jnp.where(b < me, part(came_ref, b) + part(gain_ref, b) * left, left)
        b = blocks - 1 - b
        right = jnp.where(b > me, part(came_ref, b) + part(gain_ref, b) * right, right)

    y = left + part(joint_ref, 2) * part(p_ref, 0)
    z = right + part(joint_ref, 3) * part(p_ref, rows - 1)
    before = part(joint_ref, 4) * y + part(joint_ref, 5) * z
    after = part(joint_ref, 6) * y + part(joint_ref, 7) * z
    for j in range(rows):
        x = part(p_ref, j) + part(u_ref, j) * before + part(v_ref, j) * after
        for k in range(layers):
            spot = pl.ds(j * width + k, chunks, stride=layers)
            out_ref[spot, :] = field_ref[spot, :] + x[k * chunks : (k + 1) * chunks]


def on_device(field, conduct, mode_index, mode_amp, mode_phase, step_index):
    rows, layers, columns = field.shape
    wide_count = lax.axis_size("wide")
    row_total = rows * wide_count
    grp_count = lax.axis_size("grp")
    layer_total = layers * grp_count
    chunks = columns // LANES
    width = layers * chunks
    sizes = (rows, layers, chunks, row_total, layer_total, columns)
    limit = pltpu.CompilerParams(vmem_limit_bytes=16 * 1024 * 1024)
    hbm = pl.BlockSpec(memory_space=pltpu.HBM)

    def lines(count):
        return jax.ShapeDtypeStruct((count * width, LANES), f32)

    place = lax.axis_index("wide")
    odd = place % 2 == 1
    swaps = [(i, i ^ 1) for i in range(wide_count)]
    cores = [list(range(n, wide_count, 2)) for n in range(2)]
    table_shape = (grp_count * mode_index.shape[0], LANES)
    packed_shape = (mode_index.shape[0], LANES)
    in_hbm = lambda arrays: [pltpu.with_memory_space_constraint(a, pltpu.HBM) for a in arrays]

    def pack_modes(*arrays):
        return pl.pallas_call(
            pack_kernel,
            out_shape=(jax.ShapeDtypeStruct(packed_shape, f32), lines(2)),
            in_specs=[hbm] * 4,
            scratch_shapes=[pltpu.SMEM(a.shape, a.dtype) for a in arrays[1:]]
            + [pltpu.SemaphoreType.DMA((5,))],
            compiler_params=limit,
        )(*in_hbm(arrays))

    def pack_nothing(*arrays):
        return jnp.zeros(packed_shape, f32), jnp.zeros((2 * width, LANES), f32)

    packed, both = lax.cond(
        odd, pack_modes, pack_nothing, to_lines(field), mode_index, mode_amp, mode_phase
    )
    both_came = lax.ppermute(both, "wide", swaps)

    def gather_modes(own, *arrays):
        empty = jnp.zeros((width, LANES), f32)
        return lax.all_gather(own, "grp", axis=0, tiled=True), empty, empty

    def load_rows(own, *arrays):
        return pl.pallas_call(
            row_kernel,
            out_shape=(jax.ShapeDtypeStruct(table_shape, f32), lines(1), lines(1)),
            in_specs=[hbm] * 2,
            scratch_shapes=[
                pltpu.VMEM(step_index.shape, step_index.dtype),
                pltpu.SemaphoreType.DMA((3,)),
            ],
            compiler_params=limit,
        )(*in_hbm(arrays))

    table, inner, outer = lax.cond(
        odd, gather_modes, load_rows, packed, to_lines(field), step_index
    )
    table, inner, outer, both_came = lax.optimization_barrier((table, inner, outer, both_came))

    def gather_rows(own, came):
        rows_sent = jnp.concatenate([own, came[width:]], 0)
        rows_all = lax.all_gather(rows_sent, "wide", axis_index_groups=cores, axis=0)
        chip = place // 2
        below = lax.dynamic_index_in_dim(rows_all, jnp.maximum(chip - 1, 0), 0, False)
        above = lax.dynamic_index_in_dim(
            rows_all, jnp.minimum(chip + 1, wide_count // 2 - 1), 0, False
        )
        return below[width:], above[:width]

    def no_rows(own, came):
        return jnp.zeros_like(own), jnp.zeros_like(own)

    below, above = lax.cond(odd, no_rows, gather_rows, outer, both_came)
    handed = jnp.concatenate([above, inner, table], 0)
    came = lax.ppermute(handed, "wide", swaps)
    handed, field, conduct = lax.optimization_barrier((handed, field, conduct))
    field_lines, turned = pl.pallas_call(
        functools.partial(load_kernel, sizes),
        out_shape=(lines(rows), lines(2 * rows)),
        in_specs=[hbm] * 2,
        scratch_shapes=[
            pltpu.VMEM((rows * width, LANES), f32),
            pltpu.SemaphoreType.DMA((2,)),
        ],
        compiler_params=limit,
    )(
        *(
            pltpu.with_memory_space_constraint(to_lines(a), pltpu.HBM)
            for a in (field, conduct)
        )
    )
    heights = pl.pallas_call(
        functools.partial(height_kernel, sizes),
        out_shape=jax.ShapeDtypeStruct(((row_total + 2) * chunks, LANES), f32),
        compiler_params=limit,
    )(handed, came)

    sent, p, u, v, gain, joint = pl.pallas_call(
        functools.partial(main_kernel, sizes),
        out_shape=(lines(wide_count),)
        + (lines(rows),) * 3
        + (lines(wide_count), lines(8)),
        scratch_shapes=[
            pltpu.VMEM((2 * width, LANES), f32),
            pltpu.VMEM((rows * width, LANES), f32),
        ],
        compiler_params=limit,
    )(heights, both_came, below, came, turned)

    came = lax.all_to_all(
        sent.reshape(wide_count, width, LANES), "wide", split_axis=0, concat_axis=0
    ).reshape(wide_count * width, LANES)

    advanced = pl.pallas_call(
        functools.partial(last_kernel, sizes),
        out_shape=lines(rows),
        compiler_params=limit,
    )(came, gain, joint, p, u, v, field_lines)
    return from_lines(advanced, field.shape)


def solution(mesh):
    return jax.shard_map(
        on_device,
        mesh=mesh,
        in_specs=(
            P("wide", "grp", None),
            P("wide", "grp", None),
            P("grp", None),
            P("grp"),
            P("grp"),
            P(),
        ),
        out_specs=P("wide", "grp", None),
        check_vma=False,
    )
```

```python
import functools
import math

import jax
import jax.numpy as jnp
from jax import lax
from jax.experimental import pallas as pl
from jax.experimental.pallas import tpu as pltpu
from jax.sharding import PartitionSpec as P

time_step = 600.0
implicit_weight = 0.5
weight = implicit_weight * time_step
LANES = 128
f32 = jnp.float32


def to_lines(block):
    rows, layers, columns = block.shape
    chunks = columns // LANES
    return (
        block.reshape(rows, layers, chunks, LANES)
        .transpose(0, 2, 1, 3)
        .reshape(rows * chunks * layers, LANES)
    )


def from_lines(lines, shape):
    rows, layers, columns = shape
    chunks = columns // LANES
    return (
        lines.reshape(rows, chunks, layers, LANES)
        .transpose(0, 2, 1, 3)
        .reshape(rows, layers, columns)
    )


def turns(wave, index, period):
    product = wave * index
    if period & (period - 1) == 0:
        product = product & (period - 1)
    else:
        product = lax.rem(product, jnp.int32(period))
    return product.astype(f32) * (1.0 / period)


def cos_sin(turn):
    part = turn - jnp.floor(turn + 0.5)
    square = part * part

    def series(first):
        terms = [
            (-1.0) ** n * math.pi ** (2 * n + first) / math.factorial(2 * n + first)
            for n in range(7)
        ]
        total = jnp.full_like(square, terms[-1])
        for term in terms[-2::-1]:
            total = total * square + term
        return total

    half_cos = series(0)
    half_sin = series(1) * part
    return 1.0 - 2.0 * half_sin * half_sin, 2.0 * half_sin * half_cos


def halves(values):
    high = values.astype(jnp.bfloat16)
    return high, (values - high.astype(f32)).astype(jnp.bfloat16)


def height_lines(modes, step, first_row, count, row_total, chunks, column_total):
    mode_count = modes.shape[0]
    wave_x = modes[:, 0:1].astype(jnp.int32)
    wave_y = modes[:, 1:2].astype(jnp.int32)
    moment = modes[:, 2:3] * (step * (1.0 / 64.0))
    offset = modes[:, 3:4] * (0.5 / math.pi) + (moment - jnp.floor(moment))
    offset = jnp.concatenate([offset] * (count * chunks // LANES), 1)
    amp = modes[:, 4:5]
    spot = lax.broadcasted_iota(jnp.int32, (mode_count, count * chunks), 1)
    chunk = spot % chunks
    row = jnp.clip(first_row + spot // chunks, 0, row_total - 1)
    angle = (
        turns(wave_y, row, row_total) + turns(wave_x, chunk * LANES, column_total)
    ) + offset
    left_cos, left_sin = cos_sin(angle)
    lane = lax.broadcasted_iota(jnp.int32, (mode_count, LANES), 1)
    right_cos, right_sin = cos_sin(turns(wave_x, lane, column_total))
    left = jnp.concatenate([amp * left_cos, amp * left_sin], 0)
    right = jnp.concatenate([right_cos, -right_sin], 0)
    left_high, left_low = halves(left)
    right_high, right_low = halves(right)
    return lax.dot_general(
        jnp.concatenate([left_high, left_high, left_low], 0),
        jnp.concatenate([right_high, right_low, right_high], 0),
        (((0,), (0,)), ((), ())),
        preferred_element_type=f32,
    )


def inverse(values):
    return pl.reciprocal(values, approx=False)


def from_left(values, stride, lane):
    moved = [pltpu.roll(v, stride, 1) for v in values]
    return [jnp.where(lane < stride, moved[c - 1], moved[c]) for c in range(len(values))]


def from_right(values, stride, lane):
    count = len(values)
    moved = [pltpu.roll(v, LANES - stride, 1) for v in values]
    return [
        jnp.where(lane >= LANES - stride, moved[(c + 1) % count], moved[c]) for c in range(count)
    ]


def solve_chunks(diagonal, link, rhs):
    count = len(rhs)
    if count == 1:
        return [rhs[0] * inverse(diagonal[0])]
    inv = {i: inverse(diagonal[i]) for i in range(0, count, 2)}
    scaled = {i: inv[i] * rhs[i] for i in inv}
    odd_diagonal, odd_link, odd_rhs = [], [], []
    for i in range(1, count, 2):
        d = diagonal[i] - link[i - 1] * (link[i - 1] * inv[i - 1])
        r = rhs[i] + link[i - 1] * scaled[i - 1]
        e = None
        if i + 1 < count:
            by = link[i] * inv[i + 1]
            d = d - link[i] * by
            r = r + link[i] * scaled[i + 1]
            e = by * link[i + 1] if i + 2 < count else None
        odd_diagonal.append(d)
        odd_rhs.append(r)
        odd_link.append(e)
    odd = solve_chunks(odd_diagonal, odd_link, odd_rhs)
    out = [None] * count
    out[1::2] = odd
    for i in range(0, count, 2):
        r = rhs[i]
        if i > 0:
            r = r + link[i - 1] * out[i - 1]
        if i + 1 < count:
            r = r + link[i] * out[i + 1]
        out[i] = r * inv[i]
    return out


def reduce_lanes(diagonal, link, rhs, lane, stride):
    count = len(rhs)
    while stride < LANES:
        high_r = from_right(rhs, stride, lane)
        high_e = from_right(link, stride, lane)
        inv = [inverse(d) for d in diagonal]
        w = [q * e for q, e in zip(inv, link)]
        low_d = from_left([e * v for e, v in zip(link, w)], stride, lane)
        low_r = from_left([r * v for r, v in zip(rhs, w)], stride, lane)
        by = [e * q for e, q in zip(link, from_right(inv, stride, lane))]
        diagonal = [diagonal[c] - low_d[c] - link[c] * by[c] for c in range(count)]
        rhs = [rhs[c] + low_r[c] + by[c] * high_r[c] for c in range(count)]
        link = [by[c] * high_e[c] for c in range(count)]
        stride *= 2
    return solve_chunks(diagonal, link, rhs)


def pack_pair(a, b, odd_lane):
    even = [jnp.where(odd_lane, pltpu.roll(x, 1, 1), y) for x, y in zip(a, b)]
    odd = [jnp.where(odd_lane, x, pltpu.roll(y, LANES - 1, 1)) for x, y in zip(a, b)]
    return even, odd


def unpack_pair(even, odd, odd_lane):
    a = [jnp.where(odd_lane, y, pltpu.roll(x, LANES - 1, 1)) for x, y in zip(even, odd)]
    b = [jnp.where(odd_lane, pltpu.roll(y, 1, 1), x) for x, y in zip(even, odd)]
    return a, b


def solve_x_pair(g_pair, rhs_pair, lane):
    odd_lane = (lane & 1) == 1
    first_cell = lane < 2
    last_cell = lane >= LANES - 2
    half = 0.5 * weight
    g_even, g_odd = pack_pair(*g_pair, odd_lane)
    r_even, r_odd = pack_pair(*rhs_pair, odd_lane)
    face = [half * (a + b) for a, b in zip(g_even, g_odd)]
    after = from_right(g_even, 2, lane)
    after[-1] = jnp.where(last_cell, g_odd[-1], after[-1])
    face_after = [half * (a + b) for a, b in zip(g_odd, after)]
    face_before = from_left(face_after, 2, lane)
    face_before[0] = jnp.where(first_cell, weight * g_even[0], face_before[0])
    inv = [inverse(1.0 + (a + b)) for a, b in zip(face_before, face)]
    d_odd = [1.0 + (a + b) for a, b in zip(face, face_after)]
    link = list(face_after)
    link[-1] = jnp.where(last_cell, 0.0, link[-1])
    link_before = list(face_before)
    link_before[0] = jnp.where(first_cell, 0.0, link_before[0])
    t = [q * r for q, r in zip(inv, r_even)]
    w = [q * e for q, e in zip(inv, face)]
    next_q = from_right(inv, 2, lane)
    next_t = from_right(t, 2, lane)
    next_w = from_right(w, 2, lane)
    diagonal = [
        d - e * v - l * (l * q) for d, e, v, l, q in zip(d_odd, face, w, link, next_q)
    ]
    rhs = [r + e * v + l * n for r, e, v, l, n in zip(r_odd, face, t, link, next_t)]
    x_odd = reduce_lanes(diagonal, [l * n for l, n in zip(link, next_w)], rhs, lane, 2)
    x_before = from_left(x_odd, 2, lane)
    x_even = [
        v + q * (l * b) + u * x for v, q, l, b, u, x in zip(t, inv, link_before, x_before, w, x_odd)
    ]
    return unpack_pair(x_even, x_odd, odd_lane)


def pack_kernel(
    field_ref, index_ref, amp_ref, phase_ref,
    packed_ref, both_ref,
    index_in, amp_in, phase_in, sems,
):
    width = both_ref.shape[0] // 2
    last = field_ref.shape[0] - width
    pairs = (
        (index_ref, index_in),
        (amp_ref, amp_in),
        (phase_ref, phase_in),
        (field_ref.at[pl.ds(0, width)], both_ref.at[pl.ds(0, width)]),
        (field_ref.at[pl.ds(last, width)], both_ref.at[pl.ds(width, width)]),
    )
    copies = [pltpu.make_async_copy(a, b, sems.at[n]) for n, (a, b) in enumerate(pairs)]
    for copy in copies:
        copy.start()
    for copy in copies[:3]:
        copy.wait()
    row = lax.broadcasted_iota(jnp.int32, packed_ref.shape, 0)
    lane = lax.broadcasted_iota(jnp.int32, packed_ref.shape, 1)
    total = jnp.zeros(packed_ref.shape, f32)
    for m in range(index_in.shape[0]):
        waves = [index_in[m, n].astype(f32) for n in range(3)]
        for place, value in enumerate((*waves, phase_in[m], amp_in[m])):
            total = jnp.where((row == m) & (lane == place), value, total)
    packed_ref[...] = total
    for copy in copies[3:]:
        copy.wait()


def row_kernel(field_ref, step_ref, table_ref, inner_ref, outer_ref, step_in, sems):
    width = inner_ref.shape[0]
    pairs = (
        (step_ref, step_in),
        (field_ref.at[pl.ds(field_ref.shape[0] - width, width)], inner_ref),
        (field_ref.at[pl.ds(0, width)], outer_ref),
    )
    copies = [pltpu.make_async_copy(a, b, sems.at[n]) for n, (a, b) in enumerate(pairs)]
    for copy in copies:
        copy.start()
    for copy in copies:
        copy.wait()
    step = step_in[...].astype(f32).reshape(1, 1)
    table_ref[...] = jnp.broadcast_to(step, table_ref.shape)


def load_kernel(sizes, field_ref, conduct_ref, field_out, turned_ref, conduct_in, sems):
    rows, layers, chunks, row_total, layer_total, column_total = sizes
    width = layers * chunks
    copies = (
        pltpu.make_async_copy(field_ref, field_out, sems.at[0]),
        pltpu.make_async_copy(conduct_ref, conduct_in, sems.at[1]),
    )
    for copy in copies:
        copy.start()
    for n, (copy, ref) in enumerate(zip(copies, (field_out, conduct_in))):
        copy.wait()
        for place in range(width):
            spot = (n * width + place) * rows
            turned_ref[spot : spot + rows] = ref[pl.ds(place, rows, stride=width), :]


def block_factors(face):
    inv, scaled, chain, u = [], [], [], []
    rows = len(face) - 1
    rest = 1.0 + face[0]
    for j in range(rows):
        inv.append(inverse(rest + face[j + 1]))
        scaled.append(face[j] * inv[j])
        chain.append(face[j + 1] * inv[j])
        u.append(scaled[j] * u[-1] if j else scaled[j])
        rest = 1.0 + rest * chain[j]
    v = list(chain)
    for j in range(rows - 2, -1, -1):
        u[j] = u[j] + chain[j] * u[j + 1]
        v[j] = chain[j] * v[j + 1]
    return inv, scaled, chain, u, v


def height_kernel(sizes, handed_ref, came_ref, heights_ref):
    rows, layers, chunks, row_total, layer_total, column_total = sizes
    odd = lax.rem(lax.axis_index("wide"), 2) == 1
    first = 2 * layers * chunks
    own, other = handed_ref[first:], came_ref[first:]
    modes = jnp.where(odd, own, other)
    step = jnp.where(odd, other, own)
    body = height_lines(modes, step, 0, row_total, row_total, chunks, column_total)
    heights_ref[chunks : (row_total + 1) * chunks] = body
    heights_ref[0:chunks] = body[0:chunks]
    heights_ref[(row_total + 1) * chunks : (row_total + 2) * chunks] = body[
        (row_total - 1) * chunks : row_total * chunks
    ]

def main_kernel(
    sizes, heights, both_ref, below_ref, came_ref, turned_ref,
    sent_ref, p_ref, u_ref, v_ref, gain_ref, joint_ref,
    halo, solved,
):
    rows, layers, chunks, row_total, layer_total, column_total = sizes
    width = layers * chunks
    blocks = row_total // rows
    me = lax.axis_index("wide")
    first_layer = lax.axis_index("grp") * layers
    zeta = [
        ((first_layer + k).astype(f32) + 0.5) * (1.0 / layer_total) for k in range(layers)
    ]
    half = 0.5 * weight
    own_start = pl.multiple_of(me * (rows * chunks), 8)

    def face(low, high):
        both = heights[pl.ds(low, chunks), :] + heights[pl.ds(high, chunks), :]
        return jnp.concatenate([weight + (half * z) * both for z in zeta], 0)

    def aligned(index):
        return pl.multiple_of(index, 8)

    inv, scaled, chain, u, v = block_factors(
        [face(own_start + j * chunks, own_start + (j + 1) * chunks) for j in range(rows + 1)]
    )
    for j in range(rows):
        u_ref[j * width : (j + 1) * width] = u[j]
        v_ref[j * width : (j + 1) * width] = v[j]

    def one_block(n, carry):
        rest, link, left_link = carry
        upward = n < me
        b = jnp.where(upward, n, blocks - 1 - (n - me))
        start = b * (rows * chunks) + jnp.where(upward, 0, (rows + 1) * chunks)
        step = jnp.where(upward, chunks, -chunks)
        places = [aligned(start + j * step) for j in range(rows + 2)]
        first = face(places[0], places[1])
        anew = (n == 0) | (n == me)
        left_link = jnp.where(n == me, link, left_link)
        rest = jnp.where(anew, 1.0 + first, rest)
        for j in range(rows):
            after = face(places[j + 1], places[j + 2])
            link = after * inverse(rest + after)
            through = through * link if j else link
            rest = 1.0 + rest * link
        gain_ref[pl.ds(aligned(b * width), width), :] = through * (first * inverse(after))
        return rest, link, left_link

    gain_ref[pl.ds(aligned(me * width), width), :] = u[-1]
    nothing = 0.0 * u[0]
    carry = (nothing, nothing, nothing)
    if blocks <= 8:
        for n in range(blocks - 1):
            carry = one_block(n, carry)
    else:
        carry = lax.fori_loop(0, blocks - 1, one_block, carry)
    _, link, left_link = carry
    left_link = jnp.where(me == blocks - 1, link, left_link)
    right_link = jnp.where(me == blocks - 1, 0.0, link)

    a = 1.0 - left_link * u[0]
    b = left_link * v[0]
    c = right_link * u[-1]
    d = 1.0 - right_link * v[-1]
    by = inverse(a * d - b * c)
    joint = (
        u[-1] * inverse(a) * left_link, v[0] * inverse(d) * right_link,
        left_link, right_link, d * by, b * by, c * by, a * by,
    )
    for n, value in enumerate(joint):
        joint_ref[n * width : (n + 1) * width] = value

    odd = lax.rem(me, 2) == 1
    below = jnp.where(odd, came_ref[width : 2 * width], below_ref[...])
    above = jnp.where(odd, came_ref[0:width], both_ref[0:width])
    halo[0:width] = jnp.where(me == 0, 0.0, below)
    halo[width : 2 * width] = jnp.where(me == blocks - 1, 0.0, above)
    lane = lax.broadcasted_iota(jnp.int32, (rows, LANES), 1)
    row = lax.broadcasted_iota(jnp.int32, (rows, LANES), 0)

    def neighbours(values, low, high):
        return (
            jnp.where(row == 0, low, pltpu.roll(values, 1, 0)),
            jnp.where(row == rows - 1, high, pltpu.roll(values, rows - 1, 0)),
        )

    g = [[] for _ in range(layers)]
    f = [[] for _ in range(layers)]
    rhs = [[] for _ in range(layers)]
    for c in range(chunks):
        h = heights[pl.ds(own_start + chunks + c, rows, stride=chunks), :]
        h_low, h_high = neighbours(
            h,
            heights[pl.ds(own_start + c, 1), :],
            heights[pl.ds(own_start + (rows + 1) * chunks + c, 1), :],
        )
        low_sum, high_sum = h + h_low, h + h_high
        for k in range(layers):
            place = c * layers + k
            f_mid = turned_ref[place * rows : (place + 1) * rows]
            f_low, f_high = neighbours(
                f_mid, halo[pl.ds(place, 1), :], halo[pl.ds(width + place, 1), :]
            )
            g[k].append(
                turned_ref[(width + place) * rows : (width + place + 1) * rows] * (1.0 + zeta[k] * h)
            )
            f[k].append(f_mid)
            along = (weight + (half * zeta[k]) * high_sum) * (f_high - f_mid) - (
                weight + (half * zeta[k]) * low_sum
            ) * (f_mid - f_low)
            rhs[k].append(2.0 * (f_mid + along))
    for k in range(0, layers, 2):
        both = solve_x_pair(g[k : k + 2], rhs[k : k + 2], lane)
        for n in range(2):
            for c in range(chunks):
                spot = pl.ds((k + n) * chunks + c, rows, stride=width)
                solved[spot, :] = both[n][c] - 2.0 * f[k + n][c]

    def part(ref, j):
        return ref[j * width : (j + 1) * width]

    p = [part(solved, 0) * inv[0]]
    for j in range(1, rows):
        p.append(part(solved, j) * inv[j] + scaled[j] * p[-1])
    for j in range(rows - 2, -1, -1):
        p[j] = p[j] + chain[j] * p[j + 1]
    for j in range(rows):
        p_ref[j * width : (j + 1) * width] = p[j]

    upward = p[-1] + part(joint_ref, 0) * p[0]
    downward = p[0] + part(joint_ref, 1) * p[-1]
    for b in range(blocks):
        sent_ref[b * width : (b + 1) * width] = jnp.where(b > me, upward, downward)


def last_kernel(
    sizes, came_ref, gain_ref, joint_ref, p_ref, u_ref, v_ref, field_ref,
    out_ref,
):
    rows, layers, chunks, row_total, layer_total, column_total = sizes
    width = layers * chunks
    blocks = row_total // rows
    me = lax.axis_index("wide")

    def part(ref, b):
        return ref[b * width : (b + 1) * width]

    left = jnp.zeros((width, LANES), f32)
    right = jnp.zeros((width, LANES), f32)
    for b in range(blocks - 1):
        left = jnp.where(b < me, part(came_ref, b) + part(gain_ref, b) * left, left)
        b = blocks - 1 - b
        right = jnp.where(b > me, part(came_ref, b) + part(gain_ref, b) * right, right)

    y = left + part(joint_ref, 2) * part(p_ref, 0)
    z = right + part(joint_ref, 3) * part(p_ref, rows - 1)
    before = part(joint_ref, 4) * y + part(joint_ref, 5) * z
    after = part(joint_ref, 6) * y + part(joint_ref, 7) * z
    for j in range(rows):
        x = part(p_ref, j) + part(u_ref, j) * before + part(v_ref, j) * after
        for k in range(layers):
            spot = pl.ds(j * width + k, chunks, stride=layers)
            out_ref[spot, :] = field_ref[spot, :] + x[k * chunks : (k + 1) * chunks]


def on_device(field, conduct, mode_index, mode_amp, mode_phase, step_index):
    rows, layers, columns = field.shape
    wide_count = lax.axis_size("wide")
    row_total = rows * wide_count
    grp_count = lax.axis_size("grp")
    layer_total = layers * grp_count
    chunks = columns // LANES
    width = layers * chunks
    sizes = (rows, layers, chunks, row_total, layer_total, columns)
    limit = pltpu.CompilerParams(vmem_limit_bytes=16 * 1024 * 1024)
    hbm = pl.BlockSpec(memory_space=pltpu.HBM)

    def lines(count):
        return jax.ShapeDtypeStruct((count * width, LANES), f32)

    place = lax.axis_index("wide")
    odd = place % 2 == 1
    swaps = [(i, i ^ 1) for i in range(wide_count)]
    cores = [list(range(n, wide_count, 2)) for n in range(2)]
    table_shape = (grp_count * mode_index.shape[0], LANES)
    packed_shape = (mode_index.shape[0], LANES)
    in_hbm = lambda arrays: [pltpu.with_memory_space_constraint(a, pltpu.HBM) for a in arrays]

    def pack_modes(*arrays):
        return pl.pallas_call(
            pack_kernel,
            out_shape=(jax.ShapeDtypeStruct(packed_shape, f32), lines(2)),
            in_specs=[hbm] * 4,
            scratch_shapes=[pltpu.SMEM(a.shape, a.dtype) for a in arrays[1:]]
            + [pltpu.SemaphoreType.DMA((5,))],
            compiler_params=limit,
        )(*in_hbm(arrays))

    def pack_nothing(*arrays):
        return jnp.zeros(packed_shape, f32), jnp.zeros((2 * width, LANES), f32)

    packed, both = lax.cond(
        odd, pack_modes, pack_nothing, to_lines(field), mode_index, mode_amp, mode_phase
    )
    both_came = lax.ppermute(both, "wide", swaps)

    def gather_modes(own, *arrays):
        empty = jnp.zeros((width, LANES), f32)
        return lax.all_gather(own, "grp", axis=0, tiled=True), empty, empty

    def load_rows(own, *arrays):
        return pl.pallas_call(
            row_kernel,
            out_shape=(jax.ShapeDtypeStruct(table_shape, f32), lines(1), lines(1)),
            in_specs=[hbm] * 2,
            scratch_shapes=[
                pltpu.VMEM(step_index.shape, step_index.dtype),
                pltpu.SemaphoreType.DMA((3,)),
            ],
            compiler_params=limit,
        )(*in_hbm(arrays))

    table, inner, outer = lax.cond(
        odd, gather_modes, load_rows, packed, to_lines(field), step_index
    )
    table, inner, outer, both_came = lax.optimization_barrier((table, inner, outer, both_came))

    def gather_rows(own, came):
        chip = place // 2
        to_next = jnp.arange(wide_count // 2)[:, None, None] == chip + 1
        rows_sent = jnp.where(to_next, came[None, width:], own[None])
        rows_all = lax.all_to_all(
            rows_sent, "wide", split_axis=0, concat_axis=0, axis_index_groups=cores
        )
        below = lax.dynamic_index_in_dim(rows_all, jnp.maximum(chip - 1, 0), 0, False)
        above = lax.dynamic_index_in_dim(
            rows_all, jnp.minimum(chip + 1, wide_count // 2 - 1), 0, False
        )
        return below, above

    def no_rows(own, came):
        return jnp.zeros_like(own), jnp.zeros_like(own)

    below, above = lax.cond(odd, no_rows, gather_rows, outer, both_came)
    handed = jnp.concatenate([above, inner, table], 0)
    came = lax.ppermute(handed, "wide", swaps)
    handed, field, conduct = lax.optimization_barrier((handed, field, conduct))
    field_lines, turned = pl.pallas_call(
        functools.partial(load_kernel, sizes),
        out_shape=(lines(rows), lines(2 * rows)),
        in_specs=[hbm] * 2,
        scratch_shapes=[
            pltpu.VMEM((rows * width, LANES), f32),
            pltpu.SemaphoreType.DMA((2,)),
        ],
        compiler_params=limit,
    )(
        *(
            pltpu.with_memory_space_constraint(to_lines(a), pltpu.HBM)
            for a in (field, conduct)
        )
    )
    heights = pl.pallas_call(
        functools.partial(height_kernel, sizes),
        out_shape=jax.ShapeDtypeStruct(((row_total + 2) * chunks, LANES), f32),
        compiler_params=limit,
    )(handed, came)

    sent, p, u, v, gain, joint = pl.pallas_call(
        functools.partial(main_kernel, sizes),
        out_shape=(lines(wide_count),)
        + (lines(rows),) * 3
        + (lines(wide_count), lines(8)),
        scratch_shapes=[
            pltpu.VMEM((2 * width, LANES), f32),
            pltpu.VMEM((rows * width, LANES), f32),
        ],
        compiler_params=limit,
    )(heights, both_came, below, came, turned)

    came = lax.all_to_all(
        sent.reshape(wide_count, width, LANES), "wide", split_axis=0, concat_axis=0
    ).reshape(wide_count * width, LANES)

    advanced = pl.pallas_call(
        functools.partial(last_kernel, sizes),
        out_shape=lines(rows),
        compiler_params=limit,
    )(came, gain, joint, p, u, v, field_lines)
    return from_lines(advanced, field.shape)


def solution(mesh):
    return jax.shard_map(
        on_device,
        mesh=mesh,
        in_specs=(
            P("wide", "grp", None),
            P("wide", "grp", None),
            P("grp", None),
            P("grp"),
            P("grp"),
            P(),
        ),
        out_specs=P("wide", "grp", None),
        check_vma=False,
    )
```

```python
import functools
import math

import jax
import jax.numpy as jnp
from jax import lax
from jax.experimental import pallas as pl
from jax.experimental.pallas import tpu as pltpu
from jax.sharding import PartitionSpec as P

time_step = 600.0
implicit_weight = 0.5
weight = implicit_weight * time_step
LANES = 128
f32 = jnp.float32


def to_lines(block):
    rows, layers, columns = block.shape
    chunks = columns // LANES
    return (
        block.reshape(rows, layers, chunks, LANES)
        .transpose(0, 2, 1, 3)
        .reshape(rows * chunks * layers, LANES)
    )


def from_lines(lines, shape):
    rows, layers, columns = shape
    chunks = columns // LANES
    return (
        lines.reshape(rows, chunks, layers, LANES)
        .transpose(0, 2, 1, 3)
        .reshape(rows, layers, columns)
    )


def turns(wave, index, period):
    product = wave * index
    if period & (period - 1) == 0:
        product = product & (period - 1)
    else:
        product = lax.rem(product, jnp.int32(period))
    return product.astype(f32) * (1.0 / period)


def cos_sin(turn):
    part = turn - jnp.floor(turn + 0.5)
    square = part * part

    def series(first):
        terms = [
            (-1.0) ** n * math.pi ** (2 * n + first) / math.factorial(2 * n + first)
            for n in range(7)
        ]
        total = jnp.full_like(square, terms[-1])
        for term in terms[-2::-1]:
            total = total * square + term
        return total

    half_cos = series(0)
    half_sin = series(1) * part
    return 1.0 - 2.0 * half_sin * half_sin, 2.0 * half_sin * half_cos


def halves(values):
    high = values.astype(jnp.bfloat16)
    return high, (values - high.astype(f32)).astype(jnp.bfloat16)


def height_lines(modes, step, first_row, count, row_total, chunks, column_total):
    mode_count = modes.shape[0]
    wave_x = modes[:, 0:1].astype(jnp.int32)
    wave_y = modes[:, 1:2].astype(jnp.int32)
    moment = modes[:, 2:3] * (step * (1.0 / 64.0))
    offset = modes[:, 3:4] * (0.5 / math.pi) + (moment - jnp.floor(moment))
    offset = jnp.concatenate([offset] * (count * chunks // LANES), 1)
    amp = modes[:, 4:5]
    spot = lax.broadcasted_iota(jnp.int32, (mode_count, count * chunks), 1)
    chunk = spot % chunks
    row = jnp.clip(first_row + spot // chunks, 0, row_total - 1)
    angle = (
        turns(wave_y, row, row_total) + turns(wave_x, chunk * LANES, column_total)
    ) + offset
    left_cos, left_sin = cos_sin(angle)
    lane = lax.broadcasted_iota(jnp.int32, (mode_count, LANES), 1)
    right_cos, right_sin = cos_sin(turns(wave_x, lane, column_total))
    left = jnp.concatenate([amp * left_cos, amp * left_sin], 0)
    right = jnp.concatenate([right_cos, -right_sin], 0)
    left_high, left_low = halves(left)
    right_high, right_low = halves(right)
    return lax.dot_general(
        jnp.concatenate([left_high, left_high, left_low], 0),
        jnp.concatenate([right_high, right_low, right_high], 0),
        (((0,), (0,)), ((), ())),
        preferred_element_type=f32,
    )


def inverse(values):
    return pl.reciprocal(values, approx=False)


def from_left(values, stride, lane):
    moved = [pltpu.roll(v, stride, 1) for v in values]
    return [jnp.where(lane < stride, moved[c - 1], moved[c]) for c in range(len(values))]


def from_right(values, stride, lane):
    count = len(values)
    moved = [pltpu.roll(v, LANES - stride, 1) for v in values]
    return [
        jnp.where(lane >= LANES - stride, moved[(c + 1) % count], moved[c]) for c in range(count)
    ]


def solve_chunks(diagonal, link, rhs):
    count = len(rhs)
    if count == 1:
        return [rhs[0] * inverse(diagonal[0])]
    inv = {i: inverse(diagonal[i]) for i in range(0, count, 2)}
    scaled = {i: inv[i] * rhs[i] for i in inv}
    odd_diagonal, odd_link, odd_rhs = [], [], []
    for i in range(1, count, 2):
        d = diagonal[i] - link[i - 1] * (link[i - 1] * inv[i - 1])
        r = rhs[i] + link[i - 1] * scaled[i - 1]
        e = None
        if i + 1 < count:
            by = link[i] * inv[i + 1]
            d = d - link[i] * by
            r = r + link[i] * scaled[i + 1]
            e = by * link[i + 1] if i + 2 < count else None
        odd_diagonal.append(d)
        odd_rhs.append(r)
        odd_link.append(e)
    odd = solve_chunks(odd_diagonal, odd_link, odd_rhs)
    out = [None] * count
    out[1::2] = odd
    for i in range(0, count, 2):
        r = rhs[i]
        if i > 0:
            r = r + link[i - 1] * out[i - 1]
        if i + 1 < count:
            r = r + link[i] * out[i + 1]
        out[i] = r * inv[i]
    return out


def reduce_lanes(diagonal, link, rhs, lane, stride):
    count = len(rhs)
    while stride < LANES:
        high_r = from_right(rhs, stride, lane)
        high_e = from_right(link, stride, lane)
        inv = [inverse(d) for d in diagonal]
        w = [q * e for q, e in zip(inv, link)]
        low_d = from_left([e * v for e, v in zip(link, w)], stride, lane)
        low_r = from_left([r * v for r, v in zip(rhs, w)], stride, lane)
        by = [e * q for e, q in zip(link, from_right(inv, stride, lane))]
        diagonal = [diagonal[c] - low_d[c] - link[c] * by[c] for c in range(count)]
        rhs = [rhs[c] + low_r[c] + by[c] * high_r[c] for c in range(count)]
        link = [by[c] * high_e[c] for c in range(count)]
        stride *= 2
    return solve_chunks(diagonal, link, rhs)


def pack_pair(a, b, odd_lane):
    even = [jnp.where(odd_lane, pltpu.roll(x, 1, 1), y) for x, y in zip(a, b)]
    odd = [jnp.where(odd_lane, x, pltpu.roll(y, LANES - 1, 1)) for x, y in zip(a, b)]
    return even, odd


def unpack_pair(even, odd, odd_lane):
    a = [jnp.where(odd_lane, y, pltpu.roll(x, LANES - 1, 1)) for x, y in zip(even, odd)]
    b = [jnp.where(odd_lane, pltpu.roll(y, 1, 1), x) for x, y in zip(even, odd)]
    return a, b


def solve_x_pair(g_pair, rhs_pair, lane):
    odd_lane = (lane & 1) == 1
    first_cell = lane < 2
    last_cell = lane >= LANES - 2
    half = 0.5 * weight
    g_even, g_odd = pack_pair(*g_pair, odd_lane)
    r_even, r_odd = pack_pair(*rhs_pair, odd_lane)
    face = [half * (a + b) for a, b in zip(g_even, g_odd)]
    after = from_right(g_even, 2, lane)
    after[-1] = jnp.where(last_cell, g_odd[-1], after[-1])
    face_after = [half * (a + b) for a, b in zip(g_odd, after)]
    face_before = from_left(face_after, 2, lane)
    face_before[0] = jnp.where(first_cell, weight * g_even[0], face_before[0])
    inv = [inverse(1.0 + (a + b)) for a, b in zip(face_before, face)]
    d_odd = [1.0 + (a + b) for a, b in zip(face, face_after)]
    link = list(face_after)
    link[-1] = jnp.where(last_cell, 0.0, link[-1])
    link_before = list(face_before)
    link_before[0] = jnp.where(first_cell, 0.0, link_before[0])
    t = [q * r for q, r in zip(inv, r_even)]
    w = [q * e for q, e in zip(inv, face)]
    next_q = from_right(inv, 2, lane)
    next_t = from_right(t, 2, lane)
    next_w = from_right(w, 2, lane)
    diagonal = [
        d - e * v - l * (l * q) for d, e, v, l, q in zip(d_odd, face, w, link, next_q)
    ]
    rhs = [r + e * v + l * n for r, e, v, l, n in zip(r_odd, face, t, link, next_t)]
    x_odd = reduce_lanes(diagonal, [l * n for l, n in zip(link, next_w)], rhs, lane, 2)
    x_before = from_left(x_odd, 2, lane)
    x_even = [
        v + q * (l * b) + u * x for v, q, l, b, u, x in zip(t, inv, link_before, x_before, w, x_odd)
    ]
    return unpack_pair(x_even, x_odd, odd_lane)


def pack_kernel(
    field_ref, index_ref, amp_ref, phase_ref,
    packed_ref, both_ref,
    index_in, amp_in, phase_in, sems,
):
    width = both_ref.shape[0] // 2
    last = field_ref.shape[0] - width
    pairs = (
        (index_ref, index_in),
        (amp_ref, amp_in),
        (phase_ref, phase_in),
        (field_ref.at[pl.ds(0, width)], both_ref.at[pl.ds(0, width)]),
        (field_ref.at[pl.ds(last, width)], both_ref.at[pl.ds(width, width)]),
    )
    copies = [pltpu.make_async_copy(a, b, sems.at[n]) for n, (a, b) in enumerate(pairs)]
    for copy in copies:
        copy.start()
    for copy in copies[:3]:
        copy.wait()
    row = lax.broadcasted_iota(jnp.int32, packed_ref.shape, 0)
    lane = lax.broadcasted_iota(jnp.int32, packed_ref.shape, 1)
    total = jnp.zeros(packed_ref.shape, f32)
    for m in range(index_in.shape[0]):
        waves = [index_in[m, n].astype(f32) for n in range(3)]
        for place, value in enumerate((*waves, phase_in[m], amp_in[m])):
            total = jnp.where((row == m) & (lane == place), value, total)
    packed_ref[...] = total
    for copy in copies[3:]:
        copy.wait()


def row_kernel(field_ref, step_ref, table_ref, inner_ref, outer_ref, step_in, sems):
    width = inner_ref.shape[0]
    pairs = (
        (step_ref, step_in),
        (field_ref.at[pl.ds(field_ref.shape[0] - width, width)], inner_ref),
        (field_ref.at[pl.ds(0, width)], outer_ref),
    )
    copies = [pltpu.make_async_copy(a, b, sems.at[n]) for n, (a, b) in enumerate(pairs)]
    for copy in copies:
        copy.start()
    for copy in copies:
        copy.wait()
    table_ref[...] = jnp.full(table_ref.shape, step_in[0].astype(f32), f32)


def load_kernel(sizes, field_ref, conduct_ref, field_out, turned_ref, conduct_in, sems):
    rows, layers, chunks, row_total, layer_total, column_total = sizes
    width = layers * chunks
    copies = (
        pltpu.make_async_copy(field_ref, field_out, sems.at[0]),
        pltpu.make_async_copy(conduct_ref, conduct_in, sems.at[1]),
    )
    for copy in copies:
        copy.start()
    for n, (copy, ref) in enumerate(zip(copies, (field_out, conduct_in))):
        copy.wait()
        for place in range(width):
            spot = (n * width + place) * rows
            turned_ref[spot : spot + rows] = ref[pl.ds(place, rows, stride=width), :]


def block_factors(face):
    inv, scaled, chain, u = [], [], [], []
    rows = len(face) - 1
    rest = 1.0 + face[0]
    for j in range(rows):
        inv.append(inverse(rest + face[j + 1]))
        scaled.append(face[j] * inv[j])
        chain.append(face[j + 1] * inv[j])
        u.append(scaled[j] * u[-1] if j else scaled[j])
        rest = 1.0 + rest * chain[j]
    v = list(chain)
    for j in range(rows - 2, -1, -1):
        u[j] = u[j] + chain[j] * u[j + 1]
        v[j] = chain[j] * v[j + 1]
    return inv, scaled, chain, u, v


def height_kernel(sizes, handed_ref, came_ref, heights_ref):
    rows, layers, chunks, row_total, layer_total, column_total = sizes
    odd = lax.rem(lax.axis_index("wide"), 2) == 1
    first = 2 * layers * chunks
    own, other = handed_ref[first:], came_ref[first:]
    modes = jnp.where(odd, own, other)
    step = jnp.where(odd, other, own)
    body = height_lines(modes, step, 0, row_total, row_total, chunks, column_total)
    heights_ref[chunks : (row_total + 1) * chunks] = body
    heights_ref[0:chunks] = body[0:chunks]
    heights_ref[(row_total + 1) * chunks : (row_total + 2) * chunks] = body[
        (row_total - 1) * chunks : row_total * chunks
    ]

def main_kernel(
    sizes, handed_ref, both_ref, below_ref, came_ref, turned_ref,
    sent_ref, p_ref, u_ref, v_ref, gain_ref, joint_ref,
    heights, halo, solved,
):
    rows, layers, chunks, row_total, layer_total, column_total = sizes
    width = layers * chunks
    blocks = row_total // rows
    me = lax.axis_index("wide")
    first_layer = lax.axis_index("grp") * layers
    zeta = [
        ((first_layer + k).astype(f32) + 0.5) * (1.0 / layer_total) for k in range(layers)
    ]
    half = 0.5 * weight
    height_kernel(sizes, handed_ref, came_ref, heights)
    own_start = pl.multiple_of(me * (rows * chunks), 8)

    def face(low, high):
        both = heights[pl.ds(low, chunks), :] + heights[pl.ds(high, chunks), :]
        return jnp.concatenate([weight + (half * z) * both for z in zeta], 0)

    def aligned(index):
        return pl.multiple_of(index, 8)

    inv, scaled, chain, u, v = block_factors(
        [face(own_start + j * chunks, own_start + (j + 1) * chunks) for j in range(rows + 1)]
    )
    for j in range(rows):
        u_ref[j * width : (j + 1) * width] = u[j]
        v_ref[j * width : (j + 1) * width] = v[j]

    def one_block(n, carry):
        rest, link, left_link = carry
        upward = n < me
        b = jnp.where(upward, n, blocks - 1 - (n - me))
        start = b * (rows * chunks) + jnp.where(upward, 0, (rows + 1) * chunks)
        step = jnp.where(upward, chunks, -chunks)
        places = [aligned(start + j * step) for j in range(rows + 2)]
        first = face(places[0], places[1])
        anew = (n == 0) | (n == me)
        left_link = jnp.where(n == me, link, left_link)
        rest = jnp.where(anew, 1.0 + first, rest)
        for j in range(rows):
            after = face(places[j + 1], places[j + 2])
            link = after * inverse(rest + after)
            through = through * link if j else link
            rest = 1.0 + rest * link
        gain_ref[pl.ds(aligned(b * width), width), :] = through * (first * inverse(after))
        return rest, link, left_link

    gain_ref[pl.ds(aligned(me * width), width), :] = u[-1]
    nothing = 0.0 * u[0]
    carry = (nothing, nothing, nothing)
    if blocks <= 8:
        for n in range(blocks - 1):
            carry = one_block(n, carry)
    else:
        carry = lax.fori_loop(0, blocks - 1, one_block, carry)
    _, link, left_link = carry
    left_link = jnp.where(me == blocks - 1, link, left_link)
    right_link = jnp.where(me == blocks - 1, 0.0, link)

    a = 1.0 - left_link * u[0]
    b = left_link * v[0]
    c = right_link * u[-1]
    d = 1.0 - right_link * v[-1]
    by = inverse(a * d - b * c)
    joint = (
        u[-1] * inverse(a) * left_link, v[0] * inverse(d) * right_link,
        left_link, right_link, d * by, b * by, c * by, a * by,
    )
    for n, value in enumerate(joint):
        joint_ref[n * width : (n + 1) * width] = value

    odd = lax.rem(me, 2) == 1
    below = jnp.where(odd, came_ref[width : 2 * width], below_ref[...])
    above = jnp.where(odd, came_ref[0:width], both_ref[0:width])
    halo[0:width] = jnp.where(me == 0, 0.0, below)
    halo[width : 2 * width] = jnp.where(me == blocks - 1, 0.0, above)
    lane = lax.broadcasted_iota(jnp.int32, (rows, LANES), 1)
    row = lax.broadcasted_iota(jnp.int32, (rows, LANES), 0)

    def neighbours(values, low, high):
        return (
            jnp.where(row == 0, low, pltpu.roll(values, 1, 0)),
            jnp.where(row == rows - 1, high, pltpu.roll(values, rows - 1, 0)),
        )

    g = [[] for _ in range(layers)]
    f = [[] for _ in range(layers)]
    rhs = [[] for _ in range(layers)]
    for c in range(chunks):
        h = heights[pl.ds(own_start + chunks + c, rows, stride=chunks), :]
        h_low, h_high = neighbours(
            h,
            heights[pl.ds(own_start + c, 1), :],
            heights[pl.ds(own_start + (rows + 1) * chunks + c, 1), :],
        )
        low_sum, high_sum = h + h_low, h + h_high
        for k in range(layers):
            place = c * layers + k
            f_mid = turned_ref[place * rows : (place + 1) * rows]
            f_low, f_high = neighbours(
                f_mid, halo[pl.ds(place, 1), :], halo[pl.ds(width + place, 1), :]
            )
            g[k].append(
                turned_ref[(width + place) * rows : (width + place + 1) * rows] * (1.0 + zeta[k] * h)
            )
            f[k].append(f_mid)
            along = (weight + (half * zeta[k]) * high_sum) * (f_high - f_mid) - (
                weight + (half * zeta[k]) * low_sum
            ) * (f_mid - f_low)
            rhs[k].append(2.0 * (f_mid + along))
    for k in range(0, layers, 2):
        both = solve_x_pair(g[k : k + 2], rhs[k : k + 2], lane)
        for n in range(2):
            for c in range(chunks):
                spot = pl.ds((k + n) * chunks + c, rows, stride=width)
                solved[spot, :] = both[n][c] - 2.0 * f[k + n][c]

    def part(ref, j):
        return ref[j * width : (j + 1) * width]

    p = [part(solved, 0) * inv[0]]
    for j in range(1, rows):
        p.append(part(solved, j) * inv[j] + scaled[j] * p[-1])
    for j in range(rows - 2, -1, -1):
        p[j] = p[j] + chain[j] * p[j + 1]
    for j in range(rows):
        p_ref[j * width : (j + 1) * width] = p[j]

    upward = p[-1] + part(joint_ref, 0) * p[0]
    downward = p[0] + part(joint_ref, 1) * p[-1]
    for b in range(blocks):
        sent_ref[b * width : (b + 1) * width] = jnp.where(b > me, upward, downward)


def last_kernel(
    sizes, came_ref, gain_ref, joint_ref, p_ref, u_ref, v_ref, field_ref,
    out_ref,
):
    rows, layers, chunks, row_total, layer_total, column_total = sizes
    width = layers * chunks
    blocks = row_total // rows
    me = lax.axis_index("wide")

    def part(ref, b):
        return ref[b * width : (b + 1) * width]

    left = jnp.zeros((width, LANES), f32)
    right = jnp.zeros((width, LANES), f32)
    for b in range(blocks - 1):
        left = jnp.where(b < me, part(came_ref, b) + part(gain_ref, b) * left, left)
        b = blocks - 1 - b
        right = jnp.where(b > me, part(came_ref, b) + part(gain_ref, b) * right, right)

    y = left + part(joint_ref, 2) * part(p_ref, 0)
    z = right + part(joint_ref, 3) * part(p_ref, rows - 1)
    before = part(joint_ref, 4) * y + part(joint_ref, 5) * z
    after = part(joint_ref, 6) * y + part(joint_ref, 7) * z
    for j in range(rows):
        x = part(p_ref, j) + part(u_ref, j) * before + part(v_ref, j) * after
        for k in range(layers):
            spot = pl.ds(j * width + k, chunks, stride=layers)
            out_ref[spot, :] = field_ref[spot, :] + x[k * chunks : (k + 1) * chunks]


def on_device(field, conduct, mode_index, mode_amp, mode_phase, step_index):
    rows, layers, columns = field.shape
    wide_count = lax.axis_size("wide")
    row_total = rows * wide_count
    grp_count = lax.axis_size("grp")
    layer_total = layers * grp_count
    chunks = columns // LANES
    width = layers * chunks
    sizes = (rows, layers, chunks, row_total, layer_total, columns)
    limit = pltpu.CompilerParams(vmem_limit_bytes=16 * 1024 * 1024)
    hbm = pl.BlockSpec(memory_space=pltpu.HBM)

    def lines(count):
        return jax.ShapeDtypeStruct((count * width, LANES), f32)

    place = lax.axis_index("wide")
    odd = place % 2 == 1
    swaps = [(i, i ^ 1) for i in range(wide_count)]
    cores = [list(range(n, wide_count, 2)) for n in range(2)]
    table_shape = (grp_count * mode_index.shape[0], LANES)
    packed_shape = (mode_index.shape[0], LANES)
    in_hbm = lambda arrays: [pltpu.with_memory_space_constraint(a, pltpu.HBM) for a in arrays]

    def pack_modes(*arrays):
        return pl.pallas_call(
            pack_kernel,
            out_shape=(jax.ShapeDtypeStruct(packed_shape, f32), lines(2)),
            in_specs=[hbm] * 4,
            scratch_shapes=[pltpu.SMEM(a.shape, a.dtype) for a in arrays[1:]]
            + [pltpu.SemaphoreType.DMA((5,))],
            compiler_params=limit,
        )(*in_hbm(arrays))

    def pack_nothing(*arrays):
        return jnp.zeros(packed_shape, f32), jnp.zeros((2 * width, LANES), f32)

    packed, both = lax.cond(
        odd, pack_modes, pack_nothing, to_lines(field), mode_index, mode_amp, mode_phase
    )
    both_came = lax.ppermute(both, "wide", swaps)

    def gather_modes(own, *arrays):
        empty = jnp.zeros((width, LANES), f32)
        return lax.all_gather(own, "grp", axis=0, tiled=True), empty, empty

    def load_rows(own, *arrays):
        return pl.pallas_call(
            row_kernel,
            out_shape=(jax.ShapeDtypeStruct(table_shape, f32), lines(1), lines(1)),
            in_specs=[hbm] * 2,
            scratch_shapes=[
                pltpu.SMEM(step_index.shape, step_index.dtype),
                pltpu.SemaphoreType.DMA((3,)),
            ],
            compiler_params=limit,
        )(*in_hbm(arrays))

    table, inner, outer = lax.cond(
        odd, gather_modes, load_rows, packed, to_lines(field), step_index
    )
    table, inner, outer, both_came = lax.optimization_barrier((table, inner, outer, both_came))

    def gather_rows(own, came):
        rows_sent = jnp.concatenate([own, came[width:]], 0)
        rows_all = lax.all_gather(rows_sent, "wide", axis_index_groups=cores, axis=0)
        chip = place // 2
        below = lax.dynamic_index_in_dim(rows_all, jnp.maximum(chip - 1, 0), 0, False)
        above = lax.dynamic_index_in_dim(
            rows_all, jnp.minimum(chip + 1, wide_count // 2 - 1), 0, False
        )
        return below[width:], above[:width]

    def no_rows(own, came):
        return jnp.zeros_like(own), jnp.zeros_like(own)

    below, above = lax.cond(odd, no_rows, gather_rows, outer, both_came)
    handed = jnp.concatenate([above, inner, table], 0)
    came = lax.ppermute(handed, "wide", swaps)
    handed, field, conduct = lax.optimization_barrier((handed, field, conduct))
    field_lines, turned = pl.pallas_call(
        functools.partial(load_kernel, sizes),
        out_shape=(lines(rows), lines(2 * rows)),
        in_specs=[hbm] * 2,
        scratch_shapes=[
            pltpu.VMEM((rows * width, LANES), f32),
            pltpu.SemaphoreType.DMA((2,)),
        ],
        compiler_params=limit,
    )(
        *(
            pltpu.with_memory_space_constraint(to_lines(a), pltpu.HBM)
            for a in (field, conduct)
        )
    )
    sent, p, u, v, gain, joint = pl.pallas_call(
        functools.partial(main_kernel, sizes),
        out_shape=(lines(wide_count),)
        + (lines(rows),) * 3
        + (lines(wide_count), lines(8)),
        scratch_shapes=[
            pltpu.VMEM(((row_total + 2) * chunks, LANES), f32),
            pltpu.VMEM((2 * width, LANES), f32),
            pltpu.VMEM((rows * width, LANES), f32),
        ],
        compiler_params=limit,
    )(handed, both_came, below, came, turned)

    came = lax.all_to_all(
        sent.reshape(wide_count, width, LANES), "wide", split_axis=0, concat_axis=0
    ).reshape(wide_count * width, LANES)

    advanced = pl.pallas_call(
        functools.partial(last_kernel, sizes),
        out_shape=lines(rows),
        compiler_params=limit,
    )(came, gain, joint, p, u, v, field_lines)
    return from_lines(advanced, field.shape)


def solution(mesh):
    return jax.shard_map(
        on_device,
        mesh=mesh,
        in_specs=(
            P("wide", "grp", None),
            P("wide", "grp", None),
            P("grp", None),
            P("grp"),
            P("grp"),
            P(),
        ),
        out_specs=P("wide", "grp", None),
        check_vma=False,
    )
```

```python
import functools
import math

import jax
import jax.numpy as jnp
from jax import lax
from jax.experimental import pallas as pl
from jax.experimental.pallas import tpu as pltpu
from jax.sharding import PartitionSpec as P

time_step = 600.0
implicit_weight = 0.5
weight = implicit_weight * time_step
LANES = 128
f32 = jnp.float32


def to_lines(block):
    rows, layers, columns = block.shape
    chunks = columns // LANES
    return (
        block.reshape(rows, layers, chunks, LANES)
        .transpose(0, 2, 1, 3)
        .reshape(rows * chunks * layers, LANES)
    )


def from_lines(lines, shape):
    rows, layers, columns = shape
    chunks = columns // LANES
    return (
        lines.reshape(rows, chunks, layers, LANES)
        .transpose(0, 2, 1, 3)
        .reshape(rows, layers, columns)
    )


def turns(wave, index, period):
    product = wave * index
    if period & (period - 1) == 0:
        product = product & (period - 1)
    else:
        product = lax.rem(product, jnp.int32(period))
    return product.astype(f32) * (1.0 / period)


def cos_sin(turn):
    part = turn - jnp.floor(turn + 0.5)
    square = part * part

    def series(first):
        terms = [
            (-1.0) ** n * math.pi ** (2 * n + first) / math.factorial(2 * n + first)
            for n in range(7)
        ]
        total = jnp.full_like(square, terms[-1])
        for term in terms[-2::-1]:
            total = total * square + term
        return total

    half_cos = series(0)
    half_sin = series(1) * part
    return 1.0 - 2.0 * half_sin * half_sin, 2.0 * half_sin * half_cos


def halves(values):
    high = values.astype(jnp.bfloat16)
    return high, (values - high.astype(f32)).astype(jnp.bfloat16)


def height_lines(modes, step, first_row, count, row_total, chunks, column_total):
    mode_count = modes.shape[0]
    wave_x = modes[:, 0:1].astype(jnp.int32)
    wave_y = modes[:, 1:2].astype(jnp.int32)
    moment = modes[:, 2:3] * (step * (1.0 / 64.0))
    offset = modes[:, 3:4] * (0.5 / math.pi) + (moment - jnp.floor(moment))
    offset = jnp.concatenate([offset] * (count * chunks // LANES), 1)
    amp = modes[:, 4:5]
    spot = lax.broadcasted_iota(jnp.int32, (mode_count, count * chunks), 1)
    chunk = spot % chunks
    row = jnp.clip(first_row + spot // chunks, 0, row_total - 1)
    angle = (
        turns(wave_y, row, row_total) + turns(wave_x, chunk * LANES, column_total)
    ) + offset
    left_cos, left_sin = cos_sin(angle)
    lane = lax.broadcasted_iota(jnp.int32, (mode_count, LANES), 1)
    right_cos, right_sin = cos_sin(turns(wave_x, lane, column_total))
    left = jnp.concatenate([amp * left_cos, amp * left_sin], 0)
    right = jnp.concatenate([right_cos, -right_sin], 0)
    left_high, left_low = halves(left)
    right_high, right_low = halves(right)
    return lax.dot_general(
        jnp.concatenate([left_high, left_high, left_low], 0),
        jnp.concatenate([right_high, right_low, right_high], 0),
        (((0,), (0,)), ((), ())),
        preferred_element_type=f32,
    )


def inverse(values):
    return pl.reciprocal(values, approx=False)


def from_left(values, stride, lane):
    moved = [pltpu.roll(v, stride, 1) for v in values]
    return [jnp.where(lane < stride, moved[c - 1], moved[c]) for c in range(len(values))]


def from_right(values, stride, lane):
    count = len(values)
    moved = [pltpu.roll(v, LANES - stride, 1) for v in values]
    return [
        jnp.where(lane >= LANES - stride, moved[(c + 1) % count], moved[c]) for c in range(count)
    ]


def solve_chunks(diagonal, link, rhs):
    count = len(rhs)
    if count == 1:
        return [rhs[0] * inverse(diagonal[0])]
    inv = {i: inverse(diagonal[i]) for i in range(0, count, 2)}
    scaled = {i: inv[i] * rhs[i] for i in inv}
    odd_diagonal, odd_link, odd_rhs = [], [], []
    for i in range(1, count, 2):
        d = diagonal[i] - link[i - 1] * (link[i - 1] * inv[i - 1])
        r = rhs[i] + link[i - 1] * scaled[i - 1]
        e = None
        if i + 1 < count:
            by = link[i] * inv[i + 1]
            d = d - link[i] * by
            r = r + link[i] * scaled[i + 1]
            e = by * link[i + 1] if i + 2 < count else None
        odd_diagonal.append(d)
        odd_rhs.append(r)
        odd_link.append(e)
    odd = solve_chunks(odd_diagonal, odd_link, odd_rhs)
    out = [None] * count
    out[1::2] = odd
    for i in range(0, count, 2):
        r = rhs[i]
        if i > 0:
            r = r + link[i - 1] * out[i - 1]
        if i + 1 < count:
            r = r + link[i] * out[i + 1]
        out[i] = r * inv[i]
    return out


def reduce_lanes(diagonal, link, rhs, lane, stride):
    count = len(rhs)
    while stride < LANES:
        high_r = from_right(rhs, stride, lane)
        high_e = from_right(link, stride, lane)
        inv = [inverse(d) for d in diagonal]
        w = [q * e for q, e in zip(inv, link)]
        low_d = from_left([e * v for e, v in zip(link, w)], stride, lane)
        low_r = from_left([r * v for r, v in zip(rhs, w)], stride, lane)
        by = [e * q for e, q in zip(link, from_right(inv, stride, lane))]
        diagonal = [diagonal[c] - low_d[c] - link[c] * by[c] for c in range(count)]
        rhs = [rhs[c] + low_r[c] + by[c] * high_r[c] for c in range(count)]
        link = [by[c] * high_e[c] for c in range(count)]
        stride *= 2
    return solve_chunks(diagonal, link, rhs)


def pack_pair(a, b, odd_lane):
    even = [jnp.where(odd_lane, pltpu.roll(x, 1, 1), y) for x, y in zip(a, b)]
    odd = [jnp.where(odd_lane, x, pltpu.roll(y, LANES - 1, 1)) for x, y in zip(a, b)]
    return even, odd


def unpack_pair(even, odd, odd_lane):
    a = [jnp.where(odd_lane, y, pltpu.roll(x, LANES - 1, 1)) for x, y in zip(even, odd)]
    b = [jnp.where(odd_lane, pltpu.roll(y, 1, 1), x) for x, y in zip(even, odd)]
    return a, b


def solve_x_pair(g_pair, rhs_pair, lane):
    odd_lane = (lane & 1) == 1
    first_cell = lane < 2
    last_cell = lane >= LANES - 2
    half = 0.5 * weight
    g_even, g_odd = pack_pair(*g_pair, odd_lane)
    r_even, r_odd = pack_pair(*rhs_pair, odd_lane)
    face = [half * (a + b) for a, b in zip(g_even, g_odd)]
    after = from_right(g_even, 2, lane)
    after[-1] = jnp.where(last_cell, g_odd[-1], after[-1])
    face_after = [half * (a + b) for a, b in zip(g_odd, after)]
    face_before = from_left(face_after, 2, lane)
    face_before[0] = jnp.where(first_cell, weight * g_even[0], face_before[0])
    inv = [inverse(1.0 + (a + b)) for a, b in zip(face_before, face)]
    d_odd = [1.0 + (a + b) for a, b in zip(face, face_after)]
    link = list(face_after)
    link[-1] = jnp.where(last_cell, 0.0, link[-1])
    link_before = list(face_before)
    link_before[0] = jnp.where(first_cell, 0.0, link_before[0])
    t = [q * r for q, r in zip(inv, r_even)]
    w = [q * e for q, e in zip(inv, face)]
    next_q = from_right(inv, 2, lane)
    next_t = from_right(t, 2, lane)
    next_w = from_right(w, 2, lane)
    diagonal = [
        d - e * v - l * (l * q) for d, e, v, l, q in zip(d_odd, face, w, link, next_q)
    ]
    rhs = [r + e * v + l * n for r, e, v, l, n in zip(r_odd, face, t, link, next_t)]
    x_odd = reduce_lanes(diagonal, [l * n for l, n in zip(link, next_w)], rhs, lane, 2)
    x_before = from_left(x_odd, 2, lane)
    x_even = [
        v + q * (l * b) + u * x for v, q, l, b, u, x in zip(t, inv, link_before, x_before, w, x_odd)
    ]
    return unpack_pair(x_even, x_odd, odd_lane)


def pack_kernel(
    field_ref, index_ref, amp_ref, phase_ref,
    packed_ref, both_ref,
    index_in, amp_in, phase_in, sems,
):
    width = both_ref.shape[0] // 2
    last = field_ref.shape[0] - width
    pairs = (
        (index_ref, index_in),
        (amp_ref, amp_in),
        (phase_ref, phase_in),
        (field_ref.at[pl.ds(0, width)], both_ref.at[pl.ds(0, width)]),
        (field_ref.at[pl.ds(last, width)], both_ref.at[pl.ds(width, width)]),
    )
    copies = [pltpu.make_async_copy(a, b, sems.at[n]) for n, (a, b) in enumerate(pairs)]
    for copy in copies:
        copy.start()
    for copy in copies[:3]:
        copy.wait()
    row = lax.broadcasted_iota(jnp.int32, packed_ref.shape, 0)
    lane = lax.broadcasted_iota(jnp.int32, packed_ref.shape, 1)
    total = jnp.zeros(packed_ref.shape, f32)
    for m in range(index_in.shape[0]):
        waves = [index_in[m, n].astype(f32) for n in range(3)]
        for place, value in enumerate((*waves, phase_in[m], amp_in[m])):
            total = jnp.where((row == m) & (lane == place), value, total)
    packed_ref[...] = total
    for copy in copies[3:]:
        copy.wait()


def row_kernel(field_ref, step_ref, table_ref, inner_ref, outer_ref, step_in, sems):
    width = inner_ref.shape[0]
    pairs = (
        (step_ref, step_in),
        (field_ref.at[pl.ds(field_ref.shape[0] - width, width)], inner_ref),
        (field_ref.at[pl.ds(0, width)], outer_ref),
    )
    copies = [pltpu.make_async_copy(a, b, sems.at[n]) for n, (a, b) in enumerate(pairs)]
    for copy in copies:
        copy.start()
    for copy in copies:
        copy.wait()
    table_ref[...] = jnp.full(table_ref.shape, step_in[0].astype(f32), f32)


def load_kernel(sizes, field_ref, conduct_ref, field_out, turned_ref, conduct_in, sems):
    rows, layers, chunks, row_total, layer_total, column_total = sizes
    width = layers * chunks
    copies = (
        pltpu.make_async_copy(field_ref, field_out, sems.at[0]),
        pltpu.make_async_copy(conduct_ref, conduct_in, sems.at[1]),
    )
    for copy in copies:
        copy.start()
    for n, (copy, ref) in enumerate(zip(copies, (field_out, conduct_in))):
        copy.wait()
        for place in range(width):
            spot = (n * width + place) * rows
            turned_ref[spot : spot + rows] = ref[pl.ds(place, rows, stride=width), :]


def block_factors(face):
    inv, scaled, chain, u = [], [], [], []
    rows = len(face) - 1
    rest = 1.0 + face[0]
    for j in range(rows):
        inv.append(inverse(rest + face[j + 1]))
        scaled.append(face[j] * inv[j])
        chain.append(face[j + 1] * inv[j])
        u.append(scaled[j] * u[-1] if j else scaled[j])
        rest = 1.0 + rest * chain[j]
    v = list(chain)
    for j in range(rows - 2, -1, -1):
        u[j] = u[j] + chain[j] * u[j + 1]
        v[j] = chain[j] * v[j + 1]
    return inv, scaled, chain, u, v


def height_kernel(sizes, handed_ref, came_ref, heights_ref):
    rows, layers, chunks, row_total, layer_total, column_total = sizes
    odd = lax.rem(lax.axis_index("wide"), 2) == 1
    first = 2 * layers * chunks
    own, other = handed_ref[first:], came_ref[first:]
    modes = jnp.where(odd, own, other)
    step = jnp.where(odd, other, own)
    body = height_lines(modes, step, 0, row_total, row_total, chunks, column_total)
    heights_ref[chunks : (row_total + 1) * chunks] = body
    heights_ref[0:chunks] = body[0:chunks]
    heights_ref[(row_total + 1) * chunks : (row_total + 2) * chunks] = body[
        (row_total - 1) * chunks : row_total * chunks
    ]

def main_kernel(
    sizes, handed_ref, both_ref, below_ref, came_ref, turned_ref,
    sent_ref, p_ref, u_ref, v_ref, gain_ref, joint_ref,
    heights, halo, solved,
):
    rows, layers, chunks, row_total, layer_total, column_total = sizes
    width = layers * chunks
    blocks = row_total // rows
    me = lax.axis_index("wide")
    first_layer = lax.axis_index("grp") * layers
    zeta = [
        ((first_layer + k).astype(f32) + 0.5) * (1.0 / layer_total) for k in range(layers)
    ]
    half = 0.5 * weight
    height_kernel(sizes, handed_ref, came_ref, heights)
    own_start = pl.multiple_of(me * (rows * chunks), 8)

    def row_heights(places):
        return [heights[pl.ds(place, chunks), :] for place in places]

    def face(low, high):
        both = low + high
        return jnp.concatenate([weight + (half * z) * both for z in zeta], 0)

    def aligned(index):
        return pl.multiple_of(index, 8)

    own_rows = row_heights([own_start + j * chunks for j in range(rows + 2)])
    inv, scaled, chain, u, v = block_factors(
        [face(own_rows[j], own_rows[j + 1]) for j in range(rows + 1)]
    )
    for j in range(rows):
        u_ref[j * width : (j + 1) * width] = u[j]
        v_ref[j * width : (j + 1) * width] = v[j]

    def one_block(n, carry):
        rest, link, left_link = carry
        upward = n < me
        b = jnp.where(upward, n, blocks - 1 - (n - me))
        start = b * (rows * chunks) + jnp.where(upward, 0, (rows + 1) * chunks)
        step = jnp.where(upward, chunks, -chunks)
        h = row_heights([aligned(start + j * step) for j in range(rows + 2)])
        first = face(h[0], h[1])
        anew = (n == 0) | (n == me)
        left_link = jnp.where(n == me, link, left_link)
        rest = jnp.where(anew, 1.0 + first, rest)
        for j in range(rows):
            after = face(h[j + 1], h[j + 2])
            link = after * inverse(rest + after)
            through = through * link if j else link
            rest = 1.0 + rest * link
        gain_ref[pl.ds(aligned(b * width), width), :] = through * (first * inverse(after))
        return rest, link, left_link

    gain_ref[pl.ds(aligned(me * width), width), :] = u[-1]
    nothing = 0.0 * u[0]
    carry = (nothing, nothing, nothing)
    if blocks <= 8:
        for n in range(blocks - 1):
            carry = one_block(n, carry)
    else:
        carry = lax.fori_loop(0, blocks - 1, one_block, carry)
    _, link, left_link = carry
    left_link = jnp.where(me == blocks - 1, link, left_link)
    right_link = jnp.where(me == blocks - 1, 0.0, link)

    a = 1.0 - left_link * u[0]
    b = left_link * v[0]
    c = right_link * u[-1]
    d = 1.0 - right_link * v[-1]
    by = inverse(a * d - b * c)
    joint = (
        u[-1] * inverse(a) * left_link, v[0] * inverse(d) * right_link,
        left_link, right_link, d * by, b * by, c * by, a * by,
    )
    for n, value in enumerate(joint):
        joint_ref[n * width : (n + 1) * width] = value

    odd = lax.rem(me, 2) == 1
    below = jnp.where(odd, came_ref[width : 2 * width], below_ref[...])
    above = jnp.where(odd, came_ref[0:width], both_ref[0:width])
    halo[0:width] = jnp.where(me == 0, 0.0, below)
    halo[width : 2 * width] = jnp.where(me == blocks - 1, 0.0, above)
    lane = lax.broadcasted_iota(jnp.int32, (rows, LANES), 1)
    row = lax.broadcasted_iota(jnp.int32, (rows, LANES), 0)

    def neighbours(values, low, high):
        return (
            jnp.where(row == 0, low, pltpu.roll(values, 1, 0)),
            jnp.where(row == rows - 1, high, pltpu.roll(values, rows - 1, 0)),
        )

    g = [[] for _ in range(layers)]
    f = [[] for _ in range(layers)]
    rhs = [[] for _ in range(layers)]
    for c in range(chunks):
        h = heights[pl.ds(own_start + chunks + c, rows, stride=chunks), :]
        h_low, h_high = neighbours(
            h,
            heights[pl.ds(own_start + c, 1), :],
            heights[pl.ds(own_start + (rows + 1) * chunks + c, 1), :],
        )
        low_sum, high_sum = h + h_low, h + h_high
        for k in range(layers):
            place = c * layers + k
            f_mid = turned_ref[place * rows : (place + 1) * rows]
            f_low, f_high = neighbours(
                f_mid, halo[pl.ds(place, 1), :], halo[pl.ds(width + place, 1), :]
            )
            g[k].append(
                turned_ref[(width + place) * rows : (width + place + 1) * rows] * (1.0 + zeta[k] * h)
            )
            f[k].append(f_mid)
            along = (weight + (half * zeta[k]) * high_sum) * (f_high - f_mid) - (
                weight + (half * zeta[k]) * low_sum
            ) * (f_mid - f_low)
            rhs[k].append(2.0 * (f_mid + along))
    for k in range(0, layers, 2):
        both = solve_x_pair(g[k : k + 2], rhs[k : k + 2], lane)
        for n in range(2):
            for c in range(chunks):
                spot = pl.ds((k + n) * chunks + c, rows, stride=width)
                solved[spot, :] = both[n][c] - 2.0 * f[k + n][c]

    def part(ref, j):
        return ref[j * width : (j + 1) * width]

    p = [part(solved, 0) * inv[0]]
    for j in range(1, rows):
        p.append(part(solved, j) * inv[j] + scaled[j] * p[-1])
    for j in range(rows - 2, -1, -1):
        p[j] = p[j] + chain[j] * p[j + 1]
    for j in range(rows):
        p_ref[j * width : (j + 1) * width] = p[j]

    upward = p[-1] + part(joint_ref, 0) * p[0]
    downward = p[0] + part(joint_ref, 1) * p[-1]
    for b in range(blocks):
        sent_ref[b * width : (b + 1) * width] = jnp.where(b > me, upward, downward)


def last_kernel(
    sizes, came_ref, gain_ref, joint_ref, p_ref, u_ref, v_ref, field_ref,
    out_ref,
):
    rows, layers, chunks, row_total, layer_total, column_total = sizes
    width = layers * chunks
    blocks = row_total // rows
    me = lax.axis_index("wide")

    def part(ref, b):
        return ref[b * width : (b + 1) * width]

    left = jnp.zeros((width, LANES), f32)
    right = jnp.zeros((width, LANES), f32)
    for b in range(blocks - 1):
        left = jnp.where(b < me, part(came_ref, b) + part(gain_ref, b) * left, left)
        b = blocks - 1 - b
        right = jnp.where(b > me, part(came_ref, b) + part(gain_ref, b) * right, right)

    y = left + part(joint_ref, 2) * part(p_ref, 0)
    z = right + part(joint_ref, 3) * part(p_ref, rows - 1)
    before = part(joint_ref, 4) * y + part(joint_ref, 5) * z
    after = part(joint_ref, 6) * y + part(joint_ref, 7) * z
    for j in range(rows):
        x = part(p_ref, j) + part(u_ref, j) * before + part(v_ref, j) * after
        for k in range(layers):
            spot = pl.ds(j * width + k, chunks, stride=layers)
            out_ref[spot, :] = field_ref[spot, :] + x[k * chunks : (k + 1) * chunks]


def on_device(field, conduct, mode_index, mode_amp, mode_phase, step_index):
    rows, layers, columns = field.shape
    wide_count = lax.axis_size("wide")
    row_total = rows * wide_count
    grp_count = lax.axis_size("grp")
    layer_total = layers * grp_count
    chunks = columns // LANES
    width = layers * chunks
    sizes = (rows, layers, chunks, row_total, layer_total, columns)
    limit = pltpu.CompilerParams(vmem_limit_bytes=16 * 1024 * 1024)
    hbm = pl.BlockSpec(memory_space=pltpu.HBM)

    def lines(count):
        return jax.ShapeDtypeStruct((count * width, LANES), f32)

    place = lax.axis_index("wide")
    odd = place % 2 == 1
    swaps = [(i, i ^ 1) for i in range(wide_count)]
    cores = [list(range(n, wide_count, 2)) for n in range(2)]
    table_shape = (grp_count * mode_index.shape[0], LANES)
    packed_shape = (mode_index.shape[0], LANES)
    in_hbm = lambda arrays: [pltpu.with_memory_space_constraint(a, pltpu.HBM) for a in arrays]

    def pack_modes(*arrays):
        return pl.pallas_call(
            pack_kernel,
            out_shape=(jax.ShapeDtypeStruct(packed_shape, f32), lines(2)),
            in_specs=[hbm] * 4,
            scratch_shapes=[pltpu.SMEM(a.shape, a.dtype) for a in arrays[1:]]
            + [pltpu.SemaphoreType.DMA((5,))],
            compiler_params=limit,
        )(*in_hbm(arrays))

    def pack_nothing(*arrays):
        return jnp.zeros(packed_shape, f32), jnp.zeros((2 * width, LANES), f32)

    packed, both = lax.cond(
        odd, pack_modes, pack_nothing, to_lines(field), mode_index, mode_amp, mode_phase
    )
    both_came = lax.ppermute(both, "wide", swaps)

    def gather_modes(own, *arrays):
        empty = jnp.zeros((width, LANES), f32)
        return lax.all_gather(own, "grp", axis=0, tiled=True), empty, empty

    def load_rows(own, *arrays):
        return pl.pallas_call(
            row_kernel,
            out_shape=(jax.ShapeDtypeStruct(table_shape, f32), lines(1), lines(1)),
            in_specs=[hbm] * 2,
            scratch_shapes=[
                pltpu.SMEM(step_index.shape, step_index.dtype),
                pltpu.SemaphoreType.DMA((3,)),
            ],
            compiler_params=limit,
        )(*in_hbm(arrays))

    table, inner, outer = lax.cond(
        odd, gather_modes, load_rows, packed, to_lines(field), step_index
    )
    table, inner, outer, both_came = lax.optimization_barrier((table, inner, outer, both_came))

    def gather_rows(own, came):
        rows_sent = jnp.concatenate([own, came[width:]], 0)
        rows_all = lax.all_gather(rows_sent, "wide", axis_index_groups=cores, axis=0)
        chip = place // 2
        below = lax.dynamic_index_in_dim(rows_all, jnp.maximum(chip - 1, 0), 0, False)
        above = lax.dynamic_index_in_dim(
            rows_all, jnp.minimum(chip + 1, wide_count // 2 - 1), 0, False
        )
        return below[width:], above[:width]

    def no_rows(own, came):
        return jnp.zeros_like(own), jnp.zeros_like(own)

    below, above = lax.cond(odd, no_rows, gather_rows, outer, both_came)
    handed = jnp.concatenate([above, inner, table], 0)
    came = lax.ppermute(handed, "wide", swaps)
    handed, field, conduct = lax.optimization_barrier((handed, field, conduct))
    field_lines, turned = pl.pallas_call(
        functools.partial(load_kernel, sizes),
        out_shape=(lines(rows), lines(2 * rows)),
        in_specs=[hbm] * 2,
        scratch_shapes=[
            pltpu.VMEM((rows * width, LANES), f32),
            pltpu.SemaphoreType.DMA((2,)),
        ],
        compiler_params=limit,
    )(
        *(
            pltpu.with_memory_space_constraint(to_lines(a), pltpu.HBM)
            for a in (field, conduct)
        )
    )
    sent, p, u, v, gain, joint = pl.pallas_call(
        functools.partial(main_kernel, sizes),
        out_shape=(lines(wide_count),)
        + (lines(rows),) * 3
        + (lines(wide_count), lines(8)),
        scratch_shapes=[
            pltpu.VMEM(((row_total + 2) * chunks, LANES), f32),
            pltpu.VMEM((2 * width, LANES), f32),
            pltpu.VMEM((rows * width, LANES), f32),
        ],
        compiler_params=limit,
    )(handed, both_came, below, came, turned)

    came = lax.all_to_all(
        sent.reshape(wide_count, width, LANES), "wide", split_axis=0, concat_axis=0
    ).reshape(wide_count * width, LANES)

    advanced = pl.pallas_call(
        functools.partial(last_kernel, sizes),
        out_shape=lines(rows),
        compiler_params=limit,
    )(came, gain, joint, p, u, v, field_lines)
    return from_lines(advanced, field.shape)


def solution(mesh):
    return jax.shard_map(
        on_device,
        mesh=mesh,
        in_specs=(
            P("wide", "grp", None),
            P("wide", "grp", None),
            P("grp", None),
            P("grp"),
            P("grp"),
            P(),
        ),
        out_specs=P("wide", "grp", None),
        check_vma=False,
    )
```

```python
import functools
import math

import jax
import jax.numpy as jnp
from jax import lax
from jax.experimental import pallas as pl
from jax.experimental.pallas import tpu as pltpu
from jax.sharding import PartitionSpec as P

time_step = 600.0
implicit_weight = 0.5
weight = implicit_weight * time_step
LANES = 128
f32 = jnp.float32


def to_lines(block):
    rows, layers, columns = block.shape
    chunks = columns // LANES
    return (
        block.reshape(rows, layers, chunks, LANES)
        .transpose(0, 2, 1, 3)
        .reshape(rows * chunks * layers, LANES)
    )


def from_lines(lines, shape):
    rows, layers, columns = shape
    chunks = columns // LANES
    return (
        lines.reshape(rows, chunks, layers, LANES)
        .transpose(0, 2, 1, 3)
        .reshape(rows, layers, columns)
    )


def turns(wave, index, period):
    product = wave * index
    if period & (period - 1) == 0:
        product = product & (period - 1)
    else:
        product = lax.rem(product, jnp.int32(period))
    return product.astype(f32) * (1.0 / period)


def cos_sin(turn):
    part = turn - jnp.floor(turn + 0.5)
    square = part * part

    def series(first):
        terms = [
            (-1.0) ** n * math.pi ** (2 * n + first) / math.factorial(2 * n + first)
            for n in range(7)
        ]
        total = jnp.full_like(square, terms[-1])
        for term in terms[-2::-1]:
            total = total * square + term
        return total

    half_cos = series(0)
    half_sin = series(1) * part
    return 1.0 - 2.0 * half_sin * half_sin, 2.0 * half_sin * half_cos


def halves(values):
    high = values.astype(jnp.bfloat16)
    return high, (values - high.astype(f32)).astype(jnp.bfloat16)


def height_lines(modes, step, first_row, count, row_total, chunks, column_total):
    mode_count = modes.shape[0]
    wave_x = modes[:, 0:1].astype(jnp.int32)
    wave_y = modes[:, 1:2].astype(jnp.int32)
    moment = modes[:, 2:3] * (step * (1.0 / 64.0))
    offset = modes[:, 3:4] * (0.5 / math.pi) + (moment - jnp.floor(moment))
    offset = jnp.concatenate([offset] * (count * chunks // LANES), 1)
    amp = modes[:, 4:5]
    spot = lax.broadcasted_iota(jnp.int32, (mode_count, count * chunks), 1)
    chunk = spot % chunks
    row = jnp.clip(first_row + spot // chunks, 0, row_total - 1)
    angle = (
        turns(wave_y, row, row_total) + turns(wave_x, chunk * LANES, column_total)
    ) + offset
    left_cos, left_sin = cos_sin(angle)
    lane = lax.broadcasted_iota(jnp.int32, (mode_count, LANES), 1)
    right_cos, right_sin = cos_sin(turns(wave_x, lane, column_total))
    left = jnp.concatenate([amp * left_cos, amp * left_sin], 0)
    right = jnp.concatenate([right_cos, -right_sin], 0)
    left_high, left_low = halves(left)
    right_high, right_low = halves(right)
    return lax.dot_general(
        jnp.concatenate([left_high, left_high, left_low], 0),
        jnp.concatenate([right_high, right_low, right_high], 0),
        (((0,), (0,)), ((), ())),
        preferred_element_type=f32,
    )


def inverse(values):
    return pl.reciprocal(values, approx=False)


def from_left(values, stride, lane):
    moved = [pltpu.roll(v, stride, 1) for v in values]
    return [jnp.where(lane < stride, moved[c - 1], moved[c]) for c in range(len(values))]


def from_right(values, stride, lane):
    count = len(values)
    moved = [pltpu.roll(v, LANES - stride, 1) for v in values]
    return [
        jnp.where(lane >= LANES - stride, moved[(c + 1) % count], moved[c]) for c in range(count)
    ]


def solve_chunks(diagonal, link, rhs):
    count = len(rhs)
    if count == 1:
        return [rhs[0] * inverse(diagonal[0])]
    inv = {i: inverse(diagonal[i]) for i in range(0, count, 2)}
    scaled = {i: inv[i] * rhs[i] for i in inv}
    odd_diagonal, odd_link, odd_rhs = [], [], []
    for i in range(1, count, 2):
        d = diagonal[i] - link[i - 1] * (link[i - 1] * inv[i - 1])
        r = rhs[i] + link[i - 1] * scaled[i - 1]
        e = None
        if i + 1 < count:
            by = link[i] * inv[i + 1]
            d = d - link[i] * by
            r = r + link[i] * scaled[i + 1]
            e = by * link[i + 1] if i + 2 < count else None
        odd_diagonal.append(d)
        odd_rhs.append(r)
        odd_link.append(e)
    odd = solve_chunks(odd_diagonal, odd_link, odd_rhs)
    out = [None] * count
    out[1::2] = odd
    for i in range(0, count, 2):
        r = rhs[i]
        if i > 0:
            r = r + link[i - 1] * out[i - 1]
        if i + 1 < count:
            r = r + link[i] * out[i + 1]
        out[i] = r * inv[i]
    return out


def reduce_lanes(diagonal, link, rhs, lane, stride):
    count = len(rhs)
    while stride < LANES:
        high_r = from_right(rhs, stride, lane)
        high_e = from_right(link, stride, lane)
        inv = [inverse(d) for d in diagonal]
        w = [q * e for q, e in zip(inv, link)]
        low_d = from_left([e * v for e, v in zip(link, w)], stride, lane)
        low_r = from_left([r * v for r, v in zip(rhs, w)], stride, lane)
        by = [e * q for e, q in zip(link, from_right(inv, stride, lane))]
        diagonal = [diagonal[c] - low_d[c] - link[c] * by[c] for c in range(count)]
        rhs = [rhs[c] + low_r[c] + by[c] * high_r[c] for c in range(count)]
        link = [by[c] * high_e[c] for c in range(count)]
        stride *= 2
    return solve_chunks(diagonal, link, rhs)


def pack_pair(a, b, odd_lane):
    even = [jnp.where(odd_lane, pltpu.roll(x, 1, 1), y) for x, y in zip(a, b)]
    odd = [jnp.where(odd_lane, x, pltpu.roll(y, LANES - 1, 1)) for x, y in zip(a, b)]
    return even, odd


def unpack_pair(even, odd, odd_lane):
    a = [jnp.where(odd_lane, y, pltpu.roll(x, LANES - 1, 1)) for x, y in zip(even, odd)]
    b = [jnp.where(odd_lane, pltpu.roll(y, 1, 1), x) for x, y in zip(even, odd)]
    return a, b


def solve_x_pair(g_pair, rhs_pair, lane):
    odd_lane = (lane & 1) == 1
    first_cell = lane < 2
    last_cell = lane >= LANES - 2
    half = 0.5 * weight
    g_even, g_odd = pack_pair(*g_pair, odd_lane)
    r_even, r_odd = pack_pair(*rhs_pair, odd_lane)
    face = [half * (a + b) for a, b in zip(g_even, g_odd)]
    after = from_right(g_even, 2, lane)
    after[-1] = jnp.where(last_cell, g_odd[-1], after[-1])
    face_after = [half * (a + b) for a, b in zip(g_odd, after)]
    face_before = from_left(face_after, 2, lane)
    face_before[0] = jnp.where(first_cell, weight * g_even[0], face_before[0])
    inv = [inverse(1.0 + (a + b)) for a, b in zip(face_before, face)]
    d_odd = [1.0 + (a + b) for a, b in zip(face, face_after)]
    link = list(face_after)
    link[-1] = jnp.where(last_cell, 0.0, link[-1])
    link_before = list(face_before)
    link_before[0] = jnp.where(first_cell, 0.0, link_before[0])
    t = [q * r for q, r in zip(inv, r_even)]
    w = [q * e for q, e in zip(inv, face)]
    next_q = from_right(inv, 2, lane)
    next_t = from_right(t, 2, lane)
    next_w = from_right(w, 2, lane)
    diagonal = [
        d - e * v - l * (l * q) for d, e, v, l, q in zip(d_odd, face, w, link, next_q)
    ]
    rhs = [r + e * v + l * n for r, e, v, l, n in zip(r_odd, face, t, link, next_t)]
    x_odd = reduce_lanes(diagonal, [l * n for l, n in zip(link, next_w)], rhs, lane, 2)
    x_before = from_left(x_odd, 2, lane)
    x_even = [
        v + q * (l * b) + u * x for v, q, l, b, u, x in zip(t, inv, link_before, x_before, w, x_odd)
    ]
    return unpack_pair(x_even, x_odd, odd_lane)


def pack_kernel(
    field_ref, index_ref, amp_ref, phase_ref,
    packed_ref, both_ref,
    index_in, amp_in, phase_in, sems,
):
    width = both_ref.shape[0] // 2
    last = field_ref.shape[0] - width
    pairs = (
        (index_ref, index_in),
        (amp_ref, amp_in),
        (phase_ref, phase_in),
        (field_ref.at[pl.ds(0, width)], both_ref.at[pl.ds(0, width)]),
        (field_ref.at[pl.ds(last, width)], both_ref.at[pl.ds(width, width)]),
    )
    copies = [pltpu.make_async_copy(a, b, sems.at[n]) for n, (a, b) in enumerate(pairs)]
    for copy in copies:
        copy.start()
    for copy in copies[:3]:
        copy.wait()
    row = lax.broadcasted_iota(jnp.int32, packed_ref.shape, 0)
    lane = lax.broadcasted_iota(jnp.int32, packed_ref.shape, 1)
    total = jnp.zeros(packed_ref.shape, f32)
    for m in range(index_in.shape[0]):
        waves = [index_in[m, n].astype(f32) for n in range(3)]
        for place, value in enumerate((*waves, phase_in[m], amp_in[m])):
            total = jnp.where((row == m) & (lane == place), value, total)
    packed_ref[...] = total
    for copy in copies[3:]:
        copy.wait()


def row_kernel(field_ref, step_ref, table_ref, inner_ref, outer_ref, step_in, sems):
    width = inner_ref.shape[0]
    pairs = (
        (step_ref, step_in),
        (field_ref.at[pl.ds(field_ref.shape[0] - width, width)], inner_ref),
        (field_ref.at[pl.ds(0, width)], outer_ref),
    )
    copies = [pltpu.make_async_copy(a, b, sems.at[n]) for n, (a, b) in enumerate(pairs)]
    for copy in copies:
        copy.start()
    for copy in copies:
        copy.wait()
    table_ref[...] = jnp.full(table_ref.shape, step_in[0].astype(f32), f32)


def load_kernel(sizes, field_ref, conduct_ref, field_out, turned_ref, conduct_in, sems):
    rows, layers, chunks, row_total, layer_total, column_total = sizes
    width = layers * chunks
    copies = (
        pltpu.make_async_copy(field_ref, field_out, sems.at[0]),
        pltpu.make_async_copy(conduct_ref, conduct_in, sems.at[1]),
    )
    for copy in copies:
        copy.start()
    for n, (copy, ref) in enumerate(zip(copies, (field_out, conduct_in))):
        copy.wait()
        for place in range(width):
            spot = (n * width + place) * rows
            turned_ref[spot : spot + rows] = ref[pl.ds(place, rows, stride=width), :]


def block_factors(face):
    inv, scaled, chain, u = [], [], [], []
    rows = len(face) - 1
    rest = 1.0 + face[0]
    for j in range(rows):
        inv.append(inverse(rest + face[j + 1]))
        scaled.append(face[j] * inv[j])
        chain.append(face[j + 1] * inv[j])
        u.append(scaled[j] * u[-1] if j else scaled[j])
        rest = 1.0 + rest * chain[j]
    v = list(chain)
    for j in range(rows - 2, -1, -1):
        u[j] = u[j] + chain[j] * u[j + 1]
        v[j] = chain[j] * v[j + 1]
    return inv, scaled, chain, u, v


def height_kernel(sizes, handed_ref, came_ref, heights_ref):
    rows, layers, chunks, row_total, layer_total, column_total = sizes
    odd = lax.rem(lax.axis_index("wide"), 2) == 1
    first = 2 * layers * chunks
    own, other = handed_ref[first:], came_ref[first:]
    modes = jnp.where(odd, own, other)
    step = jnp.where(odd, other, own)
    body = height_lines(modes, step, 0, row_total, row_total, chunks, column_total)
    heights_ref[chunks : (row_total + 1) * chunks] = body
    heights_ref[0:chunks] = body[0:chunks]
    heights_ref[(row_total + 1) * chunks : (row_total + 2) * chunks] = body[
        (row_total - 1) * chunks : row_total * chunks
    ]

def main_kernel(
    sizes, handed_ref, both_ref, below_ref, came_ref, turned_ref,
    sent_ref, p_ref, u_ref, v_ref, gain_ref, joint_ref,
    heights, halo, solved,
):
    rows, layers, chunks, row_total, layer_total, column_total = sizes
    width = layers * chunks
    blocks = row_total // rows
    me = lax.axis_index("wide")
    first_layer = lax.axis_index("grp") * layers
    zeta = [
        ((first_layer + k).astype(f32) + 0.5) * (1.0 / layer_total) for k in range(layers)
    ]
    half = 0.5 * weight
    height_kernel(sizes, handed_ref, came_ref, heights)
    own_start = pl.multiple_of(me * (rows * chunks), 8)

    def face(low, high):
        both = heights[pl.ds(low, chunks), :] + heights[pl.ds(high, chunks), :]
        return jnp.concatenate([weight + (half * z) * both for z in zeta], 0)

    def aligned(index):
        return pl.multiple_of(index, 8)

    inv, scaled, chain, u, v = block_factors(
        [face(own_start + j * chunks, own_start + (j + 1) * chunks) for j in range(rows + 1)]
    )
    for j in range(rows):
        u_ref[j * width : (j + 1) * width] = u[j]
        v_ref[j * width : (j + 1) * width] = v[j]

    def one_block(n, carry):
        passed, link, left_link = carry
        upward = n < me
        b = jnp.where(upward, n, blocks - 1 - (n - me))
        start = b * (rows * chunks) + jnp.where(upward, 0, (rows + 1) * chunks)
        step = jnp.where(upward, chunks, -chunks)
        places = [aligned(start + j * step) for j in range(rows + 2)]
        first = face(places[0], places[1])
        anew = (n == 0) | (n == me)
        left_link = jnp.where(n == me, link, left_link)
        passed = jnp.where(anew, first, passed)
        for j in range(rows):
            after = face(places[j + 1], places[j + 2])
            one_inv = inverse(passed + (1.0 + after))
            link = after * one_inv
            through = through * link if j else link
            passed = ((1.0 + passed) * after) * one_inv
        gain_ref[pl.ds(aligned(b * width), width), :] = through * (first * inverse(after))
        return passed, link, left_link

    gain_ref[pl.ds(aligned(me * width), width), :] = u[-1]
    nothing = 0.0 * u[0]
    carry = (nothing, nothing, nothing)
    if blocks <= 8:
        for n in range(blocks - 1):
            carry = one_block(n, carry)
    else:
        carry = lax.fori_loop(0, blocks - 1, one_block, carry)
    _, link, left_link = carry
    left_link = jnp.where(me == blocks - 1, link, left_link)
    right_link = jnp.where(me == blocks - 1, 0.0, link)

    a = 1.0 - left_link * u[0]
    b = left_link * v[0]
    c = right_link * u[-1]
    d = 1.0 - right_link * v[-1]
    by = inverse(a * d - b * c)
    joint = (
        u[-1] * inverse(a) * left_link, v[0] * inverse(d) * right_link,
        left_link, right_link, d * by, b * by, c * by, a * by,
    )
    for n, value in enumerate(joint):
        joint_ref[n * width : (n + 1) * width] = value

    odd = lax.rem(me, 2) == 1
    below = jnp.where(odd, came_ref[width : 2 * width], below_ref[...])
    above = jnp.where(odd, came_ref[0:width], both_ref[0:width])
    halo[0:width] = jnp.where(me == 0, 0.0, below)
    halo[width : 2 * width] = jnp.where(me == blocks - 1, 0.0, above)
    lane = lax.broadcasted_iota(jnp.int32, (rows, LANES), 1)
    row = lax.broadcasted_iota(jnp.int32, (rows, LANES), 0)

    def neighbours(values, low, high):
        return (
            jnp.where(row == 0, low, pltpu.roll(values, 1, 0)),
            jnp.where(row == rows - 1, high, pltpu.roll(values, rows - 1, 0)),
        )

    g = [[] for _ in range(layers)]
    f = [[] for _ in range(layers)]
    rhs = [[] for _ in range(layers)]
    for c in range(chunks):
        h = heights[pl.ds(own_start + chunks + c, rows, stride=chunks), :]
        h_low, h_high = neighbours(
            h,
            heights[pl.ds(own_start + c, 1), :],
            heights[pl.ds(own_start + (rows + 1) * chunks + c, 1), :],
        )
        low_sum, high_sum = h + h_low, h + h_high
        for k in range(layers):
            place = c * layers + k
            f_mid = turned_ref[place * rows : (place + 1) * rows]
            f_low, f_high = neighbours(
                f_mid, halo[pl.ds(place, 1), :], halo[pl.ds(width + place, 1), :]
            )
            g[k].append(
                turned_ref[(width + place) * rows : (width + place + 1) * rows] * (1.0 + zeta[k] * h)
            )
            f[k].append(f_mid)
            along = (weight + (half * zeta[k]) * high_sum) * (f_high - f_mid) - (
                weight + (half * zeta[k]) * low_sum
            ) * (f_mid - f_low)
            rhs[k].append(2.0 * (f_mid + along))
    for k in range(0, layers, 2):
        both = solve_x_pair(g[k : k + 2], rhs[k : k + 2], lane)
        for n in range(2):
            for c in range(chunks):
                spot = pl.ds((k + n) * chunks + c, rows, stride=width)
                solved[spot, :] = both[n][c] - 2.0 * f[k + n][c]

    def part(ref, j):
        return ref[j * width : (j + 1) * width]

    p = [part(solved, 0) * inv[0]]
    for j in range(1, rows):
        p.append(part(solved, j) * inv[j] + scaled[j] * p[-1])
    for j in range(rows - 2, -1, -1):
        p[j] = p[j] + chain[j] * p[j + 1]
    for j in range(rows):
        p_ref[j * width : (j + 1) * width] = p[j]

    upward = p[-1] + part(joint_ref, 0) * p[0]
    downward = p[0] + part(joint_ref, 1) * p[-1]
    for b in range(blocks):
        sent_ref[b * width : (b + 1) * width] = jnp.where(b > me, upward, downward)


def last_kernel(
    sizes, came_ref, gain_ref, joint_ref, p_ref, u_ref, v_ref, field_ref,
    out_ref,
):
    rows, layers, chunks, row_total, layer_total, column_total = sizes
    width = layers * chunks
    blocks = row_total // rows
    me = lax.axis_index("wide")

    def part(ref, b):
        return ref[b * width : (b + 1) * width]

    left = jnp.zeros((width, LANES), f32)
    right = jnp.zeros((width, LANES), f32)
    for b in range(blocks - 1):
        left = jnp.where(b < me, part(came_ref, b) + part(gain_ref, b) * left, left)
        b = blocks - 1 - b
        right = jnp.where(b > me, part(came_ref, b) + part(gain_ref, b) * right, right)

    y = left + part(joint_ref, 2) * part(p_ref, 0)
    z = right + part(joint_ref, 3) * part(p_ref, rows - 1)
    before = part(joint_ref, 4) * y + part(joint_ref, 5) * z
    after = part(joint_ref, 6) * y + part(joint_ref, 7) * z
    for j in range(rows):
        x = part(p_ref, j) + part(u_ref, j) * before + part(v_ref, j) * after
        for k in range(layers):
            spot = pl.ds(j * width + k, chunks, stride=layers)
            out_ref[spot, :] = field_ref[spot, :] + x[k * chunks : (k + 1) * chunks]


def on_device(field, conduct, mode_index, mode_amp, mode_phase, step_index):
    rows, layers, columns = field.shape
    wide_count = lax.axis_size("wide")
    row_total = rows * wide_count
    grp_count = lax.axis_size("grp")
    layer_total = layers * grp_count
    chunks = columns // LANES
    width = layers * chunks
    sizes = (rows, layers, chunks, row_total, layer_total, columns)
    limit = pltpu.CompilerParams(vmem_limit_bytes=16 * 1024 * 1024)
    hbm = pl.BlockSpec(memory_space=pltpu.HBM)

    def lines(count):
        return jax.ShapeDtypeStruct((count * width, LANES), f32)

    place = lax.axis_index("wide")
    odd = place % 2 == 1
    swaps = [(i, i ^ 1) for i in range(wide_count)]
    cores = [list(range(n, wide_count, 2)) for n in range(2)]
    table_shape = (grp_count * mode_index.shape[0], LANES)
    packed_shape = (mode_index.shape[0], LANES)
    in_hbm = lambda arrays: [pltpu.with_memory_space_constraint(a, pltpu.HBM) for a in arrays]

    def pack_modes(*arrays):
        return pl.pallas_call(
            pack_kernel,
            out_shape=(jax.ShapeDtypeStruct(packed_shape, f32), lines(2)),
            in_specs=[hbm] * 4,
            scratch_shapes=[pltpu.SMEM(a.shape, a.dtype) for a in arrays[1:]]
            + [pltpu.SemaphoreType.DMA((5,))],
            compiler_params=limit,
        )(*in_hbm(arrays))

    def pack_nothing(*arrays):
        return jnp.zeros(packed_shape, f32), jnp.zeros((2 * width, LANES), f32)

    packed, both = lax.cond(
        odd, pack_modes, pack_nothing, to_lines(field), mode_index, mode_amp, mode_phase
    )
    both_came = lax.ppermute(both, "wide", swaps)

    def gather_modes(own, *arrays):
        empty = jnp.zeros((width, LANES), f32)
        return lax.all_gather(own, "grp", axis=0, tiled=True), empty, empty

    def load_rows(own, *arrays):
        return pl.pallas_call(
            row_kernel,
            out_shape=(jax.ShapeDtypeStruct(table_shape, f32), lines(1), lines(1)),
            in_specs=[hbm] * 2,
            scratch_shapes=[
                pltpu.SMEM(step_index.shape, step_index.dtype),
                pltpu.SemaphoreType.DMA((3,)),
            ],
            compiler_params=limit,
        )(*in_hbm(arrays))

    table, inner, outer = lax.cond(
        odd, gather_modes, load_rows, packed, to_lines(field), step_index
    )
    table, inner, outer, both_came = lax.optimization_barrier((table, inner, outer, both_came))

    def gather_rows(own, came):
        rows_sent = jnp.concatenate([own, came[width:]], 0)
        rows_all = lax.all_gather(rows_sent, "wide", axis_index_groups=cores, axis=0)
        chip = place // 2
        below = lax.dynamic_index_in_dim(rows_all, jnp.maximum(chip - 1, 0), 0, False)
        above = lax.dynamic_index_in_dim(
            rows_all, jnp.minimum(chip + 1, wide_count // 2 - 1), 0, False
        )
        return below[width:], above[:width]

    def no_rows(own, came):
        return jnp.zeros_like(own), jnp.zeros_like(own)

    below, above = lax.cond(odd, no_rows, gather_rows, outer, both_came)
    handed = jnp.concatenate([above, inner, table], 0)
    came = lax.ppermute(handed, "wide", swaps)
    handed, field, conduct = lax.optimization_barrier((handed, field, conduct))
    field_lines, turned = pl.pallas_call(
        functools.partial(load_kernel, sizes),
        out_shape=(lines(rows), lines(2 * rows)),
        in_specs=[hbm] * 2,
        scratch_shapes=[
            pltpu.VMEM((rows * width, LANES), f32),
            pltpu.SemaphoreType.DMA((2,)),
        ],
        compiler_params=limit,
    )(
        *(
            pltpu.with_memory_space_constraint(to_lines(a), pltpu.HBM)
            for a in (field, conduct)
        )
    )
    sent, p, u, v, gain, joint = pl.pallas_call(
        functools.partial(main_kernel, sizes),
        out_shape=(lines(wide_count),)
        + (lines(rows),) * 3
        + (lines(wide_count), lines(8)),
        scratch_shapes=[
            pltpu.VMEM(((row_total + 2) * chunks, LANES), f32),
            pltpu.VMEM((2 * width, LANES), f32),
            pltpu.VMEM((rows * width, LANES), f32),
        ],
        compiler_params=limit,
    )(handed, both_came, below, came, turned)

    came = lax.all_to_all(
        sent.reshape(wide_count, width, LANES), "wide", split_axis=0, concat_axis=0
    ).reshape(wide_count * width, LANES)

    advanced = pl.pallas_call(
        functools.partial(last_kernel, sizes),
        out_shape=lines(rows),
        compiler_params=limit,
    )(came, gain, joint, p, u, v, field_lines)
    return from_lines(advanced, field.shape)


def solution(mesh):
    return jax.shard_map(
        on_device,
        mesh=mesh,
        in_specs=(
            P("wide", "grp", None),
            P("wide", "grp", None),
            P("grp", None),
            P("grp"),
            P("grp"),
            P(),
        ),
        out_specs=P("wide", "grp", None),
        check_vma=False,
    )
```
